32 devices in a mesh: gx: 8 (over y, x, core), gy: 4 (over z).
Axes of the slice: x: 2, y: 2, z: 4, core: 2. Of those that a mesh axis runs over, the one named last changes fastest.
Arguments:
- amplitude: bfloat16 [128, 128, 128], P('gx', 'gy'), may hold values from -6 to 6
- conv_first: bfloat16 [16, 1, 3, 3, 3], replicated, may hold values from -1.25 to 1.25
- conv_second: bfloat16 [16, 16, 3, 3, 3], replicated, may hold values from -0.4375 to 0.4375
- conv_third: bfloat16 [16, 16, 3, 3, 3], replicated, may hold values from -0.4375 to 0.4375
- conv_last: bfloat16 [1, 16, 3, 3, 3], replicated, may hold values from -0.875 to 0.875
Outputs:
- fault: bfloat16 [128, 128, 128], P('gx', 'gy')
- shift_field: float32 [128, 128, 128], P(('gx', 'gy'))
The draws below stay inside these ranges and needn't reach their ends.
All inputs are finite; a program needn't handle non-finite values.
Results may differ from the reference program's by a relative error of at most 0.0064.
Values may be sent and summed in bfloat16 or wider, within the bound.
No kernel may reach another device: no remote copies, remote signals or barrier semaphores. Data moves between devices by JAX's collectives and lax.ppermute only.
A program may use at most 192 MiB of HBM per device.

```python
import math
import jax
import jax.numpy as jnp
from jax import lax

CH = 16
CX = 16
NT = 128
ITERS = 3
NX = 128
NY = 128
N_GY = 4


def draw_amplitude(key, part):
    key = jax.random.fold_in(key, 11)
    keys = jax.random.split(key, 6)
    region_rows = CX // N_GY
    regions = NX // region_rows
    low_log, high_log = (-2.5, 0.3)
    noise = jax.random.normal(keys[5], (NX, NY, NT), jnp.float32)
    wave_gain, wave_noise = (1.2, 0.35)
    levels = jnp.exp(jax.random.uniform(keys[0], (regions,), jnp.float32, low_log, high_log))
    layered = jax.random.randint(keys[1], (regions,), 0, 2).astype(jnp.float32)
    signs = jnp.where(jnp.arange(regions, dtype=jnp.int32) % 2 == 0, 1.0, -1.0).astype(jnp.float32)
    dip_x = jax.random.uniform(keys[2], (regions,), jnp.float32, 0.3, 1.2) * signs
    dip_y = jax.random.uniform(keys[3], (regions,), jnp.float32, -0.8, 0.8)
    phases = jax.random.uniform(keys[4], (regions,), jnp.float32, -math.pi, math.pi)
    row_level = jnp.repeat(levels, region_rows, total_repeat_length=NX)
    row_layered = jnp.repeat(layered, region_rows, total_repeat_length=NX)
    row_dip_x = jnp.repeat(dip_x, region_rows, total_repeat_length=NX)
    row_dip_y = jnp.repeat(dip_y, region_rows, total_repeat_length=NX)
    row_phase = jnp.repeat(phases, region_rows, total_repeat_length=NX)
    local_x = (jnp.arange(NX, dtype=jnp.int32) % region_rows).astype(jnp.float32)
    cross = (jnp.arange(NY, dtype=jnp.int32) % 64).astype(jnp.float32)
    times = jnp.arange(NT, dtype=jnp.float32)
    argument = times[None, None, :] - row_dip_x[:, None, None] * local_x[:, None, None] - row_dip_y[:, None, None] * cross[None, :, None]
    wave = jnp.sin(argument * (2.0 * math.pi / 8.0) + row_phase[:, None, None])
    structured = wave_gain * wave + wave_noise * noise
    mixed = row_layered[:, None, None] * structured + (1.0 - row_layered[:, None, None]) * noise
    values = jnp.clip(row_level[:, None, None] * mixed, -6.0, 6.0)
    return values.astype(jnp.bfloat16)


def gaussian(rng, extent, width, limit, kind=jnp.bfloat16):
    return jnp.clip(width * jax.random.normal(rng, extent, jnp.float32), -limit, limit).astype(kind)


def setup_inputs(seed: int = 0) -> dict:
    key_of = jax.random.split(jax.random.key(seed), 6)
    return {
        "amplitude": draw_amplitude(jax.random.fold_in(key_of[5], 71), 0),
        "conv_first": gaussian(key_of[1], (CH, 1, 3, 3, 3), 27 ** -0.5, 1.25),
        "conv_second": gaussian(key_of[2], (CH, CH, 3, 3, 3), (27 * CH // 2) ** -0.5, 0.4375),
        "conv_third": gaussian(key_of[3], (CH, CH, 3, 3, 3), (27 * CH // 2) ** -0.5, 0.4375),
        "conv_last": gaussian(key_of[4], (1, CH, 3, 3, 3), (27 * CH // 8) ** -0.5, 0.875),
    }


MU_DIAG = 0.05
ETA_TIME = 0.5


def convolve(activation, weight):
    channels = weight.shape[0]
    padded = jnp.pad(activation, ((0, 0), (1, 1), (1, 1), (0, 0)))
    total_rows = activation.shape[1]
    block_rows = math.gcd(total_rows, 64)
    block_count = total_rows // block_rows

    def convolve_block(position):
        window = lax.dynamic_slice_in_dim(padded, position * block_rows, block_rows + 2, 1)
        result = lax.conv_general_dilated(window.astype(jnp.float32)[None], weight.astype(jnp.float32), (1, 1, 1), ((0, 0), (0, 0), (1, 1)), dimension_numbers=("NCDHW", "OIDHW", "NCDHW"), precision=lax.Precision.HIGHEST)
        return result[0]

    blocks = lax.map(convolve_block, jnp.arange(block_count, dtype=jnp.int32))
    return jnp.transpose(blocks, (1, 0, 2, 3, 4)).reshape(channels, total_rows, activation.shape[2], activation.shape[3])


def smooth(values):
    values = 0.25 * values[:-2] + 0.5 * values[1:-1] + 0.25 * values[2:]
    values = 0.25 * values[:, :-2] + 0.5 * values[:, 1:-1] + 0.25 * values[:, 2:]
    return 0.25 * values[:, :, :-2] + 0.5 * values[:, :, 1:-1] + 0.25 * values[:, :, 2:]


def slopes(widened):
    field = widened.astype(jnp.float32)
    grad_x = (field[2:, 1:-1, 1:-1] - field[:-2, 1:-1, 1:-1]) * 0.5
    grad_y = (field[1:-1, 2:, 1:-1] - field[1:-1, :-2, 1:-1]) * 0.5
    grad_t = (field[1:-1, 1:-1, 2:] - field[1:-1, 1:-1, :-2]) * 0.5
    tensor_xt = smooth(grad_x * grad_t)
    tensor_yt = smooth(grad_y * grad_t)
    tensor_tt = smooth(grad_t * grad_t)
    tensor_xx = smooth(grad_x * grad_x)
    tensor_yy = smooth(grad_y * grad_y)
    denominator = tensor_tt + 0.25 * (tensor_xx + tensor_yy) + 0.05
    return -tensor_xt / denominator, -tensor_yt / denominator


def harmonic(centre, neighbour):
    return 2.0 * centre * neighbour / (centre + neighbour)


def assemble(fields_wide):
    weight_wide = fields_wide[0]
    slope_x_wide = fields_wide[1]
    slope_y_wide = fields_wide[2]
    centre = weight_wide[1:-1, 1:-1]
    upper_x = harmonic(centre, weight_wide[2:, 1:-1])
    lower_x = harmonic(centre, weight_wide[:-2, 1:-1])
    upper_y = harmonic(centre, weight_wide[1:-1, 2:])
    lower_y = harmonic(centre, weight_wide[1:-1, :-2])
    own_x = slope_x_wide[1:-1, 1:-1]
    own_y = slope_y_wide[1:-1, 1:-1]
    right_side = 0.5 * (lower_x * (own_x + slope_x_wide[:-2, 1:-1]) - upper_x * (own_x + slope_x_wide[2:, 1:-1])
                        + lower_y * (own_y + slope_y_wide[1:-1, :-2]) - upper_y * (own_y + slope_y_wide[1:-1, 2:]))
    samples = centre.shape[2]
    positions = jnp.arange(samples, dtype=jnp.int32)
    time_count = (jnp.where(positions > 0, 1.0, 0.0) + jnp.where(positions < samples - 1, 1.0, 0.0)).astype(jnp.float32)
    diagonal = MU_DIAG + ETA_TIME * time_count + upper_x + lower_x + upper_y + lower_y
    return right_side, diagonal, (upper_x, lower_x, upper_y, lower_y), time_count


def apply_operator(search_wide, couplings, time_count):
    upper_x, lower_x, upper_y, lower_y = couplings
    centre = search_wide[1:-1, 1:-1]
    time_wide = jnp.pad(centre, ((0, 0), (0, 0), (1, 1)))
    result = (MU_DIAG + ETA_TIME * time_count) * centre - ETA_TIME * (time_wide[:, :, 2:] + time_wide[:, :, :-2])
    result = result + upper_x * (centre - search_wide[2:, 1:-1]) + lower_x * (centre - search_wide[:-2, 1:-1])
    result = result + upper_y * (centre - search_wide[1:-1, 2:]) + lower_y * (centre - search_wide[1:-1, :-2])
    return result


def fault_probability(amplitude, conv_first, conv_second, conv_third, conv_last):
    activation = amplitude[None]
    for weight in (conv_first, conv_second, conv_third):
        activation = jax.nn.relu(convolve(activation, weight)).astype(jnp.bfloat16)
    logit = convolve(activation, conv_last)[0]
    return jax.nn.sigmoid(logit).astype(jnp.bfloat16)


def reference(amplitude, conv_first, conv_second, conv_third, conv_last):
    fault = fault_probability(amplitude, conv_first, conv_second, conv_third, conv_last)
    slope_x, slope_y = slopes(jnp.pad(amplitude, 2))
    weight_field = 1.0 - 0.9 * fault.astype(jnp.float32)
    fields = jnp.stack([weight_field, slope_x, slope_y])
    fields_wide = jnp.pad(fields, ((0, 0), (1, 1), (1, 1), (0, 0)))
    right_side, diagonal, couplings, time_count = assemble(fields_wide)
    inverse = 1.0 / diagonal
    shift_field = jnp.zeros_like(right_side)
    residual = right_side
    precond = residual * inverse
    search = precond
    rz_now = jnp.sum(residual * precond)
    for iteration in range(ITERS):
        image = apply_operator(jnp.pad(search, ((1, 1), (1, 1), (0, 0))), couplings, time_count)
        step_size = rz_now / jnp.sum(search * image)
        shift_field = shift_field + step_size * search
        residual = residual - step_size * image
        precond = residual * inverse
        rz_next = jnp.sum(residual * precond)
        search = precond + (rz_next / rz_now) * search
        rz_now = rz_next
    return fault, shift_field
```

```python
import functools

import jax
import jax.numpy as jnp
from jax import lax
from jax.experimental import pallas as pl
from jax.experimental.pallas import tpu as pltpu
from jax.sharding import PartitionSpec as P

MU_DIAG = 0.05
ETA_TIME = 0.5

TX, NT, H = 16, 128, 8
CH = 16
XW = TX + 2 * H
BLK = 256
SUB = 16
PAD = SUB + NT + SUB

F32 = jnp.float32
BF16 = jnp.bfloat16


def iota(shape, dim):
    return lax.broadcasted_iota(jnp.int32, shape, dim)


def prep_kernel(w_ref, w1_ref, w2_ref, w3_ref, w4_ref):
    spread = jnp.where(iota((CH, BLK), 1) % CH == iota((CH, BLK), 0), 1.0, 0.0).astype(BF16)
    tiled = jnp.dot(w_ref[...], spread, preferred_element_type=F32)
    out_pos = iota((CH, BLK), 1) // CH
    for layer, ref in ((0, w2_ref), (1, w3_ref)):
        for dy in range(3):
            for dt in range(3):
                rows = [
                    tiled[(layer * 27 + dx * 9 + dy * 3 + dt) * CH :][:CH] for dx in range(3)
                ]
                for xi in range(16):
                    band = jnp.zeros((CH, BLK), F32)
                    for dx in range(3):
                        band = jnp.where(out_pos == xi - dx, rows[dx], band)
                    ref[dy * 3 + dt, xi * CH : (xi + 1) * CH, :] = band.astype(BF16)
    base = 2 * 27 * CH
    first = tiled[base : base + 32]
    last = tiled[base + 32 : base + 64]
    in_pos = iota((XW, BLK), 0)
    lane_pos = iota((XW, BLK), 1) // CH
    for dt in range(3):
        for yi in range(4):
            for yo in range(2):
                for blk in range(2):
                    band = jnp.zeros((XW, BLK), F32)
                    dy = yi - yo
                    if 0 <= dy <= 2:
                        for dx in range(3):
                            tap = dx * 9 + dy * 3 + dt
                            band = jnp.where(
                                in_pos - 14 * blk - lane_pos == dx, first[tap : tap + 1], band
                            )
                    w1_ref[
                        dt * 128 + yi * XW : dt * 128 + (yi + 1) * XW,
                        yo * 512 + blk * BLK : yo * 512 + (blk + 1) * BLK,
                    ] = band.astype(BF16)
    for dy in range(3):
        for dt in range(3):
            for blk in range(2):
                band = jnp.zeros((XW, BLK), F32)
                for dx in range(3):
                    tap = dx * 9 + dy * 3 + dt
                    band = jnp.where(
                        14 * blk + lane_pos + 4 - in_pos == dx, last[tap : tap + 1], band
                    )
                band = jnp.where(lane_pos < 14 - 2 * blk, band, 0.0)
                row = (dy * 3 + dt) * XW
                w4_ref[row : row + XW, blk * BLK : (blk + 1) * BLK] = band.astype(BF16)


def main_kernel(
    grid_x,
    grid_y,
    ty,
    pos_ref,
    amp_ref,
    xlow_ref,
    xhigh_ref,
    ylow_ref,
    yhigh_ref,
    w1_ref,
    w2_ref,
    w3_ref,
    w4_ref,
    fault_ref,
    waves_ref,
    mom_ref,
    raw,
    amp,
    act1,
    act2,
    act3,
    part,
    logit,
    prod,
    slope,
    weight,
    face,
    flux,
    inv,
    wave,
    stage,
):
    x0 = pos_ref[0]
    y0 = pos_ref[1]
    yw = ty + 2 * H
    nf = ty + 8
    dot = functools.partial(jnp.dot, preferred_element_type=F32)

    def dot_nt(a, b):
        return lax.dot_general(a, b, (((1,), (1,)), ((), ())), preferred_element_type=F32)

    def inside_y(y):
        at = y0 + y
        return jnp.where((at >= 0) & (at < grid_y), 1.0, 0.0).astype(F32)

    def lane_mask(start):
        masks = []
        for blk in range(2):
            at = x0 + start + 14 * blk + iota((1, BLK), 1) // CH
            masks.append(jnp.where((at >= 0) & (at < grid_x), 1.0, 0.0).astype(F32))
        return masks

    for x in range(XW):
        row = x * yw
        if x < H:
            mid = xlow_ref[x]
        elif x < H + TX:
            mid = amp_ref[x - H]
        else:
            mid = xhigh_ref[x - H - TX]
        raw[row + H : row + H + ty, :] = mid.astype(F32)
        raw[row : row + H, :] = ylow_ref[x].astype(F32)
        raw[row + H + ty : row + yw, :] = yhigh_ref[x].astype(F32)

    def turn(y, carry):
        amp[y] = raw[pl.ds(y, XW, stride=yw), :]
        return carry

    lax.fori_loop(0, yw, turn, 0)
    amp[yw] = jnp.zeros((XW, NT), F32)
    amp[yw + 1] = jnp.zeros((XW, NT), F32)

    tiled_row = iota((NT, NT), 0)
    natural = tiled_row // SUB + (tiled_row % SUB) * 8
    to_tiles = jnp.concatenate(
        [
            jnp.where(iota((NT, NT), 1) == natural + dt - 1, 1.0, 0.0).astype(BF16)
            for dt in range(3)
        ],
        axis=0,
    )
    from_tiles = jnp.concatenate(
        [
            jnp.where(iota((NT, NT), 1) + dt - 1 == natural, 1.0, 0.0).astype(BF16)
            for dt in range(3)
        ],
        axis=0,
    )
    sub_row = iota((SUB, BLK), 0)

    def put(act, y, blk, values):
        act[y, blk, SUB : SUB + NT, :] = values.astype(BF16)
        before = jnp.where(sub_row == 0, 0.0, pltpu.roll(values[NT - SUB :], 1, 0))
        after = jnp.where(sub_row == SUB - 1, 0.0, pltpu.roll(values[:SUB], SUB - 1, 0))
        act[y, blk, 0:SUB, :] = before.astype(BF16)
        act[y, blk, SUB + NT :, :] = after.astype(BF16)

    mask1 = lane_mask(-7)

    def first(step, carry):
        pieces = []
        for half in range(2):
            y = step * 4 + half * 2
            rows = amp[pl.ds(y, 4)].reshape(4 * XW, NT).astype(BF16)
            turned = dot_nt(to_tiles, rows).astype(BF16)
            pieces.append(
                jnp.concatenate([turned[:NT], turned[NT : 2 * NT], turned[2 * NT :]], axis=1)
            )
        result = dot(jnp.concatenate(pieces, axis=0), w1_ref[...])
        for half in range(2):
            for yo in range(2):
                y = step * 4 + half * 2 + yo
                ok = inside_y(y - 7)
                for blk in range(2):
                    lane = yo * 512 + blk * BLK
                    values = result[half * NT : (half + 1) * NT, lane : lane + BLK]
                    put(act1, y, blk, jnp.maximum(values, 0.0) * (mask1[blk] * ok))
        return carry

    lax.fori_loop(0, yw // 4, first, 0)

    def layer(source, w_ref, y, count):
        taps = []
        for dy in range(3):
            for dt in range(3):
                part_in = source[pl.ds(y + dy, count), :, SUB * dt : SUB * dt + NT, :]
                taps.append(part_in.reshape(count * 2 * NT, BLK))
        return dot(jnp.concatenate(taps, axis=1), w_ref[...].reshape(9 * BLK, BLK))

    mask2 = lane_mask(-6)
    lane_half = iota((NT, 128), 1)

    def second(step, carry):
        y = step * 4
        result = layer(act1, w2_ref, y, 4)
        for row in range(4):
            ok = inside_y(y + row - 6)
            low = result[row * 2 * NT : row * 2 * NT + NT]
            high = result[row * 2 * NT + NT : (row + 1) * 2 * NT]
            moved = jnp.where(lane_half >= 96, pltpu.roll(high[:, :128], 96, 1), low[:, 128:])
            low = jnp.concatenate([low[:, :128], moved], axis=1)
            put(act2, y + row, 0, jnp.maximum(low, 0.0) * (mask2[0] * ok))
            put(act2, y + row, 1, jnp.maximum(high, 0.0) * (mask2[1] * ok))
        return carry

    lax.fori_loop(0, (ty + 12) // 4, second, 0)

    mask3 = lane_mask(-5)

    def third(step, carry):
        y = step * 3
        result = layer(act2, w3_ref, y, 3)
        for row in range(3):
            ok = inside_y(y + row - 5)
            for blk in range(2):
                at = (row * 2 + blk) * NT
                values = jnp.maximum(result[at : at + NT], 0.0) * (mask3[blk] * ok)
                act3[y + row, :, blk * BLK : (blk + 1) * BLK] = values.astype(BF16)
        return carry

    lax.fori_loop(0, (ty + 10) // 3, third, 0)

    def fourth(y, carry):
        part[y] = dot_nt(w4_ref[...], act3[y])
        return carry

    lax.fori_loop(0, ty + 10, fourth, 0)

    def order(step, carry):
        sums = []
        for row in range(4):
            y = step * 4 + row
            total = part[y, 0:96] + part[y + 1, 96:192] + part[y + 2, 192:288]
            sums.append(
                jnp.concatenate([total[0:32], total[32:64], total[64:96]], axis=1)
            )
        sums = jnp.concatenate(sums, axis=0)
        high = sums.astype(BF16)
        low = (sums - high.astype(F32)).astype(BF16)
        both = dot(jnp.concatenate([high, low], axis=0), from_tiles)
        values = both[: 4 * XW] + both[4 * XW :]
        prob = (1.0 / (1.0 + jnp.exp(-values))).astype(BF16).astype(F32)
        for row in range(4):
            logit[step * 4 + row] = prob[row * XW : (row + 1) * XW]
        return carry

    lax.fori_loop(0, nf // 4, order, 0)

    lane = iota((XW, NT), 1)
    first_lane = lane == 0
    last_lane = lane == NT - 1

    def up_x(v):
        return pltpu.roll(v, XW - 1, 0)

    def down_x(v):
        return pltpu.roll(v, 1, 0)

    def up_t(v, edge=0.0):
        return jnp.where(last_lane, edge, pltpu.roll(v, NT - 1, 1))

    def down_t(v, edge=0.0):
        return jnp.where(first_lane, edge, pltpu.roll(v, 1, 1))

    def smooth_xt(v, edge=0.0):
        v = 0.5 * v + 0.25 * (up_t(v, edge) + down_t(v, edge))
        return 0.5 * v + 0.25 * (up_x(v) + down_x(v))

    def products(i, carry):
        here = amp[i + 3]
        grad_x = 0.5 * (up_x(here) - down_x(here))
        grad_y = 0.5 * (amp[i + 4] - amp[i + 2])
        grad_t = 0.5 * (up_t(here) - down_t(here))
        prod[0, i] = smooth_xt(grad_x * grad_t)
        prod[1, i] = smooth_xt(grad_y * grad_t)
        energy = grad_t * grad_t + 0.25 * (grad_x * grad_x + grad_y * grad_y)
        prod[2, i] = smooth_xt(energy, 0.25 * here * here)
        return carry

    lax.fori_loop(0, ty + 10, products, 0)

    at_x = x0 - H + iota((XW, NT), 0)
    mask_x = jnp.where((at_x >= 0) & (at_x < grid_x), 1.0, 0.0).astype(F32)

    def fields(k, carry):
        sums = []
        for which in range(3):
            sums.append(
                0.5 * prod[which, k + 1] + 0.25 * (prod[which, k] + prod[which, k + 2])
            )
        scale = -1.0 / (sums[2] + 0.05)
        slope[0, k] = sums[0] * scale
        slope[1, k] = sums[1] * scale
        raw_weight = 1.0 - 0.9 * logit[k]
        weight[0, k] = raw_weight
        weight[1, k] = raw_weight * (mask_x * inside_y(k - 4))
        return carry

    lax.fori_loop(0, nf, fields, 0)

    def faces(k, carry):
        raw_weight = weight[0, k]
        masked = weight[1, k]
        face_x = 2.0 * masked * up_x(masked) / (raw_weight + up_x(raw_weight))
        face_y = 2.0 * masked * weight[1, k + 1] / (raw_weight + weight[0, k + 1])
        slope_x = slope[0, k]
        face[0, k] = face_x
        face[1, k] = face_y
        flux[0, k] = 0.5 * face_x * (slope_x + up_x(slope_x))
        flux[1, k] = 0.5 * face_y * (slope[1, k] + slope[1, k + 1])
        return carry

    lax.fori_loop(0, nf - 1, faces, 0)

    time_part = MU_DIAG + ETA_TIME * (
        jnp.where(first_lane, 0.0, 1.0) + jnp.where(last_lane, 0.0, 1.0)
    )
    own = slice(H, H + TX)

    def owned(k):
        return jnp.where((k >= 4) & (k < 4 + ty), 1.0, 0.0).astype(F32)

    def start(k, total):
        flux_x = flux[0, k]
        face_x = face[0, k]
        right = down_x(flux_x) - flux_x + flux[1, k - 1] - flux[1, k]
        inverse = 1.0 / (time_part + face_x + down_x(face_x) + face[1, k] + face[1, k - 1])
        first_wave = right * inverse
        inv[k] = inverse
        wave[0, k] = first_wave
        return total + owned(k) * (right * first_wave)[own]

    zero = jnp.zeros((TX, NT), F32)
    b0 = lax.fori_loop(1, nf - 1, start, zero)

    def apply(which, k):
        here = wave[which, k]
        face_x = face[0, k]
        flow = face_x * (here - up_x(here))
        image = time_part * here - ETA_TIME * (up_t(here) + down_t(here))
        image = image + flow - down_x(flow)
        image = image + face[1, k] * (here - wave[which, k + 1])
        return here, image + face[1, k - 1] * (here - wave[which, k - 1])

    def advance(which):
        def body(k, totals):
            here, image = apply(which, k)
            after = here - image * inv[k]
            wave[which + 1, k] = after
            ok = owned(k)
            return (
                totals[0] + ok * (here * image)[own],
                totals[1] + ok * (after * image)[own],
            )

        return body

    a0, a1 = lax.fori_loop(2, nf - 2, advance(0), (zero, zero))
    a2, a3 = lax.fori_loop(3, nf - 3, advance(1), (zero, zero))

    def finish(k, total):
        here, image = apply(2, k)
        return total + (here * image)[own]

    a4 = lax.fori_loop(4, nf - 4, finish, zero)

    sums = [jnp.sum(v, axis=0, keepdims=True) for v in (b0, a0, a1, a2, a3, a4)]
    mom_ref[...] = jnp.concatenate(sums + [jnp.zeros((2, NT), F32)], axis=0)

    def own_cells(source, put_x):
        def body(y, carry):
            stage[pl.ds(y, TX, stride=ty), :] = source(y)[own]
            return carry

        lax.fori_loop(0, ty, body, 0)
        for x in range(TX):
            put_x(x, stage[x * ty : (x + 1) * ty, :].astype(BF16))

    def put_fault(x, values):
        fault_ref[x] = values

    own_cells(lambda y: logit[y + 4], put_fault)
    rows = waves_ref.shape[2]
    for which in range(3):

        def put_wave(x, values, which=which):
            waves_ref[x // rows, which, x % rows] = values

        own_cells(lambda y, which=which: wave[which, y + 4], put_wave)


def combine_kernel(ty, mom_ref, waves_ref, out_ref):
    moments = jnp.sum(jnp.sum(mom_ref[...], axis=0), axis=1, keepdims=True)
    b0, a0, a1, a2, a3, a4 = [
        jnp.broadcast_to(moments[i : i + 1], (1, NT)) for i in range(6)
    ]
    a0, a1, a2, a3, a4 = [v / b0 for v in (a0, a1, a2, a3, a4)]
    l21 = a1 / a0
    l31 = a2 / a0
    d2 = jnp.maximum(a2 - l21 * a1, 1e-7 * a2 + 1e-30)
    l32 = (a3 - l21 * a2) / d2
    d3 = jnp.maximum(a4 - l31 * a2 - l32 * l32 * d2, 1e-7 * a4 + 1e-30)
    y2 = (1.0 - a0) - l21
    y3 = (1.0 - a0 - a1) - l31 - l32 * y2
    c3 = y3 / d3
    c2 = y2 / d2 - l32 * c3
    c1 = 1.0 / a0 - l21 * c2 - l31 * c3
    for block in range(waves_ref.shape[0]):
        for x in range(waves_ref.shape[2]):
            w0, w1, w2 = [waves_ref[block, which, x].astype(F32) for which in range(3)]
            out_ref[x, block * ty : (block + 1) * ty, :] = c1 * w0 + c2 * w1 + c3 * w2


def vmem(count):
    return [pl.BlockSpec(memory_space=pltpu.VMEM)] * count


def on_device(amplitude, conv_first, conv_second, conv_third, conv_last):
    n_gx, n_gy = lax.axis_size("gx"), lax.axis_size("gy")
    ty = amplitude.shape[1]
    grid_x, grid_y = n_gx * TX, n_gy * ty
    assert amplitude.shape == (TX, ty, NT)

    def shift(values, axis, count, step):
        pairs = [(i, i + step) for i in range(count) if 0 <= i + step < count]
        return lax.ppermute(values, axis, pairs)

    xlow = shift(amplitude[TX - H :], "gx", n_gx, 1)
    xhigh = shift(amplitude[:H], "gx", n_gx, -1)
    ylow = shift(
        jnp.concatenate([xlow[:, ty - H :], amplitude[:, ty - H :], xhigh[:, ty - H :]]),
        "gy",
        n_gy,
        1,
    )
    yhigh = shift(
        jnp.concatenate([xlow[:, :H], amplitude[:, :H], xhigh[:, :H]]), "gy", n_gy, -1
    )

    def by_tap(weight):
        return jnp.transpose(weight.reshape(weight.shape[0], -1, 27), (2, 1, 0))

    small = jnp.concatenate(
        [
            by_tap(conv_second).reshape(27 * CH, CH),
            by_tap(conv_third).reshape(27 * CH, CH),
            by_tap(conv_first).reshape(27, CH),
            jnp.zeros((5, CH), BF16),
            conv_last.reshape(CH, 27).T,
            jnp.zeros((5, CH), BF16),
        ],
        axis=0,
    )
    w1, w2, w3, w4 = pl.pallas_call(
        prep_kernel,
        out_shape=[
            jax.ShapeDtypeStruct((3 * 4 * XW, 4 * BLK), BF16),
            jax.ShapeDtypeStruct((9, BLK, BLK), BF16),
            jax.ShapeDtypeStruct((9, BLK, BLK), BF16),
            jax.ShapeDtypeStruct((9 * XW, 2 * BLK), BF16),
        ],
        in_specs=vmem(1),
        out_specs=vmem(4),
        compiler_params=pltpu.CompilerParams(vmem_limit_bytes=32 * 2**20),
        cost_estimate=pl.CostEstimate(flops=10**7, bytes_accessed=4 * 10**6, transcendentals=0),
        name="band_weights",
    )(small)

    position = jnp.stack([lax.axis_index("gx") * TX, lax.axis_index("gy") * ty])
    yw, nf = ty + 2 * H, ty + 8
    scratch = [
        pltpu.VMEM((XW * yw, NT), F32),
        pltpu.VMEM((yw + 2, XW, NT), F32),
        pltpu.VMEM((yw, 2, PAD, BLK), BF16),
        pltpu.VMEM((ty + 12, 2, PAD, BLK), BF16),
        pltpu.VMEM((ty + 10, NT, 2 * BLK), BF16),
        pltpu.VMEM((ty + 10, 9 * XW, NT), F32),
        pltpu.VMEM((nf, XW, NT), F32),
        pltpu.VMEM((3, ty + 10, XW, NT), F32),
        pltpu.VMEM((2, nf, XW, NT), F32),
        pltpu.VMEM((2, nf, XW, NT), F32),
        pltpu.VMEM((2, nf, XW, NT), F32),
        pltpu.VMEM((2, nf, XW, NT), F32),
        pltpu.VMEM((nf, XW, NT), F32),
        pltpu.VMEM((3, nf, XW, NT), F32),
        pltpu.VMEM((TX * ty, NT), F32),
    ]
    fault, waves, moments = pl.pallas_call(
        functools.partial(main_kernel, grid_x, grid_y, ty),
        out_shape=[
            jax.ShapeDtypeStruct((TX, ty, NT), BF16),
            jax.ShapeDtypeStruct((n_gy, 3, TX // n_gy, ty, NT), BF16),
            jax.ShapeDtypeStruct((8, NT), F32),
        ],
        in_specs=[pl.BlockSpec(memory_space=pltpu.SMEM)] + vmem(9),
        out_specs=vmem(3),
        scratch_shapes=scratch,
        compiler_params=pltpu.CompilerParams(vmem_limit_bytes=58 * 2**20),
        cost_estimate=pl.CostEstimate(
            flops=3 * 10**10, bytes_accessed=10**7, transcendentals=10**6
        ),
        name="fault_and_waves",
    )(position, amplitude, xlow, xhigh, ylow, yhigh, w1, w2, w3, w4)

    everyone = jnp.broadcast_to(moments[None], (n_gx * n_gy, 8, NT))
    moments = lax.all_to_all(everyone, ("gx", "gy"), split_axis=0, concat_axis=0, tiled=True)
    waves = lax.all_to_all(waves, "gy", split_axis=0, concat_axis=0, tiled=True)
    shift_field = pl.pallas_call(
        functools.partial(combine_kernel, ty),
        out_shape=jax.ShapeDtypeStruct((TX // n_gy, grid_y, NT), F32),
        in_specs=vmem(2),
        out_specs=pl.BlockSpec(memory_space=pltpu.VMEM),
        compiler_params=pltpu.CompilerParams(vmem_limit_bytes=16 * 2**20),
        name="combine_waves",
    )(moments, waves)
    return (fault, shift_field)


def solution(mesh):
    return jax.shard_map(
        on_device,
        mesh=mesh,
        in_specs=(P("gx", "gy", None), P(), P(), P(), P()),
        out_specs=(P("gx", "gy", None), P(("gx", "gy"), None, None)),
        check_vma=False,
    )
```

```python
import functools

import jax
import jax.numpy as jnp
from jax import lax
from jax.experimental import pallas as pl
from jax.experimental.pallas import tpu as pltpu
from jax.sharding import PartitionSpec as P

MU_DIAG = 0.05
ETA_TIME = 0.5

TX, NT, H = 16, 128, 8
CH = 16
XW = TX + 2 * H
FX = TX + 8
RX = 4
BLK = 256
SUB = 16
PAD = SUB + NT + SUB

F32 = jnp.float32
BF16 = jnp.bfloat16


def iota(shape, dim):
    return lax.broadcasted_iota(jnp.int32, shape, dim)


def dot_nt(a, b):
    return lax.dot_general(a, b, (((1,), (1,)), ((), ())), preferred_element_type=F32)


def prep_kernel(first_ref, second_ref, third_ref, last_ref, after_ref, w1_ref, w2_ref, w3_ref, w4_ref):
    del after_ref
    spread = jnp.where(iota((CH, BLK), 1) % CH == iota((CH, BLK), 0), 1.0, 0.0).astype(BF16)
    unit = jnp.where(iota((BLK, BLK), 1) == iota((BLK, BLK), 0), 1.0, 0.0).astype(BF16)
    in_pos = iota((CH, BLK), 1) // CH
    for source, ref in ((second_ref, w2_ref), (third_ref, w3_ref)):
        tiled = jnp.dot(source[...], spread, preferred_element_type=F32)
        for dy in range(3):
            for dt in range(3):
                rows = [tiled[(dx * 9 + dy * 3 + dt) * CH :][:CH] for dx in range(3)]
                bands = []
                for xo in range(16):
                    band = jnp.zeros((CH, BLK), F32)
                    for dx in range(3):
                        band = jnp.where(in_pos == xo + dx, rows[dx], band)
                    bands.append(band.astype(BF16))
                turned = dot_nt(unit, jnp.concatenate(bands, axis=0))
                ref[dy * 3 + dt] = turned.astype(BF16)

    def taps(ref):
        found = {}
        for dx in range(3):
            for dy in range(3):
                piece = ref[0, dx, dy].astype(BF16)
                tiled = jnp.dot(piece, spread, preferred_element_type=F32)
                for dt in range(3):
                    found[dx, dy, dt] = tiled[dt : dt + 1]
        return found

    first, last = taps(first_ref), taps(last_ref)
    row_pos = iota((XW, BLK), 0)
    lane_pos = iota((XW, BLK), 1) // CH
    for dt in range(3):
        for yi in range(4):
            for yo in range(2):
                for blk in range(2):
                    band = jnp.zeros((XW, BLK), F32)
                    dy = yi - yo
                    if 0 <= dy <= 2:
                        for dx in range(3):
                            band = jnp.where(
                                row_pos - 14 * blk - lane_pos == dx, first[dx, dy, dt], band
                            )
                    w1_ref[
                        dt * 128 + yi * XW : dt * 128 + (yi + 1) * XW,
                        yo * 512 + blk * BLK : yo * 512 + (blk + 1) * BLK,
                    ] = band.astype(BF16)
    row_pos = iota((FX, BLK), 0)
    lane_pos = iota((FX, BLK), 1) // CH
    for blk in range(2):
        pieces = []
        for dy in range(3):
            for dt in range(3):
                band = jnp.zeros((FX, BLK), F32)
                for dx in range(3):
                    band = jnp.where(14 * blk + lane_pos - row_pos == dx, last[dx, dy, dt], band)
                pieces.append(jnp.where(lane_pos < 14 - 2 * blk, band, 0.0))
        pieces = jnp.concatenate(pieces, axis=0)
        w4_ref[:, blk * BLK : (blk + 1) * BLK] = pieces.astype(BF16)


def main_kernel(
    grid_x,
    grid_y,
    ty,
    amp_ref,
    xlow_ref,
    xhigh_ref,
    ylow_ref,
    yhigh_ref,
    w1_ref,
    w2_ref,
    w3_ref,
    w4_ref,
    *refs,
):
    n_gy = grid_y // ty
    fault_ref, mom_ref = refs[:2]
    waves_refs = refs[2 : 2 + n_gy]
    (raw, amp, act1, act2, act3, part, prob, prod, slope, weight, face, flux, inv, wave) = refs[
        2 + n_gy :
    ]
    place_y = lax.axis_index("gy")
    x0 = lax.axis_index("gx") * TX
    y0 = place_y * ty
    yw = ty + 2 * H
    dot = functools.partial(jnp.dot, preferred_element_type=F32)

    def inside_y(y):
        at = y0 + y
        return jnp.where((at >= 0) & (at < grid_y), 1.0, 0.0).astype(F32)

    def lane_mask(start):
        masks = []
        for blk in range(2):
            at = x0 + start + 14 * blk + iota((1, BLK), 1) // CH
            masks.append(jnp.where((at >= 0) & (at < grid_x), 1.0, 0.0).astype(F32))
        return masks

    for x in range(XW):
        row = x * yw
        if x < H:
            mid = xlow_ref[x]
        elif x < H + TX:
            mid = amp_ref[x - H]
        else:
            mid = xhigh_ref[x - H - TX]
        raw[row + H : row + H + ty, :] = mid.astype(F32)
        raw[row : row + H, :] = ylow_ref[x].astype(F32)
        raw[row + H + ty : row + yw, :] = yhigh_ref[x].astype(F32)

    def turn(y, carry):
        amp[y] = raw[pl.ds(y, XW, stride=yw), :]
        return carry

    lax.fori_loop(0, yw, turn, 0, unroll=8)
    amp[yw] = jnp.zeros((XW, NT), F32)
    amp[yw + 1] = jnp.zeros((XW, NT), F32)

    tiled_row = iota((NT, NT), 0)
    natural = tiled_row // SUB + (tiled_row % SUB) * 8
    to_tiles = jnp.concatenate(
        [
            jnp.where(iota((NT, NT), 1) == natural + dt - 1, 1.0, 0.0).astype(BF16)
            for dt in range(3)
        ],
        axis=0,
    )
    from_tiles = jnp.concatenate(
        [
            jnp.where(iota((NT, NT), 1) + dt - 1 == natural, 1.0, 0.0).astype(BF16)
            for dt in range(3)
        ],
        axis=0,
    )
    sub_row = iota((SUB, BLK), 0)

    def put(act, y, blk, values):
        act[y, blk, SUB : SUB + NT, :] = values.astype(BF16)
        before = jnp.where(sub_row == 0, 0.0, pltpu.roll(values[NT - SUB :], 1, 0))
        after = jnp.where(sub_row == SUB - 1, 0.0, pltpu.roll(values[:SUB], SUB - 1, 0))
        act[y, blk, 0:SUB, :] = before.astype(BF16)
        act[y, blk, SUB + NT :, :] = after.astype(BF16)

    mask1 = lane_mask(-7)

    def first(step, carry):
        pieces = []
        for half in range(2):
            y = step * 4 + half * 2
            rows = amp[pl.ds(y, 4)].reshape(4 * XW, NT).astype(BF16)
            turned = dot_nt(to_tiles, rows).astype(BF16)
            pieces.append(
                jnp.concatenate([turned[:NT], turned[NT : 2 * NT], turned[2 * NT :]], axis=1)
            )
        result = dot(jnp.concatenate(pieces, axis=0), w1_ref[...])
        for half in range(2):
            for yo in range(2):
                y = step * 4 + half * 2 + yo
                ok = inside_y(y - 7)
                for blk in range(2):
                    lane = yo * 512 + blk * BLK
                    values = result[half * NT : (half + 1) * NT, lane : lane + BLK]
                    put(act1, y, blk, jnp.maximum(values, 0.0) * (mask1[blk] * ok))
        return carry

    lax.fori_loop(0, yw // 4, first, 0)

    def layer(source, w_ref, y, count):
        taps = []
        for dy in range(3):
            for dt in range(3):
                part_in = source[pl.ds(y + dy, count), :, SUB * dt : SUB * dt + NT, :]
                taps.append(part_in.reshape(count * 2 * NT, BLK))
        return dot(jnp.concatenate(taps, axis=1), w_ref[...].reshape(9 * BLK, BLK))

    mask2 = lane_mask(-6)
    lane_half = iota((NT, 128), 1)

    def second(step, carry):
        y = step * 4
        result = layer(act1, w2_ref, y, 4)
        for row in range(4):
            ok = inside_y(y + row - 6)
            low = result[row * 2 * NT : row * 2 * NT + NT]
            high = result[row * 2 * NT + NT : (row + 1) * 2 * NT]
            moved = jnp.where(lane_half >= 96, pltpu.roll(high[:, :128], 96, 1), low[:, 128:])
            low = jnp.concatenate([low[:, :128], moved], axis=1)
            put(act2, y + row, 0, jnp.maximum(low, 0.0) * (mask2[0] * ok))
            put(act2, y + row, 1, jnp.maximum(high, 0.0) * (mask2[1] * ok))
        return carry

    lax.fori_loop(0, (ty + 12) // 4, second, 0)

    mask3 = lane_mask(-5)

    def third(step, carry):
        y = step * 3
        result = layer(act2, w3_ref, y, 3)
        for row in range(3):
            ok = inside_y(y + row - 5)
            for blk in range(2):
                at = (row * 2 + blk) * NT
                values = jnp.maximum(result[at : at + NT], 0.0) * (mask3[blk] * ok)
                act3[y + row, :, blk * BLK : (blk + 1) * BLK] = values.astype(BF16)
        return carry

    lax.fori_loop(0, (ty + 10) // 3, third, 0)

    def fourth(step, carry):
        y = step * 3
        result = dot_nt(w4_ref[...], act3[pl.ds(y, 3)].reshape(3 * NT, 2 * BLK))
        for row in range(3):
            part[y + row] = result[:, row * NT : (row + 1) * NT]
        return carry

    lax.fori_loop(0, (ty + 10) // 3, fourth, 0)

    for x in range(FX):
        prob[x * yw : x * yw + H, :] = jnp.zeros((H, NT), F32)
        prob[(x + 1) * yw - H : (x + 1) * yw, :] = jnp.zeros((H, NT), F32)

    def order(step, carry):
        sums = []
        for row in range(8):
            y = step * 8 + row
            total = (
                part[y, 0 : 3 * FX] + part[y + 1, 3 * FX : 6 * FX] + part[y + 2, 6 * FX : 9 * FX]
            )
            sums.append(jnp.concatenate([total[i * FX : (i + 1) * FX] for i in range(3)], axis=1))
        sums = jnp.concatenate(sums, axis=0)
        high = sums.astype(BF16)
        low = (sums - high.astype(F32)).astype(BF16)
        both = dot(jnp.concatenate([high, low], axis=0), from_tiles)
        values = both[: 8 * FX] + both[8 * FX :]
        values = (1.0 / (1.0 + jnp.exp(-values))).astype(BF16).astype(F32)
        for row in range(8):
            prob[pl.ds(step * 8 + row + 4, FX, stride=yw), :] = values[row * FX : (row + 1) * FX]
        return carry

    lax.fori_loop(0, (ty + 8) // 8, order, 0)

    block = (RX, yw, NT)
    lane = iota(block, 2)
    first_lane = lane == 0
    last_lane = lane == NT - 1

    def up_y(v):
        return pltpu.roll(v, yw - 1, 1)

    def down_y(v):
        return pltpu.roll(v, 1, 1)

    def up_t(v, edge=0.0):
        return jnp.where(last_lane, edge, pltpu.roll(v, NT - 1, 2))

    def down_t(v, edge=0.0):
        return jnp.where(first_lane, edge, pltpu.roll(v, 1, 2))

    def smooth_yt(v, edge=0.0):
        v = 0.5 * v + 0.25 * (up_t(v, edge) + down_t(v, edge))
        return 0.5 * v + 0.25 * (up_y(v) + down_y(v))

    def amp_rows(x):
        return raw[pl.ds(pl.multiple_of(x * yw, 8), RX * yw), :].reshape(block)

    def products(step, carry):
        k = step * RX
        here = amp_rows(k + 3)
        grad_x = 0.5 * (amp_rows(k + 4) - amp_rows(k + 2))
        grad_y = 0.5 * (up_y(here) - down_y(here))
        grad_t = 0.5 * (up_t(here) - down_t(here))
        at = pl.ds(k, RX)
        prod[0, at] = smooth_yt(grad_x * grad_t)
        prod[1, at] = smooth_yt(grad_y * grad_t)
        energy = grad_t * grad_t + 0.25 * (grad_x * grad_x + grad_y * grad_y)
        prod[2, at] = smooth_yt(energy, 0.25 * here * here)
        return carry

    lax.fori_loop(0, (FX + 2 + RX - 1) // RX, products, 0)

    at_y = y0 - H + iota(block, 1)
    mask_y = (at_y >= 0) & (at_y < grid_y)

    def fields(step, carry):
        k = step * RX
        at = pl.ds(k + 1, RX)
        sums = []
        for which in range(3):
            before, here, after = [prod[which, pl.ds(k + i, RX)] for i in range(3)]
            sums.append(0.5 * here + 0.25 * (before + after))
        scale = -1.0 / (sums[2] + 0.05)
        slope[0, at] = sums[0] * scale
        slope[1, at] = sums[1] * scale
        rows = prob[pl.ds(pl.multiple_of(k * yw, 8), RX * yw), :].reshape(block)
        raw_weight = 1.0 - 0.9 * rows
        at_x = x0 - 4 + k + iota(block, 0)
        weight[0, at] = raw_weight
        weight[1, at] = jnp.where(mask_y & (at_x >= 0) & (at_x < grid_x), raw_weight, 0.0)
        return carry

    lax.fori_loop(0, FX // RX, fields, 0)
    for which in range(2):
        slope[which, FX + 1] = jnp.zeros((yw, NT), F32)
        weight[which, FX + 1] = jnp.full((yw, NT), 1.0 - which, F32)
        face[which, 0] = jnp.zeros((yw, NT), F32)
        flux[which, 0] = jnp.zeros((yw, NT), F32)

    def faces(step, carry):
        k = step * RX + 1
        at, after = pl.ds(k, RX), pl.ds(k + 1, RX)
        raw_weight = weight[0, at]
        masked = weight[1, at]
        face_x = 2.0 * masked * weight[1, after] / (raw_weight + weight[0, after])
        face_y = 2.0 * masked * up_y(masked) / (raw_weight + up_y(raw_weight))
        slope_y = slope[1, at]
        face[0, at] = face_x
        face[1, at] = face_y
        flux[0, at] = 0.5 * face_x * (slope[0, at] + slope[0, after])
        flux[1, at] = 0.5 * face_y * (slope_y + up_y(slope_y))
        return carry

    lax.fori_loop(0, FX // RX, faces, 0)

    time_part = MU_DIAG + ETA_TIME * (
        jnp.where(first_lane, 0.0, 1.0) + jnp.where(last_lane, 0.0, 1.0)
    )

    def owned(total, k, values):
        for row in range(RX):
            ok = (k + row >= 5) & (k + row < 5 + TX)
            total = total + jnp.where(ok, values[row, H : H + ty], 0.0)
        return total

    def start(step, total):
        k = step * RX + 1
        at, before = pl.ds(k, RX), pl.ds(k - 1, RX)
        flux_y = flux[1, at]
        face_y = face[1, at]
        right = flux[0, before] - flux[0, at] + down_y(flux_y) - flux_y
        inverse = 1.0 / (time_part + face[0, at] + face[0, before] + face_y + down_y(face_y))
        first_wave = right * inverse
        inv[at] = inverse
        wave[0, at] = first_wave
        return owned(total, k, right * first_wave)

    zero = jnp.zeros((ty, NT), F32)
    b0 = lax.fori_loop(0, FX // RX, start, zero)

    def apply(which, k):
        at, before, after = [pl.ds(k + i, RX) for i in (0, -1, 1)]
        here = wave[which, at]
        flow = face[1, at] * (here - up_y(here))
        image = time_part * here - ETA_TIME * (up_t(here) + down_t(here))
        image = image + flow - down_y(flow)
        image = image + face[0, at] * (here - wave[which, after])
        return here, image + face[0, before] * (here - wave[which, before])

    def advance(which):
        def body(step, totals):
            k = step * RX + 3
            here, image = apply(which, k)
            at = pl.ds(k, RX)
            after = here - image * inv[at]
            wave[which + 1, at] = after
            return owned(totals[0], k, here * image), owned(totals[1], k, after * image)

        return body

    steps = (FX - 4) // RX
    a0, a1 = lax.fori_loop(0, steps, advance(0), (zero, zero))
    a2, a3 = lax.fori_loop(0, steps, advance(1), (zero, zero))

    def finish(step, total):
        k = step * RX + 5
        here, image = apply(2, k)
        return owned(total, k, here * image)

    a4 = lax.fori_loop(0, TX // RX, finish, zero)

    sums = [jnp.sum(v, axis=0, keepdims=True) for v in (b0, a0, a1, a2, a3, a4)]
    mom_ref[...] = jnp.concatenate(sums + [jnp.zeros((2, NT), F32)], axis=0)

    for x in range(TX):
        fault_ref[x] = prob[(x + 4) * yw + H : (x + 4) * yw + H + ty, :].astype(BF16)
    rows = TX // n_gy
    for place, ref in enumerate(waves_refs):
        to = lax.rem(place_y + place, n_gy) * rows + 5
        for which in range(3):
            for row in range(rows):
                ref[which, row] = wave[which, to + row, H : H + ty, :].astype(BF16)


def combine_kernel(n_gy, ty, mom_ref, *refs):
    waves_refs, out_ref = refs[:n_gy], refs[n_gy]
    place_y = lax.axis_index("gy")
    moments = jnp.sum(jnp.sum(mom_ref[...], axis=0), axis=1, keepdims=True)
    b0, a0, a1, a2, a3, a4 = [
        jnp.broadcast_to(moments[i : i + 1], (1, NT)) for i in range(6)
    ]
    a0, a1, a2, a3, a4 = [v / b0 for v in (a0, a1, a2, a3, a4)]
    l21 = a1 / a0
    l31 = a2 / a0
    d2 = jnp.maximum(a2 - l21 * a1, 1e-7 * a2 + 1e-30)
    l32 = (a3 - l21 * a2) / d2
    d3 = jnp.maximum(a4 - l31 * a2 - l32 * l32 * d2, 1e-7 * a4 + 1e-30)
    y2 = (1.0 - a0) - l21
    y3 = (1.0 - a0 - a1) - l31 - l32 * y2
    c3 = y3 / d3
    c2 = y2 / d2 - l32 * c3
    c1 = 1.0 / a0 - l21 * c2 - l31 * c3
    for place, ref in enumerate(waves_refs):
        source = lax.rem(place_y - place + n_gy, n_gy)
        at = pl.ds(pl.multiple_of(source * ty, 8), ty)
        for x in range(ref.shape[1]):
            w0, w1, w2 = [ref[which, x].astype(F32) for which in range(3)]
            out_ref[x, at, :] = c1 * w0 + c2 * w1 + c3 * w2


def vmem(count):
    return [pl.BlockSpec(memory_space=pltpu.VMEM)] * count


def on_device(amplitude, conv_first, conv_second, conv_third, conv_last):
    n_gx, n_gy = lax.axis_size("gx"), lax.axis_size("gy")
    ty = amplitude.shape[1]
    grid_x, grid_y = n_gx * TX, n_gy * ty
    assert amplitude.shape == (TX, ty, NT)

    def shift(values, axis, count, step):
        pairs = [(i, i + step) for i in range(count) if 0 <= i + step < count]
        return lax.ppermute(values, axis, pairs)

    xlow = shift(amplitude[TX - H :], "gx", n_gx, 1)
    xhigh = shift(amplitude[:H], "gx", n_gx, -1)
    ylow = shift(
        jnp.concatenate([xlow[:, ty - H :], amplitude[:, ty - H :], xhigh[:, ty - H :]]),
        "gy",
        n_gy,
        1,
    )
    yhigh = shift(
        jnp.concatenate([xlow[:, :H], amplitude[:, :H], xhigh[:, :H]]), "gy", n_gy, -1
    )

    def taps_first(weight):
        return jnp.transpose(weight, (2, 3, 4, 0, 1))

    w1, w2, w3, w4 = pl.pallas_call(
        prep_kernel,
        out_shape=[
            jax.ShapeDtypeStruct((3 * 4 * XW, 4 * BLK), BF16),
            jax.ShapeDtypeStruct((9, BLK, BLK), BF16),
            jax.ShapeDtypeStruct((9, BLK, BLK), BF16),
            jax.ShapeDtypeStruct((9 * FX, 2 * BLK), BF16),
        ],
        in_specs=vmem(4) + [pl.BlockSpec(memory_space=pl.ANY)],
        out_specs=vmem(4),
        compiler_params=pltpu.CompilerParams(vmem_limit_bytes=16 * 2**20),
        cost_estimate=pl.CostEstimate(flops=10**9, bytes_accessed=10**7, transcendentals=0),
        name="band_weights",
    )(
        jnp.transpose(conv_first, (1, 2, 3, 4, 0)),
        taps_first(conv_second).reshape(27 * CH, CH),
        taps_first(conv_third).reshape(27 * CH, CH),
        jnp.transpose(conv_last, (0, 2, 3, 4, 1)),
        xlow,
    )

    yw, nf = ty + 2 * H, FX + 2
    scratch = [
        pltpu.VMEM(((XW + 2) * yw, NT), F32),
        pltpu.VMEM((yw + 2, XW, NT), F32),
        pltpu.VMEM((yw, 2, PAD, BLK), BF16),
        pltpu.VMEM((ty + 12, 2, PAD, BLK), BF16),
        pltpu.VMEM((ty + 10, NT, 2 * BLK), BF16),
        pltpu.VMEM((ty + 10, 9 * FX, NT), F32),
        pltpu.VMEM((FX * yw, NT), F32),
        pltpu.VMEM((3, FX + 4, yw, NT), F32),
        pltpu.VMEM((2, nf, yw, NT), F32),
        pltpu.VMEM((2, nf, yw, NT), F32),
        pltpu.VMEM((2, nf, yw, NT), F32),
        pltpu.VMEM((2, nf, yw, NT), F32),
        pltpu.VMEM((nf, yw, NT), F32),
        pltpu.VMEM((3, nf, yw, NT), F32),
    ]
    rows = TX // n_gy
    fault, moments, *waves = pl.pallas_call(
        functools.partial(main_kernel, grid_x, grid_y, ty),
        out_shape=[
            jax.ShapeDtypeStruct((TX, ty, NT), BF16),
            jax.ShapeDtypeStruct((8, NT), F32),
        ]
        + [jax.ShapeDtypeStruct((3, rows, ty, NT), BF16)] * n_gy,
        in_specs=vmem(9),
        out_specs=vmem(2 + n_gy),
        scratch_shapes=scratch,
        compiler_params=pltpu.CompilerParams(vmem_limit_bytes=48 * 2**20),
        cost_estimate=pl.CostEstimate(
            flops=3 * 10**10, bytes_accessed=10**7, transcendentals=10**6
        ),
        name="fault_and_waves",
    )(amplitude, xlow, xhigh, ylow, yhigh, w1, w2, w3, w4)

    arrived = [waves[0]]
    for place in range(1, n_gy):
        pairs = [(i, (i + place) % n_gy) for i in range(n_gy)]
        arrived.append(lax.ppermute(waves[place], "gy", pairs))
    moments = lax.all_gather(moments, ("gx", "gy"), axis=0, tiled=False)
    shift_field = pl.pallas_call(
        functools.partial(combine_kernel, n_gy, ty),
        out_shape=jax.ShapeDtypeStruct((rows, grid_y, NT), F32),
        in_specs=vmem(1 + n_gy),
        out_specs=pl.BlockSpec(memory_space=pltpu.VMEM),
        compiler_params=pltpu.CompilerParams(vmem_limit_bytes=16 * 2**20),
        name="combine_waves",
    )(moments, *arrived)
    return (fault, shift_field)


def solution(mesh):
    return jax.shard_map(
        on_device,
        mesh=mesh,
        in_specs=(P("gx", "gy", None), P(), P(), P(), P()),
        out_specs=(P("gx", "gy", None), P(("gx", "gy"), None, None)),
        check_vma=False,
    )
```

```python
import functools

import jax
import jax.numpy as jnp
from jax import lax
from jax.experimental import pallas as pl
from jax.experimental.pallas import tpu as pltpu
from jax.sharding import PartitionSpec as P

MU_DIAG = 0.05
ETA_TIME = 0.5

TX, NT, H = 16, 128, 8
CH = 16
XW = TX + 2 * H
FX = TX + 8
RX = 4
SECOND, THIRD = 11, 14
BLK = 256
SUB = 16
PAD = SUB + NT + SUB

F32 = jnp.float32
BF16 = jnp.bfloat16


def iota(shape, dim):
    return lax.broadcasted_iota(jnp.int32, shape, dim)


def groups(rows):
    count = -(-rows // 5)
    ends = [rows * i // count for i in range(count + 1)]
    return [(a, b - a) for a, b in zip(ends, ends[1:])]


def dot_nt(a, b):
    return lax.dot_general(a, b, (((1,), (1,)), ((), ())), preferred_element_type=F32)


def prep_kernel(
    first_in,
    second_in,
    third_in,
    last_in,
    after_ref,
    w1_ref,
    w2_ref,
    w3_ref,
    w4_ref,
    first_ref,
    second_ref,
    third_ref,
    last_ref,
    sems,
):
    del after_ref
    pairs = ((second_in, second_ref), (third_in, third_ref), (first_in, first_ref), (last_in, last_ref))
    copies = [pltpu.make_async_copy(a, b, sems.at[i]) for i, (a, b) in enumerate(pairs)]
    for copy in copies:
        copy.start()
    for copy in copies:
        copy.wait()
    spread = jnp.where(iota((CH, BLK), 1) % CH == iota((CH, BLK), 0), 1.0, 0.0).astype(BF16)
    unit = jnp.where(iota((BLK, BLK), 1) == iota((BLK, BLK), 0), 1.0, 0.0).astype(BF16)
    in_pos = iota((CH, BLK), 1) // CH
    for source, ref in ((second_ref, w2_ref), (third_ref, w3_ref)):
        tiled = jnp.dot(source[...], spread, preferred_element_type=F32)
        for dy in range(3):
            for dt in range(3):
                rows = [tiled[(dx * 9 + dy * 3 + dt) * CH :][:CH] for dx in range(3)]
                bands = []
                for xo in range(16):
                    band = jnp.zeros((CH, BLK), F32)
                    for dx in range(3):
                        band = jnp.where(in_pos == xo + dx, rows[dx], band)
                    bands.append(band.astype(BF16))
                turned = dot_nt(unit, jnp.concatenate(bands, axis=0))
                ref[dy * 3 + dt] = turned.astype(BF16)

    def taps(ref):
        found = {}
        for dx in range(3):
            for dy in range(3):
                piece = ref[0, dx, dy].astype(BF16)
                tiled = jnp.dot(piece, spread, preferred_element_type=F32)
                for dt in range(3):
                    found[dx, dy, dt] = tiled[dt : dt + 1]
        return found

    first, last = taps(first_ref), taps(last_ref)
    row_pos = iota((XW, BLK), 0)
    lane_pos = iota((XW, BLK), 1) // CH
    for dt in range(3):
        for yi in range(4):
            for yo in range(2):
                for blk in range(2):
                    band = jnp.zeros((XW, BLK), F32)
                    dy = yi - yo
                    if 0 <= dy <= 2:
                        for dx in range(3):
                            band = jnp.where(
                                row_pos - 14 * blk - lane_pos == dx, first[dx, dy, dt], band
                            )
                    w1_ref[
                        dt * 128 + yi * XW : dt * 128 + (yi + 1) * XW,
                        yo * 512 + blk * BLK : yo * 512 + (blk + 1) * BLK,
                    ] = band.astype(BF16)
    row_pos = iota((FX, BLK), 0)
    lane_pos = iota((FX, BLK), 1) // CH
    for blk in range(2):
        pieces = []
        for dy in range(3):
            for dt in range(3):
                band = jnp.zeros((FX, BLK), F32)
                for dx in range(3):
                    band = jnp.where(14 * blk + lane_pos - row_pos == dx, last[dx, dy, dt], band)
                pieces.append(jnp.where(lane_pos < 14 - 2 * blk, band, 0.0))
        pieces = jnp.concatenate(pieces, axis=0)
        w4_ref[:, blk * BLK : (blk + 1) * BLK] = pieces.astype(BF16)


def main_kernel(
    grid_x,
    grid_y,
    ty,
    amp_ref,
    xlow_ref,
    xhigh_ref,
    ylow_ref,
    yhigh_ref,
    w1_ref,
    w2_ref,
    w3_ref,
    w4_ref,
    *refs,
):
    n_gy = grid_y // ty
    fault_ref, mom_ref = refs[:2]
    waves_refs = refs[2 : 2 + n_gy]
    (raw, amp, act1, act2, act3, part, prob, prod, slope, weight, face, flux, inv, wave) = refs[
        2 + n_gy :
    ]
    place_y = lax.axis_index("gy")
    x0 = lax.axis_index("gx") * TX
    y0 = place_y * ty
    yw = ty + 2 * H
    dot = functools.partial(jnp.dot, preferred_element_type=F32)

    def inside_y(y):
        at = y0 + y
        return jnp.where((at >= 0) & (at < grid_y), 1.0, 0.0).astype(F32)

    def lane_mask(start):
        masks = []
        for blk in range(2):
            at = x0 + start + 14 * blk + iota((1, BLK), 1) // CH
            masks.append(jnp.where((at >= 0) & (at < grid_x), 1.0, 0.0).astype(F32))
        return masks

    for x in range(XW):
        row = x * yw
        if x < H:
            mid = xlow_ref[x]
        elif x < H + TX:
            mid = amp_ref[x - H]
        else:
            mid = xhigh_ref[x - H - TX]
        raw[row + H : row + H + ty, :] = mid.astype(F32)
        raw[row : row + H, :] = ylow_ref[x].astype(F32)
        raw[row + H + ty : row + yw, :] = yhigh_ref[x].astype(F32)

    def turn(y, carry):
        amp[y] = raw[pl.ds(y, XW, stride=yw), :]
        return carry

    lax.fori_loop(0, yw, turn, 0, unroll=8)
    amp[yw] = jnp.zeros((XW, NT), F32)
    amp[yw + 1] = jnp.zeros((XW, NT), F32)

    tiled_row = iota((NT, NT), 0)
    natural = tiled_row // SUB + (tiled_row % SUB) * 8
    to_tiles = jnp.concatenate(
        [
            jnp.where(iota((NT, NT), 1) == natural + dt - 1, 1.0, 0.0).astype(BF16)
            for dt in range(3)
        ],
        axis=0,
    )
    from_tiles = jnp.concatenate(
        [
            jnp.where(iota((NT, NT), 1) + dt - 1 == natural, 1.0, 0.0).astype(BF16)
            for dt in range(3)
        ],
        axis=0,
    )
    sub_row = iota((SUB, BLK), 0)

    def put(act, y, blk, values):
        act[y, blk, SUB : SUB + NT, :] = values.astype(BF16)
        before = jnp.where(sub_row == 0, 0.0, pltpu.roll(values[NT - SUB :], 1, 0))
        after = jnp.where(sub_row == SUB - 1, 0.0, pltpu.roll(values[:SUB], SUB - 1, 0))
        act[y, blk, 0:SUB, :] = before.astype(BF16)
        act[y, blk, SUB + NT :, :] = after.astype(BF16)

    mask1 = lane_mask(-7)

    def first(step, carry):
        pieces = []
        for half in range(2):
            y = step * 4 + half * 2
            rows = amp[pl.ds(y, 4)].reshape(4 * XW, NT).astype(BF16)
            turned = dot_nt(to_tiles, rows).astype(BF16)
            pieces.append(
                jnp.concatenate([turned[:NT], turned[NT : 2 * NT], turned[2 * NT :]], axis=1)
            )
        result = dot(jnp.concatenate(pieces, axis=0), w1_ref[...])
        for half in range(2):
            for yo in range(2):
                y = step * 4 + half * 2 + yo
                ok = inside_y(y - 7)
                for blk in range(2):
                    lane = yo * 512 + blk * BLK
                    values = result[half * NT : (half + 1) * NT, lane : lane + BLK]
                    put(act1, y, blk, jnp.maximum(values, 0.0) * (mask1[blk] * ok))
        return carry

    lax.fori_loop(0, yw // 4, first, 0, unroll=2)

    def layer(source, w_ref, y, count):
        taps = []
        for dy in range(3):
            for dt in range(3):
                part_in = source[pl.ds(y + dy, count), :, SUB * dt : SUB * dt + NT, :]
                taps.append(part_in.reshape(count * 2 * NT, BLK))
        return dot(jnp.concatenate(taps, axis=1), w_ref[...].reshape(9 * BLK, BLK))

    mask2 = lane_mask(-6)
    lane_half = iota((NT, 128), 1)

    def second(step, carry):
        for begin, count in groups(SECOND):
            y = step * SECOND + begin
            result = layer(act1, w2_ref, y, count)
            for row in range(count):
                ok = inside_y(y + row - 6)
                low = result[row * 2 * NT : row * 2 * NT + NT]
                high = result[row * 2 * NT + NT : (row + 1) * 2 * NT]
                moved = jnp.where(lane_half >= 96, pltpu.roll(high[:, :128], 96, 1), low[:, 128:])
                low = jnp.concatenate([low[:, :128], moved], axis=1)
                put(act2, y + row, 0, jnp.maximum(low, 0.0) * (mask2[0] * ok))
                put(act2, y + row, 1, jnp.maximum(high, 0.0) * (mask2[1] * ok))
        return carry

    lax.fori_loop(0, (ty + 12) // SECOND, second, 0)

    mask3 = lane_mask(-5)

    def third(step, carry):
        for begin, count in groups(THIRD):
            y = step * THIRD + begin
            result = layer(act2, w3_ref, y, count)
            for row in range(count):
                ok = inside_y(y + row - 5)
                for blk in range(2):
                    at = (row * 2 + blk) * NT
                    values = jnp.maximum(result[at : at + NT], 0.0) * (mask3[blk] * ok)
                    act3[y + row, :, blk * BLK : (blk + 1) * BLK] = values.astype(BF16)
        return carry

    lax.fori_loop(0, (ty + 10) // THIRD, third, 0)

    def fourth(step, carry):
        y = step * 3
        result = dot_nt(w4_ref[...], act3[pl.ds(y, 3)].reshape(3 * NT, 2 * BLK))
        for row in range(3):
            part[y + row] = result[:, row * NT : (row + 1) * NT]
        return carry

    lax.fori_loop(0, (ty + 10) // 3, fourth, 0, unroll=7)

    for x in range(FX):
        prob[x * yw : x * yw + H, :] = jnp.zeros((H, NT), F32)
        prob[(x + 1) * yw - H : (x + 1) * yw, :] = jnp.zeros((H, NT), F32)

    def order(step, carry):
        sums = []
        for row in range(8):
            y = step * 8 + row
            total = (
                part[y, 0 : 3 * FX] + part[y + 1, 3 * FX : 6 * FX] + part[y + 2, 6 * FX : 9 * FX]
            )
            sums.append(jnp.concatenate([total[i * FX : (i + 1) * FX] for i in range(3)], axis=1))
        sums = jnp.concatenate(sums, axis=0)
        high = sums.astype(BF16)
        low = (sums - high.astype(F32)).astype(BF16)
        both = dot(jnp.concatenate([high, low], axis=0), from_tiles)
        values = both[: 8 * FX] + both[8 * FX :]
        values = (1.0 / (1.0 + jnp.exp(-values))).astype(BF16).astype(F32)
        for row in range(8):
            prob[pl.ds(step * 8 + row + 4, FX, stride=yw), :] = values[row * FX : (row + 1) * FX]
        return carry

    lax.fori_loop(0, (ty + 8) // 8, order, 0)

    block = (RX, yw, NT)
    lane = iota(block, 2)
    first_lane = lane == 0
    last_lane = lane == NT - 1

    def up_y(v):
        return pltpu.roll(v, yw - 1, 1)

    def down_y(v):
        return pltpu.roll(v, 1, 1)

    def up_t(v, edge=0.0):
        return jnp.where(last_lane, edge, pltpu.roll(v, NT - 1, 2))

    def down_t(v, edge=0.0):
        return jnp.where(first_lane, edge, pltpu.roll(v, 1, 2))

    def smooth_yt(v, edge=0.0):
        v = 0.5 * v + 0.25 * (up_t(v, edge) + down_t(v, edge))
        return 0.5 * v + 0.25 * (up_y(v) + down_y(v))

    def amp_rows(x):
        return raw[pl.ds(pl.multiple_of(x * yw, 8), RX * yw), :].reshape(block)

    def products(step, carry):
        k = step * RX
        here = amp_rows(k + 3)
        grad_x = 0.5 * (amp_rows(k + 4) - amp_rows(k + 2))
        grad_y = 0.5 * (up_y(here) - down_y(here))
        grad_t = 0.5 * (up_t(here) - down_t(here))
        at = pl.ds(k, RX)
        prod[0, at] = smooth_yt(grad_x * grad_t)
        prod[1, at] = smooth_yt(grad_y * grad_t)
        energy = grad_t * grad_t + 0.25 * (grad_x * grad_x + grad_y * grad_y)
        prod[2, at] = smooth_yt(energy, 0.25 * here * here)
        return carry

    lax.fori_loop(0, (FX + 2 + RX - 1) // RX, products, 0)

    at_y = y0 - H + iota(block, 1)
    mask_y = (at_y >= 0) & (at_y < grid_y)

    def fields(step, carry):
        k = step * RX
        at = pl.ds(k + 1, RX)
        sums = []
        for which in range(3):
            before, here, after = [prod[which, pl.ds(k + i, RX)] for i in range(3)]
            sums.append(0.5 * here + 0.25 * (before + after))
        scale = -1.0 / (sums[2] + 0.05)
        slope[0, at] = sums[0] * scale
        slope[1, at] = sums[1] * scale
        rows = prob[pl.ds(pl.multiple_of(k * yw, 8), RX * yw), :].reshape(block)
        raw_weight = 1.0 - 0.9 * rows
        at_x = x0 - 4 + k + iota(block, 0)
        weight[0, at] = raw_weight
        weight[1, at] = jnp.where(mask_y & (at_x >= 0) & (at_x < grid_x), raw_weight, 0.0)
        return carry

    lax.fori_loop(0, FX // RX, fields, 0)
    for which in range(2):
        slope[which, FX + 1] = jnp.zeros((yw, NT), F32)
        weight[which, FX + 1] = jnp.full((yw, NT), 1.0 - which, F32)
        face[which, 0] = jnp.zeros((yw, NT), F32)
        flux[which, 0] = jnp.zeros((yw, NT), F32)

    def faces(step, carry):
        k = step * RX + 1
        at, after = pl.ds(k, RX), pl.ds(k + 1, RX)
        raw_weight = weight[0, at]
        masked = weight[1, at]
        face_x = 2.0 * masked * weight[1, after] / (raw_weight + weight[0, after])
        face_y = 2.0 * masked * up_y(masked) / (raw_weight + up_y(raw_weight))
        slope_y = slope[1, at]
        face[0, at] = face_x
        face[1, at] = face_y
        flux[0, at] = 0.5 * face_x * (slope[0, at] + slope[0, after])
        flux[1, at] = 0.5 * face_y * (slope_y + up_y(slope_y))
        return carry

    lax.fori_loop(0, FX // RX, faces, 0)

    time_part = MU_DIAG + ETA_TIME * (
        jnp.where(first_lane, 0.0, 1.0) + jnp.where(last_lane, 0.0, 1.0)
    )

    def owned(total, k, values):
        for row in range(RX):
            ok = (k + row >= 5) & (k + row < 5 + TX)
            total = total + jnp.where(ok, values[row, H : H + ty], 0.0)
        return total

    def start(step, total):
        k = step * RX + 1
        at, before = pl.ds(k, RX), pl.ds(k - 1, RX)
        flux_y = flux[1, at]
        face_y = face[1, at]
        right = flux[0, before] - flux[0, at] + down_y(flux_y) - flux_y
        inverse = 1.0 / (time_part + face[0, at] + face[0, before] + face_y + down_y(face_y))
        first_wave = right * inverse
        inv[at] = inverse
        wave[0, at] = first_wave
        return owned(total, k, right * first_wave)

    zero = jnp.zeros((ty, NT), F32)
    b0 = lax.fori_loop(0, FX // RX, start, zero)

    def apply(which, k):
        at, before, after = [pl.ds(k + i, RX) for i in (0, -1, 1)]
        here = wave[which, at]
        flow = face[1, at] * (here - up_y(here))
        image = time_part * here - ETA_TIME * (up_t(here) + down_t(here))
        image = image + flow - down_y(flow)
        image = image + face[0, at] * (here - wave[which, after])
        return here, image + face[0, before] * (here - wave[which, before])

    def advance(which):
        def body(step, totals):
            k = step * RX + 3
            here, image = apply(which, k)
            at = pl.ds(k, RX)
            after = here - image * inv[at]
            wave[which + 1, at] = after
            return owned(totals[0], k, here * image), owned(totals[1], k, after * image)

        return body

    steps = (FX - 4) // RX
    a0, a1 = lax.fori_loop(0, steps, advance(0), (zero, zero))
    a2, a3 = lax.fori_loop(0, steps, advance(1), (zero, zero))

    def finish(step, total):
        k = step * RX + 5
        here, image = apply(2, k)
        return owned(total, k, here * image)

    a4 = lax.fori_loop(0, TX // RX, finish, zero)

    sums = [jnp.sum(v, axis=0, keepdims=True) for v in (b0, a0, a1, a2, a3, a4)]
    mom_ref[...] = jnp.concatenate(sums + [jnp.zeros((2, NT), F32)], axis=0)

    for x in range(TX):
        fault_ref[x] = prob[(x + 4) * yw + H : (x + 4) * yw + H + ty, :].astype(BF16)
    rows = TX // n_gy
    for place, ref in enumerate(waves_refs):
        to = lax.rem(place_y + place, n_gy) * rows + 5
        for which in range(3):
            for row in range(rows):
                ref[which, row] = wave[which, to + row, H : H + ty, :].astype(BF16)


def combine_kernel(n_gy, ty, mom_ref, *refs):
    waves_refs, out_ref = refs[:n_gy], refs[n_gy]
    place_y = lax.axis_index("gy")
    moments = jnp.sum(jnp.sum(mom_ref[...], axis=0), axis=1, keepdims=True)
    b0, a0, a1, a2, a3, a4 = [
        jnp.broadcast_to(moments[i : i + 1], (1, NT)) for i in range(6)
    ]
    a0, a1, a2, a3, a4 = [v / b0 for v in (a0, a1, a2, a3, a4)]
    l21 = a1 / a0
    l31 = a2 / a0
    d2 = jnp.maximum(a2 - l21 * a1, 1e-7 * a2 + 1e-30)
    l32 = (a3 - l21 * a2) / d2
    d3 = jnp.maximum(a4 - l31 * a2 - l32 * l32 * d2, 1e-7 * a4 + 1e-30)
    y2 = (1.0 - a0) - l21
    y3 = (1.0 - a0 - a1) - l31 - l32 * y2
    c3 = y3 / d3
    c2 = y2 / d2 - l32 * c3
    c1 = 1.0 / a0 - l21 * c2 - l31 * c3
    for place, ref in enumerate(waves_refs):
        source = lax.rem(place_y - place + n_gy, n_gy)
        at = pl.ds(pl.multiple_of(source * ty, 8), ty)
        for x in range(ref.shape[1]):
            w0, w1, w2 = [ref[which, x].astype(F32) for which in range(3)]
            out_ref[x, at, :] = c1 * w0 + c2 * w1 + c3 * w2


def vmem(count):
    return [pl.BlockSpec(memory_space=pltpu.VMEM)] * count


def on_device(amplitude, conv_first, conv_second, conv_third, conv_last):
    n_gx, n_gy = lax.axis_size("gx"), lax.axis_size("gy")
    ty = amplitude.shape[1]
    grid_x, grid_y = n_gx * TX, n_gy * ty
    assert amplitude.shape == (TX, ty, NT)

    def shift(values, axis, count, step):
        pairs = [(i, i + step) for i in range(count) if 0 <= i + step < count]
        return lax.ppermute(values, axis, pairs)

    xlow = shift(amplitude[TX - H :], "gx", n_gx, 1)
    xhigh = shift(amplitude[:H], "gx", n_gx, -1)
    ylow = shift(
        jnp.concatenate([xlow[:, ty - H :], amplitude[:, ty - H :], xhigh[:, ty - H :]]),
        "gy",
        n_gy,
        1,
    )
    yhigh = shift(
        jnp.concatenate([xlow[:, :H], amplitude[:, :H], xhigh[:, :H]]), "gy", n_gy, -1
    )

    def taps_first(weight):
        return jnp.transpose(weight, (2, 3, 4, 0, 1))

    w1, w2, w3, w4 = pl.pallas_call(
        prep_kernel,
        out_shape=[
            jax.ShapeDtypeStruct((3 * 4 * XW, 4 * BLK), BF16),
            jax.ShapeDtypeStruct((9, BLK, BLK), BF16),
            jax.ShapeDtypeStruct((9, BLK, BLK), BF16),
            jax.ShapeDtypeStruct((9 * FX, 2 * BLK), BF16),
        ],
        in_specs=[pl.BlockSpec(memory_space=pltpu.HBM)] * 4 + [pl.BlockSpec(memory_space=pl.ANY)],
        out_specs=vmem(4),
        scratch_shapes=[
            pltpu.VMEM((1, 3, 3, 3, CH), BF16),
            pltpu.VMEM((27 * CH, CH), BF16),
            pltpu.VMEM((27 * CH, CH), BF16),
            pltpu.VMEM((1, 3, 3, 3, CH), BF16),
            pltpu.SemaphoreType.DMA((4,)),
        ],
        compiler_params=pltpu.CompilerParams(vmem_limit_bytes=16 * 2**20),
        cost_estimate=pl.CostEstimate(flops=10**9, bytes_accessed=10**7, transcendentals=0),
        name="band_weights",
    )(
        jnp.transpose(conv_first, (1, 2, 3, 4, 0)),
        taps_first(conv_second).reshape(27 * CH, CH),
        taps_first(conv_third).reshape(27 * CH, CH),
        jnp.transpose(conv_last, (0, 2, 3, 4, 1)),
        xlow,
    )

    yw, nf = ty + 2 * H, FX + 2
    scratch = [
        pltpu.VMEM(((XW + 2) * yw, NT), F32),
        pltpu.VMEM((yw + 2, XW, NT), F32),
        pltpu.VMEM((yw, 2, PAD, BLK), BF16),
        pltpu.VMEM((ty + 12, 2, PAD, BLK), BF16),
        pltpu.VMEM((ty + 10, NT, 2 * BLK), BF16),
        pltpu.VMEM((ty + 10, 9 * FX, NT), F32),
        pltpu.VMEM((FX * yw, NT), F32),
        pltpu.VMEM((3, FX + 4, yw, NT), F32),
        pltpu.VMEM((2, nf, yw, NT), F32),
        pltpu.VMEM((2, nf, yw, NT), F32),
        pltpu.VMEM((2, nf, yw, NT), F32),
        pltpu.VMEM((2, nf, yw, NT), F32),
        pltpu.VMEM((nf, yw, NT), F32),
        pltpu.VMEM((3, nf, yw, NT), F32),
    ]
    rows = TX // n_gy
    fault, moments, *waves = pl.pallas_call(
        functools.partial(main_kernel, grid_x, grid_y, ty),
        out_shape=[
            jax.ShapeDtypeStruct((TX, ty, NT), BF16),
            jax.ShapeDtypeStruct((8, NT), F32),
        ]
        + [jax.ShapeDtypeStruct((3, rows, ty, NT), BF16)] * n_gy,
        in_specs=vmem(9),
        out_specs=vmem(2 + n_gy),
        scratch_shapes=scratch,
        compiler_params=pltpu.CompilerParams(vmem_limit_bytes=48 * 2**20),
        cost_estimate=pl.CostEstimate(
            flops=3 * 10**10, bytes_accessed=10**7, transcendentals=10**6
        ),
        name="fault_and_waves",
    )(amplitude, xlow, xhigh, ylow, yhigh, w1, w2, w3, w4)

    arrived = [waves[0]]
    for place in range(1, n_gy):
        pairs = [(i, (i + place) % n_gy) for i in range(n_gy)]
        arrived.append(lax.ppermute(waves[place], "gy", pairs))
    everyone = jnp.broadcast_to(moments[None], (n_gx * n_gy, 8, NT))
    moments = lax.all_to_all(everyone, ("gx", "gy"), split_axis=0, concat_axis=0, tiled=True)
    shift_field = pl.pallas_call(
        functools.partial(combine_kernel, n_gy, ty),
        out_shape=jax.ShapeDtypeStruct((rows, grid_y, NT), F32),
        in_specs=vmem(1 + n_gy),
        out_specs=pl.BlockSpec(memory_space=pltpu.VMEM),
        compiler_params=pltpu.CompilerParams(vmem_limit_bytes=16 * 2**20),
        name="combine_waves",
    )(moments, *arrived)
    return (fault, shift_field)


def solution(mesh):
    return jax.shard_map(
        on_device,
        mesh=mesh,
        in_specs=(P("gx", "gy", None), P(), P(), P(), P()),
        out_specs=(P("gx", "gy", None), P(("gx", "gy"), None, None)),
        check_vma=False,
    )
```

```python
import functools

import jax
import jax.numpy as jnp
from jax import lax
from jax.experimental import pallas as pl
from jax.experimental.pallas import tpu as pltpu
from jax.sharding import PartitionSpec as P

MU_DIAG = 0.05
ETA_TIME = 0.5

TX, NT, H = 16, 128, 8
CH = 16
XW = TX + 2 * H
FX = TX + 8
RX = 4
SECOND, THIRD = 11, 14
BLK = 256
SUB = 16
PAD = SUB + NT + SUB

F32 = jnp.float32
BF16 = jnp.bfloat16


def iota(shape, dim):
    return lax.broadcasted_iota(jnp.int32, shape, dim)


def groups(rows):
    count = -(-rows // 5)
    ends = [rows * i // count for i in range(count + 1)]
    return [(a, b - a) for a, b in zip(ends, ends[1:])]


def dot_nt(a, b):
    return lax.dot_general(a, b, (((1,), (1,)), ((), ())), preferred_element_type=F32)


def prep_kernel(
    first_in,
    second_in,
    third_in,
    last_in,
    after_ref,
    w1_ref,
    w2_ref,
    w3_ref,
    w4_ref,
    first_ref,
    second_ref,
    third_ref,
    last_ref,
    sems,
):
    del after_ref
    pairs = ((second_in, second_ref), (third_in, third_ref), (first_in, first_ref), (last_in, last_ref))
    copies = [pltpu.make_async_copy(a, b, sems.at[i]) for i, (a, b) in enumerate(pairs)]
    for copy in copies:
        copy.start()
    for copy in copies:
        copy.wait()
    spread = jnp.where(iota((CH, BLK), 1) % CH == iota((CH, BLK), 0), 1.0, 0.0).astype(BF16)
    unit = jnp.where(iota((BLK, BLK), 1) == iota((BLK, BLK), 0), 1.0, 0.0).astype(BF16)
    in_pos = iota((CH, BLK), 1) // CH
    for source, ref in ((second_ref, w2_ref), (third_ref, w3_ref)):
        tiled = jnp.dot(source[...], spread, preferred_element_type=F32)
        for dy in range(3):
            for dt in range(3):
                rows = [tiled[(dx * 9 + dy * 3 + dt) * CH :][:CH] for dx in range(3)]
                bands = []
                for xo in range(16):
                    band = jnp.zeros((CH, BLK), F32)
                    for dx in range(3):
                        band = jnp.where(in_pos == xo + dx, rows[dx], band)
                    bands.append(band.astype(BF16))
                turned = dot_nt(unit, jnp.concatenate(bands, axis=0))
                ref[dy * 3 + dt] = turned.astype(BF16)

    def taps(ref):
        found = {}
        for dx in range(3):
            for dy in range(3):
                piece = ref[0, dx, dy].astype(BF16)
                tiled = jnp.dot(piece, spread, preferred_element_type=F32)
                for dt in range(3):
                    found[dx, dy, dt] = tiled[dt : dt + 1]
        return found

    first, last = taps(first_ref), taps(last_ref)
    row_pos = iota((XW, BLK), 0)
    lane_pos = iota((XW, BLK), 1) // CH
    for dt in range(3):
        for yi in range(4):
            for yo in range(2):
                for blk in range(2):
                    band = jnp.zeros((XW, BLK), F32)
                    dy = yi - yo
                    if 0 <= dy <= 2:
                        for dx in range(3):
                            band = jnp.where(
                                row_pos - 14 * blk - lane_pos == dx, first[dx, dy, dt], band
                            )
                    w1_ref[
                        dt * 128 + yi * XW : dt * 128 + (yi + 1) * XW,
                        yo * 512 + blk * BLK : yo * 512 + (blk + 1) * BLK,
                    ] = band.astype(BF16)
    row_pos = iota((FX, BLK), 0)
    lane_pos = iota((FX, BLK), 1) // CH
    for blk in range(2):
        pieces = []
        for dy in range(3):
            for dt in range(3):
                band = jnp.zeros((FX, BLK), F32)
                for dx in range(3):
                    band = jnp.where(14 * blk + lane_pos - row_pos == dx, last[dx, dy, dt], band)
                pieces.append(jnp.where(lane_pos < 14 - 2 * blk, band, 0.0))
        pieces = jnp.concatenate(pieces, axis=0)
        w4_ref[:, blk * BLK : (blk + 1) * BLK] = pieces.astype(BF16)


def plane_shifts(yw):
    block = (RX, yw, NT)
    lane = iota(block, 2)
    first_lane = lane == 0
    last_lane = lane == NT - 1

    def up_y(v):
        return pltpu.roll(v, yw - 1, 1)

    def down_y(v):
        return pltpu.roll(v, 1, 1)

    def up_t(v, edge=0.0):
        return jnp.where(last_lane, edge, pltpu.roll(v, NT - 1, 2))

    def down_t(v, edge=0.0):
        return jnp.where(first_lane, edge, pltpu.roll(v, 1, 2))

    return block, up_y, down_y, up_t, down_t


def net_kernel(
    grid_x,
    grid_y,
    ty,
    amp_ref,
    xlow_ref,
    xhigh_ref,
    ylow_ref,
    yhigh_ref,
    w1_ref,
    w2_ref,
    w3_ref,
    w4_ref,
    fault_ref,
    prob,
    slope,
    raw,
    amp,
    act1,
    act2,
    act3,
    part,
    prod,
):
    x0 = lax.axis_index("gx") * TX
    y0 = lax.axis_index("gy") * ty
    yw = ty + 2 * H
    dot = functools.partial(jnp.dot, preferred_element_type=F32)

    def inside_y(y):
        at = y0 + y
        return jnp.where((at >= 0) & (at < grid_y), 1.0, 0.0).astype(F32)

    def lane_mask(start):
        masks = []
        for blk in range(2):
            at = x0 + start + 14 * blk + iota((1, BLK), 1) // CH
            masks.append(jnp.where((at >= 0) & (at < grid_x), 1.0, 0.0).astype(F32))
        return masks

    for x in range(XW):
        row = x * yw
        if x < H:
            mid = xlow_ref[x]
        elif x < H + TX:
            mid = amp_ref[x - H]
        else:
            mid = xhigh_ref[x - H - TX]
        raw[row + H : row + H + ty, :] = mid.astype(F32)
        raw[row : row + H, :] = ylow_ref[x].astype(F32)
        raw[row + H + ty : row + yw, :] = yhigh_ref[x].astype(F32)

    def turn(y, carry):
        amp[y] = raw[pl.ds(y, XW, stride=yw), :]
        return carry

    lax.fori_loop(0, yw, turn, 0, unroll=8)
    amp[yw] = jnp.zeros((XW, NT), F32)
    amp[yw + 1] = jnp.zeros((XW, NT), F32)

    tiled_row = iota((NT, NT), 0)
    natural = tiled_row // SUB + (tiled_row % SUB) * 8
    to_tiles = jnp.concatenate(
        [
            jnp.where(iota((NT, NT), 1) == natural + dt - 1, 1.0, 0.0).astype(BF16)
            for dt in range(3)
        ],
        axis=0,
    )
    from_tiles = jnp.concatenate(
        [
            jnp.where(iota((NT, NT), 1) + dt - 1 == natural, 1.0, 0.0).astype(BF16)
            for dt in range(3)
        ],
        axis=0,
    )
    sub_row = iota((SUB, BLK), 0)

    def put(act, y, blk, values):
        act[y, blk, SUB : SUB + NT, :] = values.astype(BF16)
        before = jnp.where(sub_row == 0, 0.0, pltpu.roll(values[NT - SUB :], 1, 0))
        after = jnp.where(sub_row == SUB - 1, 0.0, pltpu.roll(values[:SUB], SUB - 1, 0))
        act[y, blk, 0:SUB, :] = before.astype(BF16)
        act[y, blk, SUB + NT :, :] = after.astype(BF16)

    mask1 = lane_mask(-7)

    def first(step, carry):
        pieces = []
        for half in range(2):
            y = step * 4 + half * 2
            rows = amp[pl.ds(y, 4)].reshape(4 * XW, NT).astype(BF16)
            turned = dot_nt(to_tiles, rows).astype(BF16)
            pieces.append(
                jnp.concatenate([turned[:NT], turned[NT : 2 * NT], turned[2 * NT :]], axis=1)
            )
        result = dot(jnp.concatenate(pieces, axis=0), w1_ref[...])
        for half in range(2):
            for yo in range(2):
                y = step * 4 + half * 2 + yo
                ok = inside_y(y - 7)
                for blk in range(2):
                    lane = yo * 512 + blk * BLK
                    values = result[half * NT : (half + 1) * NT, lane : lane + BLK]
                    put(act1, y, blk, jnp.maximum(values, 0.0) * (mask1[blk] * ok))
        return carry

    lax.fori_loop(0, yw // 4, first, 0, unroll=2)

    def layer(source, w_ref, y, count):
        taps = []
        for dy in range(3):
            for dt in range(3):
                part_in = source[pl.ds(y + dy, count), :, SUB * dt : SUB * dt + NT, :]
                taps.append(part_in.reshape(count * 2 * NT, BLK))
        return dot(jnp.concatenate(taps, axis=1), w_ref[...].reshape(9 * BLK, BLK))

    block, up_y, down_y, up_t, down_t = plane_shifts(yw)

    def smooth_yt(v, edge=0.0):
        v = 0.5 * v + 0.25 * (up_t(v, edge) + down_t(v, edge))
        return 0.5 * v + 0.25 * (up_y(v) + down_y(v))

    def amp_rows(x):
        return raw[pl.ds(pl.multiple_of(x * yw, 8), RX * yw), :].reshape(block)

    def products(k):
        here = amp_rows(k + 3)
        grad_x = 0.5 * (amp_rows(k + 4) - amp_rows(k + 2))
        grad_y = 0.5 * (up_y(here) - down_y(here))
        grad_t = 0.5 * (up_t(here) - down_t(here))
        at = pl.ds(k, RX)
        prod[0, at] = smooth_yt(grad_x * grad_t)
        prod[1, at] = smooth_yt(grad_y * grad_t)
        energy = grad_t * grad_t + 0.25 * (grad_x * grad_x + grad_y * grad_y)
        prod[2, at] = smooth_yt(energy, 0.25 * here * here)

    def slopes(k):
        at = pl.ds(k + 1, RX)
        sums = []
        for which in range(3):
            before, here, after = [prod[which, pl.ds(k + i, RX)] for i in range(3)]
            sums.append(0.5 * here + 0.25 * (before + after))
        scale = -1.0 / (sums[2] + 0.05)
        slope[0, at] = sums[0] * scale
        slope[1, at] = sums[1] * scale

    mask2 = lane_mask(-6)
    lane_half = iota((NT, 128), 1)
    steps2, steps3 = (ty + 12) // SECOND, (ty + 10) // THIRD
    blocks2 = -(-(FX // RX + 1) // steps2)
    blocks3 = -(-(FX // RX) // steps3)

    def second(step, carry):
        for i in range(blocks2):
            products(jnp.minimum((step * blocks2 + i) * RX, FX))
        for begin, count in groups(SECOND):
            y = step * SECOND + begin
            result = layer(act1, w2_ref, y, count)
            for row in range(count):
                ok = inside_y(y + row - 6)
                low = result[row * 2 * NT : row * 2 * NT + NT]
                high = result[row * 2 * NT + NT : (row + 1) * 2 * NT]
                moved = jnp.where(lane_half >= 96, pltpu.roll(high[:, :128], 96, 1), low[:, 128:])
                low = jnp.concatenate([low[:, :128], moved], axis=1)
                put(act2, y + row, 0, jnp.maximum(low, 0.0) * (mask2[0] * ok))
                put(act2, y + row, 1, jnp.maximum(high, 0.0) * (mask2[1] * ok))
        return carry

    lax.fori_loop(0, steps2, second, 0)

    mask3 = lane_mask(-5)

    def third(step, carry):
        for i in range(blocks3):
            slopes(jnp.minimum((step * blocks3 + i) * RX, FX - RX))
        for begin, count in groups(THIRD):
            y = step * THIRD + begin
            result = layer(act2, w3_ref, y, count)
            for row in range(count):
                ok = inside_y(y + row - 5)
                for blk in range(2):
                    at = (row * 2 + blk) * NT
                    values = jnp.maximum(result[at : at + NT], 0.0) * (mask3[blk] * ok)
                    act3[y + row, :, blk * BLK : (blk + 1) * BLK] = values.astype(BF16)
        return carry

    lax.fori_loop(0, steps3, third, 0)

    def fourth(step, carry):
        y = step * 3
        result = dot_nt(w4_ref[...], act3[pl.ds(y, 3)].reshape(3 * NT, 2 * BLK))
        for row in range(3):
            part[y + row] = result[:, row * NT : (row + 1) * NT]
        return carry

    lax.fori_loop(0, (ty + 10) // 3, fourth, 0, unroll=7)

    for x in range(FX):
        prob[x * yw : x * yw + H, :] = jnp.zeros((H, NT), F32)
        prob[(x + 1) * yw - H : (x + 1) * yw, :] = jnp.zeros((H, NT), F32)

    def order(step, carry):
        sums = []
        for row in range(8):
            y = step * 8 + row
            total = (
                part[y, 0 : 3 * FX] + part[y + 1, 3 * FX : 6 * FX] + part[y + 2, 6 * FX : 9 * FX]
            )
            sums.append(jnp.concatenate([total[i * FX : (i + 1) * FX] for i in range(3)], axis=1))
        sums = jnp.concatenate(sums, axis=0)
        high = sums.astype(BF16)
        low = (sums - high.astype(F32)).astype(BF16)
        both = dot(jnp.concatenate([high, low], axis=0), from_tiles)
        values = both[: 8 * FX] + both[8 * FX :]
        values = (1.0 / (1.0 + jnp.exp(-values))).astype(BF16).astype(F32)
        for row in range(8):
            prob[pl.ds(step * 8 + row + 4, FX, stride=yw), :] = values[row * FX : (row + 1) * FX]
        return carry

    lax.fori_loop(0, (ty + 8) // 8, order, 0)

    for which in range(2):
        slope[which, FX + 1] = jnp.zeros((yw, NT), F32)
    for x in range(TX):
        fault_ref[x] = prob[(x + 4) * yw + H : (x + 4) * yw + H + ty, :].astype(BF16)


def owned(total, k, values, ty):
    for row in range(RX):
        ok = (k + row >= 5) & (k + row < 5 + TX)
        total = total + jnp.where(ok, values[row, H : H + ty], 0.0)
    return total


def image_of(wave, face, k, shifts):
    block, up_y, down_y, up_t, down_t = shifts
    at, before, after = [pl.ds(k + i, RX) for i in (0, -1, 1)]
    here = wave[at]
    flow = face[1, at] * (here - up_y(here))
    image = time_part(block) * here - ETA_TIME * (up_t(here) + down_t(here))
    image = image + flow - down_y(flow)
    image = image + face[0, at] * (here - wave[after])
    return here, image + face[0, before] * (here - wave[before])


def time_part(block):
    lane = iota(block, 2)
    count = jnp.where(lane == 0, 0.0, 1.0) + jnp.where(lane == NT - 1, 0.0, 1.0)
    return MU_DIAG + ETA_TIME * count


def waves_kernel(grid_x, grid_y, ty, prob, slope, mom_ref, face, wave2, *refs):
    n_gy = grid_y // ty
    waves_refs = refs[:n_gy]
    weight, flux, inv, wave0, wave1 = refs[n_gy:]
    place_y = lax.axis_index("gy")
    x0 = lax.axis_index("gx") * TX
    y0 = place_y * ty
    yw = ty + 2 * H
    shifts = plane_shifts(yw)
    block, up_y, down_y, up_t, down_t = shifts
    at_y = y0 - H + iota(block, 1)
    mask_y = (at_y >= 0) & (at_y < grid_y)

    def weights(step, carry):
        k = step * RX
        at = pl.ds(k + 1, RX)
        rows = prob[pl.ds(pl.multiple_of(k * yw, 8), RX * yw), :].reshape(block)
        raw_weight = 1.0 - 0.9 * rows
        at_x = x0 - 4 + k + iota(block, 0)
        weight[0, at] = raw_weight
        weight[1, at] = jnp.where(mask_y & (at_x >= 0) & (at_x < grid_x), raw_weight, 0.0)
        return carry

    lax.fori_loop(0, FX // RX, weights, 0)
    for which in range(2):
        weight[which, FX + 1] = jnp.full((yw, NT), 1.0 - which, F32)
        face[which, 0] = jnp.zeros((yw, NT), F32)
        flux[which, 0] = jnp.zeros((yw, NT), F32)

    def faces(step, carry):
        k = step * RX + 1
        at, after = pl.ds(k, RX), pl.ds(k + 1, RX)
        raw_weight = weight[0, at]
        masked = weight[1, at]
        face_x = 2.0 * masked * weight[1, after] / (raw_weight + weight[0, after])
        face_y = 2.0 * masked * up_y(masked) / (raw_weight + up_y(raw_weight))
        slope_y = slope[1, at]
        face[0, at] = face_x
        face[1, at] = face_y
        flux[0, at] = 0.5 * face_x * (slope[0, at] + slope[0, after])
        flux[1, at] = 0.5 * face_y * (slope_y + up_y(slope_y))
        return carry

    lax.fori_loop(0, FX // RX, faces, 0)

    def start(step, total):
        k = step * RX + 1
        at, before = pl.ds(k, RX), pl.ds(k - 1, RX)
        flux_y = flux[1, at]
        face_y = face[1, at]
        right = flux[0, before] - flux[0, at] + down_y(flux_y) - flux_y
        inverse = 1.0 / (time_part(block) + face[0, at] + face[0, before] + face_y + down_y(face_y))
        first_wave = right * inverse
        inv[at] = inverse
        wave0[at] = first_wave
        return owned(total, k, right * first_wave, ty)

    zero = jnp.zeros((ty, NT), F32)
    b0 = lax.fori_loop(0, FX // RX, start, zero)

    def advance(source, target):
        def body(step, totals):
            k = step * RX + 3
            here, image = image_of(source, face, k, shifts)
            at = pl.ds(k, RX)
            after = here - image * inv[at]
            target[at] = after
            return (
                owned(totals[0], k, here * image, ty),
                owned(totals[1], k, after * image, ty),
            )

        return body

    steps = (FX - 4) // RX
    a0, a1 = lax.fori_loop(0, steps, advance(wave0, wave1), (zero, zero))
    a2, a3 = lax.fori_loop(0, steps, advance(wave1, wave2), (zero, zero))
    sums = [jnp.sum(v, axis=0, keepdims=True) for v in (b0, a0, a1, a2, a3)]
    mom_ref[...] = jnp.concatenate(sums + [jnp.zeros((3, NT), F32)], axis=0)

    rows = TX // n_gy
    for place, ref in enumerate(waves_refs):
        to = lax.rem(place_y + place, n_gy) * rows + 5
        for which, wave in enumerate((wave0, wave1, wave2)):
            for row in range(rows):
                ref[which, row] = wave[to + row, H : H + ty, :].astype(BF16)


def last_kernel(ty, mom_ref, face, wave2, out_ref):
    shifts = plane_shifts(ty + 2 * H)

    def finish(step, total):
        k = step * RX + 5
        here, image = image_of(wave2, face, k, shifts)
        return owned(total, k, here * image, ty)

    total = lax.fori_loop(0, TX // RX, finish, jnp.zeros((ty, NT), F32))
    a4 = jnp.sum(total, axis=0, keepdims=True)
    values = jnp.where(iota((8, NT), 0) == 5, a4, mom_ref[...])
    for device in range(out_ref.shape[0]):
        out_ref[device] = values


def combine_kernel(n_gy, ty, mom_ref, *refs):
    waves_refs, out_ref = refs[:n_gy], refs[n_gy]
    place_y = lax.axis_index("gy")
    moments = jnp.sum(jnp.sum(mom_ref[...], axis=0), axis=1, keepdims=True)
    b0, a0, a1, a2, a3, a4 = [
        jnp.broadcast_to(moments[i : i + 1], (1, NT)) for i in range(6)
    ]
    a0, a1, a2, a3, a4 = [v / b0 for v in (a0, a1, a2, a3, a4)]
    l21 = a1 / a0
    l31 = a2 / a0
    d2 = jnp.maximum(a2 - l21 * a1, 1e-7 * a2 + 1e-30)
    l32 = (a3 - l21 * a2) / d2
    d3 = jnp.maximum(a4 - l31 * a2 - l32 * l32 * d2, 1e-7 * a4 + 1e-30)
    y2 = (1.0 - a0) - l21
    y3 = (1.0 - a0 - a1) - l31 - l32 * y2
    c3 = y3 / d3
    c2 = y2 / d2 - l32 * c3
    c1 = 1.0 / a0 - l21 * c2 - l31 * c3
    for place, ref in enumerate(waves_refs):
        source = lax.rem(place_y - place + n_gy, n_gy)
        at = pl.ds(pl.multiple_of(source * ty, 8), ty)
        for x in range(ref.shape[1]):
            w0, w1, w2 = [ref[which, x].astype(F32) for which in range(3)]
            out_ref[x, at, :] = c1 * w0 + c2 * w1 + c3 * w2


def vmem(count):
    return [pl.BlockSpec(memory_space=pltpu.VMEM)] * count


def on_device(amplitude, conv_first, conv_second, conv_third, conv_last):
    n_gx, n_gy = lax.axis_size("gx"), lax.axis_size("gy")
    ty = amplitude.shape[1]
    grid_x, grid_y = n_gx * TX, n_gy * ty
    assert amplitude.shape == (TX, ty, NT)

    def shift(values, axis, count, step):
        pairs = [(i, i + step) for i in range(count) if 0 <= i + step < count]
        return lax.ppermute(values, axis, pairs)

    xlow = shift(amplitude[TX - H :], "gx", n_gx, 1)
    xhigh = shift(amplitude[:H], "gx", n_gx, -1)
    ylow = shift(
        jnp.concatenate([xlow[:, ty - H :], amplitude[:, ty - H :], xhigh[:, ty - H :]]),
        "gy",
        n_gy,
        1,
    )
    yhigh = shift(
        jnp.concatenate([xlow[:, :H], amplitude[:, :H], xhigh[:, :H]]), "gy", n_gy, -1
    )

    def taps_first(weight):
        return jnp.transpose(weight, (2, 3, 4, 0, 1))

    w1, w2, w3, w4 = pl.pallas_call(
        prep_kernel,
        out_shape=[
            jax.ShapeDtypeStruct((3 * 4 * XW, 4 * BLK), BF16),
            jax.ShapeDtypeStruct((9, BLK, BLK), BF16),
            jax.ShapeDtypeStruct((9, BLK, BLK), BF16),
            jax.ShapeDtypeStruct((9 * FX, 2 * BLK), BF16),
        ],
        in_specs=[pl.BlockSpec(memory_space=pltpu.HBM)] * 4 + [pl.BlockSpec(memory_space=pl.ANY)],
        out_specs=vmem(4),
        scratch_shapes=[
            pltpu.VMEM((1, 3, 3, 3, CH), BF16),
            pltpu.VMEM((27 * CH, CH), BF16),
            pltpu.VMEM((27 * CH, CH), BF16),
            pltpu.VMEM((1, 3, 3, 3, CH), BF16),
            pltpu.SemaphoreType.DMA((4,)),
        ],
        compiler_params=pltpu.CompilerParams(vmem_limit_bytes=16 * 2**20),
        cost_estimate=pl.CostEstimate(flops=10**9, bytes_accessed=10**7, transcendentals=0),
        name="band_weights",
    )(
        jnp.transpose(conv_first, (1, 2, 3, 4, 0)),
        taps_first(conv_second).reshape(27 * CH, CH),
        taps_first(conv_third).reshape(27 * CH, CH),
        jnp.transpose(conv_last, (0, 2, 3, 4, 1)),
        xlow,
    )

    yw, nf = ty + 2 * H, FX + 2
    fault, prob, slope = pl.pallas_call(
        functools.partial(net_kernel, grid_x, grid_y, ty),
        out_shape=[
            jax.ShapeDtypeStruct((TX, ty, NT), BF16),
            jax.ShapeDtypeStruct((FX * yw, NT), F32),
            jax.ShapeDtypeStruct((2, nf, yw, NT), F32),
        ],
        in_specs=vmem(9),
        out_specs=vmem(3),
        scratch_shapes=[
            pltpu.VMEM(((XW + 2) * yw, NT), F32),
            pltpu.VMEM((yw + 2, XW, NT), F32),
            pltpu.VMEM((yw, 2, PAD, BLK), BF16),
            pltpu.VMEM((ty + 12, 2, PAD, BLK), BF16),
            pltpu.VMEM((ty + 10, NT, 2 * BLK), BF16),
            pltpu.VMEM((ty + 10, 9 * FX, NT), F32),
            pltpu.VMEM((3, FX + 4, yw, NT), F32),
        ],
        compiler_params=pltpu.CompilerParams(vmem_limit_bytes=46 * 2**20),
        cost_estimate=pl.CostEstimate(
            flops=3 * 10**10, bytes_accessed=10**7, transcendentals=10**6
        ),
        name="fault_net",
    )(amplitude, xlow, xhigh, ylow, yhigh, w1, w2, w3, w4)

    rows = TX // n_gy
    moments, face, wave2, *waves = pl.pallas_call(
        functools.partial(waves_kernel, grid_x, grid_y, ty),
        out_shape=[
            jax.ShapeDtypeStruct((8, NT), F32),
            jax.ShapeDtypeStruct((2, nf, yw, NT), F32),
            jax.ShapeDtypeStruct((nf, yw, NT), F32),
        ]
        + [jax.ShapeDtypeStruct((3, rows, ty, NT), BF16)] * n_gy,
        in_specs=vmem(2),
        out_specs=vmem(3 + n_gy),
        scratch_shapes=[
            pltpu.VMEM((2, nf, yw, NT), F32),
            pltpu.VMEM((2, nf, yw, NT), F32),
            pltpu.VMEM((nf, yw, NT), F32),
            pltpu.VMEM((nf, yw, NT), F32),
            pltpu.VMEM((nf, yw, NT), F32),
        ],
        compiler_params=pltpu.CompilerParams(vmem_limit_bytes=24 * 2**20),
        cost_estimate=pl.CostEstimate(flops=10**8, bytes_accessed=10**7, transcendentals=0),
        name="solver_waves",
    )(prob, slope)

    everyone = pl.pallas_call(
        functools.partial(last_kernel, ty),
        out_shape=jax.ShapeDtypeStruct((n_gx * n_gy, 8, NT), F32),
        in_specs=vmem(3),
        out_specs=pl.BlockSpec(memory_space=pltpu.VMEM),
        compiler_params=pltpu.CompilerParams(vmem_limit_bytes=16 * 2**20),
        cost_estimate=pl.CostEstimate(flops=10**9, bytes_accessed=10**8, transcendentals=0),
        name="last_moment",
    )(moments, face, wave2)

    arrived = [waves[0]]
    for place in range(1, n_gy):
        pairs = [(i, (i + place) % n_gy) for i in range(n_gy)]
        arrived.append(lax.ppermute(waves[place], "gy", pairs))
    moments = lax.all_to_all(everyone, ("gx", "gy"), split_axis=0, concat_axis=0, tiled=True)
    shift_field = pl.pallas_call(
        functools.partial(combine_kernel, n_gy, ty),
        out_shape=jax.ShapeDtypeStruct((rows, grid_y, NT), F32),
        in_specs=vmem(1 + n_gy),
        out_specs=pl.BlockSpec(memory_space=pltpu.VMEM),
        compiler_params=pltpu.CompilerParams(vmem_limit_bytes=16 * 2**20),
        name="combine_waves",
    )(moments, *arrived)
    return (fault, shift_field)


def solution(mesh):
    return jax.shard_map(
        on_device,
        mesh=mesh,
        in_specs=(P("gx", "gy", None), P(), P(), P(), P()),
        out_specs=(P("gx", "gy", None), P(("gx", "gy"), None, None)),
        check_vma=False,
    )
```

```python
import functools

import jax
import jax.numpy as jnp
from jax import lax
from jax.experimental import pallas as pl
from jax.experimental.pallas import tpu as pltpu
from jax.sharding import PartitionSpec as P

MU_DIAG = 0.05
ETA_TIME = 0.5

TX, NT, H = 16, 128, 8
CH = 16
XW = TX + 2 * H
FX = TX + 8
RX = 4
FIRST, SECOND, THIRD = 4, 11, 11
GROUP = 2
BLK = 256
EDGE = 7
SUB = 16
PAIRS = NT // 2

F32 = jnp.float32
BF16 = jnp.bfloat16


def iota(shape, dim):
    return lax.broadcasted_iota(jnp.int32, shape, dim)


def dot_nt(a, b):
    return lax.dot_general(a, b, (((1,), (1,)), ((), ())), preferred_element_type=F32)


def prep_kernel(
    first_in,
    second_in,
    third_in,
    last_in,
    after_ref,
    w1_ref,
    w2_ref,
    w3_ref,
    w4_ref,
    first_ref,
    second_ref,
    third_ref,
    last_ref,
    sems,
):
    del after_ref
    pairs = ((second_in, second_ref), (third_in, third_ref), (first_in, first_ref), (last_in, last_ref))
    copies = [pltpu.make_async_copy(a, b, sems.at[i]) for i, (a, b) in enumerate(pairs)]
    for copy in copies:
        copy.start()
    for copy in copies:
        copy.wait()
    spread = jnp.where(iota((CH, BLK), 1) % CH == iota((CH, BLK), 0), 1.0, 0.0).astype(BF16)
    unit = jnp.where(iota((BLK, BLK), 1) == iota((BLK, BLK), 0), 1.0, 0.0).astype(BF16)
    cell = iota((CH, BLK), 1) // CH
    inputs = input_cells()
    for source, ref in ((second_ref, w2_ref), (third_ref, w3_ref)):
        tiled = jnp.dot(source[...], spread, preferred_element_type=F32)
        for tile in range(6):
            bands = []
            for yo in range(2):
                for to in range(2):
                    for xo in range(4):
                        band = jnp.zeros((CH, BLK), F32)
                        for at, (y, t, x) in enumerate(inputs[tile]):
                            dx, dy, dt = x - xo + 1, y - yo + 1, t - to + 1
                            if min(dx, dy, dt) >= 0 and max(dx, dy, dt) <= 2:
                                tap = tiled[(dx * 9 + dy * 3 + dt) * CH :][:CH]
                                band = jnp.where(cell == at, tap, band)
                        bands.append(band.astype(BF16))
            turned = dot_nt(unit, jnp.concatenate(bands, axis=0))
            ref[tile * BLK : (tile + 1) * BLK, :] = turned.astype(BF16)

    def taps(ref):
        found = {}
        for dx in range(3):
            for dy in range(3):
                piece = ref[0, dx, dy].astype(BF16)
                tiled = jnp.dot(piece, spread, preferred_element_type=F32)
                for dt in range(3):
                    found[dx, dy, dt] = tiled[dt : dt + 1]
        return found

    first, last = taps(first_ref), taps(last_ref)
    row_x = iota((XW, BLK), 0)
    lane = iota((XW, BLK), 1)
    lane_yt, lane_x = lane // 64, lane // CH % 4
    offset_x = []
    for blk in range(EDGE):
        offset_x.append(row_x - 1 - 4 * blk - lane_x)
    edge = jnp.where(lane_x == 0, row_x - 29, jnp.where(lane_x == 3, row_x, -1))
    offset_x.append(edge)
    masks = [[offset_x[blk] == dx for dx in range(3)] for blk in range(EDGE + 1)]
    for j in range(4):
        for yi in range(4):
            row = (j * 4 + yi) * XW
            columns = []
            for dx in range(3):
                value = jnp.zeros((1, BLK), F32)
                for yo in range(2):
                    for to in range(2):
                        dy, dt = yi - yo, j - to
                        if 0 <= dy <= 2 and 0 <= dt <= 2:
                            value = jnp.where(
                                lane_yt[:1] == yo * 2 + to, first[dx, dy, dt], value
                            )
                columns.append(value)
            for blk in range(EDGE + 1):
                band = jnp.zeros((XW, BLK), F32)
                for dx in range(3):
                    band = jnp.where(masks[blk][dx], columns[dx], band)
                w1_ref[row : row + XW, blk * BLK : (blk + 1) * BLK] = band.astype(BF16)
    row_x = iota((FX, BLK), 0)
    lane_x = iota((FX, BLK), 1) // CH % 4
    for blk in range(EDGE):
        masks = [4 * blk + lane_x - 1 - row_x == dx for dx in range(3)]
        bands = []
        for yi in range(4):
            for j in range(4):
                band = jnp.zeros((FX, BLK), F32)
                for dx in range(3):
                    value = jnp.zeros((1, BLK), F32)
                    for y in range(2):
                        for t in range(2):
                            dy, dt = y + 2 - yi, t + 2 - j
                            if 0 <= dy <= 2 and 0 <= dt <= 2:
                                value = jnp.where(
                                    lane_yt[:1] == y * 2 + t, last[dx, dy, dt], value
                                )
                    band = jnp.where(masks[dx], value, band)
                bands.append(band)
        w4_ref[:, blk * BLK : (blk + 1) * BLK] = jnp.concatenate(bands, axis=0).astype(BF16)


def input_cells():
    tiles = []
    for times in ((0, 1), (-1, 2)):
        for rows in ((0, 1), (-1, 2)):
            tiles.append([(y, t, x) for y in rows for t in times for x in range(4)])
    for rows in ((0, 1), (-1, 2)):
        side = [(0, 4), (-1, 4), (-1, -1), (0, -1), (1, 4), (2, 4), (2, -1), (1, -1)]
        tiles.append([(y, t, x) for y in rows for t, x in side])
    return tiles


def plane_shifts(yw):
    block = (RX, yw, NT)
    lane = iota(block, 2)
    first_lane = lane == 0
    last_lane = lane == NT - 1

    def up_y(v):
        return pltpu.roll(v, yw - 1, 1)

    def down_y(v):
        return pltpu.roll(v, 1, 1)

    def up_t(v, edge=0.0):
        return jnp.where(last_lane, edge, pltpu.roll(v, NT - 1, 2))

    def down_t(v, edge=0.0):
        return jnp.where(first_lane, edge, pltpu.roll(v, 1, 2))

    return block, up_y, down_y, up_t, down_t


def net_kernel(
    grid_x,
    grid_y,
    ty,
    amp_ref,
    xlow_ref,
    xhigh_ref,
    ylow_ref,
    yhigh_ref,
    w1_ref,
    w2_ref,
    w3_ref,
    w4_ref,
    fault_ref,
    prob,
    slope,
    raw,
    amp,
    act1,
    act2,
    part,
    prod,
):
    x0 = lax.axis_index("gx") * TX
    y0 = lax.axis_index("gy") * ty
    yw = ty + 2 * H
    pairs1, pairs2 = yw // 2, ty // 2 + 6
    dot = functools.partial(jnp.dot, preferred_element_type=F32)

    for x in range(XW):
        row = x * yw
        if x < H:
            mid = xlow_ref[x]
        elif x < H + TX:
            mid = amp_ref[x - H]
        else:
            mid = xhigh_ref[x - H - TX]
        raw[row + H : row + H + ty, :] = mid.astype(F32)
        raw[row : row + H, :] = ylow_ref[x].astype(F32)
        raw[row + H + ty : row + yw, :] = yhigh_ref[x].astype(F32)

    def turn(y, carry):
        amp[y + 1] = raw[pl.ds(y, XW, stride=yw), :].astype(BF16)
        return carry

    lax.fori_loop(0, yw, turn, 0, unroll=8)
    amp[0] = jnp.zeros((XW, NT), BF16)
    amp[yw + 1] = jnp.zeros((XW, NT), BF16)

    def pair_of(row):
        return row // SUB + (row % SUB) * 4

    at_row = iota((4 * PAIRS, NT), 0)
    to_pairs = jnp.where(
        iota((4 * PAIRS, NT), 1) == 2 * pair_of(at_row % PAIRS) - 1 + at_row // PAIRS, 1.0, 0.0
    ).astype(BF16)
    at_row = iota((4 * NT, 2 * NT), 0)
    at_lane = iota((4 * NT, 2 * NT), 1)
    from_pairs = jnp.where(
        (at_lane % NT == 2 * pair_of(at_row % PAIRS) - 1 + at_row // NT)
        & (at_lane // NT == at_row % NT // PAIRS),
        1.0,
        0.0,
    ).astype(BF16)

    def lane_masks(blocks):
        slot = iota((1, BLK), 1) // CH % 4
        masks = []
        for blk in range(blocks):
            if blk < EDGE:
                at = x0 - 6 + 4 * blk + slot
            else:
                at = x0 + jnp.where(slot == 0, 22, -7)
            masks.append((at >= 0) & (at < grid_x))
        return masks

    second_row = iota((1, BLK), 1) >= 128

    def scale(mask, y):
        at = y0 + y + jnp.where(second_row, 1, 0)
        return jnp.where(mask & (at >= 0) & (at < grid_y), 1.0, 0.0)

    sub_row = iota((SUB, 128), 0)
    early = iota((PAIRS, 128), 1) < 64
    slot = iota((PAIRS, 128), 1) // CH % 4

    def put(act, pair, blk, values):
        act[0, pair, blk] = values.astype(BF16)
        for half in range(2):
            turned = pltpu.roll(values[:, half * 128 : (half + 1) * 128], 64, 1)
            head = jnp.where(sub_row == 0, 0.0, pltpu.roll(turned[PAIRS - SUB :], 1, 0))
            tail = jnp.where(sub_row == SUB - 1, 0.0, pltpu.roll(turned[:SUB], SUB - 1, 0))
            before = jnp.concatenate([head, turned[: PAIRS - SUB]], axis=0)
            after = jnp.concatenate([turned[SUB:], tail], axis=0)
            both = jnp.where(early, before, after)
            act[1, pair, blk, :, half * 128 : (half + 1) * 128] = both.astype(BF16)

    def put_sides(act, pair, blocks):
        for blk in range(EDGE):
            left, right = (blk - 1) % blocks, (blk + 1) % blocks
            for half in range(2):
                at = slice(half * 128, (half + 1) * 128)
                here = jnp.where(
                    slot == 0,
                    act[0, pair, right, :, at].astype(F32),
                    act[0, pair, left, :, at].astype(F32),
                )
                near = jnp.where(
                    slot == 1,
                    pltpu.roll(act[1, pair, right, :, at].astype(F32), CH, 1),
                    pltpu.roll(act[1, pair, left, :, at].astype(F32), 128 - CH, 1),
                )
                mixed = jnp.where((slot == 0) | (slot == 3), here, near)
                act[2, pair, blk, :, at] = mixed.astype(BF16)

    mask1 = lane_masks(EDGE + 1)

    def first(step, carry):
        pieces = []
        for i in range(FIRST):
            rows = amp[pl.ds((step * FIRST + i) * 2, 4)].reshape(4 * XW, NT)
            turned = dot_nt(to_pairs, rows).astype(BF16)
            pieces.append(
                jnp.concatenate([turned[j * PAIRS : (j + 1) * PAIRS] for j in range(4)], axis=1)
            )
        result = dot(jnp.concatenate(pieces, axis=0), w1_ref[...])
        for i in range(FIRST):
            pair = step * FIRST + i
            for blk in range(EDGE + 1):
                values = result[i * PAIRS : (i + 1) * PAIRS, blk * BLK : (blk + 1) * BLK]
                put(act1, pair, blk, jnp.maximum(values, 0.0) * scale(mask1[blk], 2 * pair - H))
            put_sides(act1, pair, EDGE + 1)
        return carry

    lax.fori_loop(0, pairs1 // FIRST, first, 0)

    def layer(source, w_ref, pair, count):
        size = count * EDGE * PAIRS
        tiles = []
        for kind in range(3):
            centre = source[kind, pl.ds(pair + 1, count), :EDGE].reshape(size, BLK)
            before = source[kind, pl.ds(pair, count), :EDGE, :, 128:].reshape(size, 128)
            after = source[kind, pl.ds(pair + 2, count), :EDGE, :, :128].reshape(size, 128)
            tiles += [centre, before, after]
        return dot(jnp.concatenate(tiles, axis=1), w_ref[...])

    block, up_y, down_y, up_t, down_t = plane_shifts(yw)

    def smooth_yt(v, edge=0.0):
        v = 0.5 * v + 0.25 * (up_t(v, edge) + down_t(v, edge))
        return 0.5 * v + 0.25 * (up_y(v) + down_y(v))

    def amp_rows(x):
        return raw[pl.ds(pl.multiple_of(x * yw, 8), RX * yw), :].reshape(block)

    def products(k):
        here = amp_rows(k + 3)
        grad_x = 0.5 * (amp_rows(k + 4) - amp_rows(k + 2))
        grad_y = 0.5 * (up_y(here) - down_y(here))
        grad_t = 0.5 * (up_t(here) - down_t(here))
        at = pl.ds(k, RX)
        prod[0, at] = smooth_yt(grad_x * grad_t)
        prod[1, at] = smooth_yt(grad_y * grad_t)
        energy = grad_t * grad_t + 0.25 * (grad_x * grad_x + grad_y * grad_y)
        prod[2, at] = smooth_yt(energy, 0.25 * here * here)

    def slopes(k):
        at = pl.ds(k + 1, RX)
        sums = []
        for which in range(3):
            before, here, after = [prod[which, pl.ds(k + i, RX)] for i in range(3)]
            sums.append(0.5 * here + 0.25 * (before + after))
        scale = -1.0 / (sums[2] + 0.05)
        slope[0, at] = sums[0] * scale
        slope[1, at] = sums[1] * scale
    steps2, steps3 = pairs2 // SECOND, pairs2 // THIRD
    blocks2 = -(-(FX // RX + 1) // steps2)
    blocks3 = -(-(FX // RX) // steps3)
    mask2 = lane_masks(EDGE)

    def second(step, carry):
        for i in range(blocks2):
            products(jnp.minimum((step * blocks2 + i) * RX, FX))
        for begin in range(0, SECOND, GROUP):
            count = min(GROUP, SECOND - begin)
            result = layer(act1, w2_ref, step * SECOND + begin, count)
            for i in range(count):
                pair = step * SECOND + begin + i
                for blk in range(EDGE):
                    at = (i * EDGE + blk) * PAIRS
                    values = jnp.maximum(result[at : at + PAIRS], 0.0)
                    put(act2, pair + 1, blk, values * scale(mask2[blk], 2 * pair - 6))
                put_sides(act2, pair + 1, EDGE)
        return carry

    for edge in (0, pairs2 + 1):
        for kind in range(3):
            act2[kind, edge] = jnp.zeros((EDGE, PAIRS, BLK), BF16)
    lax.fori_loop(0, steps2, second, 0)

    act3 = act1.at[0]

    def third(step, carry):
        for i in range(blocks3):
            slopes(jnp.minimum((step * blocks3 + i) * RX, FX - RX))
        for begin in range(0, THIRD, GROUP):
            count = min(GROUP, THIRD - begin)
            result = layer(act2, w3_ref, step * THIRD + begin, count)
            for i in range(count):
                pair = step * THIRD + begin + i
                for blk in range(EDGE):
                    at = (i * EDGE + blk) * PAIRS
                    values = jnp.maximum(result[at : at + PAIRS], 0.0)
                    values = values * scale(mask2[blk], 2 * pair - 6)
                    act3[pair, blk] = values.astype(BF16)
        return carry

    lax.fori_loop(0, steps3, third, 0)
    for pair in range(pairs2, pairs1):
        act3[pair] = jnp.zeros((EDGE + 1, PAIRS, BLK), BF16)

    def fourth(step, carry):
        pair = step * 4
        cells = [act3[pl.ds(pair, 4), blk].reshape(4 * PAIRS, BLK) for blk in range(EDGE)]
        result = dot_nt(w4_ref[...], jnp.concatenate(cells, axis=1))
        for half in range(2):
            columns = result[:, half * NT : (half + 1) * NT]
            sums = jnp.concatenate(
                [
                    jnp.concatenate(
                        [columns[(yi * 4 + j) * FX : (yi * 4 + j + 1) * FX] for j in range(4)],
                        axis=1,
                    )
                    for yi in range(4)
                ],
                axis=0,
            )
            high = sums.astype(BF16)
            low = (sums - high.astype(F32)).astype(BF16)
            both = dot(jnp.concatenate([high, low], axis=0), from_pairs)
            share = both[: 4 * FX] + both[4 * FX :]
            for i in range(2):
                part[pair + half * 2 + i] = share[:, i * NT : (i + 1) * NT]
        return carry

    lax.fori_loop(0, pairs1 // 4, fourth, 0, unroll=2)

    for x in range(FX):
        prob[x * yw : x * yw + H, :] = jnp.zeros((H, NT), F32)
        prob[(x + 1) * yw - H : (x + 1) * yw, :] = jnp.zeros((H, NT), F32)

    def order(step, carry):
        for i in range(4):
            pair = step * 4 + i + 1
            even = part[pair, FX : 2 * FX] + part[pair - 1, 3 * FX :]
            odd = part[pair, 2 * FX : 3 * FX] + part[pair + 1, :FX]
            for row, values in enumerate((even, odd)):
                values = (1.0 / (1.0 + jnp.exp(-values))).astype(BF16).astype(F32)
                prob[pl.ds(2 * pair + 2 + row, FX, stride=yw), :] = values
        return carry

    lax.fori_loop(0, (ty + 8) // 8, order, 0)

    for which in range(2):
        slope[which, FX + 1] = jnp.zeros((yw, NT), F32)
    for x in range(TX):
        fault_ref[x] = prob[(x + 4) * yw + H : (x + 4) * yw + H + ty, :].astype(BF16)


def owned(total, k, values, ty):
    for row in range(RX):
        ok = (k + row >= 5) & (k + row < 5 + TX)
        total = total + jnp.where(ok, values[row, H : H + ty], 0.0)
    return total


def image_of(wave, face, k, shifts):
    block, up_y, down_y, up_t, down_t = shifts
    at, before, after = [pl.ds(k + i, RX) for i in (0, -1, 1)]
    here = wave[at]
    flow = face[1, at] * (here - up_y(here))
    image = time_part(block) * here - ETA_TIME * (up_t(here) + down_t(here))
    image = image + flow - down_y(flow)
    image = image + face[0, at] * (here - wave[after])
    return here, image + face[0, before] * (here - wave[before])


def time_part(block):
    lane = iota(block, 2)
    count = jnp.where(lane == 0, 0.0, 1.0) + jnp.where(lane == NT - 1, 0.0, 1.0)
    return MU_DIAG + ETA_TIME * count


def waves_kernel(grid_x, grid_y, ty, prob, slope, mom_ref, face, wave2, *refs):
    n_gy = grid_y // ty
    waves_refs = refs[:n_gy]
    weight, flux, inv, wave0, wave1 = refs[n_gy:]
    place_y = lax.axis_index("gy")
    x0 = lax.axis_index("gx") * TX
    y0 = place_y * ty
    yw = ty + 2 * H
    shifts = plane_shifts(yw)
    block, up_y, down_y, up_t, down_t = shifts
    at_y = y0 - H + iota(block, 1)
    mask_y = (at_y >= 0) & (at_y < grid_y)

    def weights(step, carry):
        k = step * RX
        at = pl.ds(k + 1, RX)
        rows = prob[pl.ds(pl.multiple_of(k * yw, 8), RX * yw), :].reshape(block)
        raw_weight = 1.0 - 0.9 * rows
        at_x = x0 - 4 + k + iota(block, 0)
        weight[0, at] = raw_weight
        weight[1, at] = jnp.where(mask_y & (at_x >= 0) & (at_x < grid_x), raw_weight, 0.0)
        return carry

    lax.fori_loop(0, FX // RX, weights, 0)
    for which in range(2):
        weight[which, FX + 1] = jnp.full((yw, NT), 1.0 - which, F32)
        face[which, 0] = jnp.zeros((yw, NT), F32)
        flux[which, 0] = jnp.zeros((yw, NT), F32)

    def faces(step, carry):
        k = step * RX + 1
        at, after = pl.ds(k, RX), pl.ds(k + 1, RX)
        raw_weight = weight[0, at]
        masked = weight[1, at]
        face_x = 2.0 * masked * weight[1, after] / (raw_weight + weight[0, after])
        face_y = 2.0 * masked * up_y(masked) / (raw_weight + up_y(raw_weight))
        slope_y = slope[1, at]
        face[0, at] = face_x
        face[1, at] = face_y
        flux[0, at] = 0.5 * face_x * (slope[0, at] + slope[0, after])
        flux[1, at] = 0.5 * face_y * (slope_y + up_y(slope_y))
        return carry

    lax.fori_loop(0, FX // RX, faces, 0)

    def start(step, total):
        k = step * RX + 1
        at, before = pl.ds(k, RX), pl.ds(k - 1, RX)
        flux_y = flux[1, at]
        face_y = face[1, at]
        right = flux[0, before] - flux[0, at] + down_y(flux_y) - flux_y
        inverse = 1.0 / (time_part(block) + face[0, at] + face[0, before] + face_y + down_y(face_y))
        first_wave = right * inverse
        inv[at] = inverse
        wave0[at] = first_wave
        return owned(total, k, right * first_wave, ty)

    zero = jnp.zeros((ty, NT), F32)
    b0 = lax.fori_loop(0, FX // RX, start, zero)

    def advance(source, target):
        def body(step, totals):
            k = step * RX + 3
            here, image = image_of(source, face, k, shifts)
            at = pl.ds(k, RX)
            after = here - image * inv[at]
            target[at] = after
            return (
                owned(totals[0], k, here * image, ty),
                owned(totals[1], k, after * image, ty),
            )

        return body

    steps = (FX - 4) // RX
    a0, a1 = lax.fori_loop(0, steps, advance(wave0, wave1), (zero, zero))
    a2, a3 = lax.fori_loop(0, steps, advance(wave1, wave2), (zero, zero))
    sums = [jnp.sum(v, axis=0, keepdims=True) for v in (b0, a0, a1, a2, a3)]
    mom_ref[...] = jnp.concatenate(sums + [jnp.zeros((3, NT), F32)], axis=0)

    rows = TX // n_gy
    for place, ref in enumerate(waves_refs):
        to = lax.rem(place_y + place, n_gy) * rows + 5
        for which, wave in enumerate((wave0, wave1, wave2)):
            for row in range(rows):
                ref[which, row] = wave[to + row, H : H + ty, :].astype(BF16)


def last_kernel(ty, mom_ref, face, wave2, after_ref, out_ref):
    del after_ref
    shifts = plane_shifts(ty + 2 * H)

    def finish(step, total):
        k = step * RX + 5
        here, image = image_of(wave2, face, k, shifts)
        return owned(total, k, here * image, ty)

    total = lax.fori_loop(0, TX // RX, finish, jnp.zeros((ty, NT), F32))
    a4 = jnp.sum(total, axis=0, keepdims=True)
    values = jnp.where(iota((8, NT), 0) == 5, a4, mom_ref[...])
    for device in range(out_ref.shape[0]):
        out_ref[device] = values


def combine_kernel(n_gy, ty, mom_ref, *refs):
    waves_refs, out_ref = refs[:n_gy], refs[n_gy]
    place_y = lax.axis_index("gy")
    moments = jnp.sum(jnp.sum(mom_ref[...], axis=0), axis=1, keepdims=True)
    b0, a0, a1, a2, a3, a4 = [
        jnp.broadcast_to(moments[i : i + 1], (1, NT)) for i in range(6)
    ]
    a0, a1, a2, a3, a4 = [v / b0 for v in (a0, a1, a2, a3, a4)]
    l21 = a1 / a0
    l31 = a2 / a0
    d2 = jnp.maximum(a2 - l21 * a1, 1e-7 * a2 + 1e-30)
    l32 = (a3 - l21 * a2) / d2
    d3 = jnp.maximum(a4 - l31 * a2 - l32 * l32 * d2, 1e-7 * a4 + 1e-30)
    y2 = (1.0 - a0) - l21
    y3 = (1.0 - a0 - a1) - l31 - l32 * y2
    c3 = y3 / d3
    c2 = y2 / d2 - l32 * c3
    c1 = 1.0 / a0 - l21 * c2 - l31 * c3
    for place, ref in enumerate(waves_refs):
        source = lax.rem(place_y - place + n_gy, n_gy)
        at = pl.ds(pl.multiple_of(source * ty, 8), ty)
        for x in range(ref.shape[1]):
            w0, w1, w2 = [ref[which, x].astype(F32) for which in range(3)]
            out_ref[x, at, :] = c1 * w0 + c2 * w1 + c3 * w2


def vmem(count):
    return [pl.BlockSpec(memory_space=pltpu.VMEM)] * count


def on_device(amplitude, conv_first, conv_second, conv_third, conv_last):
    n_gx, n_gy = lax.axis_size("gx"), lax.axis_size("gy")
    ty = amplitude.shape[1]
    grid_x, grid_y = n_gx * TX, n_gy * ty
    assert amplitude.shape == (TX, ty, NT)

    def shift(values, axis, count, step):
        pairs = [(i, i + step) for i in range(count) if 0 <= i + step < count]
        return lax.ppermute(values, axis, pairs)

    xlow = shift(amplitude[TX - H :], "gx", n_gx, 1)
    xhigh = shift(amplitude[:H], "gx", n_gx, -1)
    ylow = shift(
        jnp.concatenate([xlow[:, ty - H :], amplitude[:, ty - H :], xhigh[:, ty - H :]]),
        "gy",
        n_gy,
        1,
    )
    yhigh = shift(
        jnp.concatenate([xlow[:, :H], amplitude[:, :H], xhigh[:, :H]]), "gy", n_gy, -1
    )

    def taps_first(weight):
        return jnp.transpose(weight, (2, 3, 4, 0, 1))

    w1, w2, w3, w4 = pl.pallas_call(
        prep_kernel,
        out_shape=[
            jax.ShapeDtypeStruct((16 * XW, (EDGE + 1) * BLK), BF16),
            jax.ShapeDtypeStruct((6 * BLK, BLK), BF16),
            jax.ShapeDtypeStruct((6 * BLK, BLK), BF16),
            jax.ShapeDtypeStruct((16 * FX, EDGE * BLK), BF16),
        ],
        in_specs=[pl.BlockSpec(memory_space=pltpu.HBM)] * 4 + [pl.BlockSpec(memory_space=pl.ANY)],
        out_specs=vmem(4),
        scratch_shapes=[
            pltpu.VMEM((1, 3, 3, 3, CH), BF16),
            pltpu.VMEM((27 * CH, CH), BF16),
            pltpu.VMEM((27 * CH, CH), BF16),
            pltpu.VMEM((1, 3, 3, 3, CH), BF16),
            pltpu.SemaphoreType.DMA((4,)),
        ],
        compiler_params=pltpu.CompilerParams(vmem_limit_bytes=16 * 2**20),
        cost_estimate=pl.CostEstimate(flops=10**9, bytes_accessed=10**7, transcendentals=0),
        name="band_weights",
    )(
        jnp.transpose(conv_first, (1, 2, 3, 4, 0)),
        taps_first(conv_second).reshape(27 * CH, CH),
        taps_first(conv_third).reshape(27 * CH, CH),
        jnp.transpose(conv_last, (0, 2, 3, 4, 1)),
        xlow,
    )

    yw, nf = ty + 2 * H, FX + 2
    fault, prob, slope = pl.pallas_call(
        functools.partial(net_kernel, grid_x, grid_y, ty),
        out_shape=[
            jax.ShapeDtypeStruct((TX, ty, NT), BF16),
            jax.ShapeDtypeStruct((FX * yw, NT), F32),
            jax.ShapeDtypeStruct((2, nf, yw, NT), F32),
        ],
        in_specs=vmem(9),
        out_specs=vmem(3),
        scratch_shapes=[
            pltpu.VMEM(((XW + 2) * yw, NT), F32),
            pltpu.VMEM((yw + 2, XW, NT), BF16),
            pltpu.VMEM((3, yw // 2, EDGE + 1, PAIRS, BLK), BF16),
            pltpu.VMEM((3, yw // 2, EDGE, PAIRS, BLK), BF16),
            pltpu.VMEM((yw // 2, 4 * FX, NT), F32),
            pltpu.VMEM((3, FX + 4, yw, NT), F32),
        ],
        compiler_params=pltpu.CompilerParams(vmem_limit_bytes=46 * 2**20),
        cost_estimate=pl.CostEstimate(
            flops=3 * 10**10, bytes_accessed=10**7, transcendentals=10**6
        ),
        name="fault_net",
    )(amplitude, xlow, xhigh, ylow, yhigh, w1, w2, w3, w4)

    rows = TX // n_gy
    moments, face, wave2, *waves = pl.pallas_call(
        functools.partial(waves_kernel, grid_x, grid_y, ty),
        out_shape=[
            jax.ShapeDtypeStruct((8, NT), F32),
            jax.ShapeDtypeStruct((2, nf, yw, NT), F32),
            jax.ShapeDtypeStruct((nf, yw, NT), F32),
        ]
        + [jax.ShapeDtypeStruct((3, rows, ty, NT), BF16)] * n_gy,
        in_specs=vmem(2),
        out_specs=vmem(3 + n_gy),
        scratch_shapes=[
            pltpu.VMEM((2, nf, yw, NT), F32),
            pltpu.VMEM((2, nf, yw, NT), F32),
            pltpu.VMEM((nf, yw, NT), F32),
            pltpu.VMEM((nf, yw, NT), F32),
            pltpu.VMEM((nf, yw, NT), F32),
        ],
        compiler_params=pltpu.CompilerParams(vmem_limit_bytes=24 * 2**20),
        cost_estimate=pl.CostEstimate(flops=10**8, bytes_accessed=10**7, transcendentals=0),
        name="solver_waves",
    )(prob, slope)

    arrived = [waves[0]]
    for place in range(1, n_gy):
        pairs = [(i, (i + place) % n_gy) for i in range(n_gy)]
        arrived.append(lax.ppermute(waves[place], "gy", pairs))

    everyone = pl.pallas_call(
        functools.partial(last_kernel, ty),
        out_shape=jax.ShapeDtypeStruct((n_gx * n_gy, 8, NT), F32),
        in_specs=vmem(3) + [pl.BlockSpec(memory_space=pl.ANY)],
        out_specs=pl.BlockSpec(memory_space=pltpu.VMEM),
        compiler_params=pltpu.CompilerParams(vmem_limit_bytes=16 * 2**20),
        cost_estimate=pl.CostEstimate(flops=10**9, bytes_accessed=10**8, transcendentals=0),
        name="last_moment",
    )(moments, face, wave2, arrived[-1])
    moments = lax.all_to_all(everyone, ("gx", "gy"), split_axis=0, concat_axis=0, tiled=True)
    shift_field = pl.pallas_call(
        functools.partial(combine_kernel, n_gy, ty),
        out_shape=jax.ShapeDtypeStruct((rows, grid_y, NT), F32),
        in_specs=vmem(1 + n_gy),
        out_specs=pl.BlockSpec(memory_space=pltpu.VMEM),
        compiler_params=pltpu.CompilerParams(vmem_limit_bytes=16 * 2**20),
        name="combine_waves",
    )(moments, *arrived)
    return (fault, shift_field)


def solution(mesh):
    return jax.shard_map(
        on_device,
        mesh=mesh,
        in_specs=(P("gx", "gy", None), P(), P(), P(), P()),
        out_specs=(P("gx", "gy", None), P(("gx", "gy"), None, None)),
        check_vma=False,
    )
```

```python
import functools

import jax
import jax.numpy as jnp
from jax import lax
from jax.experimental import pallas as pl
from jax.experimental.pallas import tpu as pltpu
from jax.sharding import PartitionSpec as P

MU_DIAG = 0.05
ETA_TIME = 0.5

TX, NT, H = 16, 128, 8
CH = 16
XW = TX + 2 * H
FX = TX + 8
RX = 4
FIRST, SECOND, THIRD = 4, 11, 11
GROUP = 2
BLK = 256
EDGE = 7
SUB = 16
PAIRS = NT // 2

F32 = jnp.float32
BF16 = jnp.bfloat16


def iota(shape, dim):
    return lax.broadcasted_iota(jnp.int32, shape, dim)


def dot_nt(a, b):
    return lax.dot_general(a, b, (((1,), (1,)), ((), ())), preferred_element_type=F32)


def prep_kernel(
    first_in,
    second_in,
    third_in,
    last_in,
    after_ref,
    w1_ref,
    w2_ref,
    w3_ref,
    w4_ref,
    first_ref,
    second_ref,
    third_ref,
    last_ref,
    sems,
):
    del after_ref
    pairs = ((second_in, second_ref), (third_in, third_ref), (first_in, first_ref), (last_in, last_ref))
    copies = [pltpu.make_async_copy(a, b, sems.at[i]) for i, (a, b) in enumerate(pairs)]
    for copy in copies:
        copy.start()
    for copy in copies:
        copy.wait()
    spread = jnp.where(iota((CH, BLK), 1) % CH == iota((CH, BLK), 0), 1.0, 0.0).astype(BF16)
    unit = jnp.where(iota((BLK, BLK), 1) == iota((BLK, BLK), 0), 1.0, 0.0).astype(BF16)
    cell = iota((CH, BLK), 1) // CH
    inputs = input_cells()
    for source, ref in ((second_ref, w2_ref), (third_ref, w3_ref)):
        tiled = jnp.dot(source[...], spread, preferred_element_type=F32)
        for tile in range(6):
            bands = []
            for yo in range(2):
                for to in range(2):
                    for xo in range(4):
                        band = jnp.zeros((CH, BLK), F32)
                        for at, (y, t, x) in enumerate(inputs[tile]):
                            dx, dy, dt = x - xo + 1, y - yo + 1, t - to + 1
                            if min(dx, dy, dt) >= 0 and max(dx, dy, dt) <= 2:
                                tap = tiled[(dx * 9 + dy * 3 + dt) * CH :][:CH]
                                band = jnp.where(cell == at, tap, band)
                        bands.append(band.astype(BF16))
            turned = dot_nt(unit, jnp.concatenate(bands, axis=0))
            ref[tile * BLK : (tile + 1) * BLK, :] = turned.astype(BF16)

    def taps(ref):
        found = {}
        for dx in range(3):
            for dy in range(3):
                piece = ref[0, dx, dy].astype(BF16)
                tiled = jnp.dot(piece, spread, preferred_element_type=F32)
                for dt in range(3):
                    found[dx, dy, dt] = tiled[dt : dt + 1]
        return found

    first, last = taps(first_ref), taps(last_ref)
    row_x = iota((XW, BLK), 0)
    lane = iota((XW, BLK), 1)
    lane_yt, lane_x = lane // 64, lane // CH % 4
    offset_x = []
    for blk in range(EDGE):
        offset_x.append(row_x - 1 - 4 * blk - lane_x)
    edge = jnp.where(lane_x == 0, row_x - 29, jnp.where(lane_x == 3, row_x, -1))
    offset_x.append(edge)
    masks = [[offset_x[blk] == dx for dx in range(3)] for blk in range(EDGE + 1)]
    for j in range(4):
        for yi in range(4):
            row = (j * 4 + yi) * XW
            columns = []
            for dx in range(3):
                value = jnp.zeros((1, BLK), F32)
                for yo in range(2):
                    for to in range(2):
                        dy, dt = yi - yo, j - to
                        if 0 <= dy <= 2 and 0 <= dt <= 2:
                            value = jnp.where(
                                lane_yt[:1] == yo * 2 + to, first[dx, dy, dt], value
                            )
                columns.append(value)
            for blk in range(EDGE + 1):
                band = jnp.zeros((XW, BLK), F32)
                for dx in range(3):
                    band = jnp.where(masks[blk][dx], columns[dx], band)
                w1_ref[row : row + XW, blk * BLK : (blk + 1) * BLK] = band.astype(BF16)
    row_x = iota((FX, BLK), 0)
    lane_x = iota((FX, BLK), 1) // CH % 4
    for blk in range(EDGE):
        masks = [4 * blk + lane_x - 1 - row_x == dx for dx in range(3)]
        bands = []
        for yi in range(4):
            for j in range(4):
                band = jnp.zeros((FX, BLK), F32)
                for dx in range(3):
                    value = jnp.zeros((1, BLK), F32)
                    for y in range(2):
                        for t in range(2):
                            dy, dt = y + 2 - yi, t + 2 - j
                            if 0 <= dy <= 2 and 0 <= dt <= 2:
                                value = jnp.where(
                                    lane_yt[:1] == y * 2 + t, last[dx, dy, dt], value
                                )
                    band = jnp.where(masks[dx], value, band)
                bands.append(band)
        w4_ref[:, blk * BLK : (blk + 1) * BLK] = jnp.concatenate(bands, axis=0).astype(BF16)


def input_cells():
    tiles = []
    here = [(t, x) for t in (0, 1) for x in range(4)]
    near = [(2, 2), (2, 3), (-1, 0), (-1, 1), (-1, 2), (-1, 3), (2, 0), (2, 1)]
    side = [(0, 4), (2, -1), (-1, 4), (0, -1), (1, 4), (-1, -1), (2, 4), (1, -1)]
    for cells in (here, near, side):
        for rows in ((0, 1), (-1, 2)):
            tiles.append([(y, t, x) for y in rows for t, x in cells])
    return tiles


def plane_shifts(yw):
    block = (RX, yw, NT)
    lane = iota(block, 2)
    first_lane = lane == 0
    last_lane = lane == NT - 1

    def up_y(v):
        return pltpu.roll(v, yw - 1, 1)

    def down_y(v):
        return pltpu.roll(v, 1, 1)

    def up_t(v, edge=0.0):
        return jnp.where(last_lane, edge, pltpu.roll(v, NT - 1, 2))

    def down_t(v, edge=0.0):
        return jnp.where(first_lane, edge, pltpu.roll(v, 1, 2))

    return block, up_y, down_y, up_t, down_t


def net_kernel(
    grid_x,
    grid_y,
    ty,
    amp_ref,
    xlow_ref,
    xhigh_ref,
    ylow_ref,
    yhigh_ref,
    w1_ref,
    w2_ref,
    w3_ref,
    w4_ref,
    fault_ref,
    prob,
    slope,
    raw,
    amp,
    act1,
    act2,
    part,
    prod,
):
    x0 = lax.axis_index("gx") * TX
    y0 = lax.axis_index("gy") * ty
    yw = ty + 2 * H
    pairs1, pairs2 = yw // 2, ty // 2 + 6
    dot = functools.partial(jnp.dot, preferred_element_type=F32)

    for x in range(XW):
        row = x * yw
        if x < H:
            mid = xlow_ref[x]
        elif x < H + TX:
            mid = amp_ref[x - H]
        else:
            mid = xhigh_ref[x - H - TX]
        raw[row + H : row + H + ty, :] = mid.astype(F32)
        raw[row : row + H, :] = ylow_ref[x].astype(F32)
        raw[row + H + ty : row + yw, :] = yhigh_ref[x].astype(F32)

    def turn(y, carry):
        amp[y + 1] = raw[pl.ds(y, XW, stride=yw), :].astype(BF16)
        return carry

    lax.fori_loop(0, yw, turn, 0, unroll=8)
    amp[0] = jnp.zeros((XW, NT), BF16)
    amp[yw + 1] = jnp.zeros((XW, NT), BF16)

    def pair_of(row):
        return row // SUB + (row % SUB) * 4

    at_row = iota((4 * PAIRS, NT), 0)
    to_pairs = jnp.where(
        iota((4 * PAIRS, NT), 1) == 2 * pair_of(at_row % PAIRS) - 1 + at_row // PAIRS, 1.0, 0.0
    ).astype(BF16)
    at_row = iota((4 * NT, 2 * NT), 0)
    at_lane = iota((4 * NT, 2 * NT), 1)
    from_pairs = jnp.where(
        (at_lane % NT == 2 * pair_of(at_row % PAIRS) - 1 + at_row // NT)
        & (at_lane // NT == at_row % NT // PAIRS),
        1.0,
        0.0,
    ).astype(BF16)

    def lane_masks(blocks):
        slot = iota((1, BLK), 1) // CH % 4
        masks = []
        for blk in range(blocks):
            if blk < EDGE:
                at = x0 - 6 + 4 * blk + slot
            else:
                at = x0 + jnp.where(slot == 0, 22, -7)
            masks.append(jnp.where((at >= 0) & (at < grid_x), 1.0, 0.0))
        return masks

    second_row = iota((1, BLK), 1) >= 128

    def row_mask(y):
        at = y0 + y + jnp.where(second_row, 1, 0)
        return jnp.where((at >= 0) & (at < grid_y), 1.0, 0.0)

    sub_row = iota((SUB, 128), 0)
    place = iota((PAIRS, 128), 1) // CH
    early = (place >= 2) & (place < 6)

    def put(act, pair, blk, values):
        act[0, pair, blk] = values.astype(BF16)
        for half in range(2):
            turned = pltpu.roll(values[:, half * 128 : (half + 1) * 128], 96, 1)
            head = jnp.where(sub_row == 0, 0.0, pltpu.roll(turned[PAIRS - SUB :], 1, 0))
            tail = jnp.where(sub_row == SUB - 1, 0.0, pltpu.roll(turned[:SUB], SUB - 1, 0))
            before = jnp.concatenate([head, turned[: PAIRS - SUB]], axis=0)
            after = jnp.concatenate([turned[SUB:], tail], axis=0)
            both = jnp.where(early, before, after)
            act[1, pair, blk, :, half * 128 : (half + 1) * 128] = both.astype(BF16)

    def put_sides(act, pair, blocks):
        for blk in range(EDGE):
            left, right = (blk - 1) % blocks, (blk + 1) % blocks
            for half in range(2):
                at = slice(half * 128, (half + 1) * 128)
                even = jnp.where(place % 4 == 0, act[0, pair, right, :, at], act[1, pair, right, :, at])
                odd = jnp.where(place % 4 == 3, act[0, pair, left, :, at], act[1, pair, left, :, at])
                act[2, pair, blk, :, at] = jnp.where(place % 2 == 0, even, odd)

    mask1 = lane_masks(EDGE + 1)

    def first(step, carry):
        pieces = []
        for i in range(FIRST):
            rows = amp[pl.ds((step * FIRST + i) * 2, 4)].reshape(4 * XW, NT)
            turned = dot_nt(to_pairs, rows).astype(BF16)
            pieces.append(
                jnp.concatenate([turned[j * PAIRS : (j + 1) * PAIRS] for j in range(4)], axis=1)
            )
        result = dot(jnp.concatenate(pieces, axis=0), w1_ref[...])
        for i in range(FIRST):
            pair = step * FIRST + i
            inside = row_mask(2 * pair - H)
            for blk in range(EDGE + 1):
                values = result[i * PAIRS : (i + 1) * PAIRS, blk * BLK : (blk + 1) * BLK]
                put(act1, pair, blk, jnp.maximum(values, 0.0) * (mask1[blk] * inside))
            put_sides(act1, pair, EDGE + 1)
        return carry

    lax.fori_loop(0, pairs1 // FIRST, first, 0)

    def layer(source, w_ref, pair, count):
        size = count * EDGE * PAIRS
        tiles = []
        for kind in range(3):
            centre = source[kind, pl.ds(pair + 1, count), :EDGE].reshape(size, BLK)
            before = source[kind, pl.ds(pair, count), :EDGE, :, 128:].reshape(size, 128)
            after = source[kind, pl.ds(pair + 2, count), :EDGE, :, :128].reshape(size, 128)
            tiles += [centre, before, after]
        return dot(jnp.concatenate(tiles, axis=1), w_ref[...])

    block, up_y, down_y, up_t, down_t = plane_shifts(yw)

    def smooth_yt(v, edge=0.0):
        v = 0.5 * v + 0.25 * (up_t(v, edge) + down_t(v, edge))
        return 0.5 * v + 0.25 * (up_y(v) + down_y(v))

    def amp_rows(x):
        return raw[pl.ds(pl.multiple_of(x * yw, 8), RX * yw), :].reshape(block)

    def products(k):
        here = amp_rows(k + 3)
        grad_x = 0.5 * (amp_rows(k + 4) - amp_rows(k + 2))
        grad_y = 0.5 * (up_y(here) - down_y(here))
        grad_t = 0.5 * (up_t(here) - down_t(here))
        at = pl.ds(k, RX)
        prod[0, at] = smooth_yt(grad_x * grad_t)
        prod[1, at] = smooth_yt(grad_y * grad_t)
        energy = grad_t * grad_t + 0.25 * (grad_x * grad_x + grad_y * grad_y)
        prod[2, at] = smooth_yt(energy, 0.25 * here * here)

    def slopes(k):
        at = pl.ds(k + 1, RX)
        sums = []
        for which in range(3):
            before, here, after = [prod[which, pl.ds(k + i, RX)] for i in range(3)]
            sums.append(0.5 * here + 0.25 * (before + after))
        scale = -1.0 / (sums[2] + 0.05)
        slope[0, at] = sums[0] * scale
        slope[1, at] = sums[1] * scale
    steps2, steps3 = pairs2 // SECOND, pairs2 // THIRD
    blocks2 = -(-(FX // RX + 1) // steps2)
    blocks3 = -(-(FX // RX) // steps3)
    mask2 = lane_masks(EDGE)

    def second(step, carry):
        for i in range(blocks2):
            products(jnp.minimum((step * blocks2 + i) * RX, FX))
        for begin in range(0, SECOND, GROUP):
            count = min(GROUP, SECOND - begin)
            result = layer(act1, w2_ref, step * SECOND + begin, count)
            for i in range(count):
                pair = step * SECOND + begin + i
                inside = row_mask(2 * pair - 6)
                for blk in range(EDGE):
                    at = (i * EDGE + blk) * PAIRS
                    values = jnp.maximum(result[at : at + PAIRS], 0.0)
                    put(act2, pair + 1, blk, values * (mask2[blk] * inside))
                put_sides(act2, pair + 1, EDGE)
        return carry

    for edge in (0, pairs2 + 1):
        for kind in range(3):
            act2[kind, edge] = jnp.zeros((EDGE, PAIRS, BLK), BF16)
    lax.fori_loop(0, steps2, second, 0)

    act3 = act1.at[0]

    def third(step, carry):
        for i in range(blocks3):
            slopes(jnp.minimum((step * blocks3 + i) * RX, FX - RX))
        for begin in range(0, THIRD, GROUP):
            count = min(GROUP, THIRD - begin)
            result = layer(act2, w3_ref, step * THIRD + begin, count)
            for i in range(count):
                pair = step * THIRD + begin + i
                inside = row_mask(2 * pair - 6)
                for blk in range(EDGE):
                    at = (i * EDGE + blk) * PAIRS
                    values = jnp.maximum(result[at : at + PAIRS], 0.0)
                    act3[pair, blk] = (values * (mask2[blk] * inside)).astype(BF16)
        return carry

    lax.fori_loop(0, steps3, third, 0)
    for pair in range(pairs2, pairs1):
        act3[pair] = jnp.zeros((EDGE + 1, PAIRS, BLK), BF16)

    def fourth(step, carry):
        pair = step * 4
        cells = [act3[pl.ds(pair, 4), blk].reshape(4 * PAIRS, BLK) for blk in range(EDGE)]
        result = dot_nt(w4_ref[...], jnp.concatenate(cells, axis=1))
        for half in range(2):
            columns = result[:, half * NT : (half + 1) * NT]
            sums = jnp.concatenate(
                [
                    jnp.concatenate(
                        [columns[(yi * 4 + j) * FX : (yi * 4 + j + 1) * FX] for j in range(4)],
                        axis=1,
                    )
                    for yi in range(4)
                ],
                axis=0,
            )
            high = sums.astype(BF16)
            low = (sums - high.astype(F32)).astype(BF16)
            both = dot(jnp.concatenate([high, low], axis=0), from_pairs)
            share = both[: 4 * FX] + both[4 * FX :]
            for i in range(2):
                part[pair + half * 2 + i] = share[:, i * NT : (i + 1) * NT]
        return carry

    lax.fori_loop(0, pairs1 // 4, fourth, 0, unroll=2)

    for x in range(FX):
        prob[x * yw : x * yw + H, :] = jnp.zeros((H, NT), F32)
        prob[(x + 1) * yw - H : (x + 1) * yw, :] = jnp.zeros((H, NT), F32)

    def order(step, carry):
        for i in range(4):
            pair = step * 4 + i + 1
            even = part[pair, FX : 2 * FX] + part[pair - 1, 3 * FX :]
            odd = part[pair, 2 * FX : 3 * FX] + part[pair + 1, :FX]
            for row, values in enumerate((even, odd)):
                values = (1.0 / (1.0 + jnp.exp(-values))).astype(BF16).astype(F32)
                prob[pl.ds(2 * pair + 2 + row, FX, stride=yw), :] = values
        return carry

    lax.fori_loop(0, (ty + 8) // 8, order, 0)

    for which in range(2):
        slope[which, FX + 1] = jnp.zeros((yw, NT), F32)
    for x in range(TX):
        fault_ref[x] = prob[(x + 4) * yw + H : (x + 4) * yw + H + ty, :].astype(BF16)


def owned(total, k, values, ty):
    for row in range(RX):
        ok = (k + row >= 5) & (k + row < 5 + TX)
        total = total + jnp.where(ok, values[row, H : H + ty], 0.0)
    return total


def image_of(wave, face, k, shifts):
    block, up_y, down_y, up_t, down_t = shifts
    at, before, after = [pl.ds(k + i, RX) for i in (0, -1, 1)]
    here = wave[at]
    flow = face[1, at] * (here - up_y(here))
    image = time_part(block) * here - ETA_TIME * (up_t(here) + down_t(here))
    image = image + flow - down_y(flow)
    image = image + face[0, at] * (here - wave[after])
    return here, image + face[0, before] * (here - wave[before])


def time_part(block):
    lane = iota(block, 2)
    count = jnp.where(lane == 0, 0.0, 1.0) + jnp.where(lane == NT - 1, 0.0, 1.0)
    return MU_DIAG + ETA_TIME * count


def waves_kernel(grid_x, grid_y, ty, prob, slope, mom_ref, face, wave2, *refs):
    n_gy = grid_y // ty
    waves_refs = refs[:n_gy]
    weight, flux, inv, wave0, wave1 = refs[n_gy:]
    place_y = lax.axis_index("gy")
    x0 = lax.axis_index("gx") * TX
    y0 = place_y * ty
    yw = ty + 2 * H
    shifts = plane_shifts(yw)
    block, up_y, down_y, up_t, down_t = shifts
    at_y = y0 - H + iota(block, 1)
    mask_y = (at_y >= 0) & (at_y < grid_y)

    def weights(step, carry):
        k = step * RX
        at = pl.ds(k + 1, RX)
        rows = prob[pl.ds(pl.multiple_of(k * yw, 8), RX * yw), :].reshape(block)
        raw_weight = 1.0 - 0.9 * rows
        at_x = x0 - 4 + k + iota(block, 0)
        weight[0, at] = raw_weight
        weight[1, at] = jnp.where(mask_y & (at_x >= 0) & (at_x < grid_x), raw_weight, 0.0)
        return carry

    lax.fori_loop(0, FX // RX, weights, 0)
    for which in range(2):
        weight[which, FX + 1] = jnp.full((yw, NT), 1.0 - which, F32)
        face[which, 0] = jnp.zeros((yw, NT), F32)
        flux[which, 0] = jnp.zeros((yw, NT), F32)

    def faces(step, carry):
        k = step * RX + 1
        at, after = pl.ds(k, RX), pl.ds(k + 1, RX)
        raw_weight = weight[0, at]
        masked = weight[1, at]
        face_x = 2.0 * masked * weight[1, after] / (raw_weight + weight[0, after])
        face_y = 2.0 * masked * up_y(masked) / (raw_weight + up_y(raw_weight))
        slope_y = slope[1, at]
        face[0, at] = face_x
        face[1, at] = face_y
        flux[0, at] = 0.5 * face_x * (slope[0, at] + slope[0, after])
        flux[1, at] = 0.5 * face_y * (slope_y + up_y(slope_y))
        return carry

    lax.fori_loop(0, FX // RX, faces, 0)

    def start(step, total):
        k = step * RX + 1
        at, before = pl.ds(k, RX), pl.ds(k - 1, RX)
        flux_y = flux[1, at]
        face_y = face[1, at]
        right = flux[0, before] - flux[0, at] + down_y(flux_y) - flux_y
        inverse = 1.0 / (time_part(block) + face[0, at] + face[0, before] + face_y + down_y(face_y))
        first_wave = right * inverse
        inv[at] = inverse
        wave0[at] = first_wave
        return owned(total, k, right * first_wave, ty)

    zero = jnp.zeros((ty, NT), F32)
    b0 = lax.fori_loop(0, FX // RX, start, zero)

    def advance(source, target):
        def body(step, totals):
            k = step * RX + 3
            here, image = image_of(source, face, k, shifts)
            at = pl.ds(k, RX)
            after = here - image * inv[at]
            target[at] = after
            return (
                owned(totals[0], k, here * image, ty),
                owned(totals[1], k, after * image, ty),
            )

        return body

    steps = (FX - 4) // RX
    a0, a1 = lax.fori_loop(0, steps, advance(wave0, wave1), (zero, zero))
    a2, a3 = lax.fori_loop(0, steps, advance(wave1, wave2), (zero, zero))
    sums = [jnp.sum(v, axis=0, keepdims=True) for v in (b0, a0, a1, a2, a3)]
    mom_ref[...] = jnp.concatenate(sums + [jnp.zeros((3, NT), F32)], axis=0)

    rows = TX // n_gy
    for place, ref in enumerate(waves_refs):
        to = lax.rem(place_y + place, n_gy) * rows + 5
        for which, wave in enumerate((wave0, wave1, wave2)):
            for row in range(rows):
                ref[which, row] = wave[to + row, H : H + ty, :].astype(BF16)


def last_kernel(ty, mom_ref, face, wave2, out_ref):
    shifts = plane_shifts(ty + 2 * H)

    def finish(step, total):
        k = step * RX + 5
        here, image = image_of(wave2, face, k, shifts)
        return owned(total, k, here * image, ty)

    total = lax.fori_loop(0, TX // RX, finish, jnp.zeros((ty, NT), F32))
    a4 = jnp.sum(total, axis=0, keepdims=True)
    sums = jnp.sum(jnp.where(iota((8, NT), 0) == 5, a4, mom_ref[...]), axis=1, keepdims=True)
    values = jnp.where(iota((8, NT), 0) == iota((8, NT), 1), sums, 0.0)
    values = jnp.sum(values, axis=0, keepdims=True)
    for device in range(out_ref.shape[0]):
        out_ref[device] = values


def combine_kernel(n_gy, ty, mom_ref, *refs):
    waves_refs, out_ref = refs[:n_gy], refs[n_gy]
    place_y = lax.axis_index("gy")
    moments = jnp.sum(mom_ref[...], axis=0)
    b0, a0, a1, a2, a3, a4 = [
        jnp.broadcast_to(moments[:, i : i + 1], (1, NT)) for i in range(6)
    ]
    a0, a1, a2, a3, a4 = [v / b0 for v in (a0, a1, a2, a3, a4)]
    l21 = a1 / a0
    l31 = a2 / a0
    d2 = jnp.maximum(a2 - l21 * a1, 1e-7 * a2 + 1e-30)
    l32 = (a3 - l21 * a2) / d2
    d3 = jnp.maximum(a4 - l31 * a2 - l32 * l32 * d2, 1e-7 * a4 + 1e-30)
    y2 = (1.0 - a0) - l21
    y3 = (1.0 - a0 - a1) - l31 - l32 * y2
    c3 = y3 / d3
    c2 = y2 / d2 - l32 * c3
    c1 = 1.0 / a0 - l21 * c2 - l31 * c3
    for place, ref in enumerate(waves_refs):
        source = lax.rem(place_y - place + n_gy, n_gy)
        at = pl.ds(pl.multiple_of(source * ty, 8), ty)
        for x in range(ref.shape[1]):
            w0, w1, w2 = [ref[which, x].astype(F32) for which in range(3)]
            out_ref[x, at, :] = c1 * w0 + c2 * w1 + c3 * w2


def vmem(count):
    return [pl.BlockSpec(memory_space=pltpu.VMEM)] * count


def on_device(amplitude, conv_first, conv_second, conv_third, conv_last):
    n_gx, n_gy = lax.axis_size("gx"), lax.axis_size("gy")
    ty = amplitude.shape[1]
    grid_x, grid_y = n_gx * TX, n_gy * ty
    assert amplitude.shape == (TX, ty, NT)

    def shift(values, axis, count, step):
        pairs = [(i, i + step) for i in range(count) if 0 <= i + step < count]
        return lax.ppermute(values, axis, pairs)

    xlow = shift(amplitude[TX - H :], "gx", n_gx, 1)
    xhigh = shift(amplitude[:H], "gx", n_gx, -1)
    ylow = shift(
        jnp.concatenate([xlow[:, ty - H :], amplitude[:, ty - H :], xhigh[:, ty - H :]]),
        "gy",
        n_gy,
        1,
    )
    yhigh = shift(
        jnp.concatenate([xlow[:, :H], amplitude[:, :H], xhigh[:, :H]]), "gy", n_gy, -1
    )

    def taps_first(weight):
        return jnp.transpose(weight, (2, 3, 4, 0, 1))

    w1, w2, w3, w4 = pl.pallas_call(
        prep_kernel,
        out_shape=[
            jax.ShapeDtypeStruct((16 * XW, (EDGE + 1) * BLK), BF16),
            jax.ShapeDtypeStruct((6 * BLK, BLK), BF16),
            jax.ShapeDtypeStruct((6 * BLK, BLK), BF16),
            jax.ShapeDtypeStruct((16 * FX, EDGE * BLK), BF16),
        ],
        in_specs=[pl.BlockSpec(memory_space=pltpu.HBM)] * 4 + [pl.BlockSpec(memory_space=pl.ANY)],
        out_specs=vmem(4),
        scratch_shapes=[
            pltpu.VMEM((1, 3, 3, 3, CH), BF16),
            pltpu.VMEM((27 * CH, CH), BF16),
            pltpu.VMEM((27 * CH, CH), BF16),
            pltpu.VMEM((1, 3, 3, 3, CH), BF16),
            pltpu.SemaphoreType.DMA((4,)),
        ],
        compiler_params=pltpu.CompilerParams(vmem_limit_bytes=16 * 2**20),
        cost_estimate=pl.CostEstimate(flops=10**9, bytes_accessed=10**7, transcendentals=0),
        name="band_weights",
    )(
        jnp.transpose(conv_first, (1, 2, 3, 4, 0)),
        taps_first(conv_second).reshape(27 * CH, CH),
        taps_first(conv_third).reshape(27 * CH, CH),
        jnp.transpose(conv_last, (0, 2, 3, 4, 1)),
        xlow,
    )

    yw, nf = ty + 2 * H, FX + 2
    fault, prob, slope = pl.pallas_call(
        functools.partial(net_kernel, grid_x, grid_y, ty),
        out_shape=[
            jax.ShapeDtypeStruct((TX, ty, NT), BF16),
            jax.ShapeDtypeStruct((FX * yw, NT), F32),
            jax.ShapeDtypeStruct((2, nf, yw, NT), F32),
        ],
        in_specs=vmem(9),
        out_specs=vmem(3),
        scratch_shapes=[
            pltpu.VMEM(((XW + 2) * yw, NT), F32),
            pltpu.VMEM((yw + 2, XW, NT), BF16),
            pltpu.VMEM((3, yw // 2, EDGE + 1, PAIRS, BLK), BF16),
            pltpu.VMEM((3, yw // 2, EDGE, PAIRS, BLK), BF16),
            pltpu.VMEM((yw // 2, 4 * FX, NT), F32),
            pltpu.VMEM((3, FX + 4, yw, NT), F32),
        ],
        compiler_params=pltpu.CompilerParams(vmem_limit_bytes=46 * 2**20),
        cost_estimate=pl.CostEstimate(
            flops=3 * 10**10, bytes_accessed=10**7, transcendentals=10**6
        ),
        name="fault_net",
    )(amplitude, xlow, xhigh, ylow, yhigh, w1, w2, w3, w4)

    rows = TX // n_gy
    moments, face, wave2, *waves = pl.pallas_call(
        functools.partial(waves_kernel, grid_x, grid_y, ty),
        out_shape=[
            jax.ShapeDtypeStruct((8, NT), F32),
            jax.ShapeDtypeStruct((2, nf, yw, NT), F32),
            jax.ShapeDtypeStruct((nf, yw, NT), F32),
        ]
        + [jax.ShapeDtypeStruct((3, rows, ty, NT), BF16)] * n_gy,
        in_specs=vmem(2),
        out_specs=vmem(3 + n_gy),
        scratch_shapes=[
            pltpu.VMEM((2, nf, yw, NT), F32),
            pltpu.VMEM((2, nf, yw, NT), F32),
            pltpu.VMEM((nf, yw, NT), F32),
            pltpu.VMEM((nf, yw, NT), F32),
            pltpu.VMEM((nf, yw, NT), F32),
        ],
        compiler_params=pltpu.CompilerParams(vmem_limit_bytes=24 * 2**20),
        cost_estimate=pl.CostEstimate(flops=10**8, bytes_accessed=10**7, transcendentals=0),
        name="solver_waves",
    )(prob, slope)

    arrived = [waves[0]]
    for place in range(1, n_gy):
        pairs = [(i, (i + place) % n_gy) for i in range(n_gy)]
        arrived.append(lax.ppermute(waves[place], "gy", pairs))

    everyone = pl.pallas_call(
        functools.partial(last_kernel, ty),
        out_shape=jax.ShapeDtypeStruct((n_gx * n_gy, 1, NT), F32),
        in_specs=vmem(3),
        out_specs=pl.BlockSpec(memory_space=pltpu.VMEM),
        compiler_params=pltpu.CompilerParams(vmem_limit_bytes=16 * 2**20),
        cost_estimate=pl.CostEstimate(flops=10**9, bytes_accessed=10**8, transcendentals=0),
        name="last_moment",
    )(moments, face, wave2)
    moments = lax.all_to_all(everyone, ("gx", "gy"), split_axis=0, concat_axis=0, tiled=True)
    shift_field = pl.pallas_call(
        functools.partial(combine_kernel, n_gy, ty),
        out_shape=jax.ShapeDtypeStruct((rows, grid_y, NT), F32),
        in_specs=vmem(1 + n_gy),
        out_specs=pl.BlockSpec(memory_space=pltpu.VMEM),
        compiler_params=pltpu.CompilerParams(vmem_limit_bytes=16 * 2**20),
        name="combine_waves",
    )(moments, *arrived)
    return (fault, shift_field)


def solution(mesh):
    return jax.shard_map(
        on_device,
        mesh=mesh,
        in_specs=(P("gx", "gy", None), P(), P(), P(), P()),
        out_specs=(P("gx", "gy", None), P(("gx", "gy"), None, None)),
        check_vma=False,
    )
```

```python
import functools

import jax
import jax.numpy as jnp
from jax import lax
from jax.experimental import pallas as pl
from jax.experimental.pallas import tpu as pltpu
from jax.sharding import PartitionSpec as P

MU_DIAG = 0.05
ETA_TIME = 0.5

TX, NT, H = 16, 128, 8
CH = 16
XW = TX + 2 * H
FX = TX + 8
RX = 4
FIRST, SECOND, THIRD = 8, 2, 2
GROUP = 1
BLK = 256
EDGE = 7
SUB = 16
PAIRS = NT // 2

F32 = jnp.float32
BF16 = jnp.bfloat16


def iota(shape, dim):
    return lax.broadcasted_iota(jnp.int32, shape, dim)


def dot_nt(a, b):
    return lax.dot_general(a, b, (((1,), (1,)), ((), ())), preferred_element_type=F32)


def prep_kernel(inner_ref, outer_ref, after_ref, w1_ref, w2_ref, w3_ref, w4_ref):
    del after_ref
    spread = jnp.where(iota((CH, BLK), 1) % CH == iota((CH, BLK), 0), 1.0, 0.0).astype(BF16)
    unit = jnp.where(iota((BLK, BLK), 1) == iota((BLK, BLK), 0), 1.0, 0.0).astype(BF16)
    none = jnp.zeros((CH, BLK), BF16)
    cell = iota((CH, BLK), 1) // CH
    at_cell = [cell == at for at in range(16)]
    inputs = input_cells()
    tiled = jnp.dot(inner_ref[...], spread, preferred_element_type=F32).astype(BF16)
    for layer, ref in enumerate((w2_ref, w3_ref)):
        for tile in range(6):
            bands = []
            for yo in range(2):
                for to in range(2):
                    for xo in range(4):
                        band = none
                        for at, (y, t, x) in enumerate(inputs[tile]):
                            dx, dy, dt = x - xo + 1, y - yo + 1, t - to + 1
                            if min(dx, dy, dt) >= 0 and max(dx, dy, dt) <= 2:
                                tap = tiled[(layer * 27 + dx * 9 + dy * 3 + dt) * CH :][:CH]
                                band = jnp.where(at_cell[at], tap, band)
                        bands.append(band)
            turned = dot_nt(unit, jnp.concatenate(bands, axis=0))
            ref[tile * BLK : (tile + 1) * BLK, :] = turned.astype(BF16)

    def taps(which):
        found = {}
        for dx in range(3):
            for dy in range(3):
                tiled = jnp.dot(outer_ref[which, dx, dy], spread, preferred_element_type=F32)
                for dt in range(3):
                    found[dx, dy, dt] = tiled[dt : dt + 1]
        return found

    first, last = taps(0), taps(1)
    lane_yt = iota((1, BLK), 1) // 64
    quarter = [lane_yt == at for at in range(4)]

    def by_quarter(found, dx, at):
        value = jnp.zeros((1, BLK), F32)
        for y in range(2):
            for t in range(2):
                dy, dt = at(y, t)
                if 0 <= dy <= 2 and 0 <= dt <= 2:
                    value = jnp.where(quarter[y * 2 + t], found[dx, dy, dt], value)
        return value

    def rows_of(found, rows, at):
        return [
            jnp.broadcast_to(by_quarter(found, dx, at), (rows, BLK)).astype(BF16)
            for dx in range(3)
        ]

    row_x = iota((XW, BLK), 0)
    lane_x = iota((XW, BLK), 1) // CH % 4
    offset_x = [row_x - 1 - 4 * blk - lane_x for blk in range(EDGE)]
    offset_x.append(jnp.where(lane_x == 0, row_x - 29, jnp.where(lane_x == 3, row_x, -1)))
    masks = [[offset == dx for dx in range(3)] for offset in offset_x]
    none = jnp.zeros((XW, BLK), BF16)
    for j in range(4):
        for yi in range(4):
            row = (j * 4 + yi) * XW
            values = rows_of(first, XW, lambda y, t: (yi - y, j - t))
            for blk in range(EDGE + 1):
                band = none
                for dx in range(3):
                    band = jnp.where(masks[blk][dx], values[dx], band)
                w1_ref[row : row + XW, blk * BLK : (blk + 1) * BLK] = band
    row_x = iota((FX, BLK), 0)
    lane_x = iota((FX, BLK), 1) // CH % 4
    masks = [
        [4 * blk + lane_x - 1 - row_x == dx for dx in range(3)] for blk in range(EDGE)
    ]
    none = jnp.zeros((FX, BLK), F32)
    bands = [[] for blk in range(EDGE)]
    for yi in range(4):
        for j in range(4):
            values = [
                by_quarter(last, dx, lambda y, t: (y + 2 - yi, t + 2 - j)) for dx in range(3)
            ]
            for blk in range(EDGE):
                band = none
                for dx in range(3):
                    band = jnp.where(masks[blk][dx], values[dx], band)
                bands[blk].append(band)
    for blk in range(EDGE):
        whole = jnp.concatenate(bands[blk], axis=0).astype(BF16)
        w4_ref[:, blk * BLK : (blk + 1) * BLK] = whole


def input_cells():
    tiles = []
    here = [(t, x) for t in (0, 1) for x in range(4)]
    near = [(2, 2), (2, 3), (-1, 0), (-1, 1), (-1, 2), (-1, 3), (2, 0), (2, 1)]
    side = [(0, 4), (2, -1), (-1, 4), (0, -1), (1, 4), (-1, -1), (2, 4), (1, -1)]
    for cells in (here, near, side):
        for rows in ((0, 1), (-1, 2)):
            tiles.append([(y, t, x) for y in rows for t, x in cells])
    return tiles


def plane_shifts(yw):
    block = (RX, yw, NT)
    lane = iota(block, 2)
    first_lane = lane == 0
    last_lane = lane == NT - 1

    def up_y(v):
        return pltpu.roll(v, yw - 1, 1)

    def down_y(v):
        return pltpu.roll(v, 1, 1)

    def up_t(v, edge=0.0):
        return jnp.where(last_lane, edge, pltpu.roll(v, NT - 1, 2))

    def down_t(v, edge=0.0):
        return jnp.where(first_lane, edge, pltpu.roll(v, 1, 2))

    return block, up_y, down_y, up_t, down_t


def net_kernel(
    grid_x,
    grid_y,
    ty,
    amp_ref,
    xlow_ref,
    xhigh_ref,
    ylow_ref,
    yhigh_ref,
    w1_ref,
    w2_ref,
    w3_ref,
    w4_ref,
    fault_ref,
    prob,
    slope,
    raw,
    amp,
    act1,
    act2,
    part,
    prod,
):
    x0 = lax.axis_index("gx") * TX
    y0 = lax.axis_index("gy") * ty
    yw = ty + 2 * H
    pairs1, pairs2 = yw // 2, ty // 2 + 6
    dot = functools.partial(jnp.dot, preferred_element_type=F32)

    for x in range(XW):
        row = x * yw
        if x < H:
            mid = xlow_ref[x]
        elif x < H + TX:
            mid = amp_ref[x - H]
        else:
            mid = xhigh_ref[x - H - TX]
        raw[row + H : row + H + ty, :] = mid.astype(F32)
        raw[row : row + H, :] = ylow_ref[x].astype(F32)
        raw[row + H + ty : row + yw, :] = yhigh_ref[x].astype(F32)

    def turn(y, carry):
        amp[y + 1] = raw[pl.ds(y, XW, stride=yw), :].astype(BF16)
        return carry

    lax.fori_loop(0, yw, turn, 0, unroll=8)
    amp[0] = jnp.zeros((XW, NT), BF16)
    amp[yw + 1] = jnp.zeros((XW, NT), BF16)

    def pair_of(row):
        return row // SUB + (row % SUB) * 4

    at_row = iota((4 * PAIRS, NT), 0)
    to_pairs = jnp.where(
        iota((4 * PAIRS, NT), 1) == 2 * pair_of(at_row % PAIRS) - 1 + at_row // PAIRS, 1.0, 0.0
    ).astype(BF16)
    at_row = iota((4 * NT, 2 * NT), 0)
    at_lane = iota((4 * NT, 2 * NT), 1)
    from_pairs = jnp.where(
        (at_lane % NT == 2 * pair_of(at_row % PAIRS) - 1 + at_row // NT)
        & (at_lane // NT == at_row % NT // PAIRS),
        1.0,
        0.0,
    ).astype(BF16)

    def lane_masks(blocks):
        slot = iota((1, BLK), 1) // CH % 4
        masks = []
        for blk in range(blocks):
            if blk < EDGE:
                at = x0 - 6 + 4 * blk + slot
            else:
                at = x0 + jnp.where(slot == 0, 22, -7)
            masks.append(jnp.where((at >= 0) & (at < grid_x), 1.0, 0.0))
        return masks

    second_row = iota((1, BLK), 1) >= 128

    def row_mask(y):
        at = y0 + y + jnp.where(second_row, 1, 0)
        return jnp.where((at >= 0) & (at < grid_y), 1.0, 0.0)

    sub_row = iota((SUB, 128), 0)
    place = iota((PAIRS, 128), 1) // CH
    early = (place >= 2) & (place < 6)

    def put(act, pair, blk, values):
        act[0, pair, blk] = values.astype(BF16)
        for half in range(2):
            turned = pltpu.roll(values[:, half * 128 : (half + 1) * 128], 96, 1)
            head = jnp.where(sub_row == 0, 0.0, pltpu.roll(turned[PAIRS - SUB :], 1, 0))
            tail = jnp.where(sub_row == SUB - 1, 0.0, pltpu.roll(turned[:SUB], SUB - 1, 0))
            before = jnp.concatenate([head, turned[: PAIRS - SUB]], axis=0)
            after = jnp.concatenate([turned[SUB:], tail], axis=0)
            both = jnp.where(early, before, after)
            act[1, pair, blk, :, half * 128 : (half + 1) * 128] = both.astype(BF16)

    def put_sides(act, pair, blocks):
        for blk in range(EDGE):
            left, right = (blk - 1) % blocks, (blk + 1) % blocks
            for half in range(2):
                at = slice(half * 128, (half + 1) * 128)
                even = jnp.where(place % 4 == 0, act[0, pair, right, :, at], act[1, pair, right, :, at])
                odd = jnp.where(place % 4 == 3, act[0, pair, left, :, at], act[1, pair, left, :, at])
                act[2, pair, blk, :, at] = jnp.where(place % 2 == 0, even, odd)

    mask1 = lane_masks(EDGE + 1)

    def first(step, carry):
        pieces = []
        for i in range(FIRST):
            rows = amp[pl.ds((step * FIRST + i) * 2, 4)].reshape(4 * XW, NT)
            turned = dot_nt(to_pairs, rows).astype(BF16)
            pieces.append(
                jnp.concatenate([turned[j * PAIRS : (j + 1) * PAIRS] for j in range(4)], axis=1)
            )
        result = dot(jnp.concatenate(pieces, axis=0), w1_ref[...])
        for i in range(FIRST):
            pair = step * FIRST + i
            inside = row_mask(2 * pair - H)
            for blk in range(EDGE + 1):
                values = result[i * PAIRS : (i + 1) * PAIRS, blk * BLK : (blk + 1) * BLK]
                put(act1, pair, blk, jnp.maximum(values, 0.0) * (mask1[blk] * inside))
            put_sides(act1, pair, EDGE + 1)
        return carry

    lax.fori_loop(0, pairs1 // FIRST, first, 0)

    def layer(source, w_ref, pair, count):
        size = count * EDGE * PAIRS
        tiles = []
        for kind in range(3):
            centre = source[kind, pl.ds(pair + 1, count), :EDGE].reshape(size, BLK)
            before = source[kind, pl.ds(pair, count), :EDGE, :, 128:].reshape(size, 128)
            after = source[kind, pl.ds(pair + 2, count), :EDGE, :, :128].reshape(size, 128)
            tiles += [centre, before, after]
        return dot(jnp.concatenate(tiles, axis=1), w_ref[...])

    block, up_y, down_y, up_t, down_t = plane_shifts(yw)

    def smooth_yt(v, edge=0.0):
        v = 0.5 * v + 0.25 * (up_t(v, edge) + down_t(v, edge))
        return 0.5 * v + 0.25 * (up_y(v) + down_y(v))

    def amp_rows(x):
        return raw[pl.ds(pl.multiple_of(x * yw, 8), RX * yw), :].reshape(block)

    def products(k):
        here = amp_rows(k + 3)
        grad_x = 0.5 * (amp_rows(k + 4) - amp_rows(k + 2))
        grad_y = 0.5 * (up_y(here) - down_y(here))
        grad_t = 0.5 * (up_t(here) - down_t(here))
        at = pl.ds(k, RX)
        prod[0, at] = smooth_yt(grad_x * grad_t)
        prod[1, at] = smooth_yt(grad_y * grad_t)
        energy = grad_t * grad_t + 0.25 * (grad_x * grad_x + grad_y * grad_y)
        prod[2, at] = smooth_yt(energy, 0.25 * here * here)

    def slopes(k):
        at = pl.ds(k + 1, RX)
        sums = []
        for which in range(3):
            before, here, after = [prod[which, pl.ds(k + i, RX)] for i in range(3)]
            sums.append(0.5 * here + 0.25 * (before + after))
        scale = -1.0 / (sums[2] + 0.05)
        slope[0, at] = sums[0] * scale
        slope[1, at] = sums[1] * scale
    steps2, steps3 = pairs2 // SECOND, pairs2 // THIRD
    blocks2 = -(-(FX // RX + 1) // steps2)
    blocks3 = -(-(FX // RX) // steps3)
    mask2 = lane_masks(EDGE)

    def second(step, carry):
        for i in range(blocks2):
            products(jnp.minimum((step * blocks2 + i) * RX, FX))
        for begin in range(0, SECOND, GROUP):
            count = min(GROUP, SECOND - begin)
            result = layer(act1, w2_ref, step * SECOND + begin, count)
            for i in range(count):
                pair = step * SECOND + begin + i
                inside = row_mask(2 * pair - 6)
                for blk in range(EDGE):
                    at = (i * EDGE + blk) * PAIRS
                    values = jnp.maximum(result[at : at + PAIRS], 0.0)
                    put(act2, pair + 1, blk, values * (mask2[blk] * inside))
                put_sides(act2, pair + 1, EDGE)
        return carry

    for edge in (0, pairs2 + 1):
        for kind in range(3):
            act2[kind, edge] = jnp.zeros((EDGE, PAIRS, BLK), BF16)
    lax.fori_loop(0, steps2, second, 0)

    act3 = act1.at[0]

    def third(step, carry):
        for i in range(blocks3):
            slopes(jnp.minimum((step * blocks3 + i) * RX, FX - RX))
        for begin in range(0, THIRD, GROUP):
            count = min(GROUP, THIRD - begin)
            result = layer(act2, w3_ref, step * THIRD + begin, count)
            for i in range(count):
                pair = step * THIRD + begin + i
                inside = row_mask(2 * pair - 6)
                for blk in range(EDGE):
                    at = (i * EDGE + blk) * PAIRS
                    values = jnp.maximum(result[at : at + PAIRS], 0.0)
                    act3[pair, blk] = (values * (mask2[blk] * inside)).astype(BF16)
        return carry

    lax.fori_loop(0, steps3, third, 0)
    for pair in range(pairs2, pairs1):
        act3[pair] = jnp.zeros((EDGE + 1, PAIRS, BLK), BF16)

    def fourth(step, carry):
        pair = step * 4
        cells = [act3[pl.ds(pair, 4), blk].reshape(4 * PAIRS, BLK) for blk in range(EDGE)]
        result = dot_nt(w4_ref[...], jnp.concatenate(cells, axis=1))
        for half in range(2):
            columns = result[:, half * NT : (half + 1) * NT]
            sums = jnp.concatenate(
                [
                    jnp.concatenate(
                        [columns[(yi * 4 + j) * FX : (yi * 4 + j + 1) * FX] for j in range(4)],
                        axis=1,
                    )
                    for yi in range(4)
                ],
                axis=0,
            )
            high = sums.astype(BF16)
            low = (sums - high.astype(F32)).astype(BF16)
            both = dot(jnp.concatenate([high, low], axis=0), from_pairs)
            share = both[: 4 * FX] + both[4 * FX :]
            for i in range(2):
                part[pair + half * 2 + i] = share[:, i * NT : (i + 1) * NT]
        return carry

    lax.fori_loop(0, pairs1 // 4, fourth, 0, unroll=2)

    for x in range(FX):
        prob[x * yw : x * yw + H, :] = jnp.zeros((H, NT), F32)
        prob[(x + 1) * yw - H : (x + 1) * yw, :] = jnp.zeros((H, NT), F32)

    def order(step, carry):
        for i in range(4):
            pair = step * 4 + i + 1
            even = part[pair, FX : 2 * FX] + part[pair - 1, 3 * FX :]
            odd = part[pair, 2 * FX : 3 * FX] + part[pair + 1, :FX]
            for row, values in enumerate((even, odd)):
                values = (1.0 / (1.0 + jnp.exp(-values))).astype(BF16).astype(F32)
                prob[pl.ds(2 * pair + 2 + row, FX, stride=yw), :] = values
        return carry

    lax.fori_loop(0, (ty + 8) // 8, order, 0)

    for which in range(2):
        slope[which, FX + 1] = jnp.zeros((yw, NT), F32)
    for x in range(TX):
        fault_ref[x] = prob[(x + 4) * yw + H : (x + 4) * yw + H + ty, :].astype(BF16)


def owned(total, k, values, ty):
    for row in range(RX):
        ok = (k + row >= 5) & (k + row < 5 + TX)
        total = total + jnp.where(ok, values[row, H : H + ty], 0.0)
    return total


def image_of(wave, face, k, shifts):
    block, up_y, down_y, up_t, down_t = shifts
    at, before, after = [pl.ds(k + i, RX) for i in (0, -1, 1)]
    here = wave[at]
    flow = face[1, at] * (here - up_y(here))
    image = time_part(block) * here - ETA_TIME * (up_t(here) + down_t(here))
    image = image + flow - down_y(flow)
    image = image + face[0, at] * (here - wave[after])
    return here, image + face[0, before] * (here - wave[before])


def time_part(block):
    lane = iota(block, 2)
    count = jnp.where(lane == 0, 0.0, 1.0) + jnp.where(lane == NT - 1, 0.0, 1.0)
    return MU_DIAG + ETA_TIME * count


def waves_kernel(grid_x, grid_y, ty, prob, slope, mom_ref, face, wave2, *refs):
    n_gy = grid_y // ty
    waves_refs = refs[:n_gy]
    weight, flux, inv, wave0, wave1 = refs[n_gy:]
    place_y = lax.axis_index("gy")
    x0 = lax.axis_index("gx") * TX
    y0 = place_y * ty
    yw = ty + 2 * H
    shifts = plane_shifts(yw)
    block, up_y, down_y, up_t, down_t = shifts
    at_y = y0 - H + iota(block, 1)
    mask_y = (at_y >= 0) & (at_y < grid_y)

    def weights(step, carry):
        k = step * RX
        at = pl.ds(k + 1, RX)
        rows = prob[pl.ds(pl.multiple_of(k * yw, 8), RX * yw), :].reshape(block)
        raw_weight = 1.0 - 0.9 * rows
        at_x = x0 - 4 + k + iota(block, 0)
        weight[0, at] = raw_weight
        weight[1, at] = jnp.where(mask_y & (at_x >= 0) & (at_x < grid_x), raw_weight, 0.0)
        return carry

    lax.fori_loop(0, FX // RX, weights, 0)
    for which in range(2):
        weight[which, FX + 1] = jnp.full((yw, NT), 1.0 - which, F32)
        face[which, 0] = jnp.zeros((yw, NT), F32)
        flux[which, 0] = jnp.zeros((yw, NT), F32)

    def faces(step, carry):
        k = step * RX + 1
        at, after = pl.ds(k, RX), pl.ds(k + 1, RX)
        raw_weight = weight[0, at]
        masked = weight[1, at]
        face_x = 2.0 * masked * weight[1, after] / (raw_weight + weight[0, after])
        face_y = 2.0 * masked * up_y(masked) / (raw_weight + up_y(raw_weight))
        slope_y = slope[1, at]
        face[0, at] = face_x
        face[1, at] = face_y
        flux[0, at] = 0.5 * face_x * (slope[0, at] + slope[0, after])
        flux[1, at] = 0.5 * face_y * (slope_y + up_y(slope_y))
        return carry

    lax.fori_loop(0, FX // RX, faces, 0)

    def start(step, total):
        k = step * RX + 1
        at, before = pl.ds(k, RX), pl.ds(k - 1, RX)
        flux_y = flux[1, at]
        face_y = face[1, at]
        right = flux[0, before] - flux[0, at] + down_y(flux_y) - flux_y
        inverse = 1.0 / (time_part(block) + face[0, at] + face[0, before] + face_y + down_y(face_y))
        first_wave = right * inverse
        inv[at] = inverse
        wave0[at] = first_wave
        return owned(total, k, right * first_wave, ty)

    zero = jnp.zeros((ty, NT), F32)
    b0 = lax.fori_loop(0, FX // RX, start, zero)

    def advance(source, target):
        def body(step, totals):
            k = step * RX + 3
            here, image = image_of(source, face, k, shifts)
            at = pl.ds(k, RX)
            after = here - image * inv[at]
            target[at] = after
            return (
                owned(totals[0], k, here * image, ty),
                owned(totals[1], k, after * image, ty),
            )

        return body

    steps = (FX - 4) // RX
    a0, a1 = lax.fori_loop(0, steps, advance(wave0, wave1), (zero, zero))
    a2, a3 = lax.fori_loop(0, steps, advance(wave1, wave2), (zero, zero))
    sums = [jnp.sum(v, axis=0, keepdims=True) for v in (b0, a0, a1, a2, a3)]
    mom_ref[...] = jnp.concatenate(sums + [jnp.zeros((3, NT), F32)], axis=0)

    rows = TX // n_gy
    for place, ref in enumerate(waves_refs):
        to = lax.rem(place_y + place, n_gy) * rows + 5
        for which, wave in enumerate((wave0, wave1, wave2)):
            for row in range(rows):
                ref[which, row] = wave[to + row, H : H + ty, :].astype(BF16)


def last_kernel(ty, mom_ref, face, wave2, out_ref):
    shifts = plane_shifts(ty + 2 * H)

    def finish(step, total):
        k = step * RX + 5
        here, image = image_of(wave2, face, k, shifts)
        return owned(total, k, here * image, ty)

    total = lax.fori_loop(0, TX // RX, finish, jnp.zeros((ty, NT), F32))
    a4 = jnp.sum(total, axis=0, keepdims=True)
    sums = jnp.sum(jnp.where(iota((8, NT), 0) == 5, a4, mom_ref[...]), axis=1, keepdims=True)
    values = jnp.where(iota((8, NT), 0) == iota((8, NT), 1), sums, 0.0)
    values = jnp.sum(values, axis=0, keepdims=True)
    for device in range(out_ref.shape[0]):
        out_ref[device] = values


def combine_kernel(n_gy, ty, mom_ref, *refs):
    waves_refs, out_ref = refs[:n_gy], refs[n_gy]
    place_y = lax.axis_index("gy")
    moments = jnp.sum(mom_ref[...], axis=0)
    b0, a0, a1, a2, a3, a4 = [
        jnp.broadcast_to(moments[:, i : i + 1], (1, NT)) for i in range(6)
    ]
    a0, a1, a2, a3, a4 = [v / b0 for v in (a0, a1, a2, a3, a4)]
    l21 = a1 / a0
    l31 = a2 / a0
    d2 = jnp.maximum(a2 - l21 * a1, 1e-7 * a2 + 1e-30)
    l32 = (a3 - l21 * a2) / d2
    d3 = jnp.maximum(a4 - l31 * a2 - l32 * l32 * d2, 1e-7 * a4 + 1e-30)
    y2 = (1.0 - a0) - l21
    y3 = (1.0 - a0 - a1) - l31 - l32 * y2
    c3 = y3 / d3
    c2 = y2 / d2 - l32 * c3
    c1 = 1.0 / a0 - l21 * c2 - l31 * c3
    for place, ref in enumerate(waves_refs):
        source = lax.rem(place_y - place + n_gy, n_gy)
        at = pl.ds(pl.multiple_of(source * ty, 8), ty)
        for x in range(ref.shape[1]):
            w0, w1, w2 = [ref[which, x].astype(F32) for which in range(3)]
            out_ref[x, at, :] = c1 * w0 + c2 * w1 + c3 * w2


def vmem(count):
    return [pl.BlockSpec(memory_space=pltpu.VMEM)] * count


def on_device(amplitude, conv_first, conv_second, conv_third, conv_last):
    n_gx, n_gy = lax.axis_size("gx"), lax.axis_size("gy")
    ty = amplitude.shape[1]
    grid_x, grid_y = n_gx * TX, n_gy * ty
    assert amplitude.shape == (TX, ty, NT)

    def shift(values, axis, count, step):
        pairs = [(i, i + step) for i in range(count) if 0 <= i + step < count]
        return lax.ppermute(values, axis, pairs)

    xlow = shift(amplitude[TX - H :], "gx", n_gx, 1)
    xhigh = shift(amplitude[:H], "gx", n_gx, -1)
    ylow = shift(
        jnp.concatenate([xlow[:, ty - H :], amplitude[:, ty - H :], xhigh[:, ty - H :]]),
        "gy",
        n_gy,
        1,
    )
    yhigh = shift(
        jnp.concatenate([xlow[:, :H], amplitude[:, :H], xhigh[:, :H]]), "gy", n_gy, -1
    )

    def taps_first(weight):
        return jnp.transpose(weight, (2, 3, 4, 0, 1))

    w1, w2, w3, w4 = pl.pallas_call(
        prep_kernel,
        out_shape=[
            jax.ShapeDtypeStruct((16 * XW, (EDGE + 1) * BLK), BF16),
            jax.ShapeDtypeStruct((6 * BLK, BLK), BF16),
            jax.ShapeDtypeStruct((6 * BLK, BLK), BF16),
            jax.ShapeDtypeStruct((16 * FX, EDGE * BLK), BF16),
        ],
        in_specs=vmem(2) + [pl.BlockSpec(memory_space=pl.ANY)],
        out_specs=vmem(4),
        compiler_params=pltpu.CompilerParams(vmem_limit_bytes=16 * 2**20),
        cost_estimate=pl.CostEstimate(flops=10**9, bytes_accessed=10**7, transcendentals=0),
        name="band_weights",
    )(
        jnp.concatenate([taps_first(conv_second), taps_first(conv_third)]).reshape(54 * CH, CH),
        jnp.concatenate(
            [jnp.transpose(conv_first, (1, 2, 3, 4, 0)), jnp.transpose(conv_last, (0, 2, 3, 4, 1))]
        ),
        xlow,
    )

    yw, nf = ty + 2 * H, FX + 2
    fault, prob, slope = pl.pallas_call(
        functools.partial(net_kernel, grid_x, grid_y, ty),
        out_shape=[
            jax.ShapeDtypeStruct((TX, ty, NT), BF16),
            jax.ShapeDtypeStruct((FX * yw, NT), F32),
            jax.ShapeDtypeStruct((2, nf, yw, NT), F32),
        ],
        in_specs=vmem(9),
        out_specs=vmem(3),
        scratch_shapes=[
            pltpu.VMEM(((XW + 2) * yw, NT), F32),
            pltpu.VMEM((yw + 2, XW, NT), BF16),
            pltpu.VMEM((3, yw // 2, EDGE + 1, PAIRS, BLK), BF16),
            pltpu.VMEM((3, yw // 2, EDGE, PAIRS, BLK), BF16),
            pltpu.VMEM((yw // 2, 4 * FX, NT), F32),
            pltpu.VMEM((3, FX + 4, yw, NT), F32),
        ],
        compiler_params=pltpu.CompilerParams(vmem_limit_bytes=46 * 2**20),
        cost_estimate=pl.CostEstimate(
            flops=3 * 10**10, bytes_accessed=10**7, transcendentals=10**6
        ),
        name="fault_net",
    )(amplitude, xlow, xhigh, ylow, yhigh, w1, w2, w3, w4)

    rows = TX // n_gy
    moments, face, wave2, *waves = pl.pallas_call(
        functools.partial(waves_kernel, grid_x, grid_y, ty),
        out_shape=[
            jax.ShapeDtypeStruct((8, NT), F32),
            jax.ShapeDtypeStruct((2, nf, yw, NT), F32),
            jax.ShapeDtypeStruct((nf, yw, NT), F32),
        ]
        + [jax.ShapeDtypeStruct((3, rows, ty, NT), BF16)] * n_gy,
        in_specs=vmem(2),
        out_specs=vmem(3 + n_gy),
        scratch_shapes=[
            pltpu.VMEM((2, nf, yw, NT), F32),
            pltpu.VMEM((2, nf, yw, NT), F32),
            pltpu.VMEM((nf, yw, NT), F32),
            pltpu.VMEM((nf, yw, NT), F32),
            pltpu.VMEM((nf, yw, NT), F32),
        ],
        compiler_params=pltpu.CompilerParams(vmem_limit_bytes=24 * 2**20),
        cost_estimate=pl.CostEstimate(flops=10**8, bytes_accessed=10**7, transcendentals=0),
        name="solver_waves",
    )(prob, slope)

    arrived = [waves[0]]
    for place in range(1, n_gy):
        pairs = [(i, (i + place) % n_gy) for i in range(n_gy)]
        arrived.append(lax.ppermute(waves[place], "gy", pairs))

    everyone = pl.pallas_call(
        functools.partial(last_kernel, ty),
        out_shape=jax.ShapeDtypeStruct((n_gx * n_gy, 1, NT), F32),
        in_specs=vmem(3),
        out_specs=pl.BlockSpec(memory_space=pltpu.VMEM),
        compiler_params=pltpu.CompilerParams(vmem_limit_bytes=16 * 2**20),
        cost_estimate=pl.CostEstimate(flops=10**9, bytes_accessed=10**8, transcendentals=0),
        name="last_moment",
    )(moments, face, wave2)
    moments = lax.all_to_all(everyone, ("gx", "gy"), split_axis=0, concat_axis=0, tiled=True)
    shift_field = pl.pallas_call(
        functools.partial(combine_kernel, n_gy, ty),
        out_shape=jax.ShapeDtypeStruct((rows, grid_y, NT), F32),
        in_specs=vmem(1 + n_gy),
        out_specs=pl.BlockSpec(memory_space=pltpu.VMEM),
        compiler_params=pltpu.CompilerParams(vmem_limit_bytes=16 * 2**20),
        name="combine_waves",
    )(moments, *arrived)
    return (fault, shift_field)


def solution(mesh):
    return jax.shard_map(
        on_device,
        mesh=mesh,
        in_specs=(P("gx", "gy", None), P(), P(), P(), P()),
        out_specs=(P("gx", "gy", None), P(("gx", "gy"), None, None)),
        check_vma=False,
    )
```

```python
import functools

import jax
import jax.numpy as jnp
from jax import lax
from jax.experimental import pallas as pl
from jax.experimental.pallas import tpu as pltpu
from jax.sharding import PartitionSpec as P

MU_DIAG = 0.05
ETA_TIME = 0.5

TX, NT, H = 16, 128, 8
CH = 16
XW = TX + 2 * H
FX = TX + 8
RX = 4
FIRST, SECOND, THIRD = 8, 11, 11
LIMIT = 6
GROUP = 2
BLK = 256
EDGE = 7
SUB = 16
PAIRS = NT // 2

F32 = jnp.float32
BF16 = jnp.bfloat16


def iota(shape, dim):
    return lax.broadcasted_iota(jnp.int32, shape, dim)


def dot_nt(a, b):
    return lax.dot_general(a, b, (((1,), (1,)), ((), ())), preferred_element_type=F32)


def prep_kernel(inner_ref, outer_ref, after_ref, w1_ref, w2_ref, w3_ref, w4_ref):
    del after_ref
    spread = jnp.where(iota((CH, BLK), 1) % CH == iota((CH, BLK), 0), 1.0, 0.0).astype(BF16)
    unit = jnp.where(iota((BLK, BLK), 1) == iota((BLK, BLK), 0), 1.0, 0.0).astype(BF16)
    none = jnp.zeros((CH, BLK), BF16)
    cell = iota((CH, BLK), 1) // CH
    at_cell = [cell == at for at in range(16)]
    inputs = input_cells()
    tiled = jnp.dot(inner_ref[...], spread, preferred_element_type=F32).astype(BF16)
    for layer, ref in enumerate((w2_ref, w3_ref)):
        for tile in range(6):
            bands = []
            for yo in range(2):
                for to in range(2):
                    for xo in range(4):
                        band = none
                        for at, (y, t, x) in enumerate(inputs[tile]):
                            dx, dy, dt = x - xo + 1, y - yo + 1, t - to + 1
                            if min(dx, dy, dt) >= 0 and max(dx, dy, dt) <= 2:
                                tap = tiled[(layer * 27 + dx * 9 + dy * 3 + dt) * CH :][:CH]
                                band = jnp.where(at_cell[at], tap, band)
                        bands.append(band)
            turned = dot_nt(unit, jnp.concatenate(bands, axis=0))
            ref[tile * BLK : (tile + 1) * BLK, :] = turned.astype(BF16)

    def taps(which):
        found = {}
        for dx in range(3):
            for dy in range(3):
                tiled = jnp.dot(outer_ref[which, dx, dy], spread, preferred_element_type=F32)
                for dt in range(3):
                    found[dx, dy, dt] = tiled[dt : dt + 1]
        return found

    first, last = taps(0), taps(1)
    lane_yt = iota((1, BLK), 1) // 64
    quarter = [lane_yt == at for at in range(4)]

    def by_quarter(found, dx, at):
        value = jnp.zeros((1, BLK), F32)
        for y in range(2):
            for t in range(2):
                dy, dt = at(y, t)
                if 0 <= dy <= 2 and 0 <= dt <= 2:
                    value = jnp.where(quarter[y * 2 + t], found[dx, dy, dt], value)
        return value

    def rows_of(found, rows, at):
        return [
            jnp.broadcast_to(by_quarter(found, dx, at), (rows, BLK)).astype(BF16)
            for dx in range(3)
        ]

    row_x = iota((XW, BLK), 0)
    lane_x = iota((XW, BLK), 1) // CH % 4
    offset_x = [row_x - 1 - 4 * blk - lane_x for blk in range(EDGE)]
    offset_x.append(jnp.where(lane_x == 0, row_x - 29, jnp.where(lane_x == 3, row_x, -1)))
    masks = [[offset == dx for dx in range(3)] for offset in offset_x]
    none = jnp.zeros((XW, BLK), BF16)
    for j in range(4):
        for yi in range(4):
            row = (j * 4 + yi) * XW
            values = rows_of(first, XW, lambda y, t: (yi - y, j - t))
            for blk in range(EDGE + 1):
                band = none
                for dx in range(3):
                    band = jnp.where(masks[blk][dx], values[dx], band)
                w1_ref[row : row + XW, blk * BLK : (blk + 1) * BLK] = band
    row_x = iota((FX, BLK), 0)
    lane_x = iota((FX, BLK), 1) // CH % 4
    masks = [
        [4 * blk + lane_x - 1 - row_x == dx for dx in range(3)] for blk in range(EDGE)
    ]
    none = jnp.zeros((FX, BLK), F32)
    bands = [[] for blk in range(EDGE)]
    for yi in range(4):
        for j in range(4):
            values = [
                by_quarter(last, dx, lambda y, t: (y + 2 - yi, t + 2 - j)) for dx in range(3)
            ]
            for blk in range(EDGE):
                band = none
                for dx in range(3):
                    band = jnp.where(masks[blk][dx], values[dx], band)
                bands[blk].append(band)
    for blk in range(EDGE):
        whole = jnp.concatenate(bands[blk], axis=0).astype(BF16)
        w4_ref[:, blk * BLK : (blk + 1) * BLK] = whole


def input_cells():
    tiles = []
    here = [(t, x) for t in (0, 1) for x in range(4)]
    near = [(2, 2), (2, 3), (-1, 0), (-1, 1), (-1, 2), (-1, 3), (2, 0), (2, 1)]
    side = [(0, 4), (2, -1), (-1, 4), (0, -1), (1, 4), (-1, -1), (2, 4), (1, -1)]
    for cells in (here, near, side):
        for rows in ((0, 1), (-1, 2)):
            tiles.append([(y, t, x) for y in rows for t, x in cells])
    return tiles


def plane_shifts(yw):
    block = (RX, yw, NT)
    lane = iota(block, 2)
    first_lane = lane == 0
    last_lane = lane == NT - 1

    def up_y(v):
        return pltpu.roll(v, yw - 1, 1)

    def down_y(v):
        return pltpu.roll(v, 1, 1)

    def up_t(v, edge=0.0):
        return jnp.where(last_lane, edge, pltpu.roll(v, NT - 1, 2))

    def down_t(v, edge=0.0):
        return jnp.where(first_lane, edge, pltpu.roll(v, 1, 2))

    return block, up_y, down_y, up_t, down_t


def dot(a, b):
    return jnp.dot(a, b, preferred_element_type=F32)


def pair_of(row):
    return row // SUB + (row % SUB) * 4


def lane_masks(x0, grid_x, blocks):
    slot = iota((1, BLK), 1) // CH % 4
    masks = []
    for blk in range(blocks):
        if blk < EDGE:
            at = x0 - 6 + 4 * blk + slot
        else:
            at = x0 + jnp.where(slot == 0, 22, -7)
        masks.append(jnp.where((at >= 0) & (at < grid_x), 1.0, 0.0))
    return masks


def row_mask(y, grid_y):
    at = y + jnp.where(iota((1, BLK), 1) >= 128, 1, 0)
    return jnp.where((at >= 0) & (at < grid_y), 1.0, 0.0)


def put(act, pair, blk, values):
    sub_row = iota((SUB, 128), 0)
    place = iota((PAIRS, 128), 1) // CH
    early = (place >= 2) & (place < 6)
    act[0, pair, blk] = values.astype(BF16)
    for half in range(2):
        turned = pltpu.roll(values[:, half * 128 : (half + 1) * 128], 96, 1)
        head = jnp.where(sub_row == 0, 0.0, pltpu.roll(turned[PAIRS - SUB :], 1, 0))
        tail = jnp.where(sub_row == SUB - 1, 0.0, pltpu.roll(turned[:SUB], SUB - 1, 0))
        before = jnp.concatenate([head, turned[: PAIRS - SUB]], axis=0)
        after = jnp.concatenate([turned[SUB:], tail], axis=0)
        both = jnp.where(early, before, after)
        act[1, pair, blk, :, half * 128 : (half + 1) * 128] = both.astype(BF16)


def put_sides(act, pair, blocks):
    place = iota((PAIRS, 128), 1) // CH
    for blk in range(EDGE):
        left, right = (blk - 1) % blocks, (blk + 1) % blocks
        for half in range(2):
            at = slice(half * 128, (half + 1) * 128)
            even = jnp.where(place % 4 == 0, act[0, pair, right, :, at], act[1, pair, right, :, at])
            odd = jnp.where(place % 4 == 3, act[0, pair, left, :, at], act[1, pair, left, :, at])
            act[2, pair, blk, :, at] = jnp.where(place % 2 == 0, even, odd)


def layer(source, w_ref, pair, count):
    size = count * EDGE * PAIRS
    tiles = []
    for kind in range(3):
        centre = source[kind, pl.ds(pair + 1, count), :EDGE].reshape(size, BLK)
        before = source[kind, pl.ds(pair, count), :EDGE, :, 128:].reshape(size, 128)
        after = source[kind, pl.ds(pair + 2, count), :EDGE, :, :128].reshape(size, 128)
        tiles += [centre, before, after]
    return dot(jnp.concatenate(tiles, axis=1), w_ref[...])


def first_kernel(
    grid_x,
    grid_y,
    ty,
    amp_ref,
    xlow_ref,
    xhigh_ref,
    ylow_ref,
    yhigh_ref,
    w1_ref,
    act1,
    raw,
    amp,
):
    x0 = lax.axis_index("gx") * TX
    y0 = lax.axis_index("gy") * ty
    yw = ty + 2 * H

    for x in range(XW):
        row = x * yw
        if x < H:
            mid = xlow_ref[x]
        elif x < H + TX:
            mid = amp_ref[x - H]
        else:
            mid = xhigh_ref[x - H - TX]
        raw[row + H : row + H + ty, :] = mid.astype(F32)
        raw[row : row + H, :] = ylow_ref[x].astype(F32)
        raw[row + H + ty : row + yw, :] = yhigh_ref[x].astype(F32)

    def turn(y, carry):
        amp[y + 1] = raw[pl.ds(y, XW, stride=yw), :].astype(BF16)
        return carry

    lax.fori_loop(0, yw, turn, 0, unroll=8)
    amp[0] = jnp.zeros((XW, NT), BF16)
    amp[yw + 1] = jnp.zeros((XW, NT), BF16)

    at_row = iota((4 * PAIRS, NT), 0)
    to_pairs = jnp.where(
        iota((4 * PAIRS, NT), 1) == 2 * pair_of(at_row % PAIRS) - 1 + at_row // PAIRS, 1.0, 0.0
    ).astype(BF16)
    mask1 = lane_masks(x0, grid_x, EDGE + 1)

    def first(step, carry):
        pieces = []
        for i in range(FIRST):
            rows = amp[pl.ds((step * FIRST + i) * 2, 4)].reshape(4 * XW, NT)
            turned = dot_nt(to_pairs, rows).astype(BF16)
            pieces.append(
                jnp.concatenate([turned[j * PAIRS : (j + 1) * PAIRS] for j in range(4)], axis=1)
            )
        result = dot(jnp.concatenate(pieces, axis=0), w1_ref[...])
        for i in range(FIRST):
            pair = step * FIRST + i
            inside = row_mask(y0 + 2 * pair - H, grid_y)
            for blk in range(EDGE + 1):
                values = result[i * PAIRS : (i + 1) * PAIRS, blk * BLK : (blk + 1) * BLK]
                put(act1, pair, blk, jnp.maximum(values, 0.0) * (mask1[blk] * inside))
            put_sides(act1, pair, EDGE + 1)
        return carry

    lax.fori_loop(0, yw // 2 // FIRST, first, 0)


def second_kernel(grid_x, grid_y, ty, act1, raw, w2_ref, act2, prod):
    x0 = lax.axis_index("gx") * TX
    y0 = lax.axis_index("gy") * ty
    yw = ty + 2 * H
    pairs2 = ty // 2 + 6
    block, up_y, down_y, up_t, down_t = plane_shifts(yw)

    def smooth_yt(v, edge=0.0):
        v = 0.5 * v + 0.25 * (up_t(v, edge) + down_t(v, edge))
        return 0.5 * v + 0.25 * (up_y(v) + down_y(v))

    def amp_rows(x):
        return raw[pl.ds(pl.multiple_of(x * yw, 8), RX * yw), :].reshape(block)

    def products(k):
        here = amp_rows(k + 3)
        grad_x = 0.5 * (amp_rows(k + 4) - amp_rows(k + 2))
        grad_y = 0.5 * (up_y(here) - down_y(here))
        grad_t = 0.5 * (up_t(here) - down_t(here))
        at = pl.ds(k, RX)
        prod[0, at] = smooth_yt(grad_x * grad_t)
        prod[1, at] = smooth_yt(grad_y * grad_t)
        energy = grad_t * grad_t + 0.25 * (grad_x * grad_x + grad_y * grad_y)
        prod[2, at] = smooth_yt(energy, 0.25 * here * here)

    steps2 = pairs2 // SECOND
    blocks2 = -(-(FX // RX + 1) // steps2)
    mask2 = lane_masks(x0, grid_x, EDGE)

    def second(step, carry):
        for i in range(blocks2):
            products(jnp.minimum((step * blocks2 + i) * RX, FX))
        for begin in range(0, SECOND, GROUP):
            count = min(GROUP, SECOND - begin)
            result = layer(act1, w2_ref, step * SECOND + begin, count)
            for i in range(count):
                pair = step * SECOND + begin + i
                inside = row_mask(y0 + 2 * pair - 6, grid_y)
                for blk in range(EDGE):
                    at = (i * EDGE + blk) * PAIRS
                    values = jnp.maximum(result[at : at + PAIRS], 0.0)
                    put(act2, pair + 1, blk, values * (mask2[blk] * inside))
                put_sides(act2, pair + 1, EDGE)
        return carry

    for edge in (0, pairs2 + 1):
        for kind in range(3):
            act2[kind, edge] = jnp.zeros((EDGE, PAIRS, BLK), BF16)
    lax.fori_loop(0, steps2, second, 0)


def third_kernel(
    grid_x, grid_y, ty, act2, prod, w3_ref, w4_ref, fault_ref, prob, slope, act3, part
):
    x0 = lax.axis_index("gx") * TX
    y0 = lax.axis_index("gy") * ty
    yw = ty + 2 * H
    pairs1, pairs2 = yw // 2, ty // 2 + 6
    at_row = iota((4 * NT, 2 * NT), 0)
    at_lane = iota((4 * NT, 2 * NT), 1)
    from_pairs = jnp.where(
        (at_lane % NT == 2 * pair_of(at_row % PAIRS) - 1 + at_row // NT)
        & (at_lane // NT == at_row % NT // PAIRS),
        1.0,
        0.0,
    ).astype(BF16)

    def slopes(k):
        at = pl.ds(k + 1, RX)
        sums = []
        for which in range(3):
            before, here, after = [prod[which, pl.ds(k + i, RX)] for i in range(3)]
            sums.append(0.5 * here + 0.25 * (before + after))
        scale = -1.0 / (sums[2] + 0.05)
        slope[0, at] = sums[0] * scale
        slope[1, at] = sums[1] * scale

    steps3 = pairs2 // THIRD
    blocks3 = -(-(FX // RX) // steps3)
    mask2 = lane_masks(x0, grid_x, EDGE)

    def third(step, carry):
        for i in range(blocks3):
            slopes(jnp.minimum((step * blocks3 + i) * RX, FX - RX))
        for begin in range(0, THIRD, GROUP):
            count = min(GROUP, THIRD - begin)
            result = layer(act2, w3_ref, step * THIRD + begin, count)
            for i in range(count):
                pair = step * THIRD + begin + i
                inside = row_mask(y0 + 2 * pair - 6, grid_y)
                for blk in range(EDGE):
                    at = (i * EDGE + blk) * PAIRS
                    values = jnp.maximum(result[at : at + PAIRS], 0.0)
                    act3[pair, blk] = (values * (mask2[blk] * inside)).astype(BF16)
        return carry

    lax.fori_loop(0, steps3, third, 0)
    for pair in range(pairs2, pairs1):
        act3[pair] = jnp.zeros((EDGE, PAIRS, BLK), BF16)

    def fourth(step, carry):
        pair = step * 4
        cells = [act3[pl.ds(pair, 4), blk].reshape(4 * PAIRS, BLK) for blk in range(EDGE)]
        result = dot_nt(w4_ref[...], jnp.concatenate(cells, axis=1))
        for half in range(2):
            columns = result[:, half * NT : (half + 1) * NT]
            sums = jnp.concatenate(
                [
                    jnp.concatenate(
                        [columns[(yi * 4 + j) * FX : (yi * 4 + j + 1) * FX] for j in range(4)],
                        axis=1,
                    )
                    for yi in range(4)
                ],
                axis=0,
            )
            high = sums.astype(BF16)
            low = (sums - high.astype(F32)).astype(BF16)
            both = dot(jnp.concatenate([high, low], axis=0), from_pairs)
            share = both[: 4 * FX] + both[4 * FX :]
            for i in range(2):
                part[pair + half * 2 + i] = share[:, i * NT : (i + 1) * NT]
        return carry

    lax.fori_loop(0, pairs1 // 4, fourth, 0, unroll=2)

    for x in range(FX):
        prob[x * yw : x * yw + H, :] = jnp.zeros((H, NT), F32)
        prob[(x + 1) * yw - H : (x + 1) * yw, :] = jnp.zeros((H, NT), F32)

    def order(step, carry):
        for i in range(4):
            pair = step * 4 + i + 1
            even = part[pair, FX : 2 * FX] + part[pair - 1, 3 * FX :]
            odd = part[pair, 2 * FX : 3 * FX] + part[pair + 1, :FX]
            for row, values in enumerate((even, odd)):
                values = (1.0 / (1.0 + jnp.exp(-values))).astype(BF16).astype(F32)
                prob[pl.ds(2 * pair + 2 + row, FX, stride=yw), :] = values
        return carry

    lax.fori_loop(0, (ty + 8) // 8, order, 0)

    for which in range(2):
        slope[which, FX + 1] = jnp.zeros((yw, NT), F32)
    for x in range(TX):
        fault_ref[x] = prob[(x + 4) * yw + H : (x + 4) * yw + H + ty, :].astype(BF16)


def owned(total, k, values, ty):
    for row in range(RX):
        ok = (k + row >= 5) & (k + row < 5 + TX)
        total = total + jnp.where(ok, values[row, H : H + ty], 0.0)
    return total


def image_of(wave, face, k, shifts):
    block, up_y, down_y, up_t, down_t = shifts
    at, before, after = [pl.ds(k + i, RX) for i in (0, -1, 1)]
    here = wave[at]
    flow = face[1, at] * (here - up_y(here))
    image = time_part(block) * here - ETA_TIME * (up_t(here) + down_t(here))
    image = image + flow - down_y(flow)
    image = image + face[0, at] * (here - wave[after])
    return here, image + face[0, before] * (here - wave[before])


def time_part(block):
    lane = iota(block, 2)
    count = jnp.where(lane == 0, 0.0, 1.0) + jnp.where(lane == NT - 1, 0.0, 1.0)
    return MU_DIAG + ETA_TIME * count


def waves_kernel(grid_x, grid_y, ty, prob, slope, mom_ref, face, wave2, *refs):
    n_gy = grid_y // ty
    waves_refs = refs[:n_gy]
    weight, flux, inv, wave0, wave1 = refs[n_gy:]
    place_y = lax.axis_index("gy")
    x0 = lax.axis_index("gx") * TX
    y0 = place_y * ty
    yw = ty + 2 * H
    shifts = plane_shifts(yw)
    block, up_y, down_y, up_t, down_t = shifts
    at_y = y0 - H + iota(block, 1)
    mask_y = (at_y >= 0) & (at_y < grid_y)

    def weights(step, carry):
        k = step * RX
        at = pl.ds(k + 1, RX)
        rows = prob[pl.ds(pl.multiple_of(k * yw, 8), RX * yw), :].reshape(block)
        raw_weight = 1.0 - 0.9 * rows
        at_x = x0 - 4 + k + iota(block, 0)
        weight[0, at] = raw_weight
        weight[1, at] = jnp.where(mask_y & (at_x >= 0) & (at_x < grid_x), raw_weight, 0.0)
        return carry

    lax.fori_loop(0, FX // RX, weights, 0)
    for which in range(2):
        weight[which, FX + 1] = jnp.full((yw, NT), 1.0 - which, F32)
        face[which, 0] = jnp.zeros((yw, NT), F32)
        flux[which, 0] = jnp.zeros((yw, NT), F32)

    def faces(step, carry):
        k = step * RX + 1
        at, after = pl.ds(k, RX), pl.ds(k + 1, RX)
        raw_weight = weight[0, at]
        masked = weight[1, at]
        face_x = 2.0 * masked * weight[1, after] / (raw_weight + weight[0, after])
        face_y = 2.0 * masked * up_y(masked) / (raw_weight + up_y(raw_weight))
        slope_y = slope[1, at]
        face[0, at] = face_x
        face[1, at] = face_y
        flux[0, at] = 0.5 * face_x * (slope[0, at] + slope[0, after])
        flux[1, at] = 0.5 * face_y * (slope_y + up_y(slope_y))
        return carry

    lax.fori_loop(0, FX // RX, faces, 0)

    def start(step, total):
        k = step * RX + 1
        at, before = pl.ds(k, RX), pl.ds(k - 1, RX)
        flux_y = flux[1, at]
        face_y = face[1, at]
        right = flux[0, before] - flux[0, at] + down_y(flux_y) - flux_y
        inverse = 1.0 / (time_part(block) + face[0, at] + face[0, before] + face_y + down_y(face_y))
        first_wave = right * inverse
        inv[at] = inverse
        wave0[at] = first_wave
        return owned(total, k, right * first_wave, ty)

    zero = jnp.zeros((ty, NT), F32)
    b0 = lax.fori_loop(0, FX // RX, start, zero)

    def advance(source, target):
        def body(step, totals):
            k = step * RX + 3
            here, image = image_of(source, face, k, shifts)
            at = pl.ds(k, RX)
            after = here - image * inv[at]
            target[at] = after
            return (
                owned(totals[0], k, here * image, ty),
                owned(totals[1], k, after * image, ty),
            )

        return body

    steps = (FX - 4) // RX
    a0, a1 = lax.fori_loop(0, steps, advance(wave0, wave1), (zero, zero))
    a2, a3 = lax.fori_loop(0, steps, advance(wave1, wave2), (zero, zero))
    sums = [jnp.sum(v, axis=0, keepdims=True) for v in (b0, a0, a1, a2, a3)]
    mom_ref[...] = jnp.concatenate(sums + [jnp.zeros((3, NT), F32)], axis=0)

    rows = TX // n_gy
    for place, ref in enumerate(waves_refs):
        to = lax.rem(place_y + place, n_gy) * rows + 5
        for which, wave in enumerate((wave0, wave1, wave2)):
            for row in range(rows):
                ref[which, row] = wave[to + row, H : H + ty, :].astype(BF16)


def last_kernel(ty, mom_ref, face, wave2, out_ref):
    shifts = plane_shifts(ty + 2 * H)

    def finish(step, total):
        k = step * RX + 5
        here, image = image_of(wave2, face, k, shifts)
        return owned(total, k, here * image, ty)

    total = lax.fori_loop(0, TX // RX, finish, jnp.zeros((ty, NT), F32))
    a4 = jnp.sum(total, axis=0, keepdims=True)
    sums = jnp.sum(jnp.where(iota((8, NT), 0) == 5, a4, mom_ref[...]), axis=1, keepdims=True)
    values = jnp.where(iota((8, NT), 0) == iota((8, NT), 1), sums, 0.0)
    values = jnp.sum(values, axis=0, keepdims=True)
    for device in range(out_ref.shape[0]):
        out_ref[device] = values


def combine_kernel(n_gy, ty, mom_ref, *refs):
    waves_refs, out_ref = refs[:n_gy], refs[n_gy]
    place_y = lax.axis_index("gy")
    moments = jnp.sum(mom_ref[...], axis=0)
    b0, a0, a1, a2, a3, a4 = [
        jnp.broadcast_to(moments[:, i : i + 1], (1, NT)) for i in range(6)
    ]
    a0, a1, a2, a3, a4 = [v / b0 for v in (a0, a1, a2, a3, a4)]
    l21 = a1 / a0
    l31 = a2 / a0
    d2 = jnp.maximum(a2 - l21 * a1, 1e-7 * a2 + 1e-30)
    l32 = (a3 - l21 * a2) / d2
    d3 = jnp.maximum(a4 - l31 * a2 - l32 * l32 * d2, 1e-7 * a4 + 1e-30)
    y2 = (1.0 - a0) - l21
    y3 = (1.0 - a0 - a1) - l31 - l32 * y2
    c3 = y3 / d3
    c2 = y2 / d2 - l32 * c3
    c1 = 1.0 / a0 - l21 * c2 - l31 * c3
    for place, ref in enumerate(waves_refs):
        source = lax.rem(place_y - place + n_gy, n_gy)
        at = pl.ds(pl.multiple_of(source * ty, 8), ty)
        for x in range(ref.shape[1]):
            w0, w1, w2 = [ref[which, x].astype(F32) for which in range(3)]
            out_ref[x, at, :] = c1 * w0 + c2 * w1 + c3 * w2


def vmem(count):
    return [pl.BlockSpec(memory_space=pltpu.VMEM)] * count


def on_device(amplitude, conv_first, conv_second, conv_third, conv_last):
    n_gx, n_gy = lax.axis_size("gx"), lax.axis_size("gy")
    ty = amplitude.shape[1]
    grid_x, grid_y = n_gx * TX, n_gy * ty
    assert amplitude.shape == (TX, ty, NT)

    def shift(values, axis, count, step):
        pairs = [(i, i + step) for i in range(count) if 0 <= i + step < count]
        return lax.ppermute(values, axis, pairs)

    xlow = shift(amplitude[TX - H :], "gx", n_gx, 1)
    xhigh = shift(amplitude[:H], "gx", n_gx, -1)
    ylow = shift(
        jnp.concatenate([xlow[:, ty - H :], amplitude[:, ty - H :], xhigh[:, ty - H :]]),
        "gy",
        n_gy,
        1,
    )
    yhigh = shift(
        jnp.concatenate([xlow[:, :H], amplitude[:, :H], xhigh[:, :H]]), "gy", n_gy, -1
    )

    weights = (conv_first, conv_second, conv_third, conv_last)
    (conv_first, conv_second, conv_third, conv_last), _ = lax.optimization_barrier((weights, xlow))

    def taps_first(weight):
        return jnp.transpose(weight, (2, 3, 4, 0, 1))

    w1, w2, w3, w4 = pl.pallas_call(
        prep_kernel,
        out_shape=[
            jax.ShapeDtypeStruct((16 * XW, (EDGE + 1) * BLK), BF16),
            jax.ShapeDtypeStruct((6 * BLK, BLK), BF16),
            jax.ShapeDtypeStruct((6 * BLK, BLK), BF16),
            jax.ShapeDtypeStruct((16 * FX, EDGE * BLK), BF16),
        ],
        in_specs=vmem(2) + [pl.BlockSpec(memory_space=pl.ANY)],
        out_specs=vmem(4),
        compiler_params=pltpu.CompilerParams(vmem_limit_bytes=16 * 2**20),
        cost_estimate=pl.CostEstimate(flops=10**9, bytes_accessed=10**7, transcendentals=0),
        name="band_weights",
    )(
        jnp.concatenate([taps_first(conv_second), taps_first(conv_third)]).reshape(54 * CH, CH),
        jnp.concatenate(
            [jnp.transpose(conv_first, (1, 2, 3, 4, 0)), jnp.transpose(conv_last, (0, 2, 3, 4, 1))]
        ),
        xlow,
    )

    yw, nf = ty + 2 * H, FX + 2
    act1, raw = pl.pallas_call(
        functools.partial(first_kernel, grid_x, grid_y, ty),
        out_shape=[
            jax.ShapeDtypeStruct((3, yw // 2, EDGE + 1, PAIRS, BLK), BF16),
            jax.ShapeDtypeStruct(((XW + 2) * yw, NT), F32),
        ],
        in_specs=vmem(6),
        out_specs=vmem(2),
        scratch_shapes=[pltpu.VMEM((yw + 2, XW, NT), BF16)],
        compiler_params=pltpu.CompilerParams(vmem_limit_bytes=LIMIT * 2**20),
        cost_estimate=pl.CostEstimate(flops=10**10, bytes_accessed=10**7, transcendentals=0),
        name="layer_one",
    )(amplitude, xlow, xhigh, ylow, yhigh, w1)

    act2, prod = pl.pallas_call(
        functools.partial(second_kernel, grid_x, grid_y, ty),
        out_shape=[
            jax.ShapeDtypeStruct((3, yw // 2, EDGE, PAIRS, BLK), BF16),
            jax.ShapeDtypeStruct((3, FX + 4, yw, NT), F32),
        ],
        in_specs=vmem(3),
        out_specs=vmem(2),
        compiler_params=pltpu.CompilerParams(vmem_limit_bytes=LIMIT * 2**20),
        cost_estimate=pl.CostEstimate(flops=10**10, bytes_accessed=10**7, transcendentals=0),
        name="layer_two",
    )(act1, raw, w2)

    fault, prob, slope = pl.pallas_call(
        functools.partial(third_kernel, grid_x, grid_y, ty),
        out_shape=[
            jax.ShapeDtypeStruct((TX, ty, NT), BF16),
            jax.ShapeDtypeStruct((FX * yw, NT), F32),
            jax.ShapeDtypeStruct((2, nf, yw, NT), F32),
        ],
        in_specs=vmem(4),
        out_specs=vmem(3),
        scratch_shapes=[
            pltpu.VMEM((yw // 2, EDGE, PAIRS, BLK), BF16),
            pltpu.VMEM((yw // 2, 4 * FX, NT), F32),
        ],
        compiler_params=pltpu.CompilerParams(vmem_limit_bytes=(LIMIT + 8) * 2**20),
        cost_estimate=pl.CostEstimate(
            flops=10**10, bytes_accessed=10**7, transcendentals=10**6
        ),
        name="layers_three_four",
    )(act2, prod, w3, w4)

    rows = TX // n_gy
    moments, face, wave2, *waves = pl.pallas_call(
        functools.partial(waves_kernel, grid_x, grid_y, ty),
        out_shape=[
            jax.ShapeDtypeStruct((8, NT), F32),
            jax.ShapeDtypeStruct((2, nf, yw, NT), F32),
            jax.ShapeDtypeStruct((nf, yw, NT), F32),
        ]
        + [jax.ShapeDtypeStruct((3, rows, ty, NT), BF16)] * n_gy,
        in_specs=vmem(2),
        out_specs=vmem(3 + n_gy),
        scratch_shapes=[
            pltpu.VMEM((2, nf, yw, NT), F32),
            pltpu.VMEM((2, nf, yw, NT), F32),
            pltpu.VMEM((nf, yw, NT), F32),
            pltpu.VMEM((nf, yw, NT), F32),
            pltpu.VMEM((nf, yw, NT), F32),
        ],
        compiler_params=pltpu.CompilerParams(vmem_limit_bytes=24 * 2**20),
        cost_estimate=pl.CostEstimate(flops=10**8, bytes_accessed=10**7, transcendentals=0),
        name="solver_waves",
    )(prob, slope)

    arrived = [waves[0]]
    for place in range(1, n_gy):
        pairs = [(i, (i + place) % n_gy) for i in range(n_gy)]
        arrived.append(lax.ppermute(waves[place], "gy", pairs))

    everyone = pl.pallas_call(
        functools.partial(last_kernel, ty),
        out_shape=jax.ShapeDtypeStruct((n_gx * n_gy, 1, NT), F32),
        in_specs=vmem(3),
        out_specs=pl.BlockSpec(memory_space=pltpu.VMEM),
        compiler_params=pltpu.CompilerParams(vmem_limit_bytes=16 * 2**20),
        cost_estimate=pl.CostEstimate(flops=10**9, bytes_accessed=10**8, transcendentals=0),
        name="last_moment",
    )(moments, face, wave2)
    moments = lax.all_to_all(everyone, ("gx", "gy"), split_axis=0, concat_axis=0, tiled=True)
    shift_field = pl.pallas_call(
        functools.partial(combine_kernel, n_gy, ty),
        out_shape=jax.ShapeDtypeStruct((rows, grid_y, NT), F32),
        in_specs=vmem(1 + n_gy),
        out_specs=pl.BlockSpec(memory_space=pltpu.VMEM),
        compiler_params=pltpu.CompilerParams(vmem_limit_bytes=16 * 2**20),
        name="combine_waves",
    )(moments, *arrived)
    return (fault, shift_field)


def solution(mesh):
    return jax.shard_map(
        on_device,
        mesh=mesh,
        in_specs=(P("gx", "gy", None), P(), P(), P(), P()),
        out_specs=(P("gx", "gy", None), P(("gx", "gy"), None, None)),
        check_vma=False,
    )
```

```python
import functools

import jax
import jax.numpy as jnp
from jax import lax
from jax.experimental import pallas as pl
from jax.experimental.pallas import tpu as pltpu
from jax.sharding import PartitionSpec as P

MU_DIAG = 0.05
ETA_TIME = 0.5

TX, NT, H = 16, 128, 8
CH = 16
XW = TX + 2 * H
FX = TX + 8
RX = 4
FIRST, SECOND, THIRD = 8, 11, 11
Y_SLOTS = (1, 2, 3, 0)
LIMIT = 6
GROUP = 2
BLK = 256
EDGE = 7
SUB = 16
PAIRS = NT // 2

F32 = jnp.float32
BF16 = jnp.bfloat16


def iota(shape, dim):
    return lax.broadcasted_iota(jnp.int32, shape, dim)


def dot_nt(a, b):
    return lax.dot_general(a, b, (((1,), (1,)), ((), ())), preferred_element_type=F32)


def prep_kernel(inner_ref, outer_ref, after_ref, w1_ref, w2_ref, w3_ref, w4_ref):
    del after_ref
    spread = jnp.where(iota((CH, BLK), 1) % CH == iota((CH, BLK), 0), 1.0, 0.0).astype(BF16)
    unit = jnp.where(iota((BLK, BLK), 1) == iota((BLK, BLK), 0), 1.0, 0.0).astype(BF16)
    none = jnp.zeros((CH, BLK), BF16)
    cell = iota((CH, BLK), 1) // CH
    at_cell = [cell == at for at in range(16)]
    inputs = input_cells()
    tiled = jnp.dot(inner_ref[...], spread, preferred_element_type=F32).astype(BF16)
    for layer, ref in enumerate((w2_ref, w3_ref)):
        for tile in range(6):
            bands = []
            for yo in range(2):
                for to in range(2):
                    for xo in range(4):
                        band = none
                        for at, (y, t, x) in enumerate(inputs[tile]):
                            dx, dy, dt = x - xo + 1, y - yo + 1, t - to + 1
                            if min(dx, dy, dt) >= 0 and max(dx, dy, dt) <= 2:
                                tap = tiled[(layer * 27 + dx * 9 + dy * 3 + dt) * CH :][:CH]
                                band = jnp.where(at_cell[at], tap, band)
                        bands.append(band)
            turned = dot_nt(unit, jnp.concatenate(bands, axis=0))
            ref[tile * BLK : (tile + 1) * BLK, :] = turned.astype(BF16)

    def taps(which):
        found = {}
        for dx in range(3):
            for dy in range(3):
                tiled = jnp.dot(outer_ref[which, dx, dy], spread, preferred_element_type=F32)
                for dt in range(3):
                    found[dx, dy, dt] = tiled[dt : dt + 1]
        return found

    first, last = taps(0), taps(1)
    lane_yt = iota((1, BLK), 1) // 64
    quarter = [lane_yt == at for at in range(4)]

    def by_quarter(found, dx, at):
        value = jnp.zeros((1, BLK), F32)
        for y in range(2):
            for t in range(2):
                dy, dt = at(y, t)
                if 0 <= dy <= 2 and 0 <= dt <= 2:
                    value = jnp.where(quarter[y * 2 + t], found[dx, dy, dt], value)
        return value

    def rows_of(found, rows, at):
        return [
            jnp.broadcast_to(by_quarter(found, dx, at), (rows, BLK)).astype(BF16)
            for dx in range(3)
        ]

    row_x = iota((XW, BLK), 0)
    lane_x = iota((XW, BLK), 1) // CH % 4
    offset_x = [row_x - 1 - 4 * blk - lane_x for blk in range(EDGE)]
    offset_x.append(jnp.where(lane_x == 0, row_x - 29, jnp.where(lane_x == 3, row_x, -1)))
    masks = [[offset == dx for dx in range(3)] for offset in offset_x]
    none = jnp.zeros((XW, BLK), BF16)
    for j in range(4):
        for yi in range(4):
            row = (j * 4 + yi) * XW
            values = rows_of(first, XW, lambda y, t: (yi - y, j - t))
            for blk in range(EDGE + 1):
                band = none
                for dx in range(3):
                    band = jnp.where(masks[blk][dx], values[dx], band)
                w1_ref[row : row + XW, blk * BLK : (blk + 1) * BLK] = band
    masks = [
        [4 * blk + lane_x - 1 - row_x == dx for dx in range(3)] for blk in range(EDGE)
    ]
    bands = [[] for blk in range(EDGE)]
    for j in range(4):
        for yi in Y_SLOTS:
            values = rows_of(last, XW, lambda y, t: (y + 2 - yi, t + 2 - j))
            for blk in range(EDGE):
                band = none
                for dx in range(3):
                    band = jnp.where(masks[blk][dx], values[dx], band)
                bands[blk].append(band)
    for blk in range(EDGE):
        turned = dot_nt(unit, jnp.concatenate(bands[blk], axis=0))
        w4_ref[blk * BLK : (blk + 1) * BLK, :] = turned.astype(BF16)


def input_cells():
    tiles = []
    here = [(t, x) for t in (0, 1) for x in range(4)]
    near = [(2, 2), (2, 3), (-1, 0), (-1, 1), (-1, 2), (-1, 3), (2, 0), (2, 1)]
    side = [(0, 4), (2, -1), (-1, 4), (0, -1), (1, 4), (-1, -1), (2, 4), (1, -1)]
    for cells in (here, near, side):
        for rows in ((0, 1), (-1, 2)):
            tiles.append([(y, t, x) for y in rows for t, x in cells])
    return tiles


def plane_shifts(yw):
    block = (RX, yw, NT)
    lane = iota(block, 2)
    first_lane = lane == 0
    last_lane = lane == NT - 1

    def up_y(v):
        return pltpu.roll(v, yw - 1, 1)

    def down_y(v):
        return pltpu.roll(v, 1, 1)

    def up_t(v, edge=0.0):
        return jnp.where(last_lane, edge, pltpu.roll(v, NT - 1, 2))

    def down_t(v, edge=0.0):
        return jnp.where(first_lane, edge, pltpu.roll(v, 1, 2))

    return block, up_y, down_y, up_t, down_t


def dot(a, b):
    return jnp.dot(a, b, preferred_element_type=F32)


def pair_of(row):
    return row // SUB + (row % SUB) * 4


def lane_masks(x0, grid_x, blocks):
    slot = iota((1, BLK), 1) // CH % 4
    masks = []
    for blk in range(blocks):
        if blk < EDGE:
            at = x0 - 6 + 4 * blk + slot
        else:
            at = x0 + jnp.where(slot == 0, 22, -7)
        masks.append(jnp.where((at >= 0) & (at < grid_x), 1.0, 0.0))
    return masks


def row_mask(y, grid_y):
    at = y + jnp.where(iota((1, BLK), 1) >= 128, 1, 0)
    return jnp.where((at >= 0) & (at < grid_y), 1.0, 0.0)


def put(act, pair, blk, values):
    sub_row = iota((SUB, 128), 0)
    place = iota((PAIRS, 128), 1) // CH
    early = (place >= 2) & (place < 6)
    act[0, pair, blk] = values.astype(BF16)
    for half in range(2):
        turned = pltpu.roll(values[:, half * 128 : (half + 1) * 128], 96, 1)
        head = jnp.where(sub_row == 0, 0.0, pltpu.roll(turned[PAIRS - SUB :], 1, 0))
        tail = jnp.where(sub_row == SUB - 1, 0.0, pltpu.roll(turned[:SUB], SUB - 1, 0))
        before = jnp.concatenate([head, turned[: PAIRS - SUB]], axis=0)
        after = jnp.concatenate([turned[SUB:], tail], axis=0)
        both = jnp.where(early, before, after)
        act[1, pair, blk, :, half * 128 : (half + 1) * 128] = both.astype(BF16)


def put_sides(act, pair, blocks):
    place = iota((PAIRS, 128), 1) // CH
    for blk in range(EDGE):
        left, right = (blk - 1) % blocks, (blk + 1) % blocks
        for half in range(2):
            at = slice(half * 128, (half + 1) * 128)
            even = jnp.where(place % 4 == 0, act[0, pair, right, :, at], act[1, pair, right, :, at])
            odd = jnp.where(place % 4 == 3, act[0, pair, left, :, at], act[1, pair, left, :, at])
            act[2, pair, blk, :, at] = jnp.where(place % 2 == 0, even, odd)


def layer(source, w_ref, pair, count):
    size = count * EDGE * PAIRS
    tiles = []
    for kind in range(3):
        centre = source[kind, pl.ds(pair + 1, count), :EDGE].reshape(size, BLK)
        before = source[kind, pl.ds(pair, count), :EDGE, :, 128:].reshape(size, 128)
        after = source[kind, pl.ds(pair + 2, count), :EDGE, :, :128].reshape(size, 128)
        tiles += [centre, before, after]
    return dot(jnp.concatenate(tiles, axis=1), w_ref[...])


def first_kernel(
    grid_x,
    grid_y,
    ty,
    amp_ref,
    xlow_ref,
    xhigh_ref,
    ylow_ref,
    yhigh_ref,
    w1_ref,
    act1,
    raw,
    amp,
):
    x0 = lax.axis_index("gx") * TX
    y0 = lax.axis_index("gy") * ty
    yw = ty + 2 * H

    for x in range(XW):
        row = x * yw
        if x < H:
            mid = xlow_ref[x]
        elif x < H + TX:
            mid = amp_ref[x - H]
        else:
            mid = xhigh_ref[x - H - TX]
        raw[row + H : row + H + ty, :] = mid.astype(F32)
        raw[row : row + H, :] = ylow_ref[x].astype(F32)
        raw[row + H + ty : row + yw, :] = yhigh_ref[x].astype(F32)

    def turn(y, carry):
        amp[y + 1] = raw[pl.ds(y, XW, stride=yw), :].astype(BF16)
        return carry

    lax.fori_loop(0, yw, turn, 0, unroll=8)
    amp[0] = jnp.zeros((XW, NT), BF16)
    amp[yw + 1] = jnp.zeros((XW, NT), BF16)

    at_row = iota((4 * PAIRS, NT), 0)
    to_pairs = jnp.where(
        iota((4 * PAIRS, NT), 1) == 2 * pair_of(at_row % PAIRS) - 1 + at_row // PAIRS, 1.0, 0.0
    ).astype(BF16)
    mask1 = lane_masks(x0, grid_x, EDGE + 1)

    def first(step, carry):
        pieces = []
        for i in range(FIRST):
            rows = amp[pl.ds((step * FIRST + i) * 2, 4)].reshape(4 * XW, NT)
            turned = dot_nt(to_pairs, rows).astype(BF16)
            pieces.append(
                jnp.concatenate([turned[j * PAIRS : (j + 1) * PAIRS] for j in range(4)], axis=1)
            )
        pieces = jnp.concatenate(pieces, axis=0)
        for begin in range(0, EDGE + 1, 2):
            result = dot(pieces, w1_ref[:, begin * BLK : (begin + 2) * BLK])
            for i in range(FIRST):
                pair = step * FIRST + i
                inside = row_mask(y0 + 2 * pair - H, grid_y)
                for blk in (begin, begin + 1):
                    lane = (blk - begin) * BLK
                    values = result[i * PAIRS : (i + 1) * PAIRS, lane : lane + BLK]
                    put(act1, pair, blk, jnp.maximum(values, 0.0) * (mask1[blk] * inside))
        for i in range(FIRST):
            put_sides(act1, step * FIRST + i, EDGE + 1)
        return carry

    lax.fori_loop(0, yw // 2 // FIRST, first, 0)


def second_kernel(grid_x, grid_y, ty, act1, w2_ref, act2):
    x0 = lax.axis_index("gx") * TX
    y0 = lax.axis_index("gy") * ty
    yw = ty + 2 * H
    pairs2 = ty // 2 + 6
    steps2 = pairs2 // SECOND
    mask2 = lane_masks(x0, grid_x, EDGE)

    def second(step, carry):
        for begin in range(0, SECOND, GROUP):
            count = min(GROUP, SECOND - begin)
            result = layer(act1, w2_ref, step * SECOND + begin, count)
            for i in range(count):
                pair = step * SECOND + begin + i
                inside = row_mask(y0 + 2 * pair - 6, grid_y)
                for blk in range(EDGE):
                    at = (i * EDGE + blk) * PAIRS
                    values = jnp.maximum(result[at : at + PAIRS], 0.0)
                    put(act2, pair + 1, blk, values * (mask2[blk] * inside))
                put_sides(act2, pair + 1, EDGE)
        return carry

    for edge in (0, pairs2 + 1):
        for kind in range(3):
            act2[kind, edge] = jnp.zeros((EDGE, PAIRS, BLK), BF16)
    lax.fori_loop(0, steps2, second, 0)


def third_kernel(grid_x, grid_y, ty, act2, raw, w3_ref, act3, prod):
    x0 = lax.axis_index("gx") * TX
    y0 = lax.axis_index("gy") * ty
    yw = ty + 2 * H
    pairs1, pairs2 = yw // 2, ty // 2 + 6
    block, up_y, down_y, up_t, down_t = plane_shifts(yw)

    def smooth_yt(v, edge=0.0):
        v = 0.5 * v + 0.25 * (up_t(v, edge) + down_t(v, edge))
        return 0.5 * v + 0.25 * (up_y(v) + down_y(v))

    def amp_rows(x):
        return raw[pl.ds(pl.multiple_of(x * yw, 8), RX * yw), :].reshape(block)

    def products(k):
        here = amp_rows(k + 3)
        grad_x = 0.5 * (amp_rows(k + 4) - amp_rows(k + 2))
        grad_y = 0.5 * (up_y(here) - down_y(here))
        grad_t = 0.5 * (up_t(here) - down_t(here))
        at = pl.ds(k, RX)
        prod[0, at] = smooth_yt(grad_x * grad_t)
        prod[1, at] = smooth_yt(grad_y * grad_t)
        energy = grad_t * grad_t + 0.25 * (grad_x * grad_x + grad_y * grad_y)
        prod[2, at] = smooth_yt(energy, 0.25 * here * here)

    steps3 = pairs2 // THIRD
    blocks3 = -(-(FX // RX + 1) // steps3)
    mask2 = lane_masks(x0, grid_x, EDGE)

    def third(step, carry):
        for i in range(blocks3):
            products(jnp.minimum((step * blocks3 + i) * RX, FX))
        for begin in range(0, THIRD, GROUP):
            count = min(GROUP, THIRD - begin)
            result = layer(act2, w3_ref, step * THIRD + begin, count)
            for i in range(count):
                pair = step * THIRD + begin + i
                inside = row_mask(y0 + 2 * pair - 6, grid_y)
                for blk in range(EDGE):
                    at = (i * EDGE + blk) * PAIRS
                    values = jnp.maximum(result[at : at + PAIRS], 0.0)
                    act3[pair, blk] = (values * (mask2[blk] * inside)).astype(BF16)
        return carry

    lax.fori_loop(0, steps3, third, 0)
    for pair in range(pairs2, pairs1):
        act3[pair] = jnp.zeros((EDGE, PAIRS, BLK), BF16)


def fourth_kernel(ty, act3, prod, w4_ref, fault_ref, prob, slope, part):
    yw = ty + 2 * H
    pairs1 = yw // 2
    at_lane = iota((NT, 8 * PAIRS), 1) % (4 * PAIRS)
    from_pairs = jnp.where(
        iota((NT, 8 * PAIRS), 0) == 2 * pair_of(at_lane % PAIRS) - 1 + at_lane // PAIRS, 1.0, 0.0
    ).astype(BF16)

    def slopes(k):
        at = pl.ds(k + 1, RX)
        sums = []
        for which in range(3):
            before, here, after = [prod[which, pl.ds(k + i, RX)] for i in range(3)]
            sums.append(0.5 * here + 0.25 * (before + after))
        scale = -1.0 / (sums[2] + 0.05)
        slope[0, at] = sums[0] * scale
        slope[1, at] = sums[1] * scale

    def fourth(step, carry):
        for i in range(2):
            slopes(jnp.minimum((step * 2 + i) * RX, FX - RX))
        pair = step * 8
        cells = [act3[pl.ds(pair, 8), blk].reshape(8 * PAIRS, BLK) for blk in range(EDGE)]
        result = dot(jnp.concatenate(cells, axis=1), w4_ref[...])
        for i in range(0, 8, 2):
            sides = []
            for at in (i, i + 1):
                rows = result[at * PAIRS : (at + 1) * PAIRS]
                sides.append(
                    jnp.concatenate([rows[:, j * 128 : (j + 1) * 128] for j in range(4)], axis=0)
                )
            both = jnp.concatenate(sides, axis=1)
            high = both.astype(BF16)
            low = (both - high.astype(F32)).astype(BF16)
            share = dot(from_pairs, jnp.concatenate([high, low], axis=0))
            part[pair + i] = share[:, :128]
            part[pair + i + 1] = share[:, 128:]
        return carry

    lax.fori_loop(0, pairs1 // 8, fourth, 0)

    for x in range(FX):
        prob[x * yw : x * yw + H, :] = jnp.zeros((H, NT), F32)
        prob[(x + 1) * yw - H : (x + 1) * yw, :] = jnp.zeros((H, NT), F32)
    lane = iota((NT, 128), 1)

    def order(step, carry):
        pair = 2 * step + 1
        here = part[pair]
        before = pltpu.roll(part[pair - 1], 64, 1)
        after = pltpu.roll(part[pair + 1], 64, 1)
        own = jnp.where(lane < 64, here, after)
        other = jnp.where(
            lane < 32,
            before,
            jnp.where(lane < 64, after, jnp.where(lane < 96, here, part[pair + 2])),
        )
        values = 1.0 / (1.0 + jnp.exp(-(own + other)))
        values = values.astype(BF16).astype(F32).T
        for row in range(4):
            at = pl.ds(2 * pair + 2 + row, FX, stride=yw)
            prob[at, :] = values[row * XW : row * XW + FX]
        return carry

    lax.fori_loop(0, (ty + 8) // 4, order, 0, unroll=2)

    for which in range(2):
        slope[which, FX + 1] = jnp.zeros((yw, NT), F32)
    for x in range(TX):
        fault_ref[x] = prob[(x + 4) * yw + H : (x + 4) * yw + H + ty, :].astype(BF16)


def owned(total, k, values, ty):
    for row in range(RX):
        ok = (k + row >= 5) & (k + row < 5 + TX)
        total = total + jnp.where(ok, values[row, H : H + ty], 0.0)
    return total


def image_of(wave, face, k, shifts):
    block, up_y, down_y, up_t, down_t = shifts
    at, before, after = [pl.ds(k + i, RX) for i in (0, -1, 1)]
    here = wave[at]
    flow = face[1, at] * (here - up_y(here))
    image = time_part(block) * here - ETA_TIME * (up_t(here) + down_t(here))
    image = image + flow - down_y(flow)
    image = image + face[0, at] * (here - wave[after])
    return here, image + face[0, before] * (here - wave[before])


def time_part(block):
    lane = iota(block, 2)
    count = jnp.where(lane == 0, 0.0, 1.0) + jnp.where(lane == NT - 1, 0.0, 1.0)
    return MU_DIAG + ETA_TIME * count


def waves_kernel(grid_x, grid_y, ty, prob, slope, mom_ref, face, wave2, *refs):
    n_gy = grid_y // ty
    waves_refs = refs[:n_gy]
    weight, flux, inv, wave0, wave1 = refs[n_gy:]
    place_y = lax.axis_index("gy")
    x0 = lax.axis_index("gx") * TX
    y0 = place_y * ty
    yw = ty + 2 * H
    shifts = plane_shifts(yw)
    block, up_y, down_y, up_t, down_t = shifts
    at_y = y0 - H + iota(block, 1)
    mask_y = (at_y >= 0) & (at_y < grid_y)

    def weights(step, carry):
        k = step * RX
        at = pl.ds(k + 1, RX)
        rows = prob[pl.ds(pl.multiple_of(k * yw, 8), RX * yw), :].reshape(block)
        raw_weight = 1.0 - 0.9 * rows
        at_x = x0 - 4 + k + iota(block, 0)
        weight[0, at] = raw_weight
        weight[1, at] = jnp.where(mask_y & (at_x >= 0) & (at_x < grid_x), raw_weight, 0.0)
        return carry

    lax.fori_loop(0, FX // RX, weights, 0)
    for which in range(2):
        weight[which, FX + 1] = jnp.full((yw, NT), 1.0 - which, F32)
        face[which, 0] = jnp.zeros((yw, NT), F32)
        flux[which, 0] = jnp.zeros((yw, NT), F32)

    def faces(step, carry):
        k = step * RX + 1
        at, after = pl.ds(k, RX), pl.ds(k + 1, RX)
        raw_weight = weight[0, at]
        masked = weight[1, at]
        face_x = 2.0 * masked * weight[1, after] / (raw_weight + weight[0, after])
        face_y = 2.0 * masked * up_y(masked) / (raw_weight + up_y(raw_weight))
        slope_y = slope[1, at]
        face[0, at] = face_x
        face[1, at] = face_y
        flux[0, at] = 0.5 * face_x * (slope[0, at] + slope[0, after])
        flux[1, at] = 0.5 * face_y * (slope_y + up_y(slope_y))
        return carry

    lax.fori_loop(0, FX // RX, faces, 0)

    def start(step, total):
        k = step * RX + 1
        at, before = pl.ds(k, RX), pl.ds(k - 1, RX)
        flux_y = flux[1, at]
        face_y = face[1, at]
        right = flux[0, before] - flux[0, at] + down_y(flux_y) - flux_y
        inverse = 1.0 / (time_part(block) + face[0, at] + face[0, before] + face_y + down_y(face_y))
        first_wave = right * inverse
        inv[at] = inverse
        wave0[at] = first_wave
        return owned(total, k, right * first_wave, ty)

    zero = jnp.zeros((ty, NT), F32)
    b0 = lax.fori_loop(0, FX // RX, start, zero)

    def advance(source, target):
        def body(step, totals):
            k = step * RX + 3
            here, image = image_of(source, face, k, shifts)
            at = pl.ds(k, RX)
            after = here - image * inv[at]
            target[at] = after
            return (
                owned(totals[0], k, here * image, ty),
                owned(totals[1], k, after * image, ty),
            )

        return body

    steps = (FX - 4) // RX
    a0, a1 = lax.fori_loop(0, steps, advance(wave0, wave1), (zero, zero))
    a2, a3 = lax.fori_loop(0, steps, advance(wave1, wave2), (zero, zero))
    sums = [jnp.sum(v, axis=0, keepdims=True) for v in (b0, a0, a1, a2, a3)]
    mom_ref[...] = jnp.concatenate(sums + [jnp.zeros((3, NT), F32)], axis=0)

    rows = TX // n_gy
    for place, ref in enumerate(waves_refs):
        to = lax.rem(place_y + place, n_gy) * rows + 5
        for which, wave in enumerate((wave0, wave1, wave2)):
            for row in range(rows):
                ref[which, row] = wave[to + row, H : H + ty, :].astype(BF16)


def last_kernel(ty, mom_ref, face, wave2, out_ref):
    shifts = plane_shifts(ty + 2 * H)

    def finish(step, total):
        k = step * RX + 5
        here, image = image_of(wave2, face, k, shifts)
        return owned(total, k, here * image, ty)

    total = lax.fori_loop(0, TX // RX, finish, jnp.zeros((ty, NT), F32))
    a4 = jnp.sum(total, axis=0, keepdims=True)
    sums = jnp.sum(jnp.where(iota((8, NT), 0) == 5, a4, mom_ref[...]), axis=1, keepdims=True)
    values = jnp.where(iota((8, NT), 0) == iota((8, NT), 1), sums, 0.0)
    values = jnp.sum(values, axis=0, keepdims=True)
    for device in range(out_ref.shape[0]):
        out_ref[device] = values


def combine_kernel(n_gy, ty, mom_ref, *refs):
    waves_refs, out_ref = refs[:n_gy], refs[n_gy]
    place_y = lax.axis_index("gy")
    moments = jnp.sum(mom_ref[...], axis=0)
    b0, a0, a1, a2, a3, a4 = [
        jnp.broadcast_to(moments[:, i : i + 1], (1, NT)) for i in range(6)
    ]
    a0, a1, a2, a3, a4 = [v / b0 for v in (a0, a1, a2, a3, a4)]
    l21 = a1 / a0
    l31 = a2 / a0
    d2 = jnp.maximum(a2 - l21 * a1, 1e-7 * a2 + 1e-30)
    l32 = (a3 - l21 * a2) / d2
    d3 = jnp.maximum(a4 - l31 * a2 - l32 * l32 * d2, 1e-7 * a4 + 1e-30)
    y2 = (1.0 - a0) - l21
    y3 = (1.0 - a0 - a1) - l31 - l32 * y2
    c3 = y3 / d3
    c2 = y2 / d2 - l32 * c3
    c1 = 1.0 / a0 - l21 * c2 - l31 * c3
    for place, ref in enumerate(waves_refs):
        source = lax.rem(place_y - place + n_gy, n_gy)
        at = pl.ds(pl.multiple_of(source * ty, 8), ty)
        for x in range(ref.shape[1]):
            w0, w1, w2 = [ref[which, x].astype(F32) for which in range(3)]
            out_ref[x, at, :] = c1 * w0 + c2 * w1 + c3 * w2


def vmem(count):
    return [pl.BlockSpec(memory_space=pltpu.VMEM)] * count


def on_device(amplitude, conv_first, conv_second, conv_third, conv_last):
    n_gx, n_gy = lax.axis_size("gx"), lax.axis_size("gy")
    ty = amplitude.shape[1]
    grid_x, grid_y = n_gx * TX, n_gy * ty
    assert amplitude.shape == (TX, ty, NT)

    def shift(values, axis, count, step):
        pairs = [(i, i + step) for i in range(count) if 0 <= i + step < count]
        return lax.ppermute(values, axis, pairs)

    xlow = shift(amplitude[TX - H :], "gx", n_gx, 1)
    xhigh = shift(amplitude[:H], "gx", n_gx, -1)
    ylow = shift(
        jnp.concatenate([xlow[:, ty - H :], amplitude[:, ty - H :], xhigh[:, ty - H :]]),
        "gy",
        n_gy,
        1,
    )
    yhigh = shift(
        jnp.concatenate([xlow[:, :H], amplitude[:, :H], xhigh[:, :H]]), "gy", n_gy, -1
    )

    weights = (conv_first, conv_second, conv_third, conv_last)
    (conv_first, conv_second, conv_third, conv_last), _ = lax.optimization_barrier((weights, xlow))

    def taps_first(weight):
        return jnp.transpose(weight, (2, 3, 4, 0, 1))

    w1, w2, w3, w4 = pl.pallas_call(
        prep_kernel,
        out_shape=[
            jax.ShapeDtypeStruct((16 * XW, (EDGE + 1) * BLK), BF16),
            jax.ShapeDtypeStruct((6 * BLK, BLK), BF16),
            jax.ShapeDtypeStruct((6 * BLK, BLK), BF16),
            jax.ShapeDtypeStruct((EDGE * BLK, 16 * XW), BF16),
        ],
        in_specs=vmem(2) + [pl.BlockSpec(memory_space=pl.ANY)],
        out_specs=vmem(4),
        compiler_params=pltpu.CompilerParams(vmem_limit_bytes=16 * 2**20),
        cost_estimate=pl.CostEstimate(flops=10**9, bytes_accessed=10**7, transcendentals=0),
        name="band_weights",
    )(
        jnp.concatenate([taps_first(conv_second), taps_first(conv_third)]).reshape(54 * CH, CH),
        jnp.concatenate(
            [jnp.transpose(conv_first, (1, 2, 3, 4, 0)), jnp.transpose(conv_last, (0, 2, 3, 4, 1))]
        ),
        xlow,
    )

    yw, nf = ty + 2 * H, FX + 2
    act1, raw = pl.pallas_call(
        functools.partial(first_kernel, grid_x, grid_y, ty),
        out_shape=[
            jax.ShapeDtypeStruct((3, yw // 2, EDGE + 1, PAIRS, BLK), BF16),
            jax.ShapeDtypeStruct(((XW + 2) * yw, NT), F32),
        ],
        in_specs=vmem(6),
        out_specs=vmem(2),
        scratch_shapes=[pltpu.VMEM((yw + 2, XW, NT), BF16)],
        compiler_params=pltpu.CompilerParams(vmem_limit_bytes=LIMIT * 2**20),
        cost_estimate=pl.CostEstimate(flops=10**10, bytes_accessed=10**7, transcendentals=0),
        name="layer_one",
    )(amplitude, xlow, xhigh, ylow, yhigh, w1)

    act2 = pl.pallas_call(
        functools.partial(second_kernel, grid_x, grid_y, ty),
        out_shape=jax.ShapeDtypeStruct((3, yw // 2, EDGE, PAIRS, BLK), BF16),
        in_specs=vmem(2),
        out_specs=pl.BlockSpec(memory_space=pltpu.VMEM),
        compiler_params=pltpu.CompilerParams(vmem_limit_bytes=LIMIT * 2**20),
        cost_estimate=pl.CostEstimate(flops=10**10, bytes_accessed=10**7, transcendentals=0),
        name="layer_two",
    )(act1, w2)

    act3, prod = pl.pallas_call(
        functools.partial(third_kernel, grid_x, grid_y, ty),
        out_shape=[
            jax.ShapeDtypeStruct((yw // 2, EDGE, PAIRS, BLK), BF16),
            jax.ShapeDtypeStruct((3, FX + 4, yw, NT), F32),
        ],
        in_specs=vmem(3),
        out_specs=vmem(2),
        compiler_params=pltpu.CompilerParams(vmem_limit_bytes=LIMIT * 2**20),
        cost_estimate=pl.CostEstimate(flops=10**10, bytes_accessed=10**7, transcendentals=0),
        name="layer_three",
    )(act2, raw, w3)

    fault, prob, slope = pl.pallas_call(
        functools.partial(fourth_kernel, ty),
        out_shape=[
            jax.ShapeDtypeStruct((TX, ty, NT), BF16),
            jax.ShapeDtypeStruct((FX * yw, NT), F32),
            jax.ShapeDtypeStruct((2, nf, yw, NT), F32),
        ],
        in_specs=vmem(3),
        out_specs=vmem(3),
        scratch_shapes=[pltpu.VMEM((yw // 2, NT, 128), F32)],
        compiler_params=pltpu.CompilerParams(vmem_limit_bytes=(LIMIT + 4) * 2**20),
        cost_estimate=pl.CostEstimate(
            flops=10**10, bytes_accessed=10**7, transcendentals=10**6
        ),
        name="layer_four",
    )(act3, prod, w4)

    rows = TX // n_gy
    moments, face, wave2, *waves = pl.pallas_call(
        functools.partial(waves_kernel, grid_x, grid_y, ty),
        out_shape=[
            jax.ShapeDtypeStruct((8, NT), F32),
            jax.ShapeDtypeStruct((2, nf, yw, NT), F32),
            jax.ShapeDtypeStruct((nf, yw, NT), F32),
        ]
        + [jax.ShapeDtypeStruct((3, rows, ty, NT), BF16)] * n_gy,
        in_specs=vmem(2),
        out_specs=vmem(3 + n_gy),
        scratch_shapes=[
            pltpu.VMEM((2, nf, yw, NT), F32),
            pltpu.VMEM((2, nf, yw, NT), F32),
            pltpu.VMEM((nf, yw, NT), F32),
            pltpu.VMEM((nf, yw, NT), F32),
            pltpu.VMEM((nf, yw, NT), F32),
        ],
        compiler_params=pltpu.CompilerParams(vmem_limit_bytes=24 * 2**20),
        cost_estimate=pl.CostEstimate(flops=10**8, bytes_accessed=10**7, transcendentals=0),
        name="solver_waves",
    )(prob, slope)

    arrived = [waves[0]]
    for place in range(1, n_gy):
        pairs = [(i, (i + place) % n_gy) for i in range(n_gy)]
        arrived.append(lax.ppermute(waves[place], "gy", pairs))

    everyone = pl.pallas_call(
        functools.partial(last_kernel, ty),
        out_shape=jax.ShapeDtypeStruct((n_gx * n_gy, 1, NT), F32),
        in_specs=vmem(3),
        out_specs=pl.BlockSpec(memory_space=pltpu.VMEM),
        compiler_params=pltpu.CompilerParams(vmem_limit_bytes=16 * 2**20),
        cost_estimate=pl.CostEstimate(flops=10**9, bytes_accessed=10**8, transcendentals=0),
        name="last_moment",
    )(moments, face, wave2)
    moments = lax.all_to_all(everyone, ("gx", "gy"), split_axis=0, concat_axis=0, tiled=True)
    shift_field = pl.pallas_call(
        functools.partial(combine_kernel, n_gy, ty),
        out_shape=jax.ShapeDtypeStruct((rows, grid_y, NT), F32),
        in_specs=vmem(1 + n_gy),
        out_specs=pl.BlockSpec(memory_space=pltpu.VMEM),
        compiler_params=pltpu.CompilerParams(vmem_limit_bytes=16 * 2**20),
        name="combine_waves",
    )(moments, *arrived)
    return (fault, shift_field)


def solution(mesh):
    return jax.shard_map(
        on_device,
        mesh=mesh,
        in_specs=(P("gx", "gy", None), P(), P(), P(), P()),
        out_specs=(P("gx", "gy", None), P(("gx", "gy"), None, None)),
        check_vma=False,
    )
```

```python
import functools

import jax
import jax.numpy as jnp
from jax import lax
from jax.experimental import pallas as pl
from jax.experimental.pallas import tpu as pltpu
from jax.sharding import PartitionSpec as P

MU_DIAG = 0.05
ETA_TIME = 0.5

TX, NT, H = 16, 128, 8
CH = 16
XW = TX + 2 * H
FX = TX + 8
RX = 4
FIRST, SECOND, THIRD = 8, 11, 11
Y_SLOTS = (1, 2, 3, 0)
LIMIT = 6
GROUP = 2
BLK = 256
EDGE = 7
SUB = 16
PAIRS = NT // 2

F32 = jnp.float32
BF16 = jnp.bfloat16


def iota(shape, dim):
    return lax.broadcasted_iota(jnp.int32, shape, dim)


def dot_nt(a, b):
    return lax.dot_general(a, b, (((1,), (1,)), ((), ())), preferred_element_type=F32)


def prep_kernel(inner_ref, outer_ref, after_ref, w1_ref, w2_ref, w3_ref, w4_ref):
    del after_ref
    spread = jnp.where(iota((CH, BLK), 1) % CH == iota((CH, BLK), 0), 1.0, 0.0).astype(BF16)
    unit = jnp.where(iota((BLK, BLK), 1) == iota((BLK, BLK), 0), 1.0, 0.0).astype(BF16)
    none = jnp.zeros((CH, BLK), BF16)
    cell = iota((CH, BLK), 1) // CH
    at_cell = [cell == at for at in range(16)]
    inputs = input_cells()
    tiled = jnp.dot(inner_ref[...], spread, preferred_element_type=F32).astype(BF16)
    for layer, ref in enumerate((w2_ref, w3_ref)):
        for tile in range(6):
            bands = []
            for yo in range(2):
                for to in range(2):
                    for xo in range(4):
                        band = none
                        for at, (y, t, x) in enumerate(inputs[tile]):
                            dx, dy, dt = x - xo + 1, y - yo + 1, t - to + 1
                            if min(dx, dy, dt) >= 0 and max(dx, dy, dt) <= 2:
                                tap = tiled[(layer * 27 + dx * 9 + dy * 3 + dt) * CH :][:CH]
                                band = jnp.where(at_cell[at], tap, band)
                        bands.append(band)
            turned = dot_nt(unit, jnp.concatenate(bands, axis=0))
            ref[tile * BLK : (tile + 1) * BLK, :] = turned.astype(BF16)

    def taps(which):
        found = {}
        for dx in range(3):
            for dy in range(3):
                tiled = jnp.dot(outer_ref[which, dx, dy], spread, preferred_element_type=F32)
                for dt in range(3):
                    found[dx, dy, dt] = tiled[dt : dt + 1]
        return found

    first, last = taps(0), taps(1)
    lane_yt = iota((1, BLK), 1) // 64
    quarter = [lane_yt == at for at in range(4)]

    def by_quarter(found, dx, at):
        value = jnp.zeros((1, BLK), F32)
        for y in range(2):
            for t in range(2):
                dy, dt = at(y, t)
                if 0 <= dy <= 2 and 0 <= dt <= 2:
                    value = jnp.where(quarter[y * 2 + t], found[dx, dy, dt], value)
        return value

    def rows_of(found, rows, at):
        return [
            jnp.broadcast_to(by_quarter(found, dx, at), (rows, BLK)).astype(BF16)
            for dx in range(3)
        ]

    row_x = iota((XW, BLK), 0)
    lane_x = iota((XW, BLK), 1) // CH % 4
    offset_x = [row_x - 1 - 4 * blk - lane_x for blk in range(EDGE)]
    offset_x.append(jnp.where(lane_x == 0, row_x - 29, jnp.where(lane_x == 3, row_x, -1)))
    masks = [[offset == dx for dx in range(3)] for offset in offset_x]
    none = jnp.zeros((XW, BLK), BF16)
    for j in range(4):
        for yi in range(4):
            row = (j * 4 + yi) * XW
            values = rows_of(first, XW, lambda y, t: (yi - y, j - t))
            for blk in range(EDGE + 1):
                band = none
                for dx in range(3):
                    band = jnp.where(masks[blk][dx], values[dx], band)
                w1_ref[row : row + XW, blk * BLK : (blk + 1) * BLK] = band
    masks = [
        [4 * blk + lane_x - 1 - row_x == dx for dx in range(3)] for blk in range(EDGE)
    ]
    bands = [[] for blk in range(EDGE)]
    for j in range(4):
        for yi in Y_SLOTS:
            values = rows_of(last, XW, lambda y, t: (y + 2 - yi, t + 2 - j))
            for blk in range(EDGE):
                band = none
                for dx in range(3):
                    band = jnp.where(masks[blk][dx], values[dx], band)
                bands[blk].append(band)
    for blk in range(EDGE):
        turned = dot_nt(unit, jnp.concatenate(bands[blk], axis=0))
        w4_ref[blk * BLK : (blk + 1) * BLK, :] = turned.astype(BF16)


def slices_kernel(amp_ref, first_x, last_x, first_y, last_y):
    ty = amp_ref.shape[1]
    first_x[...] = amp_ref[:H]
    last_x[...] = amp_ref[TX - H :]
    first_y[...] = amp_ref[:, :H]
    last_y[...] = amp_ref[:, ty - H :]


def input_cells():
    tiles = []
    here = [(t, x) for t in (0, 1) for x in range(4)]
    near = [(2, 2), (2, 3), (-1, 0), (-1, 1), (-1, 2), (-1, 3), (2, 0), (2, 1)]
    side = [(0, 4), (2, -1), (-1, 4), (0, -1), (1, 4), (-1, -1), (2, 4), (1, -1)]
    for cells in (here, near, side):
        for rows in ((0, 1), (-1, 2)):
            tiles.append([(y, t, x) for y in rows for t, x in cells])
    return tiles


def plane_shifts(yw):
    block = (RX, yw, NT)
    lane = iota(block, 2)
    first_lane = lane == 0
    last_lane = lane == NT - 1

    def up_y(v):
        return pltpu.roll(v, yw - 1, 1)

    def down_y(v):
        return pltpu.roll(v, 1, 1)

    def up_t(v, edge=0.0):
        return jnp.where(last_lane, edge, pltpu.roll(v, NT - 1, 2))

    def down_t(v, edge=0.0):
        return jnp.where(first_lane, edge, pltpu.roll(v, 1, 2))

    return block, up_y, down_y, up_t, down_t


def dot(a, b):
    return jnp.dot(a, b, preferred_element_type=F32)


def pair_of(row):
    return row // SUB + (row % SUB) * 4


def lane_masks(x0, grid_x, blocks):
    slot = iota((1, BLK), 1) // CH % 4
    masks = []
    for blk in range(blocks):
        if blk < EDGE:
            at = x0 - 6 + 4 * blk + slot
        else:
            at = x0 + jnp.where(slot == 0, 22, -7)
        masks.append(jnp.where((at >= 0) & (at < grid_x), 1.0, 0.0))
    return masks


def row_mask(y, grid_y):
    at = y + jnp.where(iota((1, BLK), 1) >= 128, 1, 0)
    return jnp.where((at >= 0) & (at < grid_y), 1.0, 0.0)


def lanes16():
    return iota((PAIRS, 128), 1).astype(jnp.int16)


def put(act, pair, blk, values):
    sub_row = iota((SUB, 128), 0)
    lane = lanes16()
    early = (lane >= 32) & (lane < 96)
    values = values.astype(BF16)
    act[0, pair, blk] = values
    for half in range(2):
        turned = pltpu.roll(values[:, half * 128 : (half + 1) * 128], 96, 1)
        head = pltpu.roll(turned[PAIRS - SUB :].astype(F32), 1, 0)
        head = jnp.where(sub_row == 0, 0.0, head).astype(BF16)
        tail = pltpu.roll(turned[:SUB].astype(F32), SUB - 1, 0)
        tail = jnp.where(sub_row == SUB - 1, 0.0, tail).astype(BF16)
        before = jnp.concatenate([head, turned[: PAIRS - SUB]], axis=0)
        after = jnp.concatenate([turned[SUB:], tail], axis=0)
        act[1, pair, blk, :, half * 128 : (half + 1) * 128] = jnp.where(early, before, after)


def put_sides(act, pair, blocks):
    lane = lanes16()
    slot0, slot3, even_slot = (lane & 48) == 0, (lane & 48) == 48, (lane & 16) == 0
    for blk in range(EDGE):
        left, right = (blk - 1) % blocks, (blk + 1) % blocks
        for half in range(2):
            at = slice(half * 128, (half + 1) * 128)
            even = jnp.where(slot0, act[0, pair, right, :, at], act[1, pair, right, :, at])
            odd = jnp.where(slot3, act[0, pair, left, :, at], act[1, pair, left, :, at])
            act[2, pair, blk, :, at] = jnp.where(even_slot, even, odd)


def layer(source, w_ref, pair, count):
    size = count * EDGE * PAIRS
    tiles = []
    for kind in range(3):
        centre = source[kind, pl.ds(pair + 1, count), :EDGE].reshape(size, BLK)
        before = source[kind, pl.ds(pair, count), :EDGE, :, 128:].reshape(size, 128)
        after = source[kind, pl.ds(pair + 2, count), :EDGE, :, :128].reshape(size, 128)
        tiles += [centre, before, after]
    return dot(jnp.concatenate(tiles, axis=1), w_ref[...])


def first_kernel(
    grid_x,
    grid_y,
    ty,
    amp_ref,
    xlow_ref,
    xhigh_ref,
    ylow_ref,
    yhigh_ref,
    w1_ref,
    act1,
    raw,
    amp,
):
    x0 = lax.axis_index("gx") * TX
    y0 = lax.axis_index("gy") * ty
    yw = ty + 2 * H

    for x in range(XW):
        row = x * yw
        if x < H:
            mid = xlow_ref[x]
        elif x < H + TX:
            mid = amp_ref[x - H]
        else:
            mid = xhigh_ref[x - H - TX]
        raw[row + H : row + H + ty, :] = mid.astype(F32)
        raw[row : row + H, :] = ylow_ref[x].astype(F32)
        raw[row + H + ty : row + yw, :] = yhigh_ref[x].astype(F32)

    def turn(y, carry):
        amp[y + 1] = raw[pl.ds(y, XW, stride=yw), :].astype(BF16)
        return carry

    lax.fori_loop(0, yw, turn, 0, unroll=8)
    amp[0] = jnp.zeros((XW, NT), BF16)
    amp[yw + 1] = jnp.zeros((XW, NT), BF16)

    at_row = iota((4 * PAIRS, NT), 0)
    to_pairs = jnp.where(
        iota((4 * PAIRS, NT), 1) == 2 * pair_of(at_row % PAIRS) - 1 + at_row // PAIRS, 1.0, 0.0
    ).astype(BF16)
    mask1 = lane_masks(x0, grid_x, EDGE + 1)

    def first(step, carry):
        pieces = []
        for i in range(FIRST):
            rows = amp[pl.ds((step * FIRST + i) * 2, 4)].reshape(4 * XW, NT)
            turned = dot_nt(to_pairs, rows).astype(BF16)
            pieces.append(
                jnp.concatenate([turned[j * PAIRS : (j + 1) * PAIRS] for j in range(4)], axis=1)
            )
        pieces = jnp.concatenate(pieces, axis=0)
        for begin in range(0, EDGE + 1, 2):
            result = dot(pieces, w1_ref[:, begin * BLK : (begin + 2) * BLK])
            for i in range(FIRST):
                pair = step * FIRST + i
                inside = row_mask(y0 + 2 * pair - H, grid_y)
                for blk in (begin, begin + 1):
                    lane = (blk - begin) * BLK
                    values = result[i * PAIRS : (i + 1) * PAIRS, lane : lane + BLK]
                    put(act1, pair, blk, jnp.maximum(values, 0.0) * (mask1[blk] * inside))
        for i in range(FIRST):
            put_sides(act1, step * FIRST + i, EDGE + 1)
        return carry

    lax.fori_loop(0, yw // 2 // FIRST, first, 0, unroll=True)


def second_kernel(grid_x, grid_y, ty, act1, w2_ref, act2):
    x0 = lax.axis_index("gx") * TX
    y0 = lax.axis_index("gy") * ty
    yw = ty + 2 * H
    pairs2 = ty // 2 + 6
    steps2 = pairs2 // SECOND
    mask2 = lane_masks(x0, grid_x, EDGE)

    def second(step, carry):
        for begin in range(0, SECOND, GROUP):
            count = min(GROUP, SECOND - begin)
            result = layer(act1, w2_ref, step * SECOND + begin, count)
            for i in range(count):
                pair = step * SECOND + begin + i
                inside = row_mask(y0 + 2 * pair - 6, grid_y)
                for blk in range(EDGE):
                    at = (i * EDGE + blk) * PAIRS
                    values = jnp.maximum(result[at : at + PAIRS], 0.0)
                    put(act2, pair + 1, blk, values * (mask2[blk] * inside))
                put_sides(act2, pair + 1, EDGE)
        return carry

    for edge in (0, pairs2 + 1):
        for kind in range(3):
            act2[kind, edge] = jnp.zeros((EDGE, PAIRS, BLK), BF16)
    lax.fori_loop(0, steps2, second, 0)


def third_kernel(grid_x, grid_y, ty, act2, raw, w3_ref, act3, prod):
    x0 = lax.axis_index("gx") * TX
    y0 = lax.axis_index("gy") * ty
    yw = ty + 2 * H
    pairs1, pairs2 = yw // 2, ty // 2 + 6
    block, up_y, down_y, up_t, down_t = plane_shifts(yw)

    def smooth_yt(v, edge=0.0):
        v = 0.5 * v + 0.25 * (up_t(v, edge) + down_t(v, edge))
        return 0.5 * v + 0.25 * (up_y(v) + down_y(v))

    def amp_rows(x):
        return raw[pl.ds(pl.multiple_of(x * yw, 8), RX * yw), :].reshape(block)

    def products(k):
        here = amp_rows(k + 3)
        grad_x = 0.5 * (amp_rows(k + 4) - amp_rows(k + 2))
        grad_y = 0.5 * (up_y(here) - down_y(here))
        grad_t = 0.5 * (up_t(here) - down_t(here))
        at = pl.ds(k, RX)
        prod[0, at] = smooth_yt(grad_x * grad_t)
        prod[1, at] = smooth_yt(grad_y * grad_t)
        energy = grad_t * grad_t + 0.25 * (grad_x * grad_x + grad_y * grad_y)
        prod[2, at] = smooth_yt(energy, 0.25 * here * here)

    steps3 = pairs2 // THIRD
    blocks3 = -(-(FX // RX + 1) // steps3)
    mask2 = lane_masks(x0, grid_x, EDGE)

    def third(step, carry):
        for i in range(blocks3):
            products(jnp.minimum((step * blocks3 + i) * RX, FX))
        for begin in range(0, THIRD, GROUP):
            count = min(GROUP, THIRD - begin)
            result = layer(act2, w3_ref, step * THIRD + begin, count)
            for i in range(count):
                pair = step * THIRD + begin + i
                inside = row_mask(y0 + 2 * pair - 6, grid_y)
                for blk in range(EDGE):
                    at = (i * EDGE + blk) * PAIRS
                    values = jnp.maximum(result[at : at + PAIRS], 0.0)
                    act3[pair, blk] = (values * (mask2[blk] * inside)).astype(BF16)
        return carry

    lax.fori_loop(0, steps3, third, 0)
    for pair in range(pairs2, pairs1):
        act3[pair] = jnp.zeros((EDGE, PAIRS, BLK), BF16)


def fourth_kernel(ty, act3, prod, w4_ref, fault_ref, prob, slope, part):
    yw = ty + 2 * H
    pairs1 = yw // 2
    at_lane = iota((NT, 8 * PAIRS), 1) % (4 * PAIRS)
    from_pairs = jnp.where(
        iota((NT, 8 * PAIRS), 0) == 2 * pair_of(at_lane % PAIRS) - 1 + at_lane // PAIRS, 1.0, 0.0
    ).astype(BF16)

    def slopes(k):
        at = pl.ds(k + 1, RX)
        sums = []
        for which in range(3):
            before, here, after = [prod[which, pl.ds(k + i, RX)] for i in range(3)]
            sums.append(0.5 * here + 0.25 * (before + after))
        scale = -1.0 / (sums[2] + 0.05)
        slope[0, at] = sums[0] * scale
        slope[1, at] = sums[1] * scale

    def fourth(step, carry):
        for i in range(2):
            slopes(jnp.minimum((step * 2 + i) * RX, FX - RX))
        pair = step * 8
        cells = [act3[pl.ds(pair, 8), blk].reshape(8 * PAIRS, BLK) for blk in range(EDGE)]
        result = dot(jnp.concatenate(cells, axis=1), w4_ref[...])
        for i in range(0, 8, 2):
            sides = []
            for at in (i, i + 1):
                rows = result[at * PAIRS : (at + 1) * PAIRS]
                sides.append(
                    jnp.concatenate([rows[:, j * 128 : (j + 1) * 128] for j in range(4)], axis=0)
                )
            both = jnp.concatenate(sides, axis=1)
            high = both.astype(BF16)
            low = (both - high.astype(F32)).astype(BF16)
            share = dot(from_pairs, jnp.concatenate([high, low], axis=0))
            part[pair + i] = share[:, :128]
            part[pair + i + 1] = share[:, 128:]
        return carry

    lax.fori_loop(0, pairs1 // 8, fourth, 0, unroll=True)

    for x in range(FX):
        prob[x * yw : x * yw + H, :] = jnp.zeros((H, NT), F32)
        prob[(x + 1) * yw - H : (x + 1) * yw, :] = jnp.zeros((H, NT), F32)
    lane = iota((NT, 128), 1)

    def order(step, carry):
        pair = 2 * step + 1
        here = part[pair]
        before = pltpu.roll(part[pair - 1], 64, 1)
        after = pltpu.roll(part[pair + 1], 64, 1)
        own = jnp.where(lane < 64, here, after)
        other = jnp.where(
            lane < 32,
            before,
            jnp.where(lane < 64, after, jnp.where(lane < 96, here, part[pair + 2])),
        )
        values = 1.0 / (1.0 + jnp.exp(-(own + other)))
        values = values.astype(BF16).astype(F32).T
        for row in range(4):
            at = pl.ds(2 * pair + 2 + row, FX, stride=yw)
            prob[at, :] = values[row * XW : row * XW + FX]
        return carry

    lax.fori_loop(0, (ty + 8) // 4, order, 0, unroll=5)

    for which in range(2):
        slope[which, FX + 1] = jnp.zeros((yw, NT), F32)
    for x in range(TX):
        fault_ref[x] = prob[(x + 4) * yw + H : (x + 4) * yw + H + ty, :].astype(BF16)


def owned(total, k, values, ty):
    for row in range(RX):
        ok = (k + row >= 5) & (k + row < 5 + TX)
        total = total + jnp.where(ok, values[row, H : H + ty], 0.0)
    return total


def image_of(wave, face, k, shifts):
    block, up_y, down_y, up_t, down_t = shifts
    at, before, after = [pl.ds(k + i, RX) for i in (0, -1, 1)]
    here = wave[at]
    flow = face[1, at] * (here - up_y(here))
    image = time_part(block) * here - ETA_TIME * (up_t(here) + down_t(here))
    image = image + flow - down_y(flow)
    image = image + face[0, at] * (here - wave[after])
    return here, image + face[0, before] * (here - wave[before])


def time_part(block):
    lane = iota(block, 2)
    count = jnp.where(lane == 0, 0.0, 1.0) + jnp.where(lane == NT - 1, 0.0, 1.0)
    return MU_DIAG + ETA_TIME * count


def waves_kernel(grid_x, grid_y, ty, prob, slope, mom_ref, face, wave2, *refs):
    n_gy = grid_y // ty
    waves_refs = refs[:n_gy]
    weight, flux, inv, wave0, wave1 = refs[n_gy:]
    place_y = lax.axis_index("gy")
    x0 = lax.axis_index("gx") * TX
    y0 = place_y * ty
    yw = ty + 2 * H
    shifts = plane_shifts(yw)
    block, up_y, down_y, up_t, down_t = shifts
    at_y = y0 - H + iota(block, 1)
    mask_y = (at_y >= 0) & (at_y < grid_y)

    def weights(step, carry):
        k = step * RX
        at = pl.ds(k + 1, RX)
        rows = prob[pl.ds(pl.multiple_of(k * yw, 8), RX * yw), :].reshape(block)
        raw_weight = 1.0 - 0.9 * rows
        at_x = x0 - 4 + k + iota(block, 0)
        weight[0, at] = raw_weight
        weight[1, at] = jnp.where(mask_y & (at_x >= 0) & (at_x < grid_x), raw_weight, 0.0)
        return carry

    lax.fori_loop(0, FX // RX, weights, 0)
    for which in range(2):
        weight[which, FX + 1] = jnp.full((yw, NT), 1.0 - which, F32)
        face[which, 0] = jnp.zeros((yw, NT), F32)
        flux[which, 0] = jnp.zeros((yw, NT), F32)

    def faces(step, carry):
        k = step * RX + 1
        at, after = pl.ds(k, RX), pl.ds(k + 1, RX)
        raw_weight = weight[0, at]
        masked = weight[1, at]
        face_x = 2.0 * masked * weight[1, after] / (raw_weight + weight[0, after])
        face_y = 2.0 * masked * up_y(masked) / (raw_weight + up_y(raw_weight))
        slope_y = slope[1, at]
        face[0, at] = face_x
        face[1, at] = face_y
        flux[0, at] = 0.5 * face_x * (slope[0, at] + slope[0, after])
        flux[1, at] = 0.5 * face_y * (slope_y + up_y(slope_y))
        return carry

    lax.fori_loop(0, FX // RX, faces, 0)

    def start(step, total):
        k = step * RX + 1
        at, before = pl.ds(k, RX), pl.ds(k - 1, RX)
        flux_y = flux[1, at]
        face_y = face[1, at]
        right = flux[0, before] - flux[0, at] + down_y(flux_y) - flux_y
        inverse = 1.0 / (time_part(block) + face[0, at] + face[0, before] + face_y + down_y(face_y))
        first_wave = right * inverse
        inv[at] = inverse
        wave0[at] = first_wave
        return owned(total, k, right * first_wave, ty)

    zero = jnp.zeros((ty, NT), F32)
    b0 = lax.fori_loop(0, FX // RX, start, zero)

    def advance(source, target):
        def body(step, totals):
            k = step * RX + 3
            here, image = image_of(source, face, k, shifts)
            at = pl.ds(k, RX)
            after = here - image * inv[at]
            target[at] = after
            return (
                owned(totals[0], k, here * image, ty),
                owned(totals[1], k, after * image, ty),
            )

        return body

    steps = (FX - 4) // RX
    a0, a1 = lax.fori_loop(0, steps, advance(wave0, wave1), (zero, zero))
    a2, a3 = lax.fori_loop(0, steps, advance(wave1, wave2), (zero, zero))
    sums = [jnp.sum(v, axis=0, keepdims=True) for v in (b0, a0, a1, a2, a3)]
    mom_ref[...] = jnp.concatenate(sums + [jnp.zeros((3, NT), F32)], axis=0)

    rows = TX // n_gy
    for place, ref in enumerate(waves_refs):
        to = lax.rem(place_y + place, n_gy) * rows + 5
        for which, wave in enumerate((wave0, wave1, wave2)):
            for row in range(rows):
                ref[which, row] = wave[to + row, H : H + ty, :].astype(BF16)


def last_kernel(ty, mom_ref, face, wave2, out_ref):
    shifts = plane_shifts(ty + 2 * H)

    def finish(step, total):
        k = step * RX + 5
        here, image = image_of(wave2, face, k, shifts)
        return owned(total, k, here * image, ty)

    total = lax.fori_loop(0, TX // RX, finish, jnp.zeros((ty, NT), F32))
    a4 = jnp.sum(total, axis=0, keepdims=True)
    sums = jnp.sum(jnp.where(iota((8, NT), 0) == 5, a4, mom_ref[...]), axis=1, keepdims=True)
    values = jnp.where(iota((8, NT), 0) == iota((8, NT), 1), sums, 0.0)
    values = jnp.sum(values, axis=0, keepdims=True)
    for device in range(out_ref.shape[0]):
        out_ref[device] = values


def combine_kernel(n_gy, ty, mom_ref, *refs):
    waves_refs, out_ref = refs[:n_gy], refs[n_gy]
    place_y = lax.axis_index("gy")
    moments = jnp.sum(mom_ref[...], axis=0)
    b0, a0, a1, a2, a3, a4 = [
        jnp.broadcast_to(moments[:, i : i + 1], (1, NT)) for i in range(6)
    ]
    a0, a1, a2, a3, a4 = [v / b0 for v in (a0, a1, a2, a3, a4)]
    l21 = a1 / a0
    l31 = a2 / a0
    d2 = jnp.maximum(a2 - l21 * a1, 1e-7 * a2 + 1e-30)
    l32 = (a3 - l21 * a2) / d2
    d3 = jnp.maximum(a4 - l31 * a2 - l32 * l32 * d2, 1e-7 * a4 + 1e-30)
    y2 = (1.0 - a0) - l21
    y3 = (1.0 - a0 - a1) - l31 - l32 * y2
    c3 = y3 / d3
    c2 = y2 / d2 - l32 * c3
    c1 = 1.0 / a0 - l21 * c2 - l31 * c3
    for place, ref in enumerate(waves_refs):
        source = lax.rem(place_y - place + n_gy, n_gy)
        at = pl.ds(pl.multiple_of(source * ty, 8), ty)
        for x in range(ref.shape[1]):
            w0, w1, w2 = [ref[which, x].astype(F32) for which in range(3)]
            out_ref[x, at, :] = c1 * w0 + c2 * w1 + c3 * w2


def vmem(count):
    return [pl.BlockSpec(memory_space=pltpu.VMEM)] * count


def on_device(amplitude, conv_first, conv_second, conv_third, conv_last):
    n_gx, n_gy = lax.axis_size("gx"), lax.axis_size("gy")
    ty = amplitude.shape[1]
    grid_x, grid_y = n_gx * TX, n_gy * ty
    assert amplitude.shape == (TX, ty, NT)

    def shift(values, axis, count, step):
        pairs = [(i, i + step) for i in range(count) if 0 <= i + step < count]
        return lax.ppermute(values, axis, pairs)

    first_x, last_x, first_y, last_y = pl.pallas_call(
        slices_kernel,
        out_shape=[jax.ShapeDtypeStruct((H, ty, NT), BF16)] * 2
        + [jax.ShapeDtypeStruct((TX, H, NT), BF16)] * 2,
        in_specs=vmem(1),
        out_specs=vmem(4),
        name="halo_slices",
    )(amplitude)
    xlow = shift(last_x, "gx", n_gx, 1)
    xhigh = shift(first_x, "gx", n_gx, -1)
    ylow = shift(
        jnp.concatenate([xlow[:, ty - H :], last_y, xhigh[:, ty - H :]]), "gy", n_gy, 1
    )
    yhigh = shift(jnp.concatenate([xlow[:, :H], first_y, xhigh[:, :H]]), "gy", n_gy, -1)

    weights = (conv_first, conv_second, conv_third, conv_last)
    (conv_first, conv_second, conv_third, conv_last), _ = lax.optimization_barrier((weights, xlow))

    def taps_first(weight):
        return jnp.transpose(weight, (2, 3, 4, 0, 1))

    w1, w2, w3, w4 = pl.pallas_call(
        prep_kernel,
        out_shape=[
            jax.ShapeDtypeStruct((16 * XW, (EDGE + 1) * BLK), BF16),
            jax.ShapeDtypeStruct((6 * BLK, BLK), BF16),
            jax.ShapeDtypeStruct((6 * BLK, BLK), BF16),
            jax.ShapeDtypeStruct((EDGE * BLK, 16 * XW), BF16),
        ],
        in_specs=vmem(2) + [pl.BlockSpec(memory_space=pl.ANY)],
        out_specs=vmem(4),
        compiler_params=pltpu.CompilerParams(vmem_limit_bytes=16 * 2**20),
        cost_estimate=pl.CostEstimate(flops=10**9, bytes_accessed=10**7, transcendentals=0),
        name="band_weights",
    )(
        jnp.concatenate([taps_first(conv_second), taps_first(conv_third)]).reshape(54 * CH, CH),
        jnp.concatenate(
            [jnp.transpose(conv_first, (1, 2, 3, 4, 0)), jnp.transpose(conv_last, (0, 2, 3, 4, 1))]
        ),
        xlow,
    )

    yw, nf = ty + 2 * H, FX + 2
    act1, raw = pl.pallas_call(
        functools.partial(first_kernel, grid_x, grid_y, ty),
        out_shape=[
            jax.ShapeDtypeStruct((3, yw // 2, EDGE + 1, PAIRS, BLK), BF16),
            jax.ShapeDtypeStruct(((XW + 2) * yw, NT), F32),
        ],
        in_specs=vmem(6),
        out_specs=vmem(2),
        scratch_shapes=[pltpu.VMEM((yw + 2, XW, NT), BF16)],
        compiler_params=pltpu.CompilerParams(vmem_limit_bytes=LIMIT * 2**20),
        cost_estimate=pl.CostEstimate(flops=10**10, bytes_accessed=10**7, transcendentals=0),
        name="layer_one",
    )(amplitude, xlow, xhigh, ylow, yhigh, w1)

    act2 = pl.pallas_call(
        functools.partial(second_kernel, grid_x, grid_y, ty),
        out_shape=jax.ShapeDtypeStruct((3, yw // 2, EDGE, PAIRS, BLK), BF16),
        in_specs=vmem(2),
        out_specs=pl.BlockSpec(memory_space=pltpu.VMEM),
        compiler_params=pltpu.CompilerParams(vmem_limit_bytes=LIMIT * 2**20),
        cost_estimate=pl.CostEstimate(flops=10**10, bytes_accessed=10**7, transcendentals=0),
        name="layer_two",
    )(act1, w2)

    act3, prod = pl.pallas_call(
        functools.partial(third_kernel, grid_x, grid_y, ty),
        out_shape=[
            jax.ShapeDtypeStruct((yw // 2, EDGE, PAIRS, BLK), BF16),
            jax.ShapeDtypeStruct((3, FX + 4, yw, NT), F32),
        ],
        in_specs=vmem(3),
        out_specs=vmem(2),
        compiler_params=pltpu.CompilerParams(vmem_limit_bytes=LIMIT * 2**20),
        cost_estimate=pl.CostEstimate(flops=10**10, bytes_accessed=10**7, transcendentals=0),
        name="layer_three",
    )(act2, raw, w3)

    fault, prob, slope = pl.pallas_call(
        functools.partial(fourth_kernel, ty),
        out_shape=[
            jax.ShapeDtypeStruct((TX, ty, NT), BF16),
            jax.ShapeDtypeStruct((FX * yw, NT), F32),
            jax.ShapeDtypeStruct((2, nf, yw, NT), F32),
        ],
        in_specs=vmem(3),
        out_specs=vmem(3),
        scratch_shapes=[pltpu.VMEM((yw // 2, NT, 128), F32)],
        compiler_params=pltpu.CompilerParams(vmem_limit_bytes=(LIMIT + 4) * 2**20),
        cost_estimate=pl.CostEstimate(
            flops=10**10, bytes_accessed=10**7, transcendentals=10**6
        ),
        name="layer_four",
    )(act3, prod, w4)

    rows = TX // n_gy
    moments, face, wave2, *waves = pl.pallas_call(
        functools.partial(waves_kernel, grid_x, grid_y, ty),
        out_shape=[
            jax.ShapeDtypeStruct((8, NT), F32),
            jax.ShapeDtypeStruct((2, nf, yw, NT), F32),
            jax.ShapeDtypeStruct((nf, yw, NT), F32),
        ]
        + [jax.ShapeDtypeStruct((3, rows, ty, NT), BF16)] * n_gy,
        in_specs=vmem(2),
        out_specs=vmem(3 + n_gy),
        scratch_shapes=[
            pltpu.VMEM((2, nf, yw, NT), F32),
            pltpu.VMEM((2, nf, yw, NT), F32),
            pltpu.VMEM((nf, yw, NT), F32),
            pltpu.VMEM((nf, yw, NT), F32),
            pltpu.VMEM((nf, yw, NT), F32),
        ],
        compiler_params=pltpu.CompilerParams(vmem_limit_bytes=24 * 2**20),
        cost_estimate=pl.CostEstimate(flops=10**8, bytes_accessed=10**7, transcendentals=0),
        name="solver_waves",
    )(prob, slope)

    arrived = [waves[0]]
    for place in range(1, n_gy):
        pairs = [(i, (i + place) % n_gy) for i in range(n_gy)]
        arrived.append(lax.ppermute(waves[place], "gy", pairs))

    everyone = pl.pallas_call(
        functools.partial(last_kernel, ty),
        out_shape=jax.ShapeDtypeStruct((n_gx * n_gy, 1, NT), F32),
        in_specs=vmem(3),
        out_specs=pl.BlockSpec(memory_space=pltpu.VMEM),
        compiler_params=pltpu.CompilerParams(vmem_limit_bytes=16 * 2**20),
        cost_estimate=pl.CostEstimate(flops=10**9, bytes_accessed=10**8, transcendentals=0),
        name="last_moment",
    )(moments, face, wave2)
    moments = lax.all_to_all(everyone, ("gx", "gy"), split_axis=0, concat_axis=0, tiled=True)
    shift_field = pl.pallas_call(
        functools.partial(combine_kernel, n_gy, ty),
        out_shape=jax.ShapeDtypeStruct((rows, grid_y, NT), F32),
        in_specs=vmem(1 + n_gy),
        out_specs=pl.BlockSpec(memory_space=pltpu.VMEM),
        compiler_params=pltpu.CompilerParams(vmem_limit_bytes=16 * 2**20),
        name="combine_waves",
    )(moments, *arrived)
    return (fault, shift_field)


def solution(mesh):
    return jax.shard_map(
        on_device,
        mesh=mesh,
        in_specs=(P("gx", "gy", None), P(), P(), P(), P()),
        out_specs=(P("gx", "gy", None), P(("gx", "gy"), None, None)),
        check_vma=False,
    )
```

```python
import functools

import jax
import jax.numpy as jnp
from jax import lax
from jax.experimental import pallas as pl
from jax.experimental.pallas import tpu as pltpu
from jax.sharding import PartitionSpec as P

MU_DIAG = 0.05
ETA_TIME = 0.5

TX, NT, H = 16, 128, 8
CH = 16
XW = TX + 2 * H
FX = TX + 8
RX = 4
FIRST, SECOND, THIRD = 8, 11, 11
Y_SLOTS = (1, 2, 3, 0)
LIMIT = 6
GROUP = 2
BLK = 256
EDGE = 7
SUB = 16
PAIRS = NT // 2

F32 = jnp.float32
BF16 = jnp.bfloat16


def iota(shape, dim):
    return lax.broadcasted_iota(jnp.int32, shape, dim)


def dot_nt(a, b):
    return lax.dot_general(a, b, (((1,), (1,)), ((), ())), preferred_element_type=F32)


def prep_kernel(inner_ref, outer_ref, after_ref, w1_ref, w2_ref, w3_ref, w4_ref):
    del after_ref
    spread = jnp.where(iota((CH, BLK), 1) % CH == iota((CH, BLK), 0), 1.0, 0.0).astype(BF16)
    unit = jnp.where(iota((BLK, BLK), 1) == iota((BLK, BLK), 0), 1.0, 0.0).astype(BF16)
    none = jnp.zeros((CH, BLK), BF16)
    cell = iota((CH, BLK), 1) // CH
    at_cell = [cell == at for at in range(16)]
    inputs = input_cells()
    tiled = jnp.dot(inner_ref[...], spread, preferred_element_type=F32).astype(BF16)
    for layer, ref in enumerate((w2_ref, w3_ref)):
        for tile in range(6):
            bands = []
            for yo in range(2):
                for to in range(2):
                    for xo in range(4):
                        band = none
                        for at, (y, t, x) in enumerate(inputs[tile]):
                            dx, dy, dt = x - xo + 1, y - yo + 1, t - to + 1
                            if min(dx, dy, dt) >= 0 and max(dx, dy, dt) <= 2:
                                tap = tiled[(layer * 27 + dx * 9 + dy * 3 + dt) * CH :][:CH]
                                band = jnp.where(at_cell[at], tap, band)
                        bands.append(band)
            turned = dot_nt(unit, jnp.concatenate(bands, axis=0))
            ref[tile * BLK : (tile + 1) * BLK, :] = turned.astype(BF16)

    def taps(which):
        found = {}
        for dx in range(3):
            for dy in range(3):
                tiled = jnp.dot(outer_ref[which, dx, dy], spread, preferred_element_type=F32)
                for dt in range(3):
                    found[dx, dy, dt] = tiled[dt : dt + 1]
        return found

    first, last = taps(0), taps(1)
    lane_yt = iota((1, BLK), 1) // 64
    quarter = [lane_yt == at for at in range(4)]

    def by_quarter(found, dx, at):
        value = jnp.zeros((1, BLK), F32)
        for y in range(2):
            for t in range(2):
                dy, dt = at(y, t)
                if 0 <= dy <= 2 and 0 <= dt <= 2:
                    value = jnp.where(quarter[y * 2 + t], found[dx, dy, dt], value)
        return value

    def rows_of(found, rows, at):
        return [
            jnp.broadcast_to(by_quarter(found, dx, at), (rows, BLK)).astype(BF16)
            for dx in range(3)
        ]

    row_x = iota((XW, BLK), 0)
    lane_x = iota((XW, BLK), 1) // CH % 4
    offset_x = [row_x - 1 - 4 * blk - lane_x for blk in range(EDGE)]
    offset_x.append(jnp.where(lane_x == 0, row_x - 29, jnp.where(lane_x == 3, row_x, -1)))
    masks = [[offset == dx for dx in range(3)] for offset in offset_x]
    none = jnp.zeros((XW, BLK), BF16)
    for j in range(4):
        for yi in range(4):
            row = (j * 4 + yi) * XW
            values = rows_of(first, XW, lambda y, t: (yi - y, j - t))
            for blk in range(EDGE + 1):
                band = none
                for dx in range(3):
                    band = jnp.where(masks[blk][dx], values[dx], band)
                w1_ref[row : row + XW, blk * BLK : (blk + 1) * BLK] = band
    masks = [
        [4 * blk + lane_x - 1 - row_x == dx for dx in range(3)] for blk in range(EDGE)
    ]
    bands = [[] for blk in range(EDGE)]
    for j in range(4):
        for yi in Y_SLOTS:
            values = rows_of(last, XW, lambda y, t: (y + 2 - yi, t + 2 - j))
            for blk in range(EDGE):
                band = none
                for dx in range(3):
                    band = jnp.where(masks[blk][dx], values[dx], band)
                bands[blk].append(band)
    for blk in range(EDGE):
        turned = dot_nt(unit, jnp.concatenate(bands[blk], axis=0))
        w4_ref[blk * BLK : (blk + 1) * BLK, :] = turned.astype(BF16)


def slices_kernel(amp_ref, first_x, last_x, first_y, last_y):
    ty = amp_ref.shape[1]
    first_x[...] = amp_ref[:H]
    last_x[...] = amp_ref[TX - H :]
    first_y[...] = amp_ref[:, :H]
    last_y[...] = amp_ref[:, ty - H :]


def input_cells():
    tiles = []
    here = [(t, x) for t in (0, 1) for x in range(4)]
    near = [(2, 2), (2, 3), (-1, 0), (-1, 1), (-1, 2), (-1, 3), (2, 0), (2, 1)]
    side = [(0, 4), (2, -1), (-1, 4), (0, -1), (1, 4), (-1, -1), (2, 4), (1, -1)]
    for cells in (here, near, side):
        for rows in ((0, 1), (-1, 2)):
            tiles.append([(y, t, x) for y in rows for t, x in cells])
    return tiles


def plane_shifts(yw):
    block = (RX, yw, NT)
    lane = iota(block, 2)
    first_lane = lane == 0
    last_lane = lane == NT - 1

    def up_y(v):
        return pltpu.roll(v, yw - 1, 1)

    def down_y(v):
        return pltpu.roll(v, 1, 1)

    def up_t(v, edge=0.0):
        return jnp.where(last_lane, edge, pltpu.roll(v, NT - 1, 2))

    def down_t(v, edge=0.0):
        return jnp.where(first_lane, edge, pltpu.roll(v, 1, 2))

    return block, up_y, down_y, up_t, down_t


def dot(a, b):
    return jnp.dot(a, b, preferred_element_type=F32)


def pair_of(row):
    return row // SUB + (row % SUB) * 4


def lane_masks(x0, grid_x, blocks):
    slot = iota((1, BLK), 1) // CH % 4
    masks = []
    for blk in range(blocks):
        if blk < EDGE:
            at = x0 - 6 + 4 * blk + slot
        else:
            at = x0 + jnp.where(slot == 0, 22, -7)
        masks.append(jnp.where((at >= 0) & (at < grid_x), 1.0, 0.0))
    return masks


def row_mask(y, grid_y):
    at = y + jnp.where(iota((1, BLK), 1) >= 128, 1, 0)
    return jnp.where((at >= 0) & (at < grid_y), 1.0, 0.0)


def lanes16():
    return iota((PAIRS, 128), 1).astype(jnp.int16)


def put(act, pair, blk, values):
    sub_row = iota((SUB, 128), 0)
    lane = lanes16()
    early = (lane >= 32) & (lane < 96)
    values = values.astype(BF16)
    act[0, pair, blk] = values
    for half in range(2):
        turned = pltpu.roll(values[:, half * 128 : (half + 1) * 128], 96, 1)
        head = pltpu.roll(turned[PAIRS - SUB :].astype(F32), 1, 0)
        head = jnp.where(sub_row == 0, 0.0, head).astype(BF16)
        tail = pltpu.roll(turned[:SUB].astype(F32), SUB - 1, 0)
        tail = jnp.where(sub_row == SUB - 1, 0.0, tail).astype(BF16)
        before = jnp.concatenate([head, turned[: PAIRS - SUB]], axis=0)
        after = jnp.concatenate([turned[SUB:], tail], axis=0)
        act[1, pair, blk, :, half * 128 : (half + 1) * 128] = jnp.where(early, before, after)


def put_sides(act, pair, blocks):
    lane = lanes16()
    slot0, slot3, even_slot = (lane & 48) == 0, (lane & 48) == 48, (lane & 16) == 0
    for blk in range(EDGE):
        left, right = (blk - 1) % blocks, (blk + 1) % blocks
        for half in range(2):
            at = slice(half * 128, (half + 1) * 128)
            even = jnp.where(slot0, act[0, pair, right, :, at], act[1, pair, right, :, at])
            odd = jnp.where(slot3, act[0, pair, left, :, at], act[1, pair, left, :, at])
            act[2, pair, blk, :, at] = jnp.where(even_slot, even, odd)


def layer(source, w_ref, pair, count):
    size = count * EDGE * PAIRS
    tiles = []
    for kind in range(3):
        centre = source[kind, pl.ds(pair + 1, count), :EDGE].reshape(size, BLK)
        before = source[kind, pl.ds(pair, count), :EDGE, :, 128:].reshape(size, 128)
        after = source[kind, pl.ds(pair + 2, count), :EDGE, :, :128].reshape(size, 128)
        tiles += [centre, before, after]
    return dot(jnp.concatenate(tiles, axis=1), w_ref[...])


def first_kernel(
    grid_x,
    grid_y,
    ty,
    amp_ref,
    xlow_ref,
    xhigh_ref,
    ylow_ref,
    yhigh_ref,
    w1_ref,
    act1,
    raw,
    amp,
):
    x0 = lax.axis_index("gx") * TX
    y0 = lax.axis_index("gy") * ty
    yw = ty + 2 * H

    for x in range(XW):
        row = x * yw
        if x < H:
            mid = xlow_ref[x]
        elif x < H + TX:
            mid = amp_ref[x - H]
        else:
            mid = xhigh_ref[x - H - TX]
        raw[row + H : row + H + ty, :] = mid.astype(F32)
        raw[row : row + H, :] = ylow_ref[x].astype(F32)
        raw[row + H + ty : row + yw, :] = yhigh_ref[x].astype(F32)

    def turn(y, carry):
        amp[y + 1] = raw[pl.ds(y, XW, stride=yw), :].astype(BF16)
        return carry

    lax.fori_loop(0, yw, turn, 0, unroll=8)
    amp[0] = jnp.zeros((XW, NT), BF16)
    amp[yw + 1] = jnp.zeros((XW, NT), BF16)

    at_row = iota((4 * PAIRS, NT), 0)
    to_pairs = jnp.where(
        iota((4 * PAIRS, NT), 1) == 2 * pair_of(at_row % PAIRS) - 1 + at_row // PAIRS, 1.0, 0.0
    ).astype(BF16)
    mask1 = lane_masks(x0, grid_x, EDGE + 1)

    def first(step, carry):
        pieces = []
        for i in range(0, FIRST, 2):
            y = (step * FIRST + i) * 2
            rows = [amp[pl.ds(y + 2 * k, 4)].reshape(4 * XW, NT) for k in range(2)]
            turned = dot_nt(to_pairs, jnp.concatenate(rows, axis=0)).astype(BF16)
            for k in range(2):
                parts = [turned[j * PAIRS : (j + 1) * PAIRS, k * 128 : (k + 1) * 128] for j in range(4)]
                pieces.append(jnp.concatenate(parts, axis=1))
        pieces = jnp.concatenate(pieces, axis=0)
        for begin in range(0, EDGE + 1, 2):
            result = dot(pieces, w1_ref[:, begin * BLK : (begin + 2) * BLK])
            for i in range(FIRST):
                pair = step * FIRST + i
                inside = row_mask(y0 + 2 * pair - H, grid_y)
                for blk in (begin, begin + 1):
                    lane = (blk - begin) * BLK
                    values = result[i * PAIRS : (i + 1) * PAIRS, lane : lane + BLK]
                    put(act1, pair, blk, jnp.maximum(values, 0.0) * (mask1[blk] * inside))
        for i in range(FIRST):
            put_sides(act1, step * FIRST + i, EDGE + 1)
        return carry

    lax.fori_loop(0, yw // 2 // FIRST, first, 0, unroll=True)


def second_kernel(grid_x, grid_y, ty, act1, w2_ref, act2):
    x0 = lax.axis_index("gx") * TX
    y0 = lax.axis_index("gy") * ty
    yw = ty + 2 * H
    pairs2 = ty // 2 + 6
    steps2 = pairs2 // SECOND
    mask2 = lane_masks(x0, grid_x, EDGE)

    def second(step, carry):
        for begin in range(0, SECOND, GROUP):
            count = min(GROUP, SECOND - begin)
            result = layer(act1, w2_ref, step * SECOND + begin, count)
            for i in range(count):
                pair = step * SECOND + begin + i
                inside = row_mask(y0 + 2 * pair - 6, grid_y)
                for blk in range(EDGE):
                    at = (i * EDGE + blk) * PAIRS
                    values = jnp.maximum(result[at : at + PAIRS], 0.0)
                    put(act2, pair + 1, blk, values * (mask2[blk] * inside))
                put_sides(act2, pair + 1, EDGE)
        return carry

    for edge in (0, pairs2 + 1):
        for kind in range(3):
            act2[kind, edge] = jnp.zeros((EDGE, PAIRS, BLK), BF16)
    lax.fori_loop(0, steps2, second, 0)


def third_kernel(grid_x, grid_y, ty, act2, raw, w3_ref, act3, prod):
    x0 = lax.axis_index("gx") * TX
    y0 = lax.axis_index("gy") * ty
    yw = ty + 2 * H
    pairs1, pairs2 = yw // 2, ty // 2 + 6
    block, up_y, down_y, up_t, down_t = plane_shifts(yw)

    def smooth_yt(v, edge=0.0):
        v = 0.5 * v + 0.25 * (up_t(v, edge) + down_t(v, edge))
        return 0.5 * v + 0.25 * (up_y(v) + down_y(v))

    def amp_rows(x):
        return raw[pl.ds(pl.multiple_of(x * yw, 8), RX * yw), :].reshape(block)

    def products(k):
        here = amp_rows(k + 3)
        grad_x = 0.5 * (amp_rows(k + 4) - amp_rows(k + 2))
        grad_y = 0.5 * (up_y(here) - down_y(here))
        grad_t = 0.5 * (up_t(here) - down_t(here))
        at = pl.ds(k, RX)
        prod[0, at] = smooth_yt(grad_x * grad_t)
        prod[1, at] = smooth_yt(grad_y * grad_t)
        energy = grad_t * grad_t + 0.25 * (grad_x * grad_x + grad_y * grad_y)
        prod[2, at] = smooth_yt(energy, 0.25 * here * here)

    steps3 = pairs2 // THIRD
    blocks3 = -(-(FX // RX + 1) // steps3)
    mask2 = lane_masks(x0, grid_x, EDGE)

    def third(step, carry):
        for i in range(blocks3):
            products(jnp.minimum((step * blocks3 + i) * RX, FX))
        for begin in range(0, THIRD, GROUP):
            count = min(GROUP, THIRD - begin)
            result = layer(act2, w3_ref, step * THIRD + begin, count)
            for i in range(count):
                pair = step * THIRD + begin + i
                inside = row_mask(y0 + 2 * pair - 6, grid_y)
                for blk in range(EDGE):
                    at = (i * EDGE + blk) * PAIRS
                    values = jnp.maximum(result[at : at + PAIRS], 0.0)
                    act3[pair, blk] = (values * (mask2[blk] * inside)).astype(BF16)
        return carry

    lax.fori_loop(0, steps3, third, 0)
    for pair in range(pairs2, pairs1):
        act3[pair] = jnp.zeros((EDGE, PAIRS, BLK), BF16)


def fourth_kernel(ty, act3, prod, w4_ref, fault_ref, prob, slope, part):
    yw = ty + 2 * H
    pairs1 = yw // 2
    at_lane = iota((NT, 8 * PAIRS), 1) % (4 * PAIRS)
    from_pairs = jnp.where(
        iota((NT, 8 * PAIRS), 0) == 2 * pair_of(at_lane % PAIRS) - 1 + at_lane // PAIRS, 1.0, 0.0
    ).astype(BF16)

    def slopes(k):
        at = pl.ds(k + 1, RX)
        sums = []
        for which in range(3):
            before, here, after = [prod[which, pl.ds(k + i, RX)] for i in range(3)]
            sums.append(0.5 * here + 0.25 * (before + after))
        scale = -1.0 / (sums[2] + 0.05)
        slope[0, at] = sums[0] * scale
        slope[1, at] = sums[1] * scale

    def fourth(step, carry):
        for i in range(2):
            slopes(jnp.minimum((step * 2 + i) * RX, FX - RX))
        pair = step * 8
        cells = [act3[pl.ds(pair, 8), blk].reshape(8 * PAIRS, BLK) for blk in range(EDGE)]
        result = dot(jnp.concatenate(cells, axis=1), w4_ref[...])
        for i in range(0, 8, 2):
            sides = []
            for at in (i, i + 1):
                rows = result[at * PAIRS : (at + 1) * PAIRS]
                sides.append(
                    jnp.concatenate([rows[:, j * 128 : (j + 1) * 128] for j in range(4)], axis=0)
                )
            both = jnp.concatenate(sides, axis=1)
            high = both.astype(BF16)
            low = (both - high.astype(F32)).astype(BF16)
            share = dot(from_pairs, jnp.concatenate([high, low], axis=0))
            part[pair + i] = share[:, :128]
            part[pair + i + 1] = share[:, 128:]
        return carry

    lax.fori_loop(0, pairs1 // 8, fourth, 0, unroll=True)

    for x in range(FX):
        prob[x * yw : x * yw + H, :] = jnp.zeros((H, NT), F32)
        prob[(x + 1) * yw - H : (x + 1) * yw, :] = jnp.zeros((H, NT), F32)
    lane = iota((NT, 128), 1)

    def order(step, carry):
        pair = 2 * step + 1
        here = part[pair]
        before = pltpu.roll(part[pair - 1], 64, 1)
        after = pltpu.roll(part[pair + 1], 64, 1)
        own = jnp.where(lane < 64, here, after)
        other = jnp.where(
            lane < 32,
            before,
            jnp.where(lane < 64, after, jnp.where(lane < 96, here, part[pair + 2])),
        )
        values = 1.0 / (1.0 + jnp.exp(-(own + other)))
        values = values.astype(BF16).astype(F32).T
        for row in range(4):
            at = pl.ds(2 * pair + 2 + row, FX, stride=yw)
            prob[at, :] = values[row * XW : row * XW + FX]
        return carry

    lax.fori_loop(0, (ty + 8) // 4, order, 0, unroll=5)

    for which in range(2):
        slope[which, FX + 1] = jnp.zeros((yw, NT), F32)
    for x in range(TX):
        fault_ref[x] = prob[(x + 4) * yw + H : (x + 4) * yw + H + ty, :].astype(BF16)


def owned(total, k, values, ty):
    for row in range(RX):
        ok = (k + row >= 5) & (k + row < 5 + TX)
        total = total + jnp.where(ok, values[row, H : H + ty], 0.0)
    return total


def image_of(wave, face, k, shifts):
    block, up_y, down_y, up_t, down_t = shifts
    at, before, after = [pl.ds(k + i, RX) for i in (0, -1, 1)]
    here = wave[at]
    flow = face[1, at] * (here - up_y(here))
    image = time_part(block) * here - ETA_TIME * (up_t(here) + down_t(here))
    image = image + flow - down_y(flow)
    image = image + face[0, at] * (here - wave[after])
    return here, image + face[0, before] * (here - wave[before])


def time_part(block):
    lane = iota(block, 2)
    count = jnp.where(lane == 0, 0.0, 1.0) + jnp.where(lane == NT - 1, 0.0, 1.0)
    return MU_DIAG + ETA_TIME * count


def waves_kernel(grid_x, grid_y, ty, prob, slope, mom_ref, face, wave2, *refs):
    n_gy = grid_y // ty
    waves_refs = refs[:n_gy]
    weight, flux, inv, wave0, wave1 = refs[n_gy:]
    place_y = lax.axis_index("gy")
    x0 = lax.axis_index("gx") * TX
    y0 = place_y * ty
    yw = ty + 2 * H
    shifts = plane_shifts(yw)
    block, up_y, down_y, up_t, down_t = shifts
    at_y = y0 - H + iota(block, 1)
    mask_y = (at_y >= 0) & (at_y < grid_y)

    def weights(step, carry):
        k = step * RX
        at = pl.ds(k + 1, RX)
        rows = prob[pl.ds(pl.multiple_of(k * yw, 8), RX * yw), :].reshape(block)
        raw_weight = 1.0 - 0.9 * rows
        at_x = x0 - 4 + k + iota(block, 0)
        weight[0, at] = raw_weight
        weight[1, at] = jnp.where(mask_y & (at_x >= 0) & (at_x < grid_x), raw_weight, 0.0)
        return carry

    lax.fori_loop(0, FX // RX, weights, 0)
    for which in range(2):
        weight[which, FX + 1] = jnp.full((yw, NT), 1.0 - which, F32)
        face[which, 0] = jnp.zeros((yw, NT), F32)
        flux[which, 0] = jnp.zeros((yw, NT), F32)

    def faces(step, carry):
        k = step * RX + 1
        at, after = pl.ds(k, RX), pl.ds(k + 1, RX)
        raw_weight = weight[0, at]
        masked = weight[1, at]
        face_x = 2.0 * masked * weight[1, after] / (raw_weight + weight[0, after])
        face_y = 2.0 * masked * up_y(masked) / (raw_weight + up_y(raw_weight))
        slope_y = slope[1, at]
        face[0, at] = face_x
        face[1, at] = face_y
        flux[0, at] = 0.5 * face_x * (slope[0, at] + slope[0, after])
        flux[1, at] = 0.5 * face_y * (slope_y + up_y(slope_y))
        return carry

    lax.fori_loop(0, FX // RX, faces, 0)

    def start(step, total):
        k = step * RX + 1
        at, before = pl.ds(k, RX), pl.ds(k - 1, RX)
        flux_y = flux[1, at]
        face_y = face[1, at]
        right = flux[0, before] - flux[0, at] + down_y(flux_y) - flux_y
        inverse = 1.0 / (time_part(block) + face[0, at] + face[0, before] + face_y + down_y(face_y))
        first_wave = right * inverse
        inv[at] = inverse
        wave0[at] = first_wave
        return owned(total, k, right * first_wave, ty)

    zero = jnp.zeros((ty, NT), F32)
    b0 = lax.fori_loop(0, FX // RX, start, zero)

    def advance(source, target):
        def body(step, totals):
            k = step * RX + 3
            here, image = image_of(source, face, k, shifts)
            at = pl.ds(k, RX)
            after = here - image * inv[at]
            target[at] = after
            return (
                owned(totals[0], k, here * image, ty),
                owned(totals[1], k, after * image, ty),
            )

        return body

    steps = (FX - 4) // RX
    a0, a1 = lax.fori_loop(0, steps, advance(wave0, wave1), (zero, zero))
    a2, a3 = lax.fori_loop(0, steps, advance(wave1, wave2), (zero, zero))
    sums = [jnp.sum(v, axis=0, keepdims=True) for v in (b0, a0, a1, a2, a3)]
    mom_ref[...] = jnp.concatenate(sums + [jnp.zeros((3, NT), F32)], axis=0)

    rows = TX // n_gy
    for place, ref in enumerate(waves_refs):
        to = lax.rem(place_y + place, n_gy) * rows + 5
        for which, wave in enumerate((wave0, wave1, wave2)):
            for row in range(rows):
                ref[which, row] = wave[to + row, H : H + ty, :].astype(BF16)


def last_kernel(ty, mom_ref, face, wave2, out_ref):
    shifts = plane_shifts(ty + 2 * H)

    def finish(step, total):
        k = step * RX + 5
        here, image = image_of(wave2, face, k, shifts)
        return owned(total, k, here * image, ty)

    total = lax.fori_loop(0, TX // RX, finish, jnp.zeros((ty, NT), F32))
    a4 = jnp.sum(total, axis=0, keepdims=True)
    sums = jnp.sum(jnp.where(iota((8, NT), 0) == 5, a4, mom_ref[...]), axis=1, keepdims=True)
    values = jnp.where(iota((8, NT), 0) == iota((8, NT), 1), sums, 0.0)
    values = jnp.sum(values, axis=0, keepdims=True)
    for device in range(out_ref.shape[0]):
        out_ref[device] = values


def sum_kernel(mom_ref, out_ref):
    total = jnp.sum(mom_ref[...], axis=0)
    for device in range(out_ref.shape[0]):
        out_ref[device] = total


def combine_kernel(n_gy, ty, mom_ref, *refs):
    waves_refs, out_ref = refs[:n_gy], refs[n_gy]
    place_y = lax.axis_index("gy")
    moments = jnp.sum(mom_ref[...], axis=0)
    b0, a0, a1, a2, a3, a4 = [
        jnp.broadcast_to(moments[:, i : i + 1], (1, NT)) for i in range(6)
    ]
    a0, a1, a2, a3, a4 = [v / b0 for v in (a0, a1, a2, a3, a4)]
    l21 = a1 / a0
    l31 = a2 / a0
    d2 = jnp.maximum(a2 - l21 * a1, 1e-7 * a2 + 1e-30)
    l32 = (a3 - l21 * a2) / d2
    d3 = jnp.maximum(a4 - l31 * a2 - l32 * l32 * d2, 1e-7 * a4 + 1e-30)
    y2 = (1.0 - a0) - l21
    y3 = (1.0 - a0 - a1) - l31 - l32 * y2
    c3 = y3 / d3
    c2 = y2 / d2 - l32 * c3
    c1 = 1.0 / a0 - l21 * c2 - l31 * c3
    for place, ref in enumerate(waves_refs):
        source = lax.rem(place_y - place + n_gy, n_gy)
        at = pl.ds(pl.multiple_of(source * ty, 8), ty)
        for x in range(ref.shape[1]):
            w0, w1, w2 = [ref[which, x].astype(F32) for which in range(3)]
            out_ref[x, at, :] = c1 * w0 + c2 * w1 + c3 * w2


def vmem(count):
    return [pl.BlockSpec(memory_space=pltpu.VMEM)] * count


def on_device(amplitude, conv_first, conv_second, conv_third, conv_last):
    n_gx, n_gy = lax.axis_size("gx"), lax.axis_size("gy")
    ty = amplitude.shape[1]
    grid_x, grid_y = n_gx * TX, n_gy * ty
    assert amplitude.shape == (TX, ty, NT)

    def shift(values, axis, count, step):
        pairs = [(i, i + step) for i in range(count) if 0 <= i + step < count]
        return lax.ppermute(values, axis, pairs)

    first_x, last_x, first_y, last_y = pl.pallas_call(
        slices_kernel,
        out_shape=[jax.ShapeDtypeStruct((H, ty, NT), BF16)] * 2
        + [jax.ShapeDtypeStruct((TX, H, NT), BF16)] * 2,
        in_specs=vmem(1),
        out_specs=vmem(4),
        compiler_params=pltpu.CompilerParams(vmem_limit_bytes=4 * 2**20),
        name="halo_slices",
    )(amplitude)
    xlow = shift(last_x, "gx", n_gx, 1)
    xhigh = shift(first_x, "gx", n_gx, -1)
    ylow = shift(
        jnp.concatenate([xlow[:, ty - H :], last_y, xhigh[:, ty - H :]]), "gy", n_gy, 1
    )
    yhigh = shift(jnp.concatenate([xlow[:, :H], first_y, xhigh[:, :H]]), "gy", n_gy, -1)

    weights = (conv_first, conv_second, conv_third, conv_last)
    (conv_first, conv_second, conv_third, conv_last), _ = lax.optimization_barrier((weights, xlow))

    def taps_first(weight):
        return jnp.transpose(weight, (2, 3, 4, 0, 1))

    w1, w2, w3, w4 = pl.pallas_call(
        prep_kernel,
        out_shape=[
            jax.ShapeDtypeStruct((16 * XW, (EDGE + 1) * BLK), BF16),
            jax.ShapeDtypeStruct((6 * BLK, BLK), BF16),
            jax.ShapeDtypeStruct((6 * BLK, BLK), BF16),
            jax.ShapeDtypeStruct((EDGE * BLK, 16 * XW), BF16),
        ],
        in_specs=vmem(2) + [pl.BlockSpec(memory_space=pl.ANY)],
        out_specs=vmem(4),
        compiler_params=pltpu.CompilerParams(vmem_limit_bytes=16 * 2**20),
        cost_estimate=pl.CostEstimate(flops=10**9, bytes_accessed=10**7, transcendentals=0),
        name="band_weights",
    )(
        jnp.concatenate([taps_first(conv_second), taps_first(conv_third)]).reshape(54 * CH, CH),
        jnp.concatenate(
            [jnp.transpose(conv_first, (1, 2, 3, 4, 0)), jnp.transpose(conv_last, (0, 2, 3, 4, 1))]
        ),
        xlow,
    )

    yw, nf = ty + 2 * H, FX + 2
    act1, raw = pl.pallas_call(
        functools.partial(first_kernel, grid_x, grid_y, ty),
        out_shape=[
            jax.ShapeDtypeStruct((3, yw // 2, EDGE + 1, PAIRS, BLK), BF16),
            jax.ShapeDtypeStruct(((XW + 2) * yw, NT), F32),
        ],
        in_specs=vmem(6),
        out_specs=vmem(2),
        scratch_shapes=[pltpu.VMEM((yw + 2, XW, NT), BF16)],
        compiler_params=pltpu.CompilerParams(vmem_limit_bytes=LIMIT * 2**20),
        cost_estimate=pl.CostEstimate(flops=10**10, bytes_accessed=10**7, transcendentals=0),
        name="layer_one",
    )(amplitude, xlow, xhigh, ylow, yhigh, w1)

    act2 = pl.pallas_call(
        functools.partial(second_kernel, grid_x, grid_y, ty),
        out_shape=jax.ShapeDtypeStruct((3, yw // 2, EDGE, PAIRS, BLK), BF16),
        in_specs=vmem(2),
        out_specs=pl.BlockSpec(memory_space=pltpu.VMEM),
        compiler_params=pltpu.CompilerParams(vmem_limit_bytes=LIMIT * 2**20),
        cost_estimate=pl.CostEstimate(flops=10**10, bytes_accessed=10**7, transcendentals=0),
        name="layer_two",
    )(act1, w2)

    act3, prod = pl.pallas_call(
        functools.partial(third_kernel, grid_x, grid_y, ty),
        out_shape=[
            jax.ShapeDtypeStruct((yw // 2, EDGE, PAIRS, BLK), BF16),
            jax.ShapeDtypeStruct((3, FX + 4, yw, NT), F32),
        ],
        in_specs=vmem(3),
        out_specs=vmem(2),
        compiler_params=pltpu.CompilerParams(vmem_limit_bytes=LIMIT * 2**20),
        cost_estimate=pl.CostEstimate(flops=10**10, bytes_accessed=10**7, transcendentals=0),
        name="layer_three",
    )(act2, raw, w3)

    fault, prob, slope = pl.pallas_call(
        functools.partial(fourth_kernel, ty),
        out_shape=[
            jax.ShapeDtypeStruct((TX, ty, NT), BF16),
            jax.ShapeDtypeStruct((FX * yw, NT), F32),
            jax.ShapeDtypeStruct((2, nf, yw, NT), F32),
        ],
        in_specs=vmem(3),
        out_specs=vmem(3),
        scratch_shapes=[pltpu.VMEM((yw // 2, NT, 128), F32)],
        compiler_params=pltpu.CompilerParams(vmem_limit_bytes=(LIMIT + 4) * 2**20),
        cost_estimate=pl.CostEstimate(
            flops=10**10, bytes_accessed=10**7, transcendentals=10**6
        ),
        name="layer_four",
    )(act3, prod, w4)

    rows = TX // n_gy
    moments, face, wave2, *waves = pl.pallas_call(
        functools.partial(waves_kernel, grid_x, grid_y, ty),
        out_shape=[
            jax.ShapeDtypeStruct((8, NT), F32),
            jax.ShapeDtypeStruct((2, nf, yw, NT), F32),
            jax.ShapeDtypeStruct((nf, yw, NT), F32),
        ]
        + [jax.ShapeDtypeStruct((3, rows, ty, NT), BF16)] * n_gy,
        in_specs=vmem(2),
        out_specs=vmem(3 + n_gy),
        scratch_shapes=[
            pltpu.VMEM((2, nf, yw, NT), F32),
            pltpu.VMEM((2, nf, yw, NT), F32),
            pltpu.VMEM((nf, yw, NT), F32),
            pltpu.VMEM((nf, yw, NT), F32),
            pltpu.VMEM((nf, yw, NT), F32),
        ],
        compiler_params=pltpu.CompilerParams(vmem_limit_bytes=24 * 2**20),
        cost_estimate=pl.CostEstimate(flops=10**8, bytes_accessed=10**7, transcendentals=0),
        name="solver_waves",
    )(prob, slope)

    arrived = [waves[0]]
    for place in range(1, n_gy):
        pairs = [(i, (i + place) % n_gy) for i in range(n_gy)]
        arrived.append(lax.ppermute(waves[place], "gy", pairs))

    everyone = pl.pallas_call(
        functools.partial(last_kernel, ty),
        out_shape=jax.ShapeDtypeStruct((n_gx, 1, NT), F32),
        in_specs=vmem(3),
        out_specs=pl.BlockSpec(memory_space=pltpu.VMEM),
        compiler_params=pltpu.CompilerParams(vmem_limit_bytes=16 * 2**20),
        cost_estimate=pl.CostEstimate(flops=10**9, bytes_accessed=10**8, transcendentals=0),
        name="last_moment",
    )(moments, face, wave2)
    moments = lax.all_to_all(everyone, "gx", split_axis=0, concat_axis=0, tiled=True)
    moments = pl.pallas_call(
        sum_kernel,
        out_shape=jax.ShapeDtypeStruct((n_gy, 1, NT), F32),
        in_specs=vmem(1),
        out_specs=pl.BlockSpec(memory_space=pltpu.VMEM),
        compiler_params=pltpu.CompilerParams(vmem_limit_bytes=4 * 2**20),
        name="sum_moments",
    )(moments)
    moments = lax.all_to_all(moments, "gy", split_axis=0, concat_axis=0, tiled=True)
    shift_field = pl.pallas_call(
        functools.partial(combine_kernel, n_gy, ty),
        out_shape=jax.ShapeDtypeStruct((rows, grid_y, NT), F32),
        in_specs=vmem(1 + n_gy),
        out_specs=pl.BlockSpec(memory_space=pltpu.VMEM),
        compiler_params=pltpu.CompilerParams(vmem_limit_bytes=16 * 2**20),
        name="combine_waves",
    )(moments, *arrived)
    return (fault, shift_field)


def solution(mesh):
    return jax.shard_map(
        on_device,
        mesh=mesh,
        in_specs=(P("gx", "gy", None), P(), P(), P(), P()),
        out_specs=(P("gx", "gy", None), P(("gx", "gy"), None, None)),
        check_vma=False,
    )
```

```python
import functools

import jax
import jax.numpy as jnp
from jax import lax
from jax.experimental import pallas as pl
from jax.experimental.pallas import tpu as pltpu
from jax.sharding import PartitionSpec as P

MU_DIAG = 0.05
ETA_TIME = 0.5

TX, NT, H = 16, 128, 8
CH = 16
XW = TX + 2 * H
FX = TX + 8
RX = 4
FIRST = 4
RING = 12
Y_SLOTS = (1, 2, 3, 0)
LIMIT = 6
GROUP = 2
BLK = 256
EDGE = 7
SUB = 16
PAIRS = NT // 2

F32 = jnp.float32
BF16 = jnp.bfloat16


def iota(shape, dim):
    return lax.broadcasted_iota(jnp.int32, shape, dim)


def dot_nt(a, b):
    return lax.dot_general(a, b, (((1,), (1,)), ((), ())), preferred_element_type=F32)


def prep_kernel(inner_ref, outer_ref, after_ref, w1_ref, w2_ref, w3_ref, w4_ref):
    del after_ref
    spread = jnp.where(iota((CH, BLK), 1) % CH == iota((CH, BLK), 0), 1.0, 0.0).astype(BF16)
    unit = jnp.where(iota((BLK, BLK), 1) == iota((BLK, BLK), 0), 1.0, 0.0).astype(BF16)
    none = jnp.zeros((CH, BLK), BF16)
    cell = iota((CH, BLK), 1) // CH
    at_cell = [cell == at for at in range(16)]
    inputs = input_cells()
    tiled = jnp.dot(inner_ref[...], spread, preferred_element_type=F32).astype(BF16)
    for layer, ref in enumerate((w2_ref, w3_ref)):
        for tile in range(6):
            bands = []
            for yo in range(2):
                for to in range(2):
                    for xo in range(4):
                        band = none
                        for at, (y, t, x) in enumerate(inputs[tile]):
                            dx, dy, dt = x - xo + 1, y - yo + 1, t - to + 1
                            if min(dx, dy, dt) >= 0 and max(dx, dy, dt) <= 2:
                                tap = tiled[(layer * 27 + dx * 9 + dy * 3 + dt) * CH :][:CH]
                                band = jnp.where(at_cell[at], tap, band)
                        bands.append(band)
            turned = dot_nt(unit, jnp.concatenate(bands, axis=0))
            ref[tile * BLK : (tile + 1) * BLK, :] = turned.astype(BF16)

    def taps(which):
        found = {}
        for dx in range(3):
            for dy in range(3):
                tiled = jnp.dot(outer_ref[which, dx, dy], spread, preferred_element_type=F32)
                for dt in range(3):
                    found[dx, dy, dt] = tiled[dt : dt + 1]
        return found

    first, last = taps(0), taps(1)
    lane_yt = iota((1, BLK), 1) // 64
    quarter = [lane_yt == at for at in range(4)]

    def by_quarter(found, dx, at):
        value = jnp.zeros((1, BLK), F32)
        for y in range(2):
            for t in range(2):
                dy, dt = at(y, t)
                if 0 <= dy <= 2 and 0 <= dt <= 2:
                    value = jnp.where(quarter[y * 2 + t], found[dx, dy, dt], value)
        return value

    def rows_of(found, rows, at):
        return [
            jnp.broadcast_to(by_quarter(found, dx, at), (rows, BLK)).astype(BF16)
            for dx in range(3)
        ]

    row_x = iota((XW, BLK), 0)
    lane_x = iota((XW, BLK), 1) // CH % 4
    offset_x = [row_x - 1 - 4 * blk - lane_x for blk in range(EDGE)]
    offset_x.append(jnp.where(lane_x == 0, row_x - 29, jnp.where(lane_x == 3, row_x, -1)))
    masks = [[offset == dx for dx in range(3)] for offset in offset_x]
    none = jnp.zeros((XW, BLK), BF16)
    for j in range(4):
        for yi in range(4):
            row = (j * 4 + yi) * XW
            values = rows_of(first, XW, lambda y, t: (yi - y, j - t))
            for blk in range(EDGE + 1):
                band = none
                for dx in range(3):
                    band = jnp.where(masks[blk][dx], values[dx], band)
                w1_ref[row : row + XW, blk * BLK : (blk + 1) * BLK] = band
    masks = [
        [4 * blk + lane_x - 1 - row_x == dx for dx in range(3)] for blk in range(EDGE)
    ]
    bands = [[] for blk in range(EDGE)]
    for j in range(4):
        for yi in Y_SLOTS:
            values = rows_of(last, XW, lambda y, t: (y + 2 - yi, t + 2 - j))
            for blk in range(EDGE):
                band = none
                for dx in range(3):
                    band = jnp.where(masks[blk][dx], values[dx], band)
                bands[blk].append(band)
    for blk in range(EDGE):
        turned = dot_nt(unit, jnp.concatenate(bands[blk], axis=0))
        w4_ref[blk * BLK : (blk + 1) * BLK, :] = turned.astype(BF16)


def slices_kernel(amp_ref, first_x, last_x, first_y, last_y):
    ty = amp_ref.shape[1]
    first_x[...] = amp_ref[:H]
    last_x[...] = amp_ref[TX - H :]
    first_y[...] = amp_ref[:, :H]
    last_y[...] = amp_ref[:, ty - H :]


def input_cells():
    tiles = []
    here = [(t, x) for t in (0, 1) for x in range(4)]
    near = [(2, 2), (2, 3), (-1, 0), (-1, 1), (-1, 2), (-1, 3), (2, 0), (2, 1)]
    side = [(0, 4), (2, -1), (-1, 4), (0, -1), (1, 4), (-1, -1), (2, 4), (1, -1)]
    for cells in (here, near, side):
        for rows in ((0, 1), (-1, 2)):
            tiles.append([(y, t, x) for y in rows for t, x in cells])
    return tiles


def plane_shifts(yw):
    block = (RX, yw, NT)
    lane = iota(block, 2)
    first_lane = lane == 0
    last_lane = lane == NT - 1

    def up_y(v):
        return pltpu.roll(v, yw - 1, 1)

    def down_y(v):
        return pltpu.roll(v, 1, 1)

    def up_t(v, edge=0.0):
        return jnp.where(last_lane, edge, pltpu.roll(v, NT - 1, 2))

    def down_t(v, edge=0.0):
        return jnp.where(first_lane, edge, pltpu.roll(v, 1, 2))

    return block, up_y, down_y, up_t, down_t


def dot(a, b):
    return jnp.dot(a, b, preferred_element_type=F32)


def pair_of(row):
    return row // SUB + (row % SUB) * 4


def lane_masks(x0, grid_x, blocks):
    slot = iota((1, BLK), 1) // CH % 4
    masks = []
    for blk in range(blocks):
        if blk < EDGE:
            at = x0 - 6 + 4 * blk + slot
        else:
            at = x0 + jnp.where(slot == 0, 22, -7)
        masks.append(jnp.where((at >= 0) & (at < grid_x), 1.0, 0.0))
    return masks


def row_mask(y, grid_y):
    at = y + jnp.where(iota((1, BLK), 1) >= 128, 1, 0)
    return jnp.where((at >= 0) & (at < grid_y), 1.0, 0.0)


def lanes16():
    return iota((PAIRS, 128), 1).astype(jnp.int16)


def put(act, pair, blk, values):
    sub_row = iota((SUB, 128), 0)
    lane = lanes16()
    early = (lane >= 32) & (lane < 96)
    values = values.astype(BF16)
    act[0, pair, blk] = values
    for half in range(2):
        turned = pltpu.roll(values[:, half * 128 : (half + 1) * 128], 96, 1)
        head = pltpu.roll(turned[PAIRS - SUB :].astype(F32), 1, 0)
        head = jnp.where(sub_row == 0, 0.0, head).astype(BF16)
        tail = pltpu.roll(turned[:SUB].astype(F32), SUB - 1, 0)
        tail = jnp.where(sub_row == SUB - 1, 0.0, tail).astype(BF16)
        before = jnp.concatenate([head, turned[: PAIRS - SUB]], axis=0)
        after = jnp.concatenate([turned[SUB:], tail], axis=0)
        act[1, pair, blk, :, half * 128 : (half + 1) * 128] = jnp.where(early, before, after)


def put_sides(act, pair, blocks):
    lane = lanes16()
    slot0, slot3, even_slot = (lane & 48) == 0, (lane & 48) == 48, (lane & 16) == 0
    for blk in range(EDGE):
        left, right = (blk - 1) % blocks, (blk + 1) % blocks
        for half in range(2):
            at = slice(half * 128, (half + 1) * 128)
            even = jnp.where(slot0, act[0, pair, right, :, at], act[1, pair, right, :, at])
            odd = jnp.where(slot3, act[0, pair, left, :, at], act[1, pair, left, :, at])
            act[2, pair, blk, :, at] = jnp.where(even_slot, even, odd)


def layer(source, w_ref, pair, count):
    def rows(kind, offset, at):
        found = []
        for i in range(count):
            place = (pair + offset + i) % RING
            found.append(source[kind, place, :EDGE, :, at].reshape(EDGE * PAIRS, -1))
        return jnp.concatenate(found, axis=0)

    tiles = []
    for kind in range(3):
        tiles.append(rows(kind, 1, slice(0, BLK)))
        tiles.append(rows(kind, 0, slice(128, BLK)))
        tiles.append(rows(kind, 2, slice(0, 128)))
    return dot(jnp.concatenate(tiles, axis=1), w_ref[...])


def net_kernel(
    grid_x,
    grid_y,
    ty,
    amp_ref,
    xlow_ref,
    xhigh_ref,
    ylow_ref,
    yhigh_ref,
    w1_ref,
    w2_ref,
    w3_ref,
    act3,
    prod,
    raw,
    amp,
    act1,
    act2,
):
    x0 = lax.axis_index("gx") * TX
    y0 = lax.axis_index("gy") * ty
    yw = ty + 2 * H
    pairs1, pairs2 = yw // 2, ty // 2 + 6
    for x in range(XW):
        row = x * yw
        if x < H:
            mid = xlow_ref[x]
        elif x < H + TX:
            mid = amp_ref[x - H]
        else:
            mid = xhigh_ref[x - H - TX]
        raw[row + H : row + H + ty, :] = mid.astype(F32)
        raw[row : row + H, :] = ylow_ref[x].astype(F32)
        raw[row + H + ty : row + yw, :] = yhigh_ref[x].astype(F32)

    def turn(y, carry):
        amp[y + 1] = raw[pl.ds(y, XW, stride=yw), :].astype(BF16)
        return carry

    lax.fori_loop(0, yw, turn, 0, unroll=8)
    amp[0] = jnp.zeros((XW, NT), BF16)
    amp[yw + 1] = jnp.zeros((XW, NT), BF16)

    at_row = iota((4 * PAIRS, NT), 0)
    to_pairs = jnp.where(
        iota((4 * PAIRS, NT), 1) == 2 * pair_of(at_row % PAIRS) - 1 + at_row // PAIRS, 1.0, 0.0
    ).astype(BF16)
    mask = lane_masks(x0, grid_x, EDGE + 1)

    def first(step):
        pieces = []
        for i in range(0, FIRST, 2):
            y = (step * FIRST + i) * 2
            rows = [amp[pl.ds(y + 2 * k, 4)].reshape(4 * XW, NT) for k in range(2)]
            turned = dot_nt(to_pairs, jnp.concatenate(rows, axis=0)).astype(BF16)
            for k in range(2):
                parts = [turned[j * PAIRS : (j + 1) * PAIRS, k * 128 : (k + 1) * 128] for j in range(4)]
                pieces.append(jnp.concatenate(parts, axis=1))
        pieces = jnp.concatenate(pieces, axis=0)
        for begin in range(0, EDGE + 1, 2):
            result = dot(pieces, w1_ref[:, begin * BLK : (begin + 2) * BLK])
            for i in range(FIRST):
                pair = step * FIRST + i
                inside = row_mask(y0 + 2 * pair - H, grid_y)
                for blk in (begin, begin + 1):
                    lane = (blk - begin) * BLK
                    values = result[i * PAIRS : (i + 1) * PAIRS, lane : lane + BLK]
                    put(act1, pair % RING, blk, jnp.maximum(values, 0.0) * (mask[blk] * inside))
        for i in range(FIRST):
            put_sides(act1, (step * FIRST + i) % RING, EDGE + 1)

    def second(begin, end):
        count = end - begin
        result = layer(act1, w2_ref, begin, count)
        for i in range(count):
            pair = begin + i
            inside = row_mask(y0 + 2 * pair - 6, grid_y)
            for blk in range(EDGE):
                at = (i * EDGE + blk) * PAIRS
                values = jnp.maximum(result[at : at + PAIRS], 0.0)
                put(act2, (pair + 1) % RING, blk, values * (mask[blk] * inside))
            put_sides(act2, (pair + 1) % RING, EDGE)

    def third(begin, end):
        count = end - begin
        result = layer(act2, w3_ref, begin, count)
        for i in range(count):
            pair = begin + i
            inside = row_mask(y0 + 2 * pair - 6, grid_y)
            for blk in range(EDGE):
                at = (i * EDGE + blk) * PAIRS
                values = jnp.maximum(result[at : at + PAIRS], 0.0)
                act3[pair, blk] = (values * (mask[blk] * inside)).astype(BF16)

    block, up_y, down_y, up_t, down_t = plane_shifts(yw)

    def smooth_yt(v, edge=0.0):
        v = 0.5 * v + 0.25 * (up_t(v, edge) + down_t(v, edge))
        return 0.5 * v + 0.25 * (up_y(v) + down_y(v))

    def amp_rows(x):
        return raw[pl.ds(pl.multiple_of(x * yw, 8), RX * yw), :].reshape(block)

    def products(k):
        here = amp_rows(k + 3)
        grad_x = 0.5 * (amp_rows(k + 4) - amp_rows(k + 2))
        grad_y = 0.5 * (up_y(here) - down_y(here))
        grad_t = 0.5 * (up_t(here) - down_t(here))
        at = pl.ds(k, RX)
        prod[0, at] = smooth_yt(grad_x * grad_t)
        prod[1, at] = smooth_yt(grad_y * grad_t)
        energy = grad_t * grad_t + 0.25 * (grad_x * grad_x + grad_y * grad_y)
        prod[2, at] = smooth_yt(energy, 0.25 * here * here)

    def outside(edge):
        for kind in range(3):
            act2[kind, edge % RING] = jnp.zeros((EDGE, PAIRS, BLK), BF16)

    outside(0)
    for pair in range(pairs2, pairs1):
        act3[pair] = jnp.zeros((EDGE, PAIRS, BLK), BF16)

    chunks = pairs1 // FIRST
    done2 = done3 = done_slopes = 0
    for stage in range(chunks + 2):
        end2 = min(pairs2, stage * FIRST - 2) if stage else 0
        end3 = pairs2 if stage == chunks + 1 else max(0, done2 - 1)
        if stage == chunks:
            outside(pairs2 + 1)
        work = []
        for end, done, run in ((end3, done3, third), (end2, done2, second)):
            steps = range(done, end, GROUP)
            work.append([functools.partial(run, at, min(at + GROUP, end)) for at in steps])
        if stage < chunks:
            work.append([functools.partial(first, stage)])
        if stage and done_slopes <= FX:
            work.append([functools.partial(products, done_slopes)])
            done_slopes += RX
        for turn_of in range(max(len(w) for w in work)):
            for w in work:
                if turn_of < len(w):
                    w[turn_of]()
        done2, done3 = max(done2, end2), max(done3, end3)
    assert done2 == done3 == pairs2 and done_slopes > FX


def fourth_kernel(ty, act3, prod, w4_ref, fault_ref, prob, slope, part):
    yw = ty + 2 * H
    pairs1 = yw // 2
    at_lane = iota((NT, 8 * PAIRS), 1) % (4 * PAIRS)
    from_pairs = jnp.where(
        iota((NT, 8 * PAIRS), 0) == 2 * pair_of(at_lane % PAIRS) - 1 + at_lane // PAIRS, 1.0, 0.0
    ).astype(BF16)

    def slopes(k):
        at = pl.ds(k + 1, RX)
        sums = []
        for which in range(3):
            before, here, after = [prod[which, pl.ds(k + i, RX)] for i in range(3)]
            sums.append(0.5 * here + 0.25 * (before + after))
        scale = -1.0 / (sums[2] + 0.05)
        slope[0, at] = sums[0] * scale
        slope[1, at] = sums[1] * scale

    def fourth(step, carry):
        for i in range(2):
            slopes(jnp.minimum((step * 2 + i) * RX, FX - RX))
        pair = step * 8
        cells = [act3[pl.ds(pair, 8), blk].reshape(8 * PAIRS, BLK) for blk in range(EDGE)]
        result = dot(jnp.concatenate(cells, axis=1), w4_ref[...])
        for i in range(0, 8, 2):
            sides = []
            for at in (i, i + 1):
                rows = result[at * PAIRS : (at + 1) * PAIRS]
                sides.append(
                    jnp.concatenate([rows[:, j * 128 : (j + 1) * 128] for j in range(4)], axis=0)
                )
            both = jnp.concatenate(sides, axis=1)
            high = both.astype(BF16)
            low = (both - high.astype(F32)).astype(BF16)
            share = dot(from_pairs, jnp.concatenate([high, low], axis=0))
            part[pair + i] = share[:, :128]
            part[pair + i + 1] = share[:, 128:]
        return carry

    lax.fori_loop(0, pairs1 // 8, fourth, 0, unroll=True)

    for x in range(FX):
        prob[x * yw : x * yw + H, :] = jnp.zeros((H, NT), F32)
        prob[(x + 1) * yw - H : (x + 1) * yw, :] = jnp.zeros((H, NT), F32)
    lane = iota((NT, 128), 1)

    def order(step, carry):
        pair = 2 * step + 1
        here = part[pair]
        before = pltpu.roll(part[pair - 1], 64, 1)
        after = pltpu.roll(part[pair + 1], 64, 1)
        own = jnp.where(lane < 64, here, after)
        other = jnp.where(
            lane < 32,
            before,
            jnp.where(lane < 64, after, jnp.where(lane < 96, here, part[pair + 2])),
        )
        values = 1.0 / (1.0 + jnp.exp(-(own + other)))
        values = values.astype(BF16).astype(F32).T
        for row in range(4):
            at = pl.ds(2 * pair + 2 + row, FX, stride=yw)
            prob[at, :] = values[row * XW : row * XW + FX]
        return carry

    lax.fori_loop(0, (ty + 8) // 4, order, 0, unroll=5)

    for which in range(2):
        slope[which, FX + 1] = jnp.zeros((yw, NT), F32)
    for x in range(TX):
        fault_ref[x] = prob[(x + 4) * yw + H : (x + 4) * yw + H + ty, :].astype(BF16)


def owned(total, k, values, ty):
    for row in range(RX):
        ok = (k + row >= 5) & (k + row < 5 + TX)
        total = total + jnp.where(ok, values[row, H : H + ty], 0.0)
    return total


def image_of(wave, face, k, shifts):
    block, up_y, down_y, up_t, down_t = shifts
    at, before, after = [pl.ds(k + i, RX) for i in (0, -1, 1)]
    here = wave[at]
    flow = face[1, at] * (here - up_y(here))
    image = time_part(block) * here - ETA_TIME * (up_t(here) + down_t(here))
    image = image + flow - down_y(flow)
    image = image + face[0, at] * (here - wave[after])
    return here, image + face[0, before] * (here - wave[before])


def time_part(block):
    lane = iota(block, 2)
    count = jnp.where(lane == 0, 0.0, 1.0) + jnp.where(lane == NT - 1, 0.0, 1.0)
    return MU_DIAG + ETA_TIME * count


def waves_kernel(grid_x, grid_y, ty, prob, slope, mom_ref, face, wave2, *refs):
    n_gy = grid_y // ty
    waves_refs = refs[:n_gy]
    weight, flux, inv, wave0, wave1 = refs[n_gy:]
    place_y = lax.axis_index("gy")
    x0 = lax.axis_index("gx") * TX
    y0 = place_y * ty
    yw = ty + 2 * H
    shifts = plane_shifts(yw)
    block, up_y, down_y, up_t, down_t = shifts
    at_y = y0 - H + iota(block, 1)
    mask_y = (at_y >= 0) & (at_y < grid_y)

    def weights(step, carry):
        k = step * RX
        at = pl.ds(k + 1, RX)
        rows = prob[pl.ds(pl.multiple_of(k * yw, 8), RX * yw), :].reshape(block)
        raw_weight = 1.0 - 0.9 * rows
        at_x = x0 - 4 + k + iota(block, 0)
        weight[0, at] = raw_weight
        weight[1, at] = jnp.where(mask_y & (at_x >= 0) & (at_x < grid_x), raw_weight, 0.0)
        return carry

    lax.fori_loop(0, FX // RX, weights, 0)
    for which in range(2):
        weight[which, FX + 1] = jnp.full((yw, NT), 1.0 - which, F32)
        face[which, 0] = jnp.zeros((yw, NT), F32)
        flux[which, 0] = jnp.zeros((yw, NT), F32)

    def faces(step, carry):
        k = step * RX + 1
        at, after = pl.ds(k, RX), pl.ds(k + 1, RX)
        raw_weight = weight[0, at]
        masked = weight[1, at]
        face_x = 2.0 * masked * weight[1, after] / (raw_weight + weight[0, after])
        face_y = 2.0 * masked * up_y(masked) / (raw_weight + up_y(raw_weight))
        slope_y = slope[1, at]
        face[0, at] = face_x
        face[1, at] = face_y
        flux[0, at] = 0.5 * face_x * (slope[0, at] + slope[0, after])
        flux[1, at] = 0.5 * face_y * (slope_y + up_y(slope_y))
        return carry

    lax.fori_loop(0, FX // RX, faces, 0)

    def start(step, total):
        k = step * RX + 1
        at, before = pl.ds(k, RX), pl.ds(k - 1, RX)
        flux_y = flux[1, at]
        face_y = face[1, at]
        right = flux[0, before] - flux[0, at] + down_y(flux_y) - flux_y
        inverse = 1.0 / (time_part(block) + face[0, at] + face[0, before] + face_y + down_y(face_y))
        first_wave = right * inverse
        inv[at] = inverse
        wave0[at] = first_wave
        return owned(total, k, right * first_wave, ty)

    zero = jnp.zeros((ty, NT), F32)
    b0 = lax.fori_loop(0, FX // RX, start, zero)

    def advance(source, target):
        def body(step, totals):
            k = step * RX + 3
            here, image = image_of(source, face, k, shifts)
            at = pl.ds(k, RX)
            after = here - image * inv[at]
            target[at] = after
            return (
                owned(totals[0], k, here * image, ty),
                owned(totals[1], k, after * image, ty),
            )

        return body

    steps = (FX - 4) // RX
    a0, a1 = lax.fori_loop(0, steps, advance(wave0, wave1), (zero, zero))
    a2, a3 = lax.fori_loop(0, steps, advance(wave1, wave2), (zero, zero))
    sums = [jnp.sum(v, axis=0, keepdims=True) for v in (b0, a0, a1, a2, a3)]
    mom_ref[...] = jnp.concatenate(sums + [jnp.zeros((3, NT), F32)], axis=0)

    rows = TX // n_gy
    for place, ref in enumerate(waves_refs):
        to = lax.rem(place_y + place, n_gy) * rows + 5
        for which, wave in enumerate((wave0, wave1, wave2)):
            for row in range(rows):
                ref[which, row] = wave[to + row, H : H + ty, :].astype(BF16)


def last_kernel(ty, mom_ref, face, wave2, out_ref):
    shifts = plane_shifts(ty + 2 * H)

    def finish(step, total):
        k = step * RX + 5
        here, image = image_of(wave2, face, k, shifts)
        return owned(total, k, here * image, ty)

    total = lax.fori_loop(0, TX // RX, finish, jnp.zeros((ty, NT), F32))
    a4 = jnp.sum(total, axis=0, keepdims=True)
    sums = jnp.sum(jnp.where(iota((8, NT), 0) == 5, a4, mom_ref[...]), axis=1, keepdims=True)
    values = jnp.where(iota((8, NT), 0) == iota((8, NT), 1), sums, 0.0)
    values = jnp.sum(values, axis=0, keepdims=True)
    for device in range(out_ref.shape[0]):
        out_ref[device] = values


def combine_kernel(n_gy, ty, mom_ref, *refs):
    waves_refs, out_ref = refs[:n_gy], refs[n_gy]
    place_y = lax.axis_index("gy")
    moments = jnp.sum(mom_ref[...], axis=0)
    b0, a0, a1, a2, a3, a4 = [
        jnp.broadcast_to(moments[:, i : i + 1], (1, NT)) for i in range(6)
    ]
    a0, a1, a2, a3, a4 = [v / b0 for v in (a0, a1, a2, a3, a4)]
    l21 = a1 / a0
    l31 = a2 / a0
    d2 = jnp.maximum(a2 - l21 * a1, 1e-7 * a2 + 1e-30)
    l32 = (a3 - l21 * a2) / d2
    d3 = jnp.maximum(a4 - l31 * a2 - l32 * l32 * d2, 1e-7 * a4 + 1e-30)
    y2 = (1.0 - a0) - l21
    y3 = (1.0 - a0 - a1) - l31 - l32 * y2
    c3 = y3 / d3
    c2 = y2 / d2 - l32 * c3
    c1 = 1.0 / a0 - l21 * c2 - l31 * c3
    for place, ref in enumerate(waves_refs):
        source = lax.rem(place_y - place + n_gy, n_gy)
        at = pl.ds(pl.multiple_of(source * ty, 8), ty)
        for x in range(ref.shape[1]):
            w0, w1, w2 = [ref[which, x].astype(F32) for which in range(3)]
            out_ref[x, at, :] = c1 * w0 + c2 * w1 + c3 * w2


def vmem(count):
    return [pl.BlockSpec(memory_space=pltpu.VMEM)] * count


def on_device(amplitude, conv_first, conv_second, conv_third, conv_last):
    n_gx, n_gy = lax.axis_size("gx"), lax.axis_size("gy")
    ty = amplitude.shape[1]
    grid_x, grid_y = n_gx * TX, n_gy * ty
    assert amplitude.shape == (TX, ty, NT)

    def shift(values, axis, count, step):
        pairs = [(i, i + step) for i in range(count) if 0 <= i + step < count]
        return lax.ppermute(values, axis, pairs)

    first_x, last_x, first_y, last_y = pl.pallas_call(
        slices_kernel,
        out_shape=[jax.ShapeDtypeStruct((H, ty, NT), BF16)] * 2
        + [jax.ShapeDtypeStruct((TX, H, NT), BF16)] * 2,
        in_specs=vmem(1),
        out_specs=vmem(4),
        compiler_params=pltpu.CompilerParams(vmem_limit_bytes=4 * 2**20),
        name="halo_slices",
    )(amplitude)
    xhigh = shift(first_x, "gx", n_gx, -1)
    xlow = shift(last_x, "gx", n_gx, 1)
    ylow = shift(
        jnp.concatenate([xlow[:, ty - H :], last_y, xhigh[:, ty - H :]]), "gy", n_gy, 1
    )
    yhigh = shift(jnp.concatenate([xlow[:, :H], first_y, xhigh[:, :H]]), "gy", n_gy, -1)

    weights = (conv_first, conv_second, conv_third, conv_last)
    (conv_first, conv_second, conv_third, conv_last), _ = lax.optimization_barrier((weights, xhigh))

    def taps_first(weight):
        return jnp.transpose(weight, (2, 3, 4, 0, 1))

    w1, w2, w3, w4 = pl.pallas_call(
        prep_kernel,
        out_shape=[
            jax.ShapeDtypeStruct((16 * XW, (EDGE + 1) * BLK), BF16),
            jax.ShapeDtypeStruct((6 * BLK, BLK), BF16),
            jax.ShapeDtypeStruct((6 * BLK, BLK), BF16),
            jax.ShapeDtypeStruct((EDGE * BLK, 16 * XW), BF16),
        ],
        in_specs=vmem(2) + [pl.BlockSpec(memory_space=pl.ANY)],
        out_specs=vmem(4),
        compiler_params=pltpu.CompilerParams(vmem_limit_bytes=16 * 2**20),
        cost_estimate=pl.CostEstimate(flops=10**9, bytes_accessed=10**7, transcendentals=0),
        name="band_weights",
    )(
        jnp.concatenate([taps_first(conv_second), taps_first(conv_third)]).reshape(54 * CH, CH),
        jnp.concatenate(
            [jnp.transpose(conv_first, (1, 2, 3, 4, 0)), jnp.transpose(conv_last, (0, 2, 3, 4, 1))]
        ),
        xhigh,
    )

    yw, nf = ty + 2 * H, FX + 2
    act3, prod = pl.pallas_call(
        functools.partial(net_kernel, grid_x, grid_y, ty),
        out_shape=[
            jax.ShapeDtypeStruct((yw // 2, EDGE, PAIRS, BLK), BF16),
            jax.ShapeDtypeStruct((3, FX + 4, yw, NT), F32),
        ],
        in_specs=vmem(8),
        out_specs=vmem(2),
        scratch_shapes=[
            pltpu.VMEM(((XW + 2) * yw, NT), F32),
            pltpu.VMEM((yw + 2, XW, NT), BF16),
            pltpu.VMEM((3, RING, EDGE + 1, PAIRS, BLK), BF16),
            pltpu.VMEM((3, RING, EDGE, PAIRS, BLK), BF16),
        ],
        compiler_params=pltpu.CompilerParams(vmem_limit_bytes=28 * 2**20),
        cost_estimate=pl.CostEstimate(flops=3 * 10**10, bytes_accessed=10**7, transcendentals=0),
        name="layers_one_to_three",
    )(amplitude, xlow, xhigh, ylow, yhigh, w1, w2, w3)

    fault, prob, slope = pl.pallas_call(
        functools.partial(fourth_kernel, ty),
        out_shape=[
            jax.ShapeDtypeStruct((TX, ty, NT), BF16),
            jax.ShapeDtypeStruct((FX * yw, NT), F32),
            jax.ShapeDtypeStruct((2, nf, yw, NT), F32),
        ],
        in_specs=vmem(3),
        out_specs=vmem(3),
        scratch_shapes=[pltpu.VMEM((yw // 2, NT, 128), F32)],
        compiler_params=pltpu.CompilerParams(vmem_limit_bytes=(LIMIT + 4) * 2**20),
        cost_estimate=pl.CostEstimate(
            flops=10**10, bytes_accessed=10**7, transcendentals=10**6
        ),
        name="layer_four",
    )(act3, prod, w4)

    rows = TX // n_gy
    moments, face, wave2, *waves = pl.pallas_call(
        functools.partial(waves_kernel, grid_x, grid_y, ty),
        out_shape=[
            jax.ShapeDtypeStruct((8, NT), F32),
            jax.ShapeDtypeStruct((2, nf, yw, NT), F32),
            jax.ShapeDtypeStruct((nf, yw, NT), F32),
        ]
        + [jax.ShapeDtypeStruct((3, rows, ty, NT), BF16)] * n_gy,
        in_specs=vmem(2),
        out_specs=vmem(3 + n_gy),
        scratch_shapes=[
            pltpu.VMEM((2, nf, yw, NT), F32),
            pltpu.VMEM((2, nf, yw, NT), F32),
            pltpu.VMEM((nf, yw, NT), F32),
            pltpu.VMEM((nf, yw, NT), F32),
            pltpu.VMEM((nf, yw, NT), F32),
        ],
        compiler_params=pltpu.CompilerParams(vmem_limit_bytes=24 * 2**20),
        cost_estimate=pl.CostEstimate(flops=10**8, bytes_accessed=10**7, transcendentals=0),
        name="solver_waves",
    )(prob, slope)

    arrived = [waves[0]]
    for place in range(1, n_gy):
        pairs = [(i, (i + place) % n_gy) for i in range(n_gy)]
        arrived.append(lax.ppermute(waves[place], "gy", pairs))

    everyone = pl.pallas_call(
        functools.partial(last_kernel, ty),
        out_shape=jax.ShapeDtypeStruct((n_gx * n_gy, 1, NT), F32),
        in_specs=vmem(3),
        out_specs=pl.BlockSpec(memory_space=pltpu.VMEM),
        compiler_params=pltpu.CompilerParams(vmem_limit_bytes=16 * 2**20),
        cost_estimate=pl.CostEstimate(flops=10**9, bytes_accessed=10**8, transcendentals=0),
        name="last_moment",
    )(moments, face, wave2)
    moments = lax.all_to_all(everyone, ("gx", "gy"), split_axis=0, concat_axis=0, tiled=True)
    shift_field = pl.pallas_call(
        functools.partial(combine_kernel, n_gy, ty),
        out_shape=jax.ShapeDtypeStruct((rows, grid_y, NT), F32),
        in_specs=vmem(1 + n_gy),
        out_specs=pl.BlockSpec(memory_space=pltpu.VMEM),
        compiler_params=pltpu.CompilerParams(vmem_limit_bytes=16 * 2**20),
        name="combine_waves",
    )(moments, *arrived)
    return (fault, shift_field)


def solution(mesh):
    return jax.shard_map(
        on_device,
        mesh=mesh,
        in_specs=(P("gx", "gy", None), P(), P(), P(), P()),
        out_specs=(P("gx", "gy", None), P(("gx", "gy"), None, None)),
        check_vma=False,
    )
```

```python
import functools

import jax
import jax.numpy as jnp
from jax import lax
from jax.experimental import pallas as pl
from jax.experimental.pallas import tpu as pltpu
from jax.sharding import PartitionSpec as P

MU_DIAG = 0.05
ETA_TIME = 0.5

TX, NT, H = 16, 128, 8
CH = 16
XW = TX + 2 * H
FX = TX + 8
RX = 4
FIRST = 4
RING = 12
Y_SLOTS = (1, 2, 3, 0)
GROUP = 2
BLK = 256
EDGE = 7
SUB = 16
PAIRS = NT // 2

F32 = jnp.float32
BF16 = jnp.bfloat16


def iota(shape, dim):
    return lax.broadcasted_iota(jnp.int32, shape, dim)


def dot_nt(a, b):
    return lax.dot_general(a, b, (((1,), (1,)), ((), ())), preferred_element_type=F32)


def prep_kernel(inner_ref, outer_ref, after_ref, w1_ref, w2_ref, w3_ref, w4_ref):
    del after_ref
    spread = jnp.where(iota((CH, BLK), 1) % CH == iota((CH, BLK), 0), 1.0, 0.0).astype(BF16)
    unit = jnp.where(iota((BLK, BLK), 1) == iota((BLK, BLK), 0), 1.0, 0.0).astype(BF16)
    none = jnp.zeros((CH, BLK), BF16)
    cell = iota((CH, BLK), 1) // CH
    at_cell = [cell == at for at in range(16)]
    inputs = input_cells()
    tiled = jnp.dot(inner_ref[...], spread, preferred_element_type=F32).astype(BF16)
    for layer, ref in enumerate((w2_ref, w3_ref)):
        for tile in range(6):
            bands = []
            for yo in range(2):
                for to in range(2):
                    for xo in range(4):
                        band = none
                        for at, (y, t, x) in enumerate(inputs[tile]):
                            dx, dy, dt = x - xo + 1, y - yo + 1, t - to + 1
                            if min(dx, dy, dt) >= 0 and max(dx, dy, dt) <= 2:
                                tap = tiled[(layer * 27 + dx * 9 + dy * 3 + dt) * CH :][:CH]
                                band = jnp.where(at_cell[at], tap, band)
                        bands.append(band)
            turned = dot_nt(unit, jnp.concatenate(bands, axis=0))
            ref[tile * BLK : (tile + 1) * BLK, :] = turned.astype(BF16)

    def taps(which):
        found = {}
        for dx in range(3):
            for dy in range(3):
                tiled = jnp.dot(outer_ref[which, dx, dy], spread, preferred_element_type=F32)
                for dt in range(3):
                    found[dx, dy, dt] = tiled[dt : dt + 1]
        return found

    first, last = taps(0), taps(1)
    lane_yt = iota((1, BLK), 1) // 64
    quarter = [lane_yt == at for at in range(4)]

    def by_quarter(found, dx, at):
        value = jnp.zeros((1, BLK), F32)
        for y in range(2):
            for t in range(2):
                dy, dt = at(y, t)
                if 0 <= dy <= 2 and 0 <= dt <= 2:
                    value = jnp.where(quarter[y * 2 + t], found[dx, dy, dt], value)
        return value

    def rows_of(found, rows, at):
        return [
            jnp.broadcast_to(by_quarter(found, dx, at), (rows, BLK)).astype(BF16)
            for dx in range(3)
        ]

    row_x = iota((XW, BLK), 0)
    lane_x = iota((XW, BLK), 1) // CH % 4
    offset_x = [row_x - 1 - 4 * blk - lane_x for blk in range(EDGE)]
    offset_x.append(jnp.where(lane_x == 0, row_x - 29, jnp.where(lane_x == 3, row_x, -1)))
    masks = [[offset == dx for dx in range(3)] for offset in offset_x]
    none = jnp.zeros((XW, BLK), BF16)
    for j in range(4):
        for yi in range(4):
            row = (j * 4 + yi) * XW
            values = rows_of(first, XW, lambda y, t: (yi - y, j - t))
            for blk in range(EDGE + 1):
                band = none
                for dx in range(3):
                    band = jnp.where(masks[blk][dx], values[dx], band)
                w1_ref[row : row + XW, blk * BLK : (blk + 1) * BLK] = band
    masks = [
        [4 * blk + lane_x - 1 - row_x == dx for dx in range(3)] for blk in range(EDGE)
    ]
    bands = [[] for blk in range(EDGE)]
    for j in range(4):
        for yi in Y_SLOTS:
            values = rows_of(last, XW, lambda y, t: (y + 2 - yi, t + 2 - j))
            for blk in range(EDGE):
                band = none
                for dx in range(3):
                    band = jnp.where(masks[blk][dx], values[dx], band)
                bands[blk].append(band)
    for blk in range(EDGE):
        turned = dot_nt(unit, jnp.concatenate(bands[blk], axis=0))
        w4_ref[blk * BLK : (blk + 1) * BLK, :] = turned.astype(BF16)


def slices_kernel(amp_ref, first_x, last_x, first_y, last_y):
    ty = amp_ref.shape[1]
    first_x[...] = amp_ref[:H]
    last_x[...] = amp_ref[TX - H :]
    first_y[...] = amp_ref[:, :H]
    last_y[...] = amp_ref[:, ty - H :]


def input_cells():
    tiles = []
    here = [(t, x) for t in (0, 1) for x in range(4)]
    near = [(2, 2), (2, 3), (-1, 0), (-1, 1), (-1, 2), (-1, 3), (2, 0), (2, 1)]
    side = [(0, 4), (2, -1), (-1, 4), (0, -1), (1, 4), (-1, -1), (2, 4), (1, -1)]
    for cells in (here, near, side):
        for rows in ((0, 1), (-1, 2)):
            tiles.append([(y, t, x) for y in rows for t, x in cells])
    return tiles


def plane_shifts(yw):
    block = (RX, yw, NT)
    lane = iota(block, 2)
    first_lane = lane == 0
    last_lane = lane == NT - 1

    def up_y(v):
        return pltpu.roll(v, yw - 1, 1)

    def down_y(v):
        return pltpu.roll(v, 1, 1)

    def up_t(v, edge=0.0):
        return jnp.where(last_lane, edge, pltpu.roll(v, NT - 1, 2))

    def down_t(v, edge=0.0):
        return jnp.where(first_lane, edge, pltpu.roll(v, 1, 2))

    return block, up_y, down_y, up_t, down_t


def dot(a, b):
    return jnp.dot(a, b, preferred_element_type=F32)


def pair_of(row):
    return row // SUB + (row % SUB) * 4


def lane_masks(x0, grid_x, blocks):
    slot = iota((1, BLK), 1) // CH % 4
    masks = []
    for blk in range(blocks):
        if blk < EDGE:
            at = x0 - 6 + 4 * blk + slot
        else:
            at = x0 + jnp.where(slot == 0, 22, -7)
        masks.append(jnp.where((at >= 0) & (at < grid_x), 1.0, 0.0))
    return masks


def row_mask(y, grid_y):
    at = y + jnp.where(iota((1, BLK), 1) >= 128, 1, 0)
    return jnp.where((at >= 0) & (at < grid_y), 1.0, 0.0)


def lanes16():
    return iota((PAIRS, 128), 1).astype(jnp.int16)


def put(act, pair, blk, values):
    sub_row = iota((SUB, 128), 0)
    lane = lanes16()
    early = (lane >= 32) & (lane < 96)
    values = values.astype(BF16)
    act[0, pair, blk] = values
    for half in range(2):
        turned = pltpu.roll(values[:, half * 128 : (half + 1) * 128], 96, 1)
        head = pltpu.roll(turned[PAIRS - SUB :].astype(F32), 1, 0)
        head = jnp.where(sub_row == 0, 0.0, head).astype(BF16)
        tail = pltpu.roll(turned[:SUB].astype(F32), SUB - 1, 0)
        tail = jnp.where(sub_row == SUB - 1, 0.0, tail).astype(BF16)
        before = jnp.concatenate([head, turned[: PAIRS - SUB]], axis=0)
        after = jnp.concatenate([turned[SUB:], tail], axis=0)
        act[1, pair, blk, :, half * 128 : (half + 1) * 128] = jnp.where(early, before, after)


def put_sides(act, pair, blocks):
    lane = lanes16()
    slot0, slot3, even_slot = (lane & 48) == 0, (lane & 48) == 48, (lane & 16) == 0
    for blk in range(EDGE):
        left, right = (blk - 1) % blocks, (blk + 1) % blocks
        for half in range(2):
            at = slice(half * 128, (half + 1) * 128)
            even = jnp.where(slot0, act[0, pair, right, :, at], act[1, pair, right, :, at])
            odd = jnp.where(slot3, act[0, pair, left, :, at], act[1, pair, left, :, at])
            act[2, pair, blk, :, at] = jnp.where(even_slot, even, odd)


def layer(source, w_ref, pair, count):
    def rows(kind, offset, at):
        found = []
        for i in range(count):
            place = (pair + offset + i) % RING
            found.append(source[kind, place, :EDGE, :, at].reshape(EDGE * PAIRS, -1))
        return jnp.concatenate(found, axis=0)

    tiles = []
    for kind in range(3):
        tiles.append(rows(kind, 1, slice(0, BLK)))
        tiles.append(rows(kind, 0, slice(128, BLK)))
        tiles.append(rows(kind, 2, slice(0, 128)))
    return dot(jnp.concatenate(tiles, axis=1), w_ref[...])


def net_kernel(
    grid_x,
    grid_y,
    ty,
    amp_ref,
    xlow_ref,
    xhigh_ref,
    ylow_ref,
    yhigh_ref,
    w1_ref,
    w2_ref,
    w3_ref,
    w4_ref,
    fault_ref,
    prob,
    slope,
    raw,
    amp,
    act1,
    act2,
    act3,
    prod,
    part,
):
    x0 = lax.axis_index("gx") * TX
    y0 = lax.axis_index("gy") * ty
    yw = ty + 2 * H
    pairs1, pairs2 = yw // 2, ty // 2 + 6
    for x in range(XW):
        row = x * yw
        if x < H:
            mid = xlow_ref[x]
        elif x < H + TX:
            mid = amp_ref[x - H]
        else:
            mid = xhigh_ref[x - H - TX]
        raw[row + H : row + H + ty, :] = mid.astype(F32)
        raw[row : row + H, :] = ylow_ref[x].astype(F32)
        raw[row + H + ty : row + yw, :] = yhigh_ref[x].astype(F32)

    def turn(y, carry):
        amp[y + 1] = raw[pl.ds(y, XW, stride=yw), :].astype(BF16)
        return carry

    lax.fori_loop(0, yw, turn, 0, unroll=8)
    amp[0] = jnp.zeros((XW, NT), BF16)
    amp[yw + 1] = jnp.zeros((XW, NT), BF16)

    at_row = iota((4 * PAIRS, NT), 0)
    to_pairs = jnp.where(
        iota((4 * PAIRS, NT), 1) == 2 * pair_of(at_row % PAIRS) - 1 + at_row // PAIRS, 1.0, 0.0
    ).astype(BF16)
    mask = lane_masks(x0, grid_x, EDGE + 1)

    def first(step):
        pieces = []
        for i in range(0, FIRST, 2):
            y = (step * FIRST + i) * 2
            rows = [amp[pl.ds(y + 2 * k, 4)].reshape(4 * XW, NT) for k in range(2)]
            turned = dot_nt(to_pairs, jnp.concatenate(rows, axis=0)).astype(BF16)
            for k in range(2):
                parts = [turned[j * PAIRS : (j + 1) * PAIRS, k * 128 : (k + 1) * 128] for j in range(4)]
                pieces.append(jnp.concatenate(parts, axis=1))
        pieces = jnp.concatenate(pieces, axis=0)
        for begin in range(0, EDGE + 1, 2):
            result = dot(pieces, w1_ref[:, begin * BLK : (begin + 2) * BLK])
            for i in range(FIRST):
                pair = step * FIRST + i
                inside = row_mask(y0 + 2 * pair - H, grid_y)
                for blk in (begin, begin + 1):
                    lane = (blk - begin) * BLK
                    values = result[i * PAIRS : (i + 1) * PAIRS, lane : lane + BLK]
                    put(act1, pair % RING, blk, jnp.maximum(values, 0.0) * (mask[blk] * inside))
        for i in range(FIRST):
            put_sides(act1, (step * FIRST + i) % RING, EDGE + 1)

    def second(begin, end):
        count = end - begin
        result = layer(act1, w2_ref, begin, count)
        for i in range(count):
            pair = begin + i
            inside = row_mask(y0 + 2 * pair - 6, grid_y)
            for blk in range(EDGE):
                at = (i * EDGE + blk) * PAIRS
                values = jnp.maximum(result[at : at + PAIRS], 0.0)
                put(act2, (pair + 1) % RING, blk, values * (mask[blk] * inside))
            put_sides(act2, (pair + 1) % RING, EDGE)

    def third(begin, end):
        count = end - begin
        result = layer(act2, w3_ref, begin, count)
        for i in range(count):
            pair = begin + i
            inside = row_mask(y0 + 2 * pair - 6, grid_y)
            for blk in range(EDGE):
                at = (i * EDGE + blk) * PAIRS
                values = jnp.maximum(result[at : at + PAIRS], 0.0)
                act3[pair, blk] = (values * (mask[blk] * inside)).astype(BF16)

    block, up_y, down_y, up_t, down_t = plane_shifts(yw)

    def smooth_yt(v, edge=0.0):
        v = 0.5 * v + 0.25 * (up_t(v, edge) + down_t(v, edge))
        return 0.5 * v + 0.25 * (up_y(v) + down_y(v))

    def amp_rows(x):
        return raw[pl.ds(pl.multiple_of(x * yw, 8), RX * yw), :].reshape(block)

    def products(k):
        here = amp_rows(k + 3)
        grad_x = 0.5 * (amp_rows(k + 4) - amp_rows(k + 2))
        grad_y = 0.5 * (up_y(here) - down_y(here))
        grad_t = 0.5 * (up_t(here) - down_t(here))
        at = pl.ds(k, RX)
        prod[0, at] = smooth_yt(grad_x * grad_t)
        prod[1, at] = smooth_yt(grad_y * grad_t)
        energy = grad_t * grad_t + 0.25 * (grad_x * grad_x + grad_y * grad_y)
        prod[2, at] = smooth_yt(energy, 0.25 * here * here)

    at_lane = iota((NT, 8 * PAIRS), 1) % (4 * PAIRS)
    from_pairs = jnp.where(
        iota((NT, 8 * PAIRS), 0) == 2 * pair_of(at_lane % PAIRS) - 1 + at_lane // PAIRS, 1.0, 0.0
    ).astype(BF16)

    def slopes(k):
        at = pl.ds(k + 1, RX)
        sums = []
        for which in range(3):
            before, here, after = [prod[which, pl.ds(k + i, RX)] for i in range(3)]
            sums.append(0.5 * here + 0.25 * (before + after))
        scale = -1.0 / (sums[2] + 0.05)
        slope[0, at] = sums[0] * scale
        slope[1, at] = sums[1] * scale

    def fourth(begin, end):
        cells = [
            act3[begin:end, blk].reshape((end - begin) * PAIRS, BLK) for blk in range(EDGE)
        ]
        result = dot(jnp.concatenate(cells, axis=1), w4_ref[...])
        for pair in range(begin, end, 2):
            sides = []
            for at in (pair - begin, pair - begin + 1):
                rows = result[at * PAIRS : (at + 1) * PAIRS]
                sides.append(
                    jnp.concatenate([rows[:, j * 128 : (j + 1) * 128] for j in range(4)], axis=0)
                )
            both = jnp.concatenate(sides, axis=1)
            high = both.astype(BF16)
            low = (both - high.astype(F32)).astype(BF16)
            share = dot(from_pairs, jnp.concatenate([high, low], axis=0))
            part[pair] = share[:, :128]
            part[pair + 1] = share[:, 128:]

    lane = iota((NT, 128), 1)

    def order(pair):
        here = part[pair]
        before = pltpu.roll(part[pair - 1], 64, 1)
        after = pltpu.roll(part[pair + 1], 64, 1)
        own = jnp.where(lane < 64, here, after)
        other = jnp.where(
            lane < 32,
            before,
            jnp.where(lane < 64, after, jnp.where(lane < 96, here, part[pair + 2])),
        )
        values = 1.0 / (1.0 + jnp.exp(-(own + other)))
        values = values.astype(BF16).astype(F32).T
        for row in range(4):
            at = pl.ds(2 * pair + 2 + row, FX, stride=yw)
            prob[at, :] = values[row * XW : row * XW + FX]

    def outside(edge):
        for kind in range(3):
            act2[kind, edge % RING] = jnp.zeros((EDGE, PAIRS, BLK), BF16)

    outside(0)
    for pair in range(pairs2, pairs1):
        act3[pair] = jnp.zeros((EDGE, PAIRS, BLK), BF16)

    for x in range(FX):
        prob[x * yw : x * yw + H, :] = jnp.zeros((H, NT), F32)
        prob[(x + 1) * yw - H : (x + 1) * yw, :] = jnp.zeros((H, NT), F32)
    for which in range(2):
        slope[which, FX + 1] = jnp.zeros((yw, NT), F32)

    chunks = pairs1 // FIRST
    done2 = done3 = done4 = 0
    next_products = next_slopes = 0
    next_order = 1
    last_order = pairs1 - 5
    for stage in range(chunks + 4):
        if stage == chunks:
            outside(pairs2 + 1)
        end2 = max(0, min(pairs2, stage * FIRST - 2))
        end3 = pairs2 if done2 == pairs2 else max(0, done2 - 1)
        end4 = pairs1 if done3 == pairs2 else done3 // 4 * 4
        work = []
        for end, done, run in ((end3, done3, third), (end2, done2, second)):
            steps = range(done, end, GROUP)
            work.append([functools.partial(run, at, min(at + GROUP, end)) for at in steps])
        if stage < chunks:
            work.append([functools.partial(first, stage)])
        if end4 > done4:
            work.append([functools.partial(fourth, done4, end4)])
        ready = []
        while next_order <= last_order and next_order + 2 < done4:
            ready.append(functools.partial(order, next_order))
            next_order += 2
        work.append(ready)
        if stage and next_slopes < FX and next_slopes + RX < next_products:
            work.append([functools.partial(slopes, next_slopes)])
            next_slopes += RX
        if stage and next_products <= FX:
            work.append([functools.partial(products, next_products)])
            next_products += RX
        for turn_of in range(max(len(w) for w in work)):
            for w in work:
                if turn_of < len(w):
                    w[turn_of]()
        done2, done3, done4 = end2, end3, end4
    assert done4 == pairs1 and next_order > last_order and next_slopes == FX

    for x in range(TX):
        fault_ref[x] = prob[(x + 4) * yw + H : (x + 4) * yw + H + ty, :].astype(BF16)


def owned(total, k, values, ty):
    for row in range(RX):
        ok = (k + row >= 5) & (k + row < 5 + TX)
        total = total + jnp.where(ok, values[row, H : H + ty], 0.0)
    return total


def image_of(wave, face, k, shifts):
    block, up_y, down_y, up_t, down_t = shifts
    at, before, after = [pl.ds(k + i, RX) for i in (0, -1, 1)]
    here = wave[at]
    flow = face[1, at] * (here - up_y(here))
    image = time_part(block) * here - ETA_TIME * (up_t(here) + down_t(here))
    image = image + flow - down_y(flow)
    image = image + face[0, at] * (here - wave[after])
    return here, image + face[0, before] * (here - wave[before])


def time_part(block):
    lane = iota(block, 2)
    count = jnp.where(lane == 0, 0.0, 1.0) + jnp.where(lane == NT - 1, 0.0, 1.0)
    return MU_DIAG + ETA_TIME * count


def waves_kernel(grid_x, grid_y, ty, prob, slope, mom_ref, face, wave2, *refs):
    n_gy = grid_y // ty
    waves_refs = refs[:n_gy]
    weight, flux, inv, wave0, wave1 = refs[n_gy:]
    place_y = lax.axis_index("gy")
    x0 = lax.axis_index("gx") * TX
    y0 = place_y * ty
    yw = ty + 2 * H
    shifts = plane_shifts(yw)
    block, up_y, down_y, up_t, down_t = shifts
    at_y = y0 - H + iota(block, 1)
    mask_y = (at_y >= 0) & (at_y < grid_y)

    def weights(step, carry):
        k = step * RX
        at = pl.ds(k + 1, RX)
        rows = prob[pl.ds(pl.multiple_of(k * yw, 8), RX * yw), :].reshape(block)
        raw_weight = 1.0 - 0.9 * rows
        at_x = x0 - 4 + k + iota(block, 0)
        weight[0, at] = raw_weight
        weight[1, at] = jnp.where(mask_y & (at_x >= 0) & (at_x < grid_x), raw_weight, 0.0)
        return carry

    lax.fori_loop(0, FX // RX, weights, 0)
    for which in range(2):
        weight[which, FX + 1] = jnp.full((yw, NT), 1.0 - which, F32)
        face[which, 0] = jnp.zeros((yw, NT), F32)
        flux[which, 0] = jnp.zeros((yw, NT), F32)

    def faces(step, carry):
        k = step * RX + 1
        at, after = pl.ds(k, RX), pl.ds(k + 1, RX)
        raw_weight = weight[0, at]
        masked = weight[1, at]
        face_x = 2.0 * masked * weight[1, after] / (raw_weight + weight[0, after])
        face_y = 2.0 * masked * up_y(masked) / (raw_weight + up_y(raw_weight))
        slope_y = slope[1, at]
        face[0, at] = face_x
        face[1, at] = face_y
        flux[0, at] = 0.5 * face_x * (slope[0, at] + slope[0, after])
        flux[1, at] = 0.5 * face_y * (slope_y + up_y(slope_y))
        return carry

    lax.fori_loop(0, FX // RX, faces, 0)

    def start(step, total):
        k = step * RX + 1
        at, before = pl.ds(k, RX), pl.ds(k - 1, RX)
        flux_y = flux[1, at]
        face_y = face[1, at]
        right = flux[0, before] - flux[0, at] + down_y(flux_y) - flux_y
        inverse = 1.0 / (time_part(block) + face[0, at] + face[0, before] + face_y + down_y(face_y))
        first_wave = right * inverse
        inv[at] = inverse
        wave0[at] = first_wave
        return owned(total, k, right * first_wave, ty)

    zero = jnp.zeros((ty, NT), F32)
    b0 = lax.fori_loop(0, FX // RX, start, zero)

    def advance(source, target):
        def body(step, totals):
            k = step * RX + 3
            here, image = image_of(source, face, k, shifts)
            at = pl.ds(k, RX)
            after = here - image * inv[at]
            target[at] = after
            return (
                owned(totals[0], k, here * image, ty),
                owned(totals[1], k, after * image, ty),
            )

        return body

    steps = (FX - 4) // RX
    a0, a1 = lax.fori_loop(0, steps, advance(wave0, wave1), (zero, zero))
    a2, a3 = lax.fori_loop(0, steps, advance(wave1, wave2), (zero, zero))
    sums = [jnp.sum(v, axis=0, keepdims=True) for v in (b0, a0, a1, a2, a3)]
    mom_ref[...] = jnp.concatenate(sums + [jnp.zeros((3, NT), F32)], axis=0)

    rows = TX // n_gy
    for place, ref in enumerate(waves_refs):
        to = lax.rem(place_y + place, n_gy) * rows + 5
        for which, wave in enumerate((wave0, wave1, wave2)):
            for row in range(rows):
                ref[which, row] = wave[to + row, H : H + ty, :].astype(BF16)


def last_kernel(ty, mom_ref, face, wave2, out_ref):
    shifts = plane_shifts(ty + 2 * H)

    def finish(step, total):
        k = step * RX + 5
        here, image = image_of(wave2, face, k, shifts)
        return owned(total, k, here * image, ty)

    total = lax.fori_loop(0, TX // RX, finish, jnp.zeros((ty, NT), F32))
    a4 = jnp.sum(total, axis=0, keepdims=True)
    sums = jnp.sum(jnp.where(iota((8, NT), 0) == 5, a4, mom_ref[...]), axis=1, keepdims=True)
    values = jnp.where(iota((8, NT), 0) == iota((8, NT), 1), sums, 0.0)
    values = jnp.sum(values, axis=0, keepdims=True)
    for device in range(out_ref.shape[0]):
        out_ref[device] = values


def combine_kernel(n_gy, ty, mom_ref, *refs):
    waves_refs, out_ref = refs[:n_gy], refs[n_gy]
    place_y = lax.axis_index("gy")
    moments = jnp.sum(mom_ref[...], axis=0)
    b0, a0, a1, a2, a3, a4 = [
        jnp.broadcast_to(moments[:, i : i + 1], (1, NT)) for i in range(6)
    ]
    a0, a1, a2, a3, a4 = [v / b0 for v in (a0, a1, a2, a3, a4)]
    l21 = a1 / a0
    l31 = a2 / a0
    d2 = jnp.maximum(a2 - l21 * a1, 1e-7 * a2 + 1e-30)
    l32 = (a3 - l21 * a2) / d2
    d3 = jnp.maximum(a4 - l31 * a2 - l32 * l32 * d2, 1e-7 * a4 + 1e-30)
    y2 = (1.0 - a0) - l21
    y3 = (1.0 - a0 - a1) - l31 - l32 * y2
    c3 = y3 / d3
    c2 = y2 / d2 - l32 * c3
    c1 = 1.0 / a0 - l21 * c2 - l31 * c3
    for place, ref in enumerate(waves_refs):
        source = lax.rem(place_y - place + n_gy, n_gy)
        at = pl.ds(pl.multiple_of(source * ty, 8), ty)
        for x in range(ref.shape[1]):
            w0, w1, w2 = [ref[which, x].astype(F32) for which in range(3)]
            out_ref[x, at, :] = c1 * w0 + c2 * w1 + c3 * w2


def vmem(count):
    return [pl.BlockSpec(memory_space=pltpu.VMEM)] * count


def on_device(amplitude, conv_first, conv_second, conv_third, conv_last):
    n_gx, n_gy = lax.axis_size("gx"), lax.axis_size("gy")
    ty = amplitude.shape[1]
    grid_x, grid_y = n_gx * TX, n_gy * ty
    assert amplitude.shape == (TX, ty, NT)

    def shift(values, axis, count, step):
        pairs = [(i, i + step) for i in range(count) if 0 <= i + step < count]
        return lax.ppermute(values, axis, pairs)

    first_x, last_x, first_y, last_y = pl.pallas_call(
        slices_kernel,
        out_shape=[jax.ShapeDtypeStruct((H, ty, NT), BF16)] * 2
        + [jax.ShapeDtypeStruct((TX, H, NT), BF16)] * 2,
        in_specs=vmem(1),
        out_specs=vmem(4),
        compiler_params=pltpu.CompilerParams(vmem_limit_bytes=4 * 2**20),
        name="halo_slices",
    )(amplitude)
    xhigh = shift(first_x, "gx", n_gx, -1)
    xlow = shift(last_x, "gx", n_gx, 1)
    ylow = shift(
        jnp.concatenate([xlow[:, ty - H :], last_y, xhigh[:, ty - H :]]), "gy", n_gy, 1
    )
    yhigh = shift(jnp.concatenate([xlow[:, :H], first_y, xhigh[:, :H]]), "gy", n_gy, -1)

    weights = (conv_first, conv_second, conv_third, conv_last)
    (conv_first, conv_second, conv_third, conv_last), _ = lax.optimization_barrier((weights, xhigh))

    def taps_first(weight):
        return jnp.transpose(weight, (2, 3, 4, 0, 1))

    w1, w2, w3, w4 = pl.pallas_call(
        prep_kernel,
        out_shape=[
            jax.ShapeDtypeStruct((16 * XW, (EDGE + 1) * BLK), BF16),
            jax.ShapeDtypeStruct((6 * BLK, BLK), BF16),
            jax.ShapeDtypeStruct((6 * BLK, BLK), BF16),
            jax.ShapeDtypeStruct((EDGE * BLK, 16 * XW), BF16),
        ],
        in_specs=vmem(2) + [pl.BlockSpec(memory_space=pl.ANY)],
        out_specs=vmem(4),
        compiler_params=pltpu.CompilerParams(vmem_limit_bytes=16 * 2**20),
        cost_estimate=pl.CostEstimate(flops=10**9, bytes_accessed=10**7, transcendentals=0),
        name="band_weights",
    )(
        jnp.concatenate([taps_first(conv_second), taps_first(conv_third)]).reshape(54 * CH, CH),
        jnp.concatenate(
            [jnp.transpose(conv_first, (1, 2, 3, 4, 0)), jnp.transpose(conv_last, (0, 2, 3, 4, 1))]
        ),
        xhigh,
    )

    yw, nf = ty + 2 * H, FX + 2
    fault, prob, slope = pl.pallas_call(
        functools.partial(net_kernel, grid_x, grid_y, ty),
        out_shape=[
            jax.ShapeDtypeStruct((TX, ty, NT), BF16),
            jax.ShapeDtypeStruct((FX * yw, NT), F32),
            jax.ShapeDtypeStruct((2, nf, yw, NT), F32),
        ],
        in_specs=vmem(9),
        out_specs=vmem(3),
        scratch_shapes=[
            pltpu.VMEM(((XW + 2) * yw, NT), F32),
            pltpu.VMEM((yw + 2, XW, NT), BF16),
            pltpu.VMEM((3, RING, EDGE + 1, PAIRS, BLK), BF16),
            pltpu.VMEM((3, RING, EDGE, PAIRS, BLK), BF16),
            pltpu.VMEM((yw // 2, EDGE, PAIRS, BLK), BF16),
            pltpu.VMEM((3, FX + 4, yw, NT), F32),
            pltpu.VMEM((yw // 2, NT, 128), F32),
        ],
        compiler_params=pltpu.CompilerParams(vmem_limit_bytes=40 * 2**20),
        cost_estimate=pl.CostEstimate(
            flops=3 * 10**10, bytes_accessed=10**7, transcendentals=10**6
        ),
        name="fault_net",
    )(amplitude, xlow, xhigh, ylow, yhigh, w1, w2, w3, w4)

    rows = TX // n_gy
    moments, face, wave2, *waves = pl.pallas_call(
        functools.partial(waves_kernel, grid_x, grid_y, ty),
        out_shape=[
            jax.ShapeDtypeStruct((8, NT), F32),
            jax.ShapeDtypeStruct((2, nf, yw, NT), F32),
            jax.ShapeDtypeStruct((nf, yw, NT), F32),
        ]
        + [jax.ShapeDtypeStruct((3, rows, ty, NT), BF16)] * n_gy,
        in_specs=vmem(2),
        out_specs=vmem(3 + n_gy),
        scratch_shapes=[
            pltpu.VMEM((2, nf, yw, NT), F32),
            pltpu.VMEM((2, nf, yw, NT), F32),
            pltpu.VMEM((nf, yw, NT), F32),
            pltpu.VMEM((nf, yw, NT), F32),
            pltpu.VMEM((nf, yw, NT), F32),
        ],
        compiler_params=pltpu.CompilerParams(vmem_limit_bytes=24 * 2**20),
        cost_estimate=pl.CostEstimate(flops=10**8, bytes_accessed=10**7, transcendentals=0),
        name="solver_waves",
    )(prob, slope)

    arrived = [waves[0]]
    for place in range(1, n_gy):
        pairs = [(i, (i + place) % n_gy) for i in range(n_gy)]
        arrived.append(lax.ppermute(waves[place], "gy", pairs))

    everyone = pl.pallas_call(
        functools.partial(last_kernel, ty),
        out_shape=jax.ShapeDtypeStruct((n_gx * n_gy, 1, NT), F32),
        in_specs=vmem(3),
        out_specs=pl.BlockSpec(memory_space=pltpu.VMEM),
        compiler_params=pltpu.CompilerParams(vmem_limit_bytes=16 * 2**20),
        cost_estimate=pl.CostEstimate(flops=10**9, bytes_accessed=10**8, transcendentals=0),
        name="last_moment",
    )(moments, face, wave2)
    moments = lax.all_to_all(everyone, ("gx", "gy"), split_axis=0, concat_axis=0, tiled=True)
    shift_field = pl.pallas_call(
        functools.partial(combine_kernel, n_gy, ty),
        out_shape=jax.ShapeDtypeStruct((rows, grid_y, NT), F32),
        in_specs=vmem(1 + n_gy),
        out_specs=pl.BlockSpec(memory_space=pltpu.VMEM),
        compiler_params=pltpu.CompilerParams(vmem_limit_bytes=16 * 2**20),
        name="combine_waves",
    )(moments, *arrived)
    return (fault, shift_field)


def solution(mesh):
    return jax.shard_map(
        on_device,
        mesh=mesh,
        in_specs=(P("gx", "gy", None), P(), P(), P(), P()),
        out_specs=(P("gx", "gy", None), P(("gx", "gy"), None, None)),
        check_vma=False,
    )
```

```python
import functools

import jax
import jax.numpy as jnp
from jax import lax
from jax.experimental import pallas as pl
from jax.experimental.pallas import tpu as pltpu
from jax.sharding import PartitionSpec as P

MU_DIAG = 0.05
ETA_TIME = 0.5

TX, NT, H = 16, 128, 8
CH = 16
XW = TX + 2 * H
FX = TX + 8
RX = 4
FIRST, STEP = 8, 4
RING1, RING2 = 16, 12
Y_SLOTS = (1, 2, 3, 0)
GROUP = 5
BLK = 256
EDGE = 7
SUB = 16
PAIRS = NT // 2

F32 = jnp.float32
BF16 = jnp.bfloat16


def iota(shape, dim):
    return lax.broadcasted_iota(jnp.int32, shape, dim)


def dot_nt(a, b):
    return lax.dot_general(a, b, (((1,), (1,)), ((), ())), preferred_element_type=F32)


def prep_kernel(inner_ref, outer_ref, after_ref, w1_ref, w2_ref, w3_ref, w4_ref):
    del after_ref
    spread = jnp.where(iota((CH, BLK), 1) % CH == iota((CH, BLK), 0), 1.0, 0.0).astype(BF16)
    unit = jnp.where(iota((BLK, BLK), 1) == iota((BLK, BLK), 0), 1.0, 0.0).astype(BF16)
    none = jnp.zeros((CH, BLK), BF16)
    cell = iota((CH, BLK), 1) // CH
    at_cell = [cell == at for at in range(16)]
    inputs = input_cells()
    tiled = jnp.dot(inner_ref[...], spread, preferred_element_type=F32).astype(BF16)
    for layer, ref in enumerate((w2_ref, w3_ref)):
        for tile in range(6):
            bands = []
            for yo in range(2):
                for to in range(2):
                    for xo in range(4):
                        band = none
                        for at, (y, t, x) in enumerate(inputs[tile]):
                            dx, dy, dt = x - xo + 1, y - yo + 1, t - to + 1
                            if min(dx, dy, dt) >= 0 and max(dx, dy, dt) <= 2:
                                tap = tiled[(layer * 27 + dx * 9 + dy * 3 + dt) * CH :][:CH]
                                band = jnp.where(at_cell[at], tap, band)
                        bands.append(band)
            turned = dot_nt(unit, jnp.concatenate(bands, axis=0))
            ref[tile * BLK : (tile + 1) * BLK, :] = turned.astype(BF16)

    def taps(which):
        found = {}
        for dx in range(3):
            for dy in range(3):
                tiled = jnp.dot(outer_ref[which, dx, dy], spread, preferred_element_type=F32)
                for dt in range(3):
                    found[dx, dy, dt] = tiled[dt : dt + 1]
        return found

    first, last = taps(0), taps(1)
    lane_yt = iota((1, BLK), 1) // 64
    quarter = [lane_yt == at for at in range(4)]

    def by_quarter(found, dx, at):
        value = jnp.zeros((1, BLK), F32)
        for y in range(2):
            for t in range(2):
                dy, dt = at(y, t)
                if 0 <= dy <= 2 and 0 <= dt <= 2:
                    value = jnp.where(quarter[y * 2 + t], found[dx, dy, dt], value)
        return value

    def rows_of(found, rows, at):
        return [
            jnp.broadcast_to(by_quarter(found, dx, at), (rows, BLK)).astype(BF16)
            for dx in range(3)
        ]

    row_x = iota((XW, BLK), 0)
    lane_x = iota((XW, BLK), 1) // CH % 4
    offset_x = [row_x - 1 - 4 * blk - lane_x for blk in range(EDGE)]
    offset_x.append(jnp.where(lane_x == 0, row_x - 29, jnp.where(lane_x == 3, row_x, -1)))
    masks = [[offset == dx for dx in range(3)] for offset in offset_x]
    none = jnp.zeros((XW, BLK), BF16)
    for j in range(4):
        for yi in range(4):
            row = (j * 4 + yi) * XW
            values = rows_of(first, XW, lambda y, t: (yi - y, j - t))
            for blk in range(EDGE + 1):
                band = none
                for dx in range(3):
                    band = jnp.where(masks[blk][dx], values[dx], band)
                w1_ref[row : row + XW, blk * BLK : (blk + 1) * BLK] = band
    masks = [
        [4 * blk + lane_x - 1 - row_x == dx for dx in range(3)] for blk in range(EDGE)
    ]
    bands = [[] for blk in range(EDGE)]
    for j in range(4):
        for yi in Y_SLOTS:
            values = rows_of(last, XW, lambda y, t: (y + 2 - yi, t + 2 - j))
            for blk in range(EDGE):
                band = none
                for dx in range(3):
                    band = jnp.where(masks[blk][dx], values[dx], band)
                bands[blk].append(band)
    for blk in range(EDGE):
        turned = dot_nt(unit, jnp.concatenate(bands[blk], axis=0))
        w4_ref[blk * BLK : (blk + 1) * BLK, :] = turned.astype(BF16)


def slices_kernel(amp_ref, first_x, last_x, first_y, last_y):
    ty = amp_ref.shape[1]
    first_x[...] = amp_ref[:H]
    last_x[...] = amp_ref[TX - H :]
    first_y[...] = amp_ref[:, :H]
    last_y[...] = amp_ref[:, ty - H :]


def input_cells():
    tiles = []
    here = [(t, x) for t in (0, 1) for x in range(4)]
    near = [(2, 2), (2, 3), (-1, 0), (-1, 1), (-1, 2), (-1, 3), (2, 0), (2, 1)]
    side = [(0, 4), (2, -1), (-1, 4), (0, -1), (1, 4), (-1, -1), (2, 4), (1, -1)]
    for cells in (here, near, side):
        for rows in ((0, 1), (-1, 2)):
            tiles.append([(y, t, x) for y in rows for t, x in cells])
    return tiles


def plane_shifts(yw):
    block = (RX, yw, NT)
    lane = iota(block, 2)
    first_lane = lane == 0
    last_lane = lane == NT - 1

    def up_y(v):
        return pltpu.roll(v, yw - 1, 1)

    def down_y(v):
        return pltpu.roll(v, 1, 1)

    def up_t(v, edge=0.0):
        return jnp.where(last_lane, edge, pltpu.roll(v, NT - 1, 2))

    def down_t(v, edge=0.0):
        return jnp.where(first_lane, edge, pltpu.roll(v, 1, 2))

    return block, up_y, down_y, up_t, down_t


def dot(a, b):
    return jnp.dot(a, b, preferred_element_type=F32)


def pair_of(row):
    return row // SUB + (row % SUB) * 4


def lane_masks(x0, grid_x, blocks):
    slot = iota((1, BLK), 1) // CH % 4
    masks = []
    for blk in range(blocks):
        if blk < EDGE:
            at = x0 - 6 + 4 * blk + slot
        else:
            at = x0 + jnp.where(slot == 0, 22, -7)
        masks.append(jnp.where((at >= 0) & (at < grid_x), 1.0, 0.0))
    return masks


def row_mask(y, grid_y):
    at = y + jnp.where(iota((1, BLK), 1) >= 128, 1, 0)
    return jnp.where((at >= 0) & (at < grid_y), 1.0, 0.0)


def lanes16():
    return iota((PAIRS, 128), 1).astype(jnp.int16)


def put(act, pair, blk, values):
    sub_row = iota((SUB, 128), 0)
    lane = lanes16()
    early = (lane >= 32) & (lane < 96)
    values = values.astype(BF16)
    act[0, pair, blk] = values
    for half in range(2):
        turned = pltpu.roll(values[:, half * 128 : (half + 1) * 128], 96, 1)
        head = pltpu.roll(turned[PAIRS - SUB :].astype(F32), 1, 0)
        head = jnp.where(sub_row == 0, 0.0, head).astype(BF16)
        tail = pltpu.roll(turned[:SUB].astype(F32), SUB - 1, 0)
        tail = jnp.where(sub_row == SUB - 1, 0.0, tail).astype(BF16)
        before = jnp.concatenate([head, turned[: PAIRS - SUB]], axis=0)
        after = jnp.concatenate([turned[SUB:], tail], axis=0)
        act[1, pair, blk, :, half * 128 : (half + 1) * 128] = jnp.where(early, before, after)


def put_sides(act, pair, blocks):
    lane = lanes16()
    slot0, slot3, even_slot = (lane & 48) == 0, (lane & 48) == 48, (lane & 16) == 0
    for blk in range(EDGE):
        left, right = (blk - 1) % blocks, (blk + 1) % blocks
        for half in range(2):
            at = slice(half * 128, (half + 1) * 128)
            even = jnp.where(slot0, act[0, pair, right, :, at], act[1, pair, right, :, at])
            odd = jnp.where(slot3, act[0, pair, left, :, at], act[1, pair, left, :, at])
            act[2, pair, blk, :, at] = jnp.where(even_slot, even, odd)


def layer(source, w_ref, pair, count):
    def rows(kind, offset, at):
        found = []
        for i in range(count):
            place = (pair + offset + i) % source.shape[1]
            found.append(source[kind, place, :EDGE, :, at].reshape(EDGE * PAIRS, -1))
        return jnp.concatenate(found, axis=0)

    tiles = []
    for kind in range(3):
        tiles.append(rows(kind, 1, slice(0, BLK)))
        tiles.append(rows(kind, 0, slice(128, BLK)))
        tiles.append(rows(kind, 2, slice(0, 128)))
    return dot(jnp.concatenate(tiles, axis=1), w_ref[...])


def net_kernel(
    grid_x,
    grid_y,
    ty,
    amp_ref,
    xlow_ref,
    xhigh_ref,
    ylow_ref,
    yhigh_ref,
    w1_ref,
    w2_ref,
    w3_ref,
    w4_ref,
    fault_ref,
    prob,
    slope,
    raw,
    amp,
    act1,
    act2,
    act3,
    prod,
    part,
):
    x0 = lax.axis_index("gx") * TX
    y0 = lax.axis_index("gy") * ty
    yw = ty + 2 * H
    pairs1, pairs2 = yw // 2, ty // 2 + 6
    for x in range(XW):
        row = x * yw
        if x < H:
            mid = xlow_ref[x]
        elif x < H + TX:
            mid = amp_ref[x - H]
        else:
            mid = xhigh_ref[x - H - TX]
        raw[row + H : row + H + ty, :] = mid.astype(F32)
        raw[row : row + H, :] = ylow_ref[x].astype(F32)
        raw[row + H + ty : row + yw, :] = yhigh_ref[x].astype(F32)

    def turn(y, carry):
        amp[y + 1] = raw[pl.ds(y, XW, stride=yw), :].astype(BF16)
        return carry

    lax.fori_loop(0, yw, turn, 0, unroll=8)
    amp[0] = jnp.zeros((XW, NT), BF16)
    amp[yw + 1] = jnp.zeros((XW, NT), BF16)

    at_row = iota((4 * PAIRS, NT), 0)
    to_pairs = jnp.where(
        iota((4 * PAIRS, NT), 1) == 2 * pair_of(at_row % PAIRS) - 1 + at_row // PAIRS, 1.0, 0.0
    ).astype(BF16)
    mask = lane_masks(x0, grid_x, EDGE + 1)

    def first(step):
        pieces = []
        for i in range(0, FIRST, 2):
            y = (step * FIRST + i) * 2
            rows = [amp[pl.ds(y + 2 * k, 4)].reshape(4 * XW, NT) for k in range(2)]
            turned = dot_nt(to_pairs, jnp.concatenate(rows, axis=0)).astype(BF16)
            for k in range(2):
                parts = [turned[j * PAIRS : (j + 1) * PAIRS, k * 128 : (k + 1) * 128] for j in range(4)]
                pieces.append(jnp.concatenate(parts, axis=1))
        pieces = jnp.concatenate(pieces, axis=0)
        for begin in range(0, EDGE + 1, 2):
            result = dot(pieces, w1_ref[:, begin * BLK : (begin + 2) * BLK])
            for i in range(FIRST):
                pair = step * FIRST + i
                inside = row_mask(y0 + 2 * pair - H, grid_y)
                for blk in (begin, begin + 1):
                    lane = (blk - begin) * BLK
                    values = result[i * PAIRS : (i + 1) * PAIRS, lane : lane + BLK]
                    put(act1, pair % RING1, blk, jnp.maximum(values, 0.0) * (mask[blk] * inside))
        for i in range(FIRST):
            put_sides(act1, (step * FIRST + i) % RING1, EDGE + 1)

    def second(begin, end):
        count = end - begin
        result = layer(act1, w2_ref, begin, count)
        for i in range(count):
            pair = begin + i
            inside = row_mask(y0 + 2 * pair - 6, grid_y)
            for blk in range(EDGE):
                at = (i * EDGE + blk) * PAIRS
                values = jnp.maximum(result[at : at + PAIRS], 0.0)
                put(act2, (pair + 1) % RING2, blk, values * (mask[blk] * inside))
            put_sides(act2, (pair + 1) % RING2, EDGE)

    def third(begin, end):
        count = end - begin
        result = layer(act2, w3_ref, begin, count)
        for i in range(count):
            pair = begin + i
            inside = row_mask(y0 + 2 * pair - 6, grid_y)
            for blk in range(EDGE):
                at = (i * EDGE + blk) * PAIRS
                values = jnp.maximum(result[at : at + PAIRS], 0.0)
                act3[pair, blk] = (values * (mask[blk] * inside)).astype(BF16)

    block, up_y, down_y, up_t, down_t = plane_shifts(yw)

    def smooth_yt(v, edge=0.0):
        v = 0.5 * v + 0.25 * (up_t(v, edge) + down_t(v, edge))
        return 0.5 * v + 0.25 * (up_y(v) + down_y(v))

    def amp_rows(x):
        return raw[pl.ds(pl.multiple_of(x * yw, 8), RX * yw), :].reshape(block)

    def products(k):
        here = amp_rows(k + 3)
        grad_x = 0.5 * (amp_rows(k + 4) - amp_rows(k + 2))
        grad_y = 0.5 * (up_y(here) - down_y(here))
        grad_t = 0.5 * (up_t(here) - down_t(here))
        at = pl.ds(k, RX)
        prod[0, at] = smooth_yt(grad_x * grad_t)
        prod[1, at] = smooth_yt(grad_y * grad_t)
        energy = grad_t * grad_t + 0.25 * (grad_x * grad_x + grad_y * grad_y)
        prod[2, at] = smooth_yt(energy, 0.25 * here * here)

    at_lane = iota((NT, 8 * PAIRS), 1) % (4 * PAIRS)
    from_pairs = jnp.where(
        iota((NT, 8 * PAIRS), 0) == 2 * pair_of(at_lane % PAIRS) - 1 + at_lane // PAIRS, 1.0, 0.0
    ).astype(BF16)

    def slopes(k):
        at = pl.ds(k + 1, RX)
        sums = []
        for which in range(3):
            before, here, after = [prod[which, pl.ds(k + i, RX)] for i in range(3)]
            sums.append(0.5 * here + 0.25 * (before + after))
        scale = -1.0 / (sums[2] + 0.05)
        slope[0, at] = sums[0] * scale
        slope[1, at] = sums[1] * scale

    def fourth(begin, end):
        cells = [
            act3[begin:end, blk].reshape((end - begin) * PAIRS, BLK) for blk in range(EDGE)
        ]
        result = dot(jnp.concatenate(cells, axis=1), w4_ref[...])
        for pair in range(begin, end, 2):
            sides = []
            for at in (pair - begin, pair - begin + 1):
                rows = result[at * PAIRS : (at + 1) * PAIRS]
                sides.append(
                    jnp.concatenate([rows[:, j * 128 : (j + 1) * 128] for j in range(4)], axis=0)
                )
            both = jnp.concatenate(sides, axis=1)
            high = both.astype(BF16)
            low = (both - high.astype(F32)).astype(BF16)
            share = dot(from_pairs, jnp.concatenate([high, low], axis=0))
            part[pair] = share[:, :128]
            part[pair + 1] = share[:, 128:]

    lane = iota((NT, 128), 1)

    def order(pair):
        here = part[pair]
        before = pltpu.roll(part[pair - 1], 64, 1)
        after = pltpu.roll(part[pair + 1], 64, 1)
        own = jnp.where(lane < 64, here, after)
        other = jnp.where(
            lane < 32,
            before,
            jnp.where(lane < 64, after, jnp.where(lane < 96, here, part[pair + 2])),
        )
        values = 1.0 / (1.0 + jnp.exp(-(own + other)))
        values = values.astype(BF16).astype(F32).T
        for row in range(4):
            at = pl.ds(2 * pair + 2 + row, FX, stride=yw)
            prob[at, :] = values[row * XW : row * XW + FX]

    def outside(edge):
        for kind in range(3):
            act2[kind, edge % RING2] = jnp.zeros((EDGE, PAIRS, BLK), BF16)

    outside(0)
    for pair in range(pairs2, pairs1):
        act3[pair] = jnp.zeros((EDGE, PAIRS, BLK), BF16)

    for x in range(FX):
        prob[x * yw : x * yw + H, :] = jnp.zeros((H, NT), F32)
        prob[(x + 1) * yw - H : (x + 1) * yw, :] = jnp.zeros((H, NT), F32)
    for which in range(2):
        slope[which, FX + 1] = jnp.zeros((yw, NT), F32)

    done1 = done2 = done3 = done4 = 0
    next_products = next_slopes = 0
    next_order = 1
    last_order = pairs1 - 5
    stage = 0
    while done4 < pairs1 or next_order <= last_order:
        if done2 == pairs2 - STEP:
            outside(pairs2 + 1)
        end1 = min(pairs1, done1 + FIRST) if stage % 2 == 0 else done1
        end2 = max(0, min(pairs2, done2 + STEP, done1 - 2))
        end3 = pairs2 if done2 == pairs2 else max(0, min(done3 + STEP, done2 - 1))
        end4 = pairs1 if done3 == pairs2 else done3 // 8 * 8
        work = []
        for end, done, run in ((end3, done3, third), (end2, done2, second)):
            steps = range(done, end, GROUP)
            work.append([functools.partial(run, at, min(at + GROUP, end)) for at in steps])
        if end1 > done1:
            work.append([functools.partial(first, done1 // FIRST)])
        if end4 > done4:
            work.append([functools.partial(fourth, done4, end4)])
        ready = []
        while next_order <= last_order and next_order + 2 < done4:
            ready.append(functools.partial(order, next_order))
            next_order += 2
        work.append(ready)
        if stage and next_slopes < FX and next_slopes + RX < next_products:
            work.append([functools.partial(slopes, next_slopes)])
            next_slopes += RX
        if stage and next_products <= FX:
            work.append([functools.partial(products, next_products)])
            next_products += RX
        for turn_of in range(max(len(w) for w in work)):
            for w in work:
                if turn_of < len(w):
                    w[turn_of]()
        done1, done2, done3, done4 = end1, end2, end3, end4
        stage += 1
    assert done3 == pairs2 and next_slopes == FX

    for x in range(TX):
        fault_ref[x] = prob[(x + 4) * yw + H : (x + 4) * yw + H + ty, :].astype(BF16)


def owned(total, k, values, ty):
    for row in range(RX):
        ok = (k + row >= 5) & (k + row < 5 + TX)
        total = total + jnp.where(ok, values[row, H : H + ty], 0.0)
    return total


def image_of(wave, face, k, shifts):
    block, up_y, down_y, up_t, down_t = shifts
    at, before, after = [pl.ds(k + i, RX) for i in (0, -1, 1)]
    here = wave[at]
    flow = face[1, at] * (here - up_y(here))
    image = time_part(block) * here - ETA_TIME * (up_t(here) + down_t(here))
    image = image + flow - down_y(flow)
    image = image + face[0, at] * (here - wave[after])
    return here, image + face[0, before] * (here - wave[before])


def time_part(block):
    lane = iota(block, 2)
    count = jnp.where(lane == 0, 0.0, 1.0) + jnp.where(lane == NT - 1, 0.0, 1.0)
    return MU_DIAG + ETA_TIME * count


def waves_kernel(grid_x, grid_y, ty, prob, slope, mom_ref, face, wave2, *refs):
    n_gy = grid_y // ty
    waves_refs = refs[:n_gy]
    weight, flux, inv, wave0, wave1 = refs[n_gy:]
    place_y = lax.axis_index("gy")
    x0 = lax.axis_index("gx") * TX
    y0 = place_y * ty
    yw = ty + 2 * H
    shifts = plane_shifts(yw)
    block, up_y, down_y, up_t, down_t = shifts
    at_y = y0 - H + iota(block, 1)
    mask_y = (at_y >= 0) & (at_y < grid_y)

    def weights(step, carry):
        k = step * RX
        at = pl.ds(k + 1, RX)
        rows = prob[pl.ds(pl.multiple_of(k * yw, 8), RX * yw), :].reshape(block)
        raw_weight = 1.0 - 0.9 * rows
        at_x = x0 - 4 + k + iota(block, 0)
        weight[0, at] = raw_weight
        weight[1, at] = jnp.where(mask_y & (at_x >= 0) & (at_x < grid_x), raw_weight, 0.0)
        return carry

    lax.fori_loop(0, FX // RX, weights, 0)
    for which in range(2):
        weight[which, FX + 1] = jnp.full((yw, NT), 1.0 - which, F32)
        face[which, 0] = jnp.zeros((yw, NT), F32)
        flux[which, 0] = jnp.zeros((yw, NT), F32)

    def faces(step, carry):
        k = step * RX + 1
        at, after = pl.ds(k, RX), pl.ds(k + 1, RX)
        raw_weight = weight[0, at]
        masked = weight[1, at]
        face_x = 2.0 * masked * weight[1, after] / (raw_weight + weight[0, after])
        face_y = 2.0 * masked * up_y(masked) / (raw_weight + up_y(raw_weight))
        slope_y = slope[1, at]
        face[0, at] = face_x
        face[1, at] = face_y
        flux[0, at] = 0.5 * face_x * (slope[0, at] + slope[0, after])
        flux[1, at] = 0.5 * face_y * (slope_y + up_y(slope_y))
        return carry

    lax.fori_loop(0, FX // RX, faces, 0)

    def start(step, total):
        k = step * RX + 1
        at, before = pl.ds(k, RX), pl.ds(k - 1, RX)
        flux_y = flux[1, at]
        face_y = face[1, at]
        right = flux[0, before] - flux[0, at] + down_y(flux_y) - flux_y
        inverse = 1.0 / (time_part(block) + face[0, at] + face[0, before] + face_y + down_y(face_y))
        first_wave = right * inverse
        inv[at] = inverse
        wave0[at] = first_wave
        return owned(total, k, right * first_wave, ty)

    zero = jnp.zeros((ty, NT), F32)
    b0 = lax.fori_loop(0, FX // RX, start, zero)

    def advance(source, target):
        def body(step, totals):
            k = step * RX + 3
            here, image = image_of(source, face, k, shifts)
            at = pl.ds(k, RX)
            after = here - image * inv[at]
            target[at] = after
            return (
                owned(totals[0], k, here * image, ty),
                owned(totals[1], k, after * image, ty),
            )

        return body

    steps = (FX - 4) // RX
    a0, a1 = lax.fori_loop(0, steps, advance(wave0, wave1), (zero, zero))
    a2, a3 = lax.fori_loop(0, steps, advance(wave1, wave2), (zero, zero))
    sums = [jnp.sum(v, axis=0, keepdims=True) for v in (b0, a0, a1, a2, a3)]
    mom_ref[...] = jnp.concatenate(sums + [jnp.zeros((3, NT), F32)], axis=0)

    rows = TX // n_gy
    for place, ref in enumerate(waves_refs):
        to = lax.rem(place_y + place, n_gy) * rows + 5
        for which, wave in enumerate((wave0, wave1, wave2)):
            for row in range(rows):
                ref[which, row] = wave[to + row, H : H + ty, :].astype(BF16)


def last_kernel(ty, mom_ref, face, wave2, out_ref):
    shifts = plane_shifts(ty + 2 * H)

    def finish(step, total):
        k = step * RX + 5
        here, image = image_of(wave2, face, k, shifts)
        return owned(total, k, here * image, ty)

    total = lax.fori_loop(0, TX // RX, finish, jnp.zeros((ty, NT), F32))
    a4 = jnp.sum(total, axis=0, keepdims=True)
    sums = jnp.sum(jnp.where(iota((8, NT), 0) == 5, a4, mom_ref[...]), axis=1, keepdims=True)
    values = jnp.where(iota((8, NT), 0) == iota((8, NT), 1), sums, 0.0)
    values = jnp.sum(values, axis=0, keepdims=True)
    for device in range(out_ref.shape[0]):
        out_ref[device] = values


def combine_kernel(n_gy, ty, mom_ref, *refs):
    waves_refs, out_ref = refs[:n_gy], refs[n_gy]
    place_y = lax.axis_index("gy")
    moments = jnp.sum(mom_ref[...], axis=0)
    b0, a0, a1, a2, a3, a4 = [
        jnp.broadcast_to(moments[:, i : i + 1], (1, NT)) for i in range(6)
    ]
    a0, a1, a2, a3, a4 = [v / b0 for v in (a0, a1, a2, a3, a4)]
    l21 = a1 / a0
    l31 = a2 / a0
    d2 = jnp.maximum(a2 - l21 * a1, 1e-7 * a2 + 1e-30)
    l32 = (a3 - l21 * a2) / d2
    d3 = jnp.maximum(a4 - l31 * a2 - l32 * l32 * d2, 1e-7 * a4 + 1e-30)
    y2 = (1.0 - a0) - l21
    y3 = (1.0 - a0 - a1) - l31 - l32 * y2
    c3 = y3 / d3
    c2 = y2 / d2 - l32 * c3
    c1 = 1.0 / a0 - l21 * c2 - l31 * c3
    for place, ref in enumerate(waves_refs):
        source = lax.rem(place_y - place + n_gy, n_gy)
        at = pl.ds(pl.multiple_of(source * ty, 8), ty)
        for x in range(ref.shape[1]):
            w0, w1, w2 = [ref[which, x].astype(F32) for which in range(3)]
            out_ref[x, at, :] = c1 * w0 + c2 * w1 + c3 * w2


def vmem(count):
    return [pl.BlockSpec(memory_space=pltpu.VMEM)] * count


def on_device(amplitude, conv_first, conv_second, conv_third, conv_last):
    n_gx, n_gy = lax.axis_size("gx"), lax.axis_size("gy")
    ty = amplitude.shape[1]
    grid_x, grid_y = n_gx * TX, n_gy * ty
    assert amplitude.shape == (TX, ty, NT)

    def shift(values, axis, count, step):
        pairs = [(i, i + step) for i in range(count) if 0 <= i + step < count]
        return lax.ppermute(values, axis, pairs)

    first_x, last_x, first_y, last_y = pl.pallas_call(
        slices_kernel,
        out_shape=[jax.ShapeDtypeStruct((H, ty, NT), BF16)] * 2
        + [jax.ShapeDtypeStruct((TX, H, NT), BF16)] * 2,
        in_specs=vmem(1),
        out_specs=vmem(4),
        compiler_params=pltpu.CompilerParams(vmem_limit_bytes=4 * 2**20),
        name="halo_slices",
    )(amplitude)
    xhigh = shift(first_x, "gx", n_gx, -1)
    xlow = shift(last_x, "gx", n_gx, 1)
    ylow = shift(
        jnp.concatenate([xlow[:, ty - H :], last_y, xhigh[:, ty - H :]]), "gy", n_gy, 1
    )
    yhigh = shift(jnp.concatenate([xlow[:, :H], first_y, xhigh[:, :H]]), "gy", n_gy, -1)

    weights = (conv_first, conv_second, conv_third, conv_last)
    (conv_first, conv_second, conv_third, conv_last), _ = lax.optimization_barrier((weights, xhigh))

    def taps_first(weight):
        return jnp.transpose(weight, (2, 3, 4, 0, 1))

    w1, w2, w3, w4 = pl.pallas_call(
        prep_kernel,
        out_shape=[
            jax.ShapeDtypeStruct((16 * XW, (EDGE + 1) * BLK), BF16),
            jax.ShapeDtypeStruct((6 * BLK, BLK), BF16),
            jax.ShapeDtypeStruct((6 * BLK, BLK), BF16),
            jax.ShapeDtypeStruct((EDGE * BLK, 16 * XW), BF16),
        ],
        in_specs=vmem(2) + [pl.BlockSpec(memory_space=pl.ANY)],
        out_specs=vmem(4),
        compiler_params=pltpu.CompilerParams(vmem_limit_bytes=16 * 2**20),
        cost_estimate=pl.CostEstimate(flops=10**9, bytes_accessed=10**7, transcendentals=0),
        name="band_weights",
    )(
        jnp.concatenate([taps_first(conv_second), taps_first(conv_third)]).reshape(54 * CH, CH),
        jnp.concatenate(
            [jnp.transpose(conv_first, (1, 2, 3, 4, 0)), jnp.transpose(conv_last, (0, 2, 3, 4, 1))]
        ),
        xhigh,
    )

    yw, nf = ty + 2 * H, FX + 2
    fault, prob, slope = pl.pallas_call(
        functools.partial(net_kernel, grid_x, grid_y, ty),
        out_shape=[
            jax.ShapeDtypeStruct((TX, ty, NT), BF16),
            jax.ShapeDtypeStruct((FX * yw, NT), F32),
            jax.ShapeDtypeStruct((2, nf, yw, NT), F32),
        ],
        in_specs=vmem(9),
        out_specs=vmem(3),
        scratch_shapes=[
            pltpu.VMEM(((XW + 2) * yw, NT), F32),
            pltpu.VMEM((yw + 2, XW, NT), BF16),
            pltpu.VMEM((3, RING1, EDGE + 1, PAIRS, BLK), BF16),
            pltpu.VMEM((3, RING2, EDGE, PAIRS, BLK), BF16),
            pltpu.VMEM((yw // 2, EDGE, PAIRS, BLK), BF16),
            pltpu.VMEM((3, FX + 4, yw, NT), F32),
            pltpu.VMEM((yw // 2, NT, 128), F32),
        ],
        compiler_params=pltpu.CompilerParams(vmem_limit_bytes=40 * 2**20),
        cost_estimate=pl.CostEstimate(
            flops=3 * 10**10, bytes_accessed=10**7, transcendentals=10**6
        ),
        name="fault_net",
    )(amplitude, xlow, xhigh, ylow, yhigh, w1, w2, w3, w4)

    rows = TX // n_gy
    moments, face, wave2, *waves = pl.pallas_call(
        functools.partial(waves_kernel, grid_x, grid_y, ty),
        out_shape=[
            jax.ShapeDtypeStruct((8, NT), F32),
            jax.ShapeDtypeStruct((2, nf, yw, NT), F32),
            jax.ShapeDtypeStruct((nf, yw, NT), F32),
        ]
        + [jax.ShapeDtypeStruct((3, rows, ty, NT), BF16)] * n_gy,
        in_specs=vmem(2),
        out_specs=vmem(3 + n_gy),
        scratch_shapes=[
            pltpu.VMEM((2, nf, yw, NT), F32),
            pltpu.VMEM((2, nf, yw, NT), F32),
            pltpu.VMEM((nf, yw, NT), F32),
            pltpu.VMEM((nf, yw, NT), F32),
            pltpu.VMEM((nf, yw, NT), F32),
        ],
        compiler_params=pltpu.CompilerParams(vmem_limit_bytes=24 * 2**20),
        cost_estimate=pl.CostEstimate(flops=10**8, bytes_accessed=10**7, transcendentals=0),
        name="solver_waves",
    )(prob, slope)

    arrived = [waves[0]]
    for place in range(1, n_gy):
        pairs = [(i, (i + place) % n_gy) for i in range(n_gy)]
        arrived.append(lax.ppermute(waves[place], "gy", pairs))

    everyone = pl.pallas_call(
        functools.partial(last_kernel, ty),
        out_shape=jax.ShapeDtypeStruct((n_gx * n_gy, 1, NT), F32),
        in_specs=vmem(3),
        out_specs=pl.BlockSpec(memory_space=pltpu.VMEM),
        compiler_params=pltpu.CompilerParams(vmem_limit_bytes=16 * 2**20),
        cost_estimate=pl.CostEstimate(flops=10**9, bytes_accessed=10**8, transcendentals=0),
        name="last_moment",
    )(moments, face, wave2)
    moments = lax.all_to_all(everyone, ("gx", "gy"), split_axis=0, concat_axis=0, tiled=True)
    shift_field = pl.pallas_call(
        functools.partial(combine_kernel, n_gy, ty),
        out_shape=jax.ShapeDtypeStruct((rows, grid_y, NT), F32),
        in_specs=vmem(1 + n_gy),
        out_specs=pl.BlockSpec(memory_space=pltpu.VMEM),
        compiler_params=pltpu.CompilerParams(vmem_limit_bytes=16 * 2**20),
        name="combine_waves",
    )(moments, *arrived)
    return (fault, shift_field)


def solution(mesh):
    return jax.shard_map(
        on_device,
        mesh=mesh,
        in_specs=(P("gx", "gy", None), P(), P(), P(), P()),
        out_specs=(P("gx", "gy", None), P(("gx", "gy"), None, None)),
        check_vma=False,
    )
```

```python
import functools

import jax
import jax.numpy as jnp
from jax import lax
from jax.experimental import pallas as pl
from jax.experimental.pallas import tpu as pltpu
from jax.sharding import PartitionSpec as P

MU_DIAG = 0.05
ETA_TIME = 0.5

TX, NT, H = 16, 128, 8
CH = 16
XW = TX + 2 * H
FX = TX + 8
RX = 4
FIRST = 4
RING = 12
Y_SLOTS = (1, 2, 3, 0)
GROUP = 1
BLK = 256
EDGE = 7
SUB = 16
PAIRS = NT // 2

F32 = jnp.float32
BF16 = jnp.bfloat16


def iota(shape, dim):
    return lax.broadcasted_iota(jnp.int32, shape, dim)


def dot_nt(a, b):
    return lax.dot_general(a, b, (((1,), (1,)), ((), ())), preferred_element_type=F32)


def prep_kernel(inner_ref, outer_ref, after_ref, w1_ref, w2_ref, w3_ref, w4_ref):
    del after_ref
    spread = jnp.where(iota((CH, BLK), 1) % CH == iota((CH, BLK), 0), 1.0, 0.0).astype(BF16)
    unit = jnp.where(iota((BLK, BLK), 1) == iota((BLK, BLK), 0), 1.0, 0.0).astype(BF16)
    none = jnp.zeros((CH, BLK), BF16)
    cell = iota((CH, BLK), 1) // CH
    at_cell = [cell == at for at in range(16)]
    inputs = input_cells()
    tiled = jnp.dot(inner_ref[...], spread, preferred_element_type=F32).astype(BF16)
    for layer, ref in enumerate((w2_ref, w3_ref)):
        for tile in range(6):
            bands = []
            for yo in range(2):
                for to in range(2):
                    for xo in range(4):
                        band = none
                        for at, (y, t, x) in enumerate(inputs[tile]):
                            dx, dy, dt = x - xo + 1, y - yo + 1, t - to + 1
                            if min(dx, dy, dt) >= 0 and max(dx, dy, dt) <= 2:
                                tap = tiled[(layer * 27 + dx * 9 + dy * 3 + dt) * CH :][:CH]
                                band = jnp.where(at_cell[at], tap, band)
                        bands.append(band)
            turned = dot_nt(unit, jnp.concatenate(bands, axis=0))
            ref[tile * BLK : (tile + 1) * BLK, :] = turned.astype(BF16)

    def taps(which):
        found = {}
        for dx in range(3):
            for dy in range(3):
                tiled = jnp.dot(outer_ref[which, dx, dy], spread, preferred_element_type=F32)
                for dt in range(3):
                    found[dx, dy, dt] = tiled[dt : dt + 1]
        return found

    first, last = taps(0), taps(1)
    lane_yt = iota((1, BLK), 1) // 64
    quarter = [lane_yt == at for at in range(4)]

    def by_quarter(found, dx, at):
        value = jnp.zeros((1, BLK), F32)
        for y in range(2):
            for t in range(2):
                dy, dt = at(y, t)
                if 0 <= dy <= 2 and 0 <= dt <= 2:
                    value = jnp.where(quarter[y * 2 + t], found[dx, dy, dt], value)
        return value

    def rows_of(found, rows, at):
        return [
            jnp.broadcast_to(by_quarter(found, dx, at), (rows, BLK)).astype(BF16)
            for dx in range(3)
        ]

    row_x = iota((XW, BLK), 0)
    lane_x = iota((XW, BLK), 1) // CH % 4
    offset_x = [row_x - 1 - 4 * blk - lane_x for blk in range(EDGE)]
    offset_x.append(jnp.where(lane_x == 0, row_x - 29, jnp.where(lane_x == 3, row_x, -1)))
    masks = [[offset == dx for dx in range(3)] for offset in offset_x]
    none = jnp.zeros((XW, BLK), BF16)
    for j in range(4):
        for yi in range(4):
            row = (j * 4 + yi) * XW
            values = rows_of(first, XW, lambda y, t: (yi - y, j - t))
            for blk in range(EDGE + 1):
                band = none
                for dx in range(3):
                    band = jnp.where(masks[blk][dx], values[dx], band)
                w1_ref[row : row + XW, blk * BLK : (blk + 1) * BLK] = band
    masks = [
        [4 * blk + lane_x - 1 - row_x == dx for dx in range(3)] for blk in range(EDGE)
    ]
    bands = [[] for blk in range(EDGE)]
    for j in range(4):
        for yi in Y_SLOTS:
            values = rows_of(last, XW, lambda y, t: (y + 2 - yi, t + 2 - j))
            for blk in range(EDGE):
                band = none
                for dx in range(3):
                    band = jnp.where(masks[blk][dx], values[dx], band)
                bands[blk].append(band)
    for blk in range(EDGE):
        turned = dot_nt(unit, jnp.concatenate(bands[blk], axis=0))
        w4_ref[blk * BLK : (blk + 1) * BLK, :] = turned.astype(BF16)


def slices_kernel(amp_ref, first_x, last_x, first_y, last_y):
    ty = amp_ref.shape[1]
    first_x[...] = amp_ref[:H]
    last_x[...] = amp_ref[TX - H :]
    first_y[...] = amp_ref[:, :H]
    last_y[...] = amp_ref[:, ty - H :]


def input_cells():
    tiles = []
    here = [(t, x) for t in (0, 1) for x in range(4)]
    near = [(2, 2), (2, 3), (-1, 0), (-1, 1), (-1, 2), (-1, 3), (2, 0), (2, 1)]
    side = [(0, 4), (2, -1), (-1, 4), (0, -1), (1, 4), (-1, -1), (2, 4), (1, -1)]
    for cells in (here, near, side):
        for rows in ((0, 1), (-1, 2)):
            tiles.append([(y, t, x) for y in rows for t, x in cells])
    return tiles


def plane_shifts(yw):
    block = (RX, yw, NT)
    lane = iota(block, 2)
    first_lane = lane == 0
    last_lane = lane == NT - 1

    def up_y(v):
        return pltpu.roll(v, yw - 1, 1)

    def down_y(v):
        return pltpu.roll(v, 1, 1)

    def up_t(v, edge=0.0):
        return jnp.where(last_lane, edge, pltpu.roll(v, NT - 1, 2))

    def down_t(v, edge=0.0):
        return jnp.where(first_lane, edge, pltpu.roll(v, 1, 2))

    return block, up_y, down_y, up_t, down_t


def dot(a, b):
    return jnp.dot(a, b, preferred_element_type=F32)


def pair_of(row):
    return row // SUB + (row % SUB) * 4


def lane_masks(x0, grid_x, blocks):
    slot = iota((1, BLK), 1) // CH % 4
    masks = []
    for blk in range(blocks):
        if blk < EDGE:
            at = x0 - 6 + 4 * blk + slot
        else:
            at = x0 + jnp.where(slot == 0, 22, -7)
        masks.append(jnp.where((at >= 0) & (at < grid_x), 1.0, 0.0))
    return masks


def row_mask(y, grid_y):
    at = y + jnp.where(iota((1, BLK), 1) >= 128, 1, 0)
    return jnp.where((at >= 0) & (at < grid_y), 1.0, 0.0)


def lanes16():
    return iota((PAIRS, 128), 1).astype(jnp.int16)


def put(act, pair, blk, values):
    sub_row = iota((SUB, 128), 0)
    lane = lanes16()
    early = (lane >= 32) & (lane < 96)
    values = values.astype(BF16)
    act[0, pair, blk] = values
    for half in range(2):
        turned = pltpu.roll(values[:, half * 128 : (half + 1) * 128], 96, 1)
        head = pltpu.roll(turned[PAIRS - SUB :].astype(F32), 1, 0)
        head = jnp.where(sub_row == 0, 0.0, head).astype(BF16)
        tail = pltpu.roll(turned[:SUB].astype(F32), SUB - 1, 0)
        tail = jnp.where(sub_row == SUB - 1, 0.0, tail).astype(BF16)
        before = jnp.concatenate([head, turned[: PAIRS - SUB]], axis=0)
        after = jnp.concatenate([turned[SUB:], tail], axis=0)
        act[1, pair, blk, :, half * 128 : (half + 1) * 128] = jnp.where(early, before, after)


def put_sides(act, pair, blocks):
    lane = lanes16()
    slot0, slot3, even_slot = (lane & 48) == 0, (lane & 48) == 48, (lane & 16) == 0
    for blk in range(EDGE):
        left, right = (blk - 1) % blocks, (blk + 1) % blocks
        for half in range(2):
            at = slice(half * 128, (half + 1) * 128)
            even = jnp.where(slot0, act[0, pair, right, :, at], act[1, pair, right, :, at])
            odd = jnp.where(slot3, act[0, pair, left, :, at], act[1, pair, left, :, at])
            act[2, pair, blk, :, at] = jnp.where(even_slot, even, odd)


def layer(source, w_ref, pair, count):
    def rows(kind, offset, at):
        found = []
        for i in range(count):
            place = (pair + offset + i) % RING
            found.append(source[kind, place, :EDGE, :, at].reshape(EDGE * PAIRS, -1))
        return jnp.concatenate(found, axis=0)

    tiles = []
    for kind in range(3):
        tiles.append(rows(kind, 1, slice(0, BLK)))
        tiles.append(rows(kind, 0, slice(128, BLK)))
        tiles.append(rows(kind, 2, slice(0, 128)))
    return dot(jnp.concatenate(tiles, axis=1), w_ref[...])


def net_kernel(
    grid_x,
    grid_y,
    ty,
    amp_ref,
    xlow_ref,
    xhigh_ref,
    ylow_ref,
    yhigh_ref,
    w1_ref,
    w2_ref,
    w3_ref,
    w4_ref,
    fault_ref,
    prob,
    slope,
    raw,
    amp,
    act1,
    act2,
    act3,
    prod,
    part,
):
    x0 = lax.axis_index("gx") * TX
    y0 = lax.axis_index("gy") * ty
    yw = ty + 2 * H
    pairs1, pairs2 = yw // 2, ty // 2 + 6
    for x in range(XW):
        row = x * yw
        if x < H:
            mid = xlow_ref[x]
        elif x < H + TX:
            mid = amp_ref[x - H]
        else:
            mid = xhigh_ref[x - H - TX]
        raw[row + H : row + H + ty, :] = mid.astype(F32)
        raw[row : row + H, :] = ylow_ref[x].astype(F32)
        raw[row + H + ty : row + yw, :] = yhigh_ref[x].astype(F32)

    def turn(y, carry):
        amp[y + 1] = raw[pl.ds(y, XW, stride=yw), :].astype(BF16)
        return carry

    lax.fori_loop(0, yw, turn, 0, unroll=8)
    amp[0] = jnp.zeros((XW, NT), BF16)
    amp[yw + 1] = jnp.zeros((XW, NT), BF16)

    at_row = iota((4 * PAIRS, NT), 0)
    to_pairs = jnp.where(
        iota((4 * PAIRS, NT), 1) == 2 * pair_of(at_row % PAIRS) - 1 + at_row // PAIRS, 1.0, 0.0
    ).astype(BF16)
    mask = lane_masks(x0, grid_x, EDGE + 1)

    def first(step):
        pieces = []
        for i in range(0, FIRST, 2):
            y = (step * FIRST + i) * 2
            rows = [amp[pl.ds(y + 2 * k, 4)].reshape(4 * XW, NT) for k in range(2)]
            turned = dot_nt(to_pairs, jnp.concatenate(rows, axis=0)).astype(BF16)
            for k in range(2):
                parts = [turned[j * PAIRS : (j + 1) * PAIRS, k * 128 : (k + 1) * 128] for j in range(4)]
                pieces.append(jnp.concatenate(parts, axis=1))
        pieces = jnp.concatenate(pieces, axis=0)
        for begin in range(0, EDGE + 1, 2):
            result = dot(pieces, w1_ref[:, begin * BLK : (begin + 2) * BLK])
            for i in range(FIRST):
                pair = step * FIRST + i
                inside = row_mask(y0 + 2 * pair - H, grid_y)
                for blk in (begin, begin + 1):
                    lane = (blk - begin) * BLK
                    values = result[i * PAIRS : (i + 1) * PAIRS, lane : lane + BLK]
                    put(act1, pair % RING, blk, jnp.maximum(values, 0.0) * (mask[blk] * inside))
        for i in range(FIRST):
            put_sides(act1, (step * FIRST + i) % RING, EDGE + 1)

    def second(begin, end):
        count = end - begin
        result = layer(act1, w2_ref, begin, count)
        for i in range(count):
            pair = begin + i
            inside = row_mask(y0 + 2 * pair - 6, grid_y)
            for blk in range(EDGE):
                at = (i * EDGE + blk) * PAIRS
                values = jnp.maximum(result[at : at + PAIRS], 0.0)
                put(act2, (pair + 1) % RING, blk, values * (mask[blk] * inside))
            put_sides(act2, (pair + 1) % RING, EDGE)

    def third(begin, end):
        count = end - begin
        result = layer(act2, w3_ref, begin, count)
        for i in range(count):
            pair = begin + i
            inside = row_mask(y0 + 2 * pair - 6, grid_y)
            for blk in range(EDGE):
                at = (i * EDGE + blk) * PAIRS
                values = jnp.maximum(result[at : at + PAIRS], 0.0)
                act3[pair, blk] = (values * (mask[blk] * inside)).astype(BF16)

    block, up_y, down_y, up_t, down_t = plane_shifts(yw)

    def smooth_yt(v, edge=0.0):
        v = 0.5 * v + 0.25 * (up_t(v, edge) + down_t(v, edge))
        return 0.5 * v + 0.25 * (up_y(v) + down_y(v))

    def amp_rows(x):
        return raw[pl.ds(pl.multiple_of(x * yw, 8), RX * yw), :].reshape(block)

    def products(k):
        here = amp_rows(k + 3)
        grad_x = 0.5 * (amp_rows(k + 4) - amp_rows(k + 2))
        grad_y = 0.5 * (up_y(here) - down_y(here))
        grad_t = 0.5 * (up_t(here) - down_t(here))
        at = pl.ds(k, RX)
        prod[0, at] = smooth_yt(grad_x * grad_t)
        prod[1, at] = smooth_yt(grad_y * grad_t)
        energy = grad_t * grad_t + 0.25 * (grad_x * grad_x + grad_y * grad_y)
        prod[2, at] = smooth_yt(energy, 0.25 * here * here)

    at_lane = iota((NT, 8 * PAIRS), 1) % (4 * PAIRS)
    from_pairs = jnp.where(
        iota((NT, 8 * PAIRS), 0) == 2 * pair_of(at_lane % PAIRS) - 1 + at_lane // PAIRS, 1.0, 0.0
    ).astype(BF16)

    def slopes(k):
        at = pl.ds(k + 1, RX)
        sums = []
        for which in range(3):
            before, here, after = [prod[which, pl.ds(k + i, RX)] for i in range(3)]
            sums.append(0.5 * here + 0.25 * (before + after))
        scale = -1.0 / (sums[2] + 0.05)
        slope[0, at] = sums[0] * scale
        slope[1, at] = sums[1] * scale

    def fourth(begin, end):
        cells = [
            act3[begin:end, blk].reshape((end - begin) * PAIRS, BLK) for blk in range(EDGE)
        ]
        result = dot(jnp.concatenate(cells, axis=1), w4_ref[...])
        for pair in range(begin, end, 2):
            sides = []
            for at in (pair - begin, pair - begin + 1):
                rows = result[at * PAIRS : (at + 1) * PAIRS]
                sides.append(
                    jnp.concatenate([rows[:, j * 128 : (j + 1) * 128] for j in range(4)], axis=0)
                )
            both = jnp.concatenate(sides, axis=1)
            high = both.astype(BF16)
            low = (both - high.astype(F32)).astype(BF16)
            share = dot(from_pairs, jnp.concatenate([high, low], axis=0))
            part[pair] = share[:, :128]
            part[pair + 1] = share[:, 128:]

    lane = iota((NT, 128), 1)

    def order(pair):
        here = part[pair]
        before = pltpu.roll(part[pair - 1], 64, 1)
        after = pltpu.roll(part[pair + 1], 64, 1)
        own = jnp.where(lane < 64, here, after)
        other = jnp.where(
            lane < 32,
            before,
            jnp.where(lane < 64, after, jnp.where(lane < 96, here, part[pair + 2])),
        )
        values = 1.0 / (1.0 + jnp.exp(-(own + other)))
        values = values.astype(BF16).astype(F32).T
        for row in range(4):
            at = pl.ds(2 * pair + 2 + row, FX, stride=yw)
            prob[at, :] = values[row * XW : row * XW + FX]

    def outside(edge):
        for kind in range(3):
            act2[kind, edge % RING] = jnp.zeros((EDGE, PAIRS, BLK), BF16)

    outside(0)
    for pair in range(pairs2, pairs1):
        act3[pair] = jnp.zeros((EDGE, PAIRS, BLK), BF16)

    for x in range(FX):
        prob[x * yw : x * yw + H, :] = jnp.zeros((H, NT), F32)
        prob[(x + 1) * yw - H : (x + 1) * yw, :] = jnp.zeros((H, NT), F32)
    for which in range(2):
        slope[which, FX + 1] = jnp.zeros((yw, NT), F32)

    chunks = pairs1 // FIRST
    done2 = done3 = done4 = 0
    next_products = next_slopes = 0
    next_order = 1
    last_order = pairs1 - 5
    for stage in range(chunks + 4):
        if stage == chunks:
            outside(pairs2 + 1)
        end2 = max(0, min(pairs2, stage * FIRST - 2))
        end3 = pairs2 if done2 == pairs2 else max(0, done2 - 1)
        end4 = pairs1 if done3 == pairs2 else done3 // 4 * 4
        work = []
        for end, done, run in ((end3, done3, third), (end2, done2, second)):
            steps = range(done, end, GROUP)
            work.append([functools.partial(run, at, min(at + GROUP, end)) for at in steps])
        if stage < chunks:
            work.append([functools.partial(first, stage)])
        if end4 > done4:
            work.append([functools.partial(fourth, done4, end4)])
        ready = []
        while next_order <= last_order and next_order + 2 < done4:
            ready.append(functools.partial(order, next_order))
            next_order += 2
        work.append(ready)
        if stage and next_slopes < FX and next_slopes + RX < next_products:
            work.append([functools.partial(slopes, next_slopes)])
            next_slopes += RX
        if stage and next_products <= FX:
            work.append([functools.partial(products, next_products)])
            next_products += RX
        for turn_of in range(max(len(w) for w in work)):
            for w in work:
                if turn_of < len(w):
                    w[turn_of]()
        done2, done3, done4 = end2, end3, end4
    assert done4 == pairs1 and next_order > last_order and next_slopes == FX

    for x in range(TX):
        fault_ref[x] = prob[(x + 4) * yw + H : (x + 4) * yw + H + ty, :].astype(BF16)


def owned(total, k, values, ty):
    for row in range(RX):
        ok = (k + row >= 5) & (k + row < 5 + TX)
        total = total + jnp.where(ok, values[row, H : H + ty], 0.0)
    return total


def image_of(wave, face, k, shifts):
    block, up_y, down_y, up_t, down_t = shifts
    at, before, after = [pl.ds(k + i, RX) for i in (0, -1, 1)]
    here = wave[at]
    flow = face[1, at] * (here - up_y(here))
    image = time_part(block) * here - ETA_TIME * (up_t(here) + down_t(here))
    image = image + flow - down_y(flow)
    image = image + face[0, at] * (here - wave[after])
    return here, image + face[0, before] * (here - wave[before])


def time_part(block):
    lane = iota(block, 2)
    count = jnp.where(lane == 0, 0.0, 1.0) + jnp.where(lane == NT - 1, 0.0, 1.0)
    return MU_DIAG + ETA_TIME * count


def waves_kernel(grid_x, grid_y, ty, prob, slope, mom_ref, face, wave2, *refs):
    n_gy = grid_y // ty
    waves_refs = refs[:n_gy]
    weight, flux, inv, wave0, wave1 = refs[n_gy:]
    place_y = lax.axis_index("gy")
    x0 = lax.axis_index("gx") * TX
    y0 = place_y * ty
    yw = ty + 2 * H
    shifts = plane_shifts(yw)
    block, up_y, down_y, up_t, down_t = shifts
    at_y = y0 - H + iota(block, 1)
    mask_y = (at_y >= 0) & (at_y < grid_y)

    def weights(step, carry):
        k = step * RX
        at = pl.ds(k + 1, RX)
        rows = prob[pl.ds(pl.multiple_of(k * yw, 8), RX * yw), :].reshape(block)
        raw_weight = 1.0 - 0.9 * rows
        at_x = x0 - 4 + k + iota(block, 0)
        weight[0, at] = raw_weight
        weight[1, at] = jnp.where(mask_y & (at_x >= 0) & (at_x < grid_x), raw_weight, 0.0)
        return carry

    lax.fori_loop(0, FX // RX, weights, 0)
    for which in range(2):
        weight[which, FX + 1] = jnp.full((yw, NT), 1.0 - which, F32)
        face[which, 0] = jnp.zeros((yw, NT), F32)
        flux[which, 0] = jnp.zeros((yw, NT), F32)

    def faces(step, carry):
        k = step * RX + 1
        at, after = pl.ds(k, RX), pl.ds(k + 1, RX)
        raw_weight = weight[0, at]
        masked = weight[1, at]
        face_x = 2.0 * masked * weight[1, after] / (raw_weight + weight[0, after])
        face_y = 2.0 * masked * up_y(masked) / (raw_weight + up_y(raw_weight))
        slope_y = slope[1, at]
        face[0, at] = face_x
        face[1, at] = face_y
        flux[0, at] = 0.5 * face_x * (slope[0, at] + slope[0, after])
        flux[1, at] = 0.5 * face_y * (slope_y + up_y(slope_y))
        return carry

    lax.fori_loop(0, FX // RX, faces, 0)

    def start(step, total):
        k = step * RX + 1
        at, before = pl.ds(k, RX), pl.ds(k - 1, RX)
        flux_y = flux[1, at]
        face_y = face[1, at]
        right = flux[0, before] - flux[0, at] + down_y(flux_y) - flux_y
        inverse = 1.0 / (time_part(block) + face[0, at] + face[0, before] + face_y + down_y(face_y))
        first_wave = right * inverse
        inv[at] = inverse
        wave0[at] = first_wave
        return owned(total, k, right * first_wave, ty)

    zero = jnp.zeros((ty, NT), F32)
    b0 = lax.fori_loop(0, FX // RX, start, zero)

    def advance(source, target):
        def body(step, totals):
            k = step * RX + 3
            here, image = image_of(source, face, k, shifts)
            at = pl.ds(k, RX)
            after = here - image * inv[at]
            target[at] = after
            return (
                owned(totals[0], k, here * image, ty),
                owned(totals[1], k, after * image, ty),
            )

        return body

    steps = (FX - 4) // RX
    a0, a1 = lax.fori_loop(0, steps, advance(wave0, wave1), (zero, zero))
    a2, a3 = lax.fori_loop(0, steps, advance(wave1, wave2), (zero, zero))
    sums = [jnp.sum(v, axis=0, keepdims=True) for v in (b0, a0, a1, a2, a3)]
    mom_ref[...] = jnp.concatenate(sums + [jnp.zeros((3, NT), F32)], axis=0)

    rows = TX // n_gy
    for place, ref in enumerate(waves_refs):
        to = lax.rem(place_y + place, n_gy) * rows + 5
        for which, wave in enumerate((wave0, wave1, wave2)):
            for row in range(rows):
                ref[which, row] = wave[to + row, H : H + ty, :].astype(BF16)


def last_kernel(ty, mom_ref, face, wave2, out_ref):
    shifts = plane_shifts(ty + 2 * H)

    def finish(step, total):
        k = step * RX + 5
        here, image = image_of(wave2, face, k, shifts)
        return owned(total, k, here * image, ty)

    total = lax.fori_loop(0, TX // RX, finish, jnp.zeros((ty, NT), F32))
    a4 = jnp.sum(total, axis=0, keepdims=True)
    sums = jnp.sum(jnp.where(iota((8, NT), 0) == 5, a4, mom_ref[...]), axis=1, keepdims=True)
    values = jnp.where(iota((8, NT), 0) == iota((8, NT), 1), sums, 0.0)
    values = jnp.sum(values, axis=0, keepdims=True)
    for device in range(out_ref.shape[0]):
        out_ref[device] = values


def combine_kernel(n_gy, ty, mom_ref, *refs):
    waves_refs, out_ref = refs[:n_gy], refs[n_gy]
    place_y = lax.axis_index("gy")
    moments = jnp.sum(mom_ref[...], axis=0)
    b0, a0, a1, a2, a3, a4 = [
        jnp.broadcast_to(moments[:, i : i + 1], (1, NT)) for i in range(6)
    ]
    a0, a1, a2, a3, a4 = [v / b0 for v in (a0, a1, a2, a3, a4)]
    l21 = a1 / a0
    l31 = a2 / a0
    d2 = jnp.maximum(a2 - l21 * a1, 1e-7 * a2 + 1e-30)
    l32 = (a3 - l21 * a2) / d2
    d3 = jnp.maximum(a4 - l31 * a2 - l32 * l32 * d2, 1e-7 * a4 + 1e-30)
    y2 = (1.0 - a0) - l21
    y3 = (1.0 - a0 - a1) - l31 - l32 * y2
    c3 = y3 / d3
    c2 = y2 / d2 - l32 * c3
    c1 = 1.0 / a0 - l21 * c2 - l31 * c3
    for place, ref in enumerate(waves_refs):
        source = lax.rem(place_y - place + n_gy, n_gy)
        at = pl.ds(pl.multiple_of(source * ty, 8), ty)
        for x in range(ref.shape[1]):
            w0, w1, w2 = [ref[which, x].astype(F32) for which in range(3)]
            out_ref[x, at, :] = c1 * w0 + c2 * w1 + c3 * w2


def vmem(count):
    return [pl.BlockSpec(memory_space=pltpu.VMEM)] * count


def on_device(amplitude, conv_first, conv_second, conv_third, conv_last):
    n_gx, n_gy = lax.axis_size("gx"), lax.axis_size("gy")
    ty = amplitude.shape[1]
    grid_x, grid_y = n_gx * TX, n_gy * ty
    assert amplitude.shape == (TX, ty, NT)

    def shift(values, axis, count, step):
        pairs = [(i, i + step) for i in range(count) if 0 <= i + step < count]
        return lax.ppermute(values, axis, pairs)

    first_x, last_x, first_y, last_y = pl.pallas_call(
        slices_kernel,
        out_shape=[jax.ShapeDtypeStruct((H, ty, NT), BF16)] * 2
        + [jax.ShapeDtypeStruct((TX, H, NT), BF16)] * 2,
        in_specs=vmem(1),
        out_specs=vmem(4),
        compiler_params=pltpu.CompilerParams(vmem_limit_bytes=4 * 2**20),
        name="halo_slices",
    )(amplitude)
    xhigh = shift(first_x, "gx", n_gx, -1)
    xlow = shift(last_x, "gx", n_gx, 1)
    ylow = shift(
        jnp.concatenate([xlow[:, ty - H :], last_y, xhigh[:, ty - H :]]), "gy", n_gy, 1
    )
    yhigh = shift(jnp.concatenate([xlow[:, :H], first_y, xhigh[:, :H]]), "gy", n_gy, -1)

    weights = (conv_first, conv_second, conv_third, conv_last)
    (conv_first, conv_second, conv_third, conv_last), _ = lax.optimization_barrier((weights, xhigh))

    def taps_first(weight):
        return jnp.transpose(weight, (2, 3, 4, 0, 1))

    w1, w2, w3, w4 = pl.pallas_call(
        prep_kernel,
        out_shape=[
            jax.ShapeDtypeStruct((16 * XW, (EDGE + 1) * BLK), BF16),
            jax.ShapeDtypeStruct((6 * BLK, BLK), BF16),
            jax.ShapeDtypeStruct((6 * BLK, BLK), BF16),
            jax.ShapeDtypeStruct((EDGE * BLK, 16 * XW), BF16),
        ],
        in_specs=vmem(2) + [pl.BlockSpec(memory_space=pl.ANY)],
        out_specs=vmem(4),
        compiler_params=pltpu.CompilerParams(vmem_limit_bytes=16 * 2**20),
        cost_estimate=pl.CostEstimate(flops=10**9, bytes_accessed=10**7, transcendentals=0),
        name="band_weights",
    )(
        jnp.concatenate([taps_first(conv_second), taps_first(conv_third)]).reshape(54 * CH, CH),
        jnp.concatenate(
            [jnp.transpose(conv_first, (1, 2, 3, 4, 0)), jnp.transpose(conv_last, (0, 2, 3, 4, 1))]
        ),
        xhigh,
    )

    yw, nf = ty + 2 * H, FX + 2
    fault, prob, slope = pl.pallas_call(
        functools.partial(net_kernel, grid_x, grid_y, ty),
        out_shape=[
            jax.ShapeDtypeStruct((TX, ty, NT), BF16),
            jax.ShapeDtypeStruct((FX * yw, NT), F32),
            jax.ShapeDtypeStruct((2, nf, yw, NT), F32),
        ],
        in_specs=vmem(9),
        out_specs=vmem(3),
        scratch_shapes=[
            pltpu.VMEM(((XW + 2) * yw, NT), F32),
            pltpu.VMEM((yw + 2, XW, NT), BF16),
            pltpu.VMEM((3, RING, EDGE + 1, PAIRS, BLK), BF16),
            pltpu.VMEM((3, RING, EDGE, PAIRS, BLK), BF16),
            pltpu.VMEM((yw // 2, EDGE, PAIRS, BLK), BF16),
            pltpu.VMEM((3, FX + 4, yw, NT), F32),
            pltpu.VMEM((yw // 2, NT, 128), F32),
        ],
        compiler_params=pltpu.CompilerParams(vmem_limit_bytes=40 * 2**20),
        cost_estimate=pl.CostEstimate(
            flops=3 * 10**10, bytes_accessed=10**7, transcendentals=10**6
        ),
        name="fault_net",
    )(amplitude, xlow, xhigh, ylow, yhigh, w1, w2, w3, w4)

    rows = TX // n_gy
    moments, face, wave2, *waves = pl.pallas_call(
        functools.partial(waves_kernel, grid_x, grid_y, ty),
        out_shape=[
            jax.ShapeDtypeStruct((8, NT), F32),
            jax.ShapeDtypeStruct((2, nf, yw, NT), F32),
            jax.ShapeDtypeStruct((nf, yw, NT), F32),
        ]
        + [jax.ShapeDtypeStruct((3, rows, ty, NT), BF16)] * n_gy,
        in_specs=vmem(2),
        out_specs=vmem(3 + n_gy),
        scratch_shapes=[
            pltpu.VMEM((2, nf, yw, NT), F32),
            pltpu.VMEM((2, nf, yw, NT), F32),
            pltpu.VMEM((nf, yw, NT), F32),
            pltpu.VMEM((nf, yw, NT), F32),
            pltpu.VMEM((nf, yw, NT), F32),
        ],
        compiler_params=pltpu.CompilerParams(vmem_limit_bytes=24 * 2**20),
        cost_estimate=pl.CostEstimate(flops=10**8, bytes_accessed=10**7, transcendentals=0),
        name="solver_waves",
    )(prob, slope)

    arrived = [waves[0]]
    for place in range(1, n_gy):
        pairs = [(i, (i + place) % n_gy) for i in range(n_gy)]
        arrived.append(lax.ppermute(waves[place], "gy", pairs))

    everyone = pl.pallas_call(
        functools.partial(last_kernel, ty),
        out_shape=jax.ShapeDtypeStruct((n_gx * n_gy, 1, NT), F32),
        in_specs=vmem(3),
        out_specs=pl.BlockSpec(memory_space=pltpu.VMEM),
        compiler_params=pltpu.CompilerParams(vmem_limit_bytes=16 * 2**20),
        cost_estimate=pl.CostEstimate(flops=10**9, bytes_accessed=10**8, transcendentals=0),
        name="last_moment",
    )(moments, face, wave2)
    moments = lax.all_to_all(everyone, ("gx", "gy"), split_axis=0, concat_axis=0, tiled=True)
    shift_field = pl.pallas_call(
        functools.partial(combine_kernel, n_gy, ty),
        out_shape=jax.ShapeDtypeStruct((rows, grid_y, NT), F32),
        in_specs=vmem(1 + n_gy),
        out_specs=pl.BlockSpec(memory_space=pltpu.VMEM),
        compiler_params=pltpu.CompilerParams(vmem_limit_bytes=16 * 2**20),
        name="combine_waves",
    )(moments, *arrived)
    return (fault, shift_field)


def solution(mesh):
    return jax.shard_map(
        on_device,
        mesh=mesh,
        in_specs=(P("gx", "gy", None), P(), P(), P(), P()),
        out_specs=(P("gx", "gy", None), P(("gx", "gy"), None, None)),
        check_vma=False,
    )
```
